128 devices in a mesh: ctx: 8 (over y_hi, z), fsdp: 16 (over x, y_lo, core).
Axes of the slice: x: 4, y: 4 (y_hi: 2, y_lo: 2; y = y_hi * 2 + y_lo), z: 4, core: 2. Of those that a mesh axis runs over, the one named last changes fastest.
Arguments:
- hidden_in: bfloat16 [16384, 2048], P(('ctx', 'fsdp')), may hold values from -6 to 6
- teacher: bfloat16 [16384, 2048], P(('ctx', 'fsdp')), may hold values from -6 to 6
- doc_ids: int32 [16, 1024], P('fsdp'), may hold values from 0 to 3, as said below
- valid_mask: int32 [16384], P(('ctx', 'fsdp')), may hold values from 0 to 1
- norm1_gain: bfloat16 [2048], P('fsdp'), may hold values from 0.5 to 1.5
- w_query: bfloat16 [2048, 2048], P('fsdp'), may hold values from -0.125 to 0.125
- w_key: bfloat16 [2048, 256], P('fsdp'), may hold values from -0.125 to 0.125
- w_value: bfloat16 [2048, 256], P('fsdp'), may hold values from -0.125 to 0.125
- w_out: bfloat16 [2048, 2048], P('fsdp'), may hold values from -0.75 to 0.75
- norm2_gain: bfloat16 [2048], P('fsdp'), may hold values from 0.5 to 1.5
- w_gate: bfloat16 [2048, 5632], P('fsdp'), may hold values from -0.125 to 0.125
- w_up: bfloat16 [2048, 5632], P('fsdp'), may hold values from -0.125 to 0.125
- w_down: bfloat16 [5632, 2048], P('fsdp'), may hold values from -0.078125 to 0.078125
Outputs:
- layer_out: bfloat16 [16384, 2048], P(('ctx', 'fsdp'))
- mean_loss: float32 [], replicated
- input_grad: float32 [16384, 2048], P(('ctx', 'fsdp'))
- grad_norm1_gain: float32 [2048], P('fsdp')
- grad_w_query: float32 [2048, 2048], P('fsdp')
- grad_w_key: float32 [2048, 256], P('fsdp')
- grad_w_value: float32 [2048, 256], P('fsdp')
- grad_w_out: float32 [2048, 2048], P('fsdp')
- grad_norm2_gain: float32 [2048], P('fsdp')
- grad_w_gate: float32 [2048, 5632], P('fsdp')
- grad_w_up: float32 [2048, 5632], P('fsdp')
- grad_w_down: float32 [5632, 2048], P('fsdp')
The draws below stay inside these ranges and needn't reach their ends.
Inputs may be any that keep to these rules, and one draw needn't show every extreme that they name: `doc_ids`: document numbers never fall along a sequence; every sequence holds exactly four documents; its first or its last document has 512 positions or more, the others 1024 // 10 or more.
All inputs are finite; a program needn't handle non-finite values.
Results may differ from the reference program's by a relative error of at most 0.023.
Values may be sent and summed in bfloat16 or wider, within the bound.
A program may use at most 320 MiB of HBM per device.

```python
import math
import jax
import jax.numpy as jnp
from jax import lax

D = 2048
HEADS = 32
KV_HEADS = 4
HEAD_DIM = 64
FF = 5632
LENGTH = 1024
SEQ_DEV = 1
BLK = 64
TOK_DEV = 128
SEQS = 16
TOKENS = 16384
QD = 2048
KVD = 256
N_CTX = 8
N_FSDP = 16


def draw_doc_ids(key, part):
    key = jax.random.fold_in(key, 11)
    key_cut = jax.random.fold_in(key, 1)
    key_side = jax.random.fold_in(key, 2)
    least = LENGTH // 10
    longest = LENGTH // 2
    spare = LENGTH - longest - 3 * least
    offsets = jax.random.randint(key_cut, (3, SEQS, 1), 0, spare + 1)
    lowest = jnp.minimum(jnp.minimum(offsets[0], offsets[1]), offsets[2])
    highest = jnp.maximum(jnp.maximum(offsets[0], offsets[1]), offsets[2])
    middle = offsets[0] + offsets[1] + offsets[2] - lowest - highest
    side = jax.random.randint(key_side, (SEQS, 1), 0, 2)
    first_len = least + lowest + side * (longest - least)
    second_len = least + middle - lowest
    third_len = least + highest - middle
    bound_one = first_len
    bound_two = bound_one + second_len
    bound_three = bound_two + third_len
    positions = jnp.arange(LENGTH, dtype=jnp.int32)[None, :]
    first = (positions >= bound_one).astype(jnp.int32)
    second = (positions >= bound_two).astype(jnp.int32)
    third = (positions >= bound_three).astype(jnp.int32)
    return first + second + third


def draw_valid_mask(key, part):
    key = jax.random.fold_in(key, 23)
    row_ids = jnp.arange(TOKENS, dtype=jnp.int32)
    device_ids = row_ids // TOK_DEV
    last_device = max(TOKENS // TOK_DEV - 1, 1)
    limits = 250 + 500 * device_ids // last_device
    draws = jax.random.randint(key, (TOKENS,), 0, 1000)
    return (draws < limits).astype(jnp.int32)


def levels(stream_key, shape, split, low, top_value):
    loudness = 1.0
    for dim, shards_of in split:
        steps = jax.random.uniform(jax.random.fold_in(jax.random.fold_in(stream_key, 6), dim), (shards_of,), jnp.float32, low / len(split), top_value / len(split))
        loudness = loudness * jnp.repeat(jnp.exp(steps), shape[dim] // shards_of).reshape((-1,) + (1,) * (len(shape) - 1 - dim))
    return loudness


def normal_values(rng, shape, deviation, limit, pieces=(), held_as=jnp.bfloat16):
    array = jax.random.normal(rng, shape, jnp.float32) * deviation
    if len(pieces) > 0:
        array = levels(rng, shape, pieces, -0.22, 0.18) * array
    return jnp.clip(array, min=-limit, max=limit).astype(held_as)


def setup_inputs(seed: int = 0) -> dict:
    key_of = jax.random.split(jax.random.key(seed), 14)
    hidden_in = normal_values(key_of[0], (TOKENS, D), 1.0, 6.0, ((0, 128),))
    teacher = normal_values(key_of[1], (TOKENS, D), 1.0, 6.0, ((0, 128),))
    doc_ids = draw_doc_ids(jax.random.fold_in(key_of[13], 71), 0)
    valid_mask = draw_valid_mask(jax.random.fold_in(key_of[13], 71), 0)
    norm1_gain = jnp.clip(1.0 + 0.1 * jax.random.normal(key_of[4], (D,), jnp.float32), 0.5, 1.5).astype(jnp.bfloat16)
    w_query = normal_values(key_of[5], (D, QD), D ** -0.5, 0.125, ((0, 16),))
    w_key = normal_values(key_of[6], (D, KVD), D ** -0.5, 0.125, ((0, 16),))
    w_value = normal_values(key_of[7], (D, KVD), D ** -0.5, 0.125, ((0, 16),))
    w_out = normal_values(key_of[8], (QD, D), (QD // 32) ** -0.5, 0.75, ((0, 16),))
    norm2_gain = jnp.clip(1.0 + 0.1 * jax.random.normal(key_of[9], (D,), jnp.float32), 0.5, 1.5).astype(jnp.bfloat16)
    w_gate = normal_values(key_of[10], (D, FF), D ** -0.5, 0.125, ((0, 16),))
    w_up = normal_values(key_of[11], (D, FF), D ** -0.5, 0.125, ((0, 16),))
    w_down = normal_values(key_of[12], (FF, D), FF ** -0.5, 0.078125, ((0, 16),))
    return dict(hidden_in=hidden_in, teacher=teacher, doc_ids=doc_ids, valid_mask=valid_mask, norm1_gain=norm1_gain, w_query=w_query, w_key=w_key, w_value=w_value, w_out=w_out, norm2_gain=norm2_gain, w_gate=w_gate, w_up=w_up, w_down=w_down)


EPSILON = 1e-05
THETA = 10000.0
NEGATIVE = -1e+30
HIGH = lax.Precision.HIGHEST

@jax.custom_vjp
def low(v):
    return lax.optimization_barrier(v.astype(jnp.bfloat16)).astype(jnp.float32)

@jax.custom_vjp
def low_back(v):
    return v

def low_keep(v):
    return (low(v), None)

def low_pass(kept, grad):
    return (grad,)

def back_keep(v):
    return (v, None)

def back_low(kept, grad):
    return (low(grad),)
low.defvjp(low_keep, low_pass)
low_back.defvjp(back_keep, back_low)

def tables(positions):
    indices = jnp.arange(HEAD_DIM // 2, dtype=jnp.int32).astype(jnp.float32)
    frequency = THETA ** (-(indices * 2.0 / HEAD_DIM))
    angles = positions.astype(jnp.float32)[:, None] * frequency[None, :]
    angles = jnp.concatenate([angles, angles], axis=1)
    return (jnp.cos(angles), jnp.sin(angles))

def rotate(values, cosines, sines):
    half_dim = values.shape[-1] // 2
    turned = jnp.concatenate([-values[..., half_dim:], values[..., :half_dim]], axis=-1)
    return values * cosines[None, :, None, :] + turned * sines[None, :, None, :]

def attention(queries, key_rot, value_rot, documents):
    seq_count, length = (queries.shape[0], queries.shape[1])
    row_block = min(512, length)
    factor = 1.0 / math.sqrt(HEAD_DIM)
    key_pos = jnp.arange(length, dtype=jnp.int32)
    grouped = queries.reshape(seq_count, length, KV_HEADS, HEADS // KV_HEADS, HEAD_DIM)

    def one_block(index):
        first_row = index * row_block
        query_block = lax.dynamic_slice_in_dim(grouped, first_row, row_block, 1)
        query_docs = lax.dynamic_slice_in_dim(documents, first_row, row_block, 1)
        query_pos = first_row + jnp.arange(row_block, dtype=jnp.int32)
        raw_scores = jnp.einsum('grkhd,gskd->gkhrs', query_block, key_rot, precision=HIGH)
        scores = low_back(raw_scores * factor)
        allowed = (query_pos[:, None] >= key_pos[None, :])[None] & (query_docs[:, :, None] == documents[:, None, :])
        masked = jnp.where(allowed[:, None, None], scores, NEGATIVE)
        highest = lax.optimization_barrier(jnp.max(masked, axis=-1, keepdims=True))
        exponent = jnp.exp(masked - highest)
        weights_soft = exponent / lax.optimization_barrier(jnp.sum(exponent, axis=-1, keepdims=True))
        mixed_out = jnp.einsum('gkhrs,gskd->grkhd', low(weights_soft), value_rot, precision=HIGH)
        return mixed_out.reshape(seq_count, row_block, HEADS * HEAD_DIM)
    blocks = lax.map(jax.checkpoint(one_block), jnp.arange(length // row_block, dtype=jnp.int32))
    return jnp.moveaxis(blocks, 0, 1).reshape(seq_count, length, HEADS * HEAD_DIM)

def forward_pass(params, inputs, targets, weights_valid, documents, count_all):
    gain1, query_weight, key_weight, value_weight, out_weight, gain2, gate_weight, up_weight, down_weight = params
    seq_count, length = (inputs.shape[0], inputs.shape[1])
    flat_in = inputs.reshape(seq_count * length, D)
    normed1 = flat_in * lax.rsqrt(lax.optimization_barrier(jnp.mean(flat_in * flat_in, axis=1, keepdims=True)) + EPSILON)
    hidden1 = low(normed1 * gain1)
    query_proj = low_back(jnp.dot(hidden1, query_weight, precision=HIGH))
    key_proj = low_back(jnp.dot(hidden1, key_weight, precision=HIGH))
    value_proj = low(low_back(jnp.dot(hidden1, value_weight, precision=HIGH)))
    cosines, sines = tables(jnp.arange(length, dtype=jnp.int32))
    query_rot = low(rotate(query_proj.reshape(seq_count, length, HEADS, HEAD_DIM), cosines, sines))
    key_rot = low(rotate(key_proj.reshape(seq_count, length, KV_HEADS, HEAD_DIM), cosines, sines))
    value_rot = value_proj.reshape(seq_count, length, KV_HEADS, HEAD_DIM)
    attended = attention(query_rot, key_rot, value_rot, documents)
    mixed_low = low(low_back(attended)).reshape(seq_count * length, HEADS * HEAD_DIM)
    resid1 = flat_in + low_back(jnp.dot(mixed_low, out_weight, precision=HIGH))
    normed2 = resid1 * lax.rsqrt(lax.optimization_barrier(jnp.mean(resid1 * resid1, axis=1, keepdims=True)) + EPSILON)
    hidden2 = low(normed2 * gain2)
    gate_proj = low_back(jnp.dot(hidden2, gate_weight, precision=HIGH))
    up_proj = low_back(jnp.dot(hidden2, up_weight, precision=HIGH))
    product = low(jax.nn.silu(gate_proj) * up_proj)
    result = resid1 + low_back(jnp.dot(product, down_weight, precision=HIGH))
    mismatch = result - targets.reshape(seq_count * length, D)
    loss_value = jnp.sum(weights_valid.reshape(-1) * lax.optimization_barrier(jnp.mean(mismatch * mismatch, axis=1))) / count_all
    return (loss_value, result.reshape(seq_count, length, D))

def reference(hidden_in, teacher, doc_ids, valid_mask, norm1_gain, w_query, w_key, w_value, w_out, norm2_gain, w_gate, w_up, w_down):
    natural_blocks = jnp.arange(2 * N_CTX, dtype=jnp.int32)
    owners = jnp.minimum(natural_blocks, 2 * N_CTX - 1 - natural_blocks).astype(jnp.int32)
    slots = (natural_blocks >= N_CTX).astype(jnp.int32)
    ctx_ids = jnp.arange(N_CTX, dtype=jnp.int32)
    placed = jnp.stack([ctx_ids, 2 * N_CTX - 1 - ctx_ids], axis=1).astype(jnp.int32)

    def to_natural(values):
        tail = values.shape[1:]
        layered = values.reshape((N_CTX, N_FSDP, 2, BLK, SEQ_DEV) + tail)
        picked = layered[owners, :, slots]
        order = (1, 3, 0, 2) + tuple(range(4, picked.ndim))
        return jnp.transpose(picked, order).reshape((SEQS, LENGTH) + tail)

    def from_natural(values):
        tail = values.shape[2:]
        layered = values.reshape((N_FSDP, SEQ_DEV, 2 * N_CTX, BLK) + tail)
        picked = layered[:, :, placed]
        order = (2, 0, 3, 4, 1) + tuple(range(5, picked.ndim))
        return jnp.transpose(picked, order).reshape((TOKENS,) + tail)
    params = tuple((w.astype(jnp.float32) for w in (norm1_gain, w_query, w_key, w_value, w_out, norm2_gain, w_gate, w_up, w_down)))
    per_group = math.gcd(SEQS, max(1, 4096 // LENGTH))
    rounds = SEQS // per_group
    inputs_all = to_natural(hidden_in.astype(jnp.float32)).reshape(rounds, per_group, LENGTH, D)
    targets_all = to_natural(teacher.astype(jnp.float32)).reshape(rounds, per_group, LENGTH, D)
    masks_all = to_natural(valid_mask.astype(jnp.float32)).reshape(rounds, per_group, LENGTH)
    docs_all = doc_ids.reshape(rounds, per_group, LENGTH)
    count_all = jnp.sum(valid_mask.astype(jnp.float32))

    def one_round(totals, entries):
        inputs_g, targets_g, masks_g, docs_g = entries

        def run(pars, inputs_here):
            return forward_pass(pars, inputs_here, targets_g, masks_g, docs_g, count_all)
        loss_value, pull, result = jax.vjp(run, params, inputs_g, has_aux=True)
        grad_params, grad_inputs = pull(jnp.ones_like(loss_value))
        totals = jax.tree.map(jnp.add, totals, (grad_params, loss_value))
        return (totals, (result, grad_inputs))
    start_totals = (tuple((jnp.zeros_like(p) for p in params)), jnp.zeros((), jnp.float32))
    totals, outputs = lax.scan(one_round, start_totals, (inputs_all, targets_all, masks_all, docs_all))
    grad_params, loss_value = totals
    results, grad_inputs = outputs
    layer_out = from_natural(results.reshape(SEQS, LENGTH, D)).astype(jnp.bfloat16)
    input_grad = from_natural(grad_inputs.reshape(SEQS, LENGTH, D))
    return (layer_out, loss_value, input_grad, grad_params[0], grad_params[1], grad_params[2], grad_params[3], grad_params[4], grad_params[5], grad_params[6], grad_params[7], grad_params[8])
```

```python
import math

import jax
import jax.numpy as jnp
from jax import lax
from jax.sharding import Mesh, PartitionSpec as P

D = 2048
HEADS = 32
KV_HEADS = 4
HD = 64
FF = 5632
KVD = 256
EPSILON = 1e-05
THETA = 10000.0
NEGATIVE = -1e30
AXES = ("y_hi", "z", "x", "y_lo", "core")
TP = ("x", "core")
CTX = ("y_hi", "z")
BF = jnp.bfloat16
F32 = jnp.float32


def dot(a, b, ca, cb):
    return lax.dot_general(a, b, (((ca,), (cb,)), ((), ())), preferred_element_type=F32)


def tables(positions):
    indices = jnp.arange(HD // 2, dtype=jnp.int32).astype(F32)
    frequency = THETA ** (-(indices * 2.0 / HD))
    angles = positions.astype(F32)[:, None] * frequency[None, :]
    angles = jnp.concatenate([angles, angles], axis=1)
    return jnp.cos(angles), jnp.sin(angles)


def positions_of(c):
    t = jnp.arange(64, dtype=jnp.int32)
    return jnp.concatenate([c * 64 + t, (15 - c) * 64 + t])


def rotate(u, cos, sin):
    turned = jnp.concatenate([-u[..., HD // 2 :], u[..., : HD // 2]], axis=-1)
    return u * cos + turned * sin


def unrotate(w, cos, sin):
    s = w * sin
    turned = jnp.concatenate([s[..., HD // 2 :], -s[..., : HD // 2]], axis=-1)
    return w * cos + turned


def ag_tp(v):
    return lax.all_gather(v, TP, axis=0, tiled=True)


def rs_tp(v):
    return lax.psum_scatter(v.astype(BF), TP, scatter_dimension=0, tiled=True).astype(F32)


def spread_columns(w):
    n = w.shape[1] // 16
    parts = w.reshape(128, 4, 2, 2, n).transpose(1, 3, 0, 2, 4).reshape(8, 128, 2 * n)
    got = lax.all_to_all(parts, TP, 0, 0)
    got = lax.all_gather(got, "y_lo", axis=0)
    got = got.reshape(2, 4, 2, 128, 2 * n).transpose(1, 0, 2, 3, 4)
    return got.reshape(D, 2 * n)


def spread_kv(w):
    parts = w.reshape(128, 4, 1, 64).transpose(1, 2, 0, 3)
    parts = jnp.broadcast_to(parts, (4, 2, 128, 64)).reshape(8, 128, 64)
    got = lax.all_to_all(parts, TP, 0, 0)
    got = lax.all_gather(got, "y_lo", axis=0)
    return got.reshape(2, 4, 2, 128, 64).transpose(1, 0, 2, 3, 4).reshape(D, 64)


def return_rows(g):
    n = g.shape[1]
    g = g.astype(BF).reshape(4, 2, 2, 8, 16, n).transpose(1, 3, 0, 2, 4, 5)
    g = lax.psum_scatter(g.reshape(16, 8 * 16, n), ("y_lo", "y_hi", "z"), scatter_dimension=0, tiled=True)
    g = lax.all_to_all(g.reshape(8, 16, n), TP, 0, 0)
    g = lax.all_gather(g, CTX, axis=0)
    return g.transpose(0, 2, 1, 3).reshape(128, 8, n).astype(F32)


def return_columns(g):
    r = g.shape[0] // 2
    g = g.astype(BF).reshape(2, r, 8, 256).transpose(0, 2, 1, 3).reshape(16, r, 256)
    g = lax.psum_scatter(g, ("y_lo", "y_hi", "z"), scatter_dimension=0, tiled=True)
    g = lax.all_gather(g.reshape(r, 256), CTX, axis=1, tiled=True)
    return g.astype(F32)


def local(hidden_in, teacher, doc_ids, valid_mask, norm1_gain, w_query, w_key, w_value, w_out, norm2_gain, w_gate, w_up, w_down):
    c = lax.axis_index(CTX)
    factor = 1.0 / math.sqrt(HD)
    g1 = norm1_gain.astype(F32)
    g2 = norm2_gain.astype(F32)
    valid = valid_mask.astype(F32)
    count = lax.psum(jnp.sum(valid), AXES)

    def fold(g, w):
        return (g[:, None] * w.astype(F32)).astype(BF)

    wqkv = jnp.concatenate([spread_columns(fold(g1, w_query)), spread_kv(fold(g1, w_key)), spread_kv(fold(g1, w_value))], axis=1)
    wgu = jnp.concatenate([spread_columns(fold(g2, w_gate)), spread_columns(fold(g2, w_up))], axis=1)
    wo = lax.all_gather(w_out, "y_lo", axis=0, tiled=True)
    wd = lax.all_gather(w_down, "y_lo", axis=0, tiled=True)
    docs = ag_tp(doc_ids)

    qpos = positions_of(c)
    kpos = jax.vmap(positions_of)(jnp.arange(8, dtype=jnp.int32)).reshape(1024)
    cos, sin = tables(qpos)
    qdoc = jnp.take(docs, qpos, axis=1)
    kdoc = jnp.take(docs, kpos, axis=1)
    allowed = (qpos[:, None] >= kpos[None, :])[None] & (qdoc[:, :, None] == kdoc[:, None, :])

    x = hidden_in.astype(F32)
    r1 = lax.rsqrt(jnp.mean(x * x, axis=1, keepdims=True) + EPSILON)
    n1 = x * r1
    n1_all = ag_tp(n1.astype(BF))
    qkv = dot(n1_all, wqkv, 1, 0)
    q = rotate(qkv[:, :256].reshape(8, 128, 4, HD), cos[None, :, None], sin[None, :, None]).astype(BF)
    k = rotate(qkv[:, 256:320].reshape(8, 128, HD), cos[None], sin[None]).astype(BF)
    v = qkv[:, 320:].reshape(8, 128, HD).astype(BF)
    kv = lax.all_gather(jnp.concatenate([k, v], axis=2), CTX, axis=1, tiled=True)
    k_all, v_all = kv[..., :HD], kv[..., HD:]

    s = jnp.einsum("sqhd,skd->shqk", q, k_all, preferred_element_type=F32) * factor
    s = jnp.where(allowed[:, None], s, NEGATIVE)
    top = jnp.max(s, axis=-1, keepdims=True)
    e = jnp.exp(s - top)
    total = jnp.sum(e, axis=-1, keepdims=True)
    lse = top + jnp.log(total)
    a = jnp.einsum("shqk,skd->sqhd", (e / total).astype(BF), v_all, preferred_element_type=F32)
    a = a.astype(BF).reshape(1024, 256)

    y1 = x + rs_tp(dot(a, wo, 1, 0))
    r2 = lax.rsqrt(jnp.mean(y1 * y1, axis=1, keepdims=True) + EPSILON)
    n2 = y1 * r2
    n2_all = ag_tp(n2.astype(BF))
    gu = dot(n2_all, wgu, 1, 0)
    gate, up = gu[:, :704], gu[:, 704:]
    sg = jax.nn.sigmoid(gate)
    act = gate * sg
    mid = (act * up).astype(BF)
    y = y1 + rs_tp(dot(mid, wd, 1, 0))
    miss = y - teacher.astype(F32)
    loss_here = jnp.sum(valid * jnp.mean(miss * miss, axis=1))
    dy = valid[:, None] * miss
    dy_all = ag_tp(dy.astype(BF))

    grad_down = dot(mid, dy_all, 0, 0)
    dmid = dot(dy_all, wd, 1, 1)
    dgate = (dmid * up * sg * (1.0 + gate * (1.0 - sg))).astype(BF)
    dup = (dmid * act).astype(BF)
    dgu = jnp.concatenate([dgate, dup], axis=1)
    grad_gu = dot(n2_all, dgu, 0, 0)
    u2 = rs_tp(dot(dgu, wgu, 1, 1))
    dy1 = dy + r2 * (u2 - n2 * jnp.mean(u2 * n2, axis=1, keepdims=True))
    da_all = ag_tp(dy1.astype(BF))
    grad_out = dot(a, da_all, 0, 0)
    da = dot(da_all, wo, 1, 1).astype(BF).reshape(8, 128, 4, HD)

    s = jnp.einsum("sqhd,skd->shqk", q, k_all, preferred_element_type=F32) * factor
    probs = jnp.exp(jnp.where(allowed[:, None], s, NEGATIVE) - lse)
    dv = jnp.einsum("shqk,sqhd->skd", probs.astype(BF), da, preferred_element_type=F32)
    dp = jnp.einsum("sqhd,skd->shqk", da, v_all, preferred_element_type=F32)
    ds = (probs * (dp - jnp.sum(probs * dp, axis=-1, keepdims=True))).astype(BF)
    dq = jnp.einsum("shqk,skd->sqhd", ds, k_all, preferred_element_type=F32) * factor
    dk = jnp.einsum("shqk,sqhd->skd", ds, q, preferred_element_type=F32) * factor
    dkv = jnp.concatenate([dk, dv], axis=2).astype(BF)
    dkv = lax.psum_scatter(dkv, CTX, scatter_dimension=1, tiled=True).astype(F32)
    dq = unrotate(dq, cos[None, :, None], sin[None, :, None]).astype(BF).reshape(1024, 256)
    dk = unrotate(dkv[..., :HD], cos[None], sin[None]).astype(BF).reshape(1024, HD)
    dv = dkv[..., HD:].astype(BF).reshape(1024, HD)
    dqkv = jnp.concatenate([dq, dk, dv], axis=1)
    grad_qkv = dot(n1_all, dqkv, 0, 0)
    u1 = rs_tp(dot(dqkv, wqkv, 1, 1))
    loss = lax.psum(loss_here, AXES) / count
    scale = 2.0 / (D * count)
    input_grad = (dy1 + r1 * (u1 - n1 * jnp.mean(u1 * n1, axis=1, keepdims=True))) * scale

    ga = return_rows(jnp.concatenate([grad_qkv, grad_gu], axis=1))
    gb = return_columns(jnp.concatenate([grad_out.reshape(2, 128, D), grad_down.reshape(2, 352, D)], axis=1).reshape(960, D))

    def columns(part):
        n = part.shape[2] // 2
        return part.reshape(128, 4, 2, 2, n).transpose(0, 1, 3, 2, 4).reshape(128, 16 * n)

    gq = columns(ga[:, :, :256])
    gk = ga[:, :, 256:320].reshape(128, 4, 2, HD).sum(2).reshape(128, KVD)
    gv = ga[:, :, 320:384].reshape(128, 4, 2, HD).sum(2).reshape(128, KVD)
    gg = columns(ga[:, :, 384 : 384 + 704])
    gp = columns(ga[:, :, 384 + 704 :])

    def rowsum(w, g):
        return jnp.sum(w.astype(F32) * g, axis=1)

    gain1 = (rowsum(w_query, gq) + rowsum(w_key, gk) + rowsum(w_value, gv)) * scale
    gain2 = (rowsum(w_gate, gg) + rowsum(w_up, gp)) * scale
    s1 = (g1 * scale)[:, None]
    s2 = (g2 * scale)[:, None]
    return (
        y.astype(BF), loss, input_grad, gain1, gq * s1, gk * s1, gv * s1, gb[:128] * scale,
        gain2, gg * s2, gp * s2, gb[128:] * scale,
    )


def solution(mesh):
    fine = Mesh(mesh.devices.reshape(2, 4, 4, 2, 2), AXES)
    rows = ("y_hi", "z", "x", "y_lo", "core")
    fs = ("x", "y_lo", "core")
    token, shard = P(rows, None), P(fs, None)
    return jax.shard_map(
        local,
        mesh=fine,
        in_specs=(token, token, shard, P(rows), P(fs), shard, shard, shard, shard, P(fs), shard, shard, shard),
        out_specs=(token, P(), token, P(fs), shard, shard, shard, shard, P(fs), shard, shard, shard),
        check_vma=False,
    )
```

```python
import functools
import math

import jax
import jax.numpy as jnp
from jax import lax
from jax.experimental import pallas as pl
from jax.experimental.pallas import tpu as pltpu
from jax.sharding import Mesh, PartitionSpec as P

D = 2048
HEADS = 32
KV_HEADS = 4
HD = 64
FF = 5632
KVD = 256
EPSILON = 1e-05
THETA = 10000.0
NEGATIVE = -1e30
AXES = ("y_hi", "z", "x", "y_lo", "core")
TP = ("x", "core")
CTX = ("y_hi", "z")
BF = jnp.bfloat16
F32 = jnp.float32


def dot(a, b, ca, cb):
    return lax.dot_general(a, b, (((ca,), (cb,)), ((), ())), preferred_element_type=F32)


def tables(positions):
    indices = jnp.arange(HD // 2, dtype=jnp.int32).astype(F32)
    frequency = THETA ** (-(indices * 2.0 / HD))
    angles = positions.astype(F32)[:, None] * frequency[None, :]
    angles = jnp.concatenate([angles, angles], axis=1)
    return jnp.cos(angles), jnp.sin(angles)


def positions_of(c):
    t = jnp.arange(64, dtype=jnp.int32)
    return jnp.concatenate([c * 64 + t, (15 - c) * 64 + t])


def rotate(u, cos, sin):
    turned = jnp.concatenate([-u[..., HD // 2 :], u[..., : HD // 2]], axis=-1)
    return u * cos + turned * sin


def unrotate(w, cos, sin):
    s = w * sin
    turned = jnp.concatenate([s[..., HD // 2 :], -s[..., : HD // 2]], axis=-1)
    return w * cos + turned


MESH = pl.DeviceIdType.MESH
HALVES = (pl.ds(0, 64), pl.ds(64, 64))
VM = pl.BlockSpec(memory_space=pltpu.VMEM)
HB = pl.BlockSpec(memory_space=pl.ANY)


def params(number):
    return pltpu.CompilerParams(collective_id=number, has_side_effects=True, vmem_limit_bytes=56 * 2**20)


def send(src, dst, sems, i, device):
    copy = pltpu.make_async_remote_copy(
        src_ref=src, dst_ref=dst, send_sem=sems[0].at[i], recv_sem=sems[1].at[i], device_id=device, device_id_type=MESH
    )
    copy.start()
    return copy


def meet(devices):
    barrier = pltpu.get_barrier_semaphore()
    for device in devices:
        pl.semaphore_signal(barrier, inc=1, device_id=device, device_id_type=MESH)
    pl.semaphore_wait(barrier, len(devices))


class Ring:
    def __init__(self):
        x, core = lax.axis_index("x"), lax.axis_index("core")
        self.x, self.core = x, core
        self.right_x, self.left_x, self.far_x = lax.rem(x + 1, 4), lax.rem(x + 3, 4), lax.rem(x + 2, 4)
        self.right, self.left, self.sibling = {"x": self.right_x}, {"x": self.left_x}, {"core": 1 - core}


class Gather:
    def __init__(self, ring, own, out, sems, local_sem):
        self.r, self.own, self.out, self.sems, self.local_sem = ring, own, out, sems, local_sem
        self.c = {}

    def slot(self, x, half):
        return self.out.at[x * 2 + self.r.core, HALVES[half]]

    def start(self, half):
        r, src, dst = self.r, self.own.at[HALVES[half]], self.slot(self.r.x, half)
        first, second = (r.right, r.left) if half == 0 else (r.left, r.right)
        i, j = (0, 3) if half == 0 else (2, 1)
        self.c[i] = send(src, dst, self.sems, i, first)
        self.c[j] = send(src, dst, self.sems, j, second)
        self.c[6 + half] = send(src, dst, self.sems, 6 + half, r.sibling)
        copy = pltpu.make_async_copy(src, dst, self.local_sem.at[half])
        copy.start()
        self.c[14 + half] = copy

    def finish(self):
        r, c = self.r, self.c
        for got, x, half, onward, core_i in (
            (0, r.left_x, 0, (4, r.right), 8),
            (2, r.right_x, 1, (5, r.left), 11),
            (1, r.left_x, 1, None, 9),
            (3, r.right_x, 0, None, 10),
            (4, r.far_x, 0, None, 12),
            (5, r.far_x, 1, None, 13),
        ):
            c[got].wait_recv()
            block = self.slot(x, half)
            if onward is not None:
                c[onward[0]] = send(block, block, self.sems, onward[0], onward[1])
            c[core_i] = send(block, block, self.sems, core_i, r.sibling)
        for i in range(6, 14):
            c[i].wait_recv()
        for i in range(14):
            c[i].wait_send()
        c[14].wait()
        c[15].wait()


class Scatter:
    def __init__(self, ring, parts, held, got, sems):
        self.r, self.parts, self.held, self.got, self.sems = ring, parts, held, got, sems
        self.c = {}

    def pair(self, i, half):
        r = self.r
        x = (r.far_x, r.right_x, r.left_x, r.x)[i]

        def body(k, _):
            rows = pl.ds(half * 64 + k * 16, 16)
            total = self.parts[x * 2 + r.core, rows, :].astype(F32) + self.got[i, rows, :].astype(F32)
            self.held[i, rows, :] = total.astype(BF)
            return 0

        lax.fori_loop(0, 4, body, 0)

    def onward(self, i, half, slot):
        def body(k, _):
            rows = pl.ds(half * 64 + k * 16, 16)
            total = self.held[i, rows, :].astype(F32) + self.got[slot, rows, :].astype(F32)
            self.held[i, rows, :] = total.astype(BF)
            return 0

        lax.fori_loop(0, 4, body, 0)

    def run(self):
        r, c, held, got, sems = self.r, self.c, self.held, self.got, self.sems
        blocks = (r.far_x, r.right_x, r.left_x, r.x)
        for i in range(4):
            c[i] = send(self.parts.at[blocks[i] * 2 + (1 - r.core)], got.at[i], sems, i, r.sibling)
        a, b = HALVES
        c[0].wait_recv()
        self.pair(0, 0)
        c[4] = send(held.at[0, a], got.at[4, a], sems, 4, r.right)
        self.pair(0, 1)
        c[5] = send(held.at[0, b], got.at[4, b], sems, 5, r.left)
        c[1].wait_recv()
        self.pair(1, 1)
        c[6] = send(held.at[1, b], got.at[5, b], sems, 6, r.right)
        c[2].wait_recv()
        self.pair(2, 0)
        c[7] = send(held.at[2, a], got.at[5, a], sems, 7, r.left)
        self.pair(1, 0)
        self.pair(2, 1)
        c[4].wait_recv()
        self.onward(1, 0, 4)
        c[8] = send(held.at[1, a], got.at[6, a], sems, 8, r.right)
        c[5].wait_recv()
        self.onward(2, 1, 4)
        c[9] = send(held.at[2, b], got.at[6, b], sems, 9, r.left)
        c[3].wait_recv()

    def ready(self, half):
        c = self.c
        if half == 0:
            c[7].wait_recv()
            c[8].wait_recv()
        else:
            c[6].wait_recv()
            c[9].wait_recv()

    def total(self, rows):
        r = self.r
        return (
            self.parts[r.x * 2 + r.core, rows, :].astype(F32)
            + self.got[3, rows, :].astype(F32)
            + self.got[5, rows, :].astype(F32)
            + self.got[6, rows, :].astype(F32)
        )

    def finish(self):
        for i in range(10):
            self.c[i].wait_send()


def norm_scale(v):
    return lax.rsqrt(jnp.mean(v * v, axis=1, keepdims=True) + EPSILON)


def exchange(number, op, parts, inputs, outs, gather=True):
    n_in, n_out = len(inputs), len(outs)

    def kernel(*refs):
        parts_ref, ins = refs[0], refs[1 : 1 + n_in]
        out_refs = refs[1 + n_in : 1 + n_in + n_out]
        rest = refs[1 + n_in + n_out :]
        if gather:
            all_ref, rest = rest[0], rest[1:]
        held, got, rs_s, rs_r = rest[:4]
        ring = Ring()
        meet((ring.right, ring.left, ring.sibling))
        scatter = Scatter(ring, parts_ref, held, got, (rs_s, rs_r))
        if gather:
            own, ag_s, ag_r, loc = rest[4:]
            gath = Gather(ring, own, all_ref, (ag_s, ag_r), loc)
        scatter.run()
        for half in range(2):
            scatter.ready(half)

            def body(k, _, half=half):
                rows = pl.ds(half * 64 + k * 16, 16)
                last = op(rows, scatter.total(rows), ins, out_refs)
                if gather:
                    own[rows, :] = last.astype(BF)
                return 0

            lax.fori_loop(0, 4, body, 0)
            if gather:
                gath.start(half)
        if gather:
            gath.finish()
        scatter.finish()

    shapes = list(outs)
    scratch = [
        pltpu.VMEM((4, 128, D), BF),
        pltpu.VMEM((7, 128, D), BF),
        pltpu.SemaphoreType.DMA((10,)),
        pltpu.SemaphoreType.DMA((10,)),
    ]
    specs = [VM] * n_out
    if gather:
        shapes.append(jax.ShapeDtypeStruct((8, 128, D), BF))
        specs.append(HB)
        scratch += [
            pltpu.VMEM((128, D), BF),
            pltpu.SemaphoreType.DMA((14,)),
            pltpu.SemaphoreType.DMA((14,)),
            pltpu.SemaphoreType.DMA((2,)),
        ]
    return pl.pallas_call(
        kernel,
        out_shape=shapes,
        in_specs=[VM] * (1 + n_in),
        out_specs=specs,
        scratch_shapes=scratch,
        compiler_params=params(number),
        name="exchange%d" % number,
    )(parts, *inputs)


def op_mid(rows, total, ins, outs):
    (x_ref,), (y1_ref,) = ins, outs
    y1 = x_ref[rows, :].astype(F32) + total
    y1_ref[rows, :] = y1
    return y1 * norm_scale(y1)


def op_loss(rows, total, ins, outs):
    y1_ref, teacher_ref, valid_ref = ins
    out_ref, dy_ref, loss_ref = outs
    y = y1_ref[rows, :] + total
    out_ref[rows, :] = y.astype(BF)
    miss = y - teacher_ref[rows, :].astype(F32)
    valid = valid_ref[rows, :]
    loss_ref[rows, :] = valid * jnp.mean(miss * miss, axis=1, keepdims=True)
    dy = valid * miss
    dy_ref[rows, :] = dy
    return dy


def back_norm(v, grad, u):
    r = norm_scale(v)
    n = v * r
    return grad + r * (u - n * jnp.mean(u * n, axis=1, keepdims=True))


def op_back(rows, total, ins, outs):
    (y1_ref, dy_ref), (dy1_ref,) = ins, outs
    dy1 = back_norm(y1_ref[rows, :], dy_ref[rows, :], total)
    dy1_ref[rows, :] = dy1
    return dy1


def op_input(rows, total, ins, outs):
    (x_ref, dy1_ref), (grad_ref,) = ins, outs
    grad_ref[rows, :] = back_norm(x_ref[rows, :].astype(F32), dy1_ref[rows, :], total)
    return None


def ag_tp(v):
    return lax.all_gather(v, TP, axis=0, tiled=True)


def rs_tp(v):
    return lax.psum_scatter(v.astype(BF), TP, scatter_dimension=0, tiled=True).astype(F32)


def spread_columns(w):
    n = w.shape[1] // 16
    parts = w.reshape(128, 4, 2, 2, n).transpose(1, 3, 0, 2, 4).reshape(8, 128, 2 * n)
    got = lax.all_to_all(parts, TP, 0, 0)
    got = lax.all_gather(got, "y_lo", axis=0)
    got = got.reshape(2, 4, 2, 128, 2 * n).transpose(1, 0, 2, 3, 4)
    return got.reshape(D, 2 * n)


def spread_kv(w):
    parts = w.reshape(128, 4, 1, 64).transpose(1, 2, 0, 3)
    parts = jnp.broadcast_to(parts, (4, 2, 128, 64)).reshape(8, 128, 64)
    got = lax.all_to_all(parts, TP, 0, 0)
    got = lax.all_gather(got, "y_lo", axis=0)
    return got.reshape(2, 4, 2, 128, 64).transpose(1, 0, 2, 3, 4).reshape(D, 64)


def return_rows(g):
    n = g.shape[1]
    g = g.astype(BF).reshape(4, 2, 2, 8, 16, n).transpose(1, 3, 0, 2, 4, 5)
    g = lax.psum_scatter(g.reshape(16, 8 * 16, n), ("y_lo", "y_hi", "z"), scatter_dimension=0, tiled=True)
    g = lax.all_to_all(g.reshape(8, 16, n), TP, 0, 0)
    g = lax.all_gather(g, CTX, axis=0)
    return g.transpose(0, 2, 1, 3).reshape(128, 8, n).astype(F32)


def return_columns(g):
    r = g.shape[0] // 2
    g = g.astype(BF).reshape(2, r, 8, 256).transpose(0, 2, 1, 3).reshape(16, r, 256)
    g = lax.psum_scatter(g, ("y_lo", "y_hi", "z"), scatter_dimension=0, tiled=True)
    g = lax.all_gather(g.reshape(r, 256), CTX, axis=1, tiled=True)
    return g.astype(F32)


def local(hidden_in, teacher, doc_ids, valid_mask, norm1_gain, w_query, w_key, w_value, w_out, norm2_gain, w_gate, w_up, w_down):
    c = lax.axis_index(CTX)
    factor = 1.0 / math.sqrt(HD)
    g1 = norm1_gain.astype(F32)
    g2 = norm2_gain.astype(F32)
    valid = valid_mask.astype(F32)
    count = lax.psum(jnp.sum(valid), AXES)

    def fold(g, w):
        return (g[:, None] * w.astype(F32)).astype(BF)

    wqkv = jnp.concatenate([spread_columns(fold(g1, w_query)), spread_kv(fold(g1, w_key)), spread_kv(fold(g1, w_value))], axis=1)
    wgu = jnp.concatenate([spread_columns(fold(g2, w_gate)), spread_columns(fold(g2, w_up))], axis=1)
    wo = lax.all_gather(w_out, "y_lo", axis=0, tiled=True)
    wd = lax.all_gather(w_down, "y_lo", axis=0, tiled=True)
    docs = ag_tp(doc_ids)

    qpos = positions_of(c)
    kpos = jax.vmap(positions_of)(jnp.arange(8, dtype=jnp.int32)).reshape(1024)
    cos, sin = tables(qpos)
    qdoc = jnp.take(docs, qpos, axis=1)
    kdoc = jnp.take(docs, kpos, axis=1)
    allowed = (qpos[:, None] >= kpos[None, :])[None] & (qdoc[:, :, None] == kdoc[:, None, :])

    x = hidden_in.astype(F32)
    r1 = lax.rsqrt(jnp.mean(x * x, axis=1, keepdims=True) + EPSILON)
    n1 = x * r1
    n1_all = ag_tp(n1.astype(BF))
    qkv = dot(n1_all, wqkv, 1, 0)
    q = rotate(qkv[:, :256].reshape(8, 128, 4, HD), cos[None, :, None], sin[None, :, None]).astype(BF)
    k = rotate(qkv[:, 256:320].reshape(8, 128, HD), cos[None], sin[None]).astype(BF)
    v = qkv[:, 320:].reshape(8, 128, HD).astype(BF)
    kv = lax.all_gather(jnp.concatenate([k, v], axis=2), CTX, axis=1, tiled=True)
    k_all, v_all = kv[..., :HD], kv[..., HD:]

    s = jnp.einsum("sqhd,skd->shqk", q, k_all, preferred_element_type=F32) * factor
    s = jnp.where(allowed[:, None], s, NEGATIVE)
    top = jnp.max(s, axis=-1, keepdims=True)
    e = jnp.exp(s - top)
    total = jnp.sum(e, axis=-1, keepdims=True)
    lse = top + jnp.log(total)
    a = jnp.einsum("shqk,skd->sqhd", (e / total).astype(BF), v_all, preferred_element_type=F32)
    a = a.astype(BF).reshape(1024, 256)

    def parts(v):
        return v.astype(BF).reshape(8, 128, D)

    wide = jax.ShapeDtypeStruct((128, D), F32)
    y1, n2_all = exchange(1, op_mid, parts(dot(a, wo, 1, 0)), (hidden_in,), (wide,))
    n2_all = n2_all.reshape(1024, D)
    gu = dot(n2_all, wgu, 1, 0)
    gate, up = gu[:, :704], gu[:, 704:]
    sg = jax.nn.sigmoid(gate)
    act = gate * sg
    mid = (act * up).astype(BF)
    layer_out, dy, loss_rows, dy_all = exchange(
        2,
        op_loss,
        parts(dot(mid, wd, 1, 0)),
        (y1, teacher, valid[:, None]),
        (jax.ShapeDtypeStruct((128, D), BF), wide, jax.ShapeDtypeStruct((128, 1), F32)),
    )
    dy_all = dy_all.reshape(1024, D)

    grad_down = dot(mid, dy_all, 0, 0)
    dmid = dot(dy_all, wd, 1, 1)
    dgate = (dmid * up * sg * (1.0 + gate * (1.0 - sg))).astype(BF)
    dup = (dmid * act).astype(BF)
    dgu = jnp.concatenate([dgate, dup], axis=1)
    grad_gu = dot(n2_all, dgu, 0, 0)
    dy1, da_all = exchange(3, op_back, parts(dot(dgu, wgu, 1, 1)), (y1, dy), (wide,))
    da_all = da_all.reshape(1024, D)
    grad_out = dot(a, da_all, 0, 0)
    da = dot(da_all, wo, 1, 1).astype(BF).reshape(8, 128, 4, HD)

    s = jnp.einsum("sqhd,skd->shqk", q, k_all, preferred_element_type=F32) * factor
    probs = jnp.exp(jnp.where(allowed[:, None], s, NEGATIVE) - lse)
    dv = jnp.einsum("shqk,sqhd->skd", probs.astype(BF), da, preferred_element_type=F32)
    dp = jnp.einsum("sqhd,skd->shqk", da, v_all, preferred_element_type=F32)
    ds = (probs * (dp - jnp.sum(probs * dp, axis=-1, keepdims=True))).astype(BF)
    dq = jnp.einsum("shqk,skd->sqhd", ds, k_all, preferred_element_type=F32) * factor
    dk = jnp.einsum("shqk,sqhd->skd", ds, q, preferred_element_type=F32) * factor
    dkv = jnp.concatenate([dk, dv], axis=2).astype(BF)
    dkv = lax.psum_scatter(dkv, CTX, scatter_dimension=1, tiled=True).astype(F32)
    dq = unrotate(dq, cos[None, :, None], sin[None, :, None]).astype(BF).reshape(1024, 256)
    dk = unrotate(dkv[..., :HD], cos[None], sin[None]).astype(BF).reshape(1024, HD)
    dv = dkv[..., HD:].astype(BF).reshape(1024, HD)
    dqkv = jnp.concatenate([dq, dk, dv], axis=1)
    grad_qkv = dot(n1_all, dqkv, 0, 0)
    (grad_in,) = exchange(4, op_input, parts(dot(dqkv, wqkv, 1, 1)), (hidden_in, dy1), (wide,), gather=False)
    loss = lax.psum(jnp.sum(loss_rows), AXES) / count
    scale = 2.0 / (D * count)
    input_grad = grad_in * scale

    ga = return_rows(jnp.concatenate([grad_qkv, grad_gu], axis=1))
    gb = return_columns(jnp.concatenate([grad_out.reshape(2, 128, D), grad_down.reshape(2, 352, D)], axis=1).reshape(960, D))

    def columns(part):
        n = part.shape[2] // 2
        return part.reshape(128, 4, 2, 2, n).transpose(0, 1, 3, 2, 4).reshape(128, 16 * n)

    gq = columns(ga[:, :, :256])
    gk = ga[:, :, 256:320].reshape(128, 4, 2, HD).sum(2).reshape(128, KVD)
    gv = ga[:, :, 320:384].reshape(128, 4, 2, HD).sum(2).reshape(128, KVD)
    gg = columns(ga[:, :, 384 : 384 + 704])
    gp = columns(ga[:, :, 384 + 704 :])

    def rowsum(w, g):
        return jnp.sum(w.astype(F32) * g, axis=1)

    gain1 = (rowsum(w_query, gq) + rowsum(w_key, gk) + rowsum(w_value, gv)) * scale
    gain2 = (rowsum(w_gate, gg) + rowsum(w_up, gp)) * scale
    s1 = (g1 * scale)[:, None]
    s2 = (g2 * scale)[:, None]
    return (
        layer_out, loss, input_grad, gain1, gq * s1, gk * s1, gv * s1, gb[:128] * scale,
        gain2, gg * s2, gp * s2, gb[128:] * scale,
    )


def solution(mesh):
    fine = Mesh(mesh.devices.reshape(2, 4, 4, 2, 2), AXES)
    rows = ("y_hi", "z", "x", "y_lo", "core")
    fs = ("x", "y_lo", "core")
    token, shard = P(rows, None), P(fs, None)
    return jax.shard_map(
        local,
        mesh=fine,
        in_specs=(token, token, shard, P(rows), P(fs), shard, shard, shard, shard, P(fs), shard, shard, shard),
        out_specs=(token, P(), token, P(fs), shard, shard, shard, shard, P(fs), shard, shard, shard),
        check_vma=False,
    )
```

```python
import functools

import jax
import jax.numpy as jnp
from jax import lax
from jax.experimental import pallas as pl
from jax.experimental.pallas import tpu as pltpu
from jax.sharding import Mesh, PartitionSpec as P

D = 2048
HEADS = 32
KV_HEADS = 4
HD = 64
FF = 5632
KVD = 256
EPSILON = 1e-05
THETA = 10000.0
NEGATIVE = -1e30
AXES = ("y_hi", "z", "x", "y_lo", "core")
BF = jnp.bfloat16
F32 = jnp.float32


def dot(a, b, ca, cb):
    return lax.dot_general(a, b, (((ca,), (cb,)), ((), ())), preferred_element_type=F32)


def tables(positions):
    indices = jnp.arange(HD // 2, dtype=jnp.int32).astype(F32)
    frequency = THETA ** (-(indices * 2.0 / HD))
    angles = positions.astype(F32)[:, None] * frequency[None, :]
    angles = jnp.concatenate([angles, angles], axis=1)
    return jnp.cos(angles), jnp.sin(angles)


def positions_of(c):
    t = jnp.arange(64, dtype=jnp.int32)
    return jnp.concatenate([c * 64 + t, (15 - c) * 64 + t])


MESH = pl.DeviceIdType.MESH
HALVES = (pl.ds(0, 64), pl.ds(64, 64))
VM = pl.BlockSpec(memory_space=pltpu.VMEM)
HB = pl.BlockSpec(memory_space=pl.ANY)


def params(number):
    return pltpu.CompilerParams(collective_id=number, has_side_effects=True, vmem_limit_bytes=56 * 2**20)


def send(src, dst, sems, i, device):
    copy = pltpu.make_async_remote_copy(
        src_ref=src, dst_ref=dst, send_sem=sems[0].at[i], recv_sem=sems[1].at[i], device_id=device, device_id_type=MESH
    )
    copy.start()
    return copy


def meet(devices):
    barrier = pltpu.get_barrier_semaphore()
    for device in devices:
        pl.semaphore_signal(barrier, inc=1, device_id=device, device_id_type=MESH)
    pl.semaphore_wait(barrier, len(devices))


class Ring:
    def __init__(self):
        x, core = lax.axis_index("x"), lax.axis_index("core")
        self.x, self.core = x, core
        self.right_x, self.left_x, self.far_x = lax.rem(x + 1, 4), lax.rem(x + 3, 4), lax.rem(x + 2, 4)
        self.right, self.left, self.sibling = {"x": self.right_x}, {"x": self.left_x}, {"core": 1 - core}


class Gather:
    def __init__(self, ring, own, out, sems, local_sem):
        self.r, self.own, self.out, self.sems, self.local_sem = ring, own, out, sems, local_sem
        self.c = {}

    def slot(self, x, half):
        return self.out.at[x * 2 + self.r.core, HALVES[half]]

    def start(self, half):
        r, src, dst = self.r, self.own.at[HALVES[half]], self.slot(self.r.x, half)
        first, second = (r.right, r.left) if half == 0 else (r.left, r.right)
        i, j = (0, 3) if half == 0 else (2, 1)
        self.c[i] = send(src, dst, self.sems, i, first)
        self.c[j] = send(src, dst, self.sems, j, second)
        self.c[6 + half] = send(src, dst, self.sems, 6 + half, r.sibling)
        copy = pltpu.make_async_copy(src, dst, self.local_sem.at[half])
        copy.start()
        self.c[14 + half] = copy

    def forward(self):
        r, c = self.r, self.c
        for got, x, half, onward, core_i in (
            (0, r.left_x, 0, (4, r.right), 8),
            (2, r.right_x, 1, (5, r.left), 11),
            (1, r.left_x, 1, None, 9),
            (3, r.right_x, 0, None, 10),
            (4, r.far_x, 0, None, 12),
            (5, r.far_x, 1, None, 13),
        ):
            c[got].wait_recv()
            block = self.slot(x, half)
            if onward is not None:
                c[onward[0]] = send(block, block, self.sems, onward[0], onward[1])
            c[core_i] = send(block, block, self.sems, core_i, r.sibling)

    def finish(self):
        c = self.c
        for i in range(6, 14):
            c[i].wait_recv()
        for i in range(14):
            c[i].wait_send()
        c[14].wait()
        c[15].wait()


class Scatter:
    def __init__(self, ring, parts, held, got, sems):
        self.r, self.parts, self.held, self.got, self.sems = ring, parts, held, got, sems
        self.c = {}

    def pair(self, i, half):
        r = self.r
        x = (r.far_x, r.right_x, r.left_x, r.x)[i]

        def body(k, _):
            rows = pl.ds(half * 64 + k * 16, 16)
            total = self.parts[x * 2 + r.core, rows, :].astype(F32) + self.got[i, rows, :].astype(F32)
            self.held[i, rows, :] = total.astype(BF)
            return 0

        lax.fori_loop(0, 4, body, 0)

    def onward(self, i, half, slot):
        def body(k, _):
            rows = pl.ds(half * 64 + k * 16, 16)
            total = self.held[i, rows, :].astype(F32) + self.got[slot, rows, :].astype(F32)
            self.held[i, rows, :] = total.astype(BF)
            return 0

        lax.fori_loop(0, 4, body, 0)

    def begin(self):
        r = self.r
        for i, x in enumerate((r.far_x, r.right_x, r.left_x, r.x)):
            self.c[i] = send(self.parts.at[x * 2 + (1 - r.core)], self.got.at[i], self.sems, i, r.sibling)

    def run(self):
        r, c, held, got, sems = self.r, self.c, self.held, self.got, self.sems
        a, b = HALVES
        c[0].wait_recv()
        self.pair(0, 0)
        c[4] = send(held.at[0, a], got.at[4, a], sems, 4, r.right)
        self.pair(0, 1)
        c[5] = send(held.at[0, b], got.at[4, b], sems, 5, r.left)
        c[1].wait_recv()
        self.pair(1, 1)
        c[6] = send(held.at[1, b], got.at[5, b], sems, 6, r.right)
        c[2].wait_recv()
        self.pair(2, 0)
        c[7] = send(held.at[2, a], got.at[5, a], sems, 7, r.left)
        self.pair(1, 0)
        self.pair(2, 1)
        c[4].wait_recv()
        self.onward(1, 0, 4)
        c[8] = send(held.at[1, a], got.at[6, a], sems, 8, r.right)
        c[5].wait_recv()
        self.onward(2, 1, 4)
        c[9] = send(held.at[2, b], got.at[6, b], sems, 9, r.left)
        c[3].wait_recv()

    def ready(self, half):
        c = self.c
        if half == 0:
            c[7].wait_recv()
            c[8].wait_recv()
        else:
            c[6].wait_recv()
            c[9].wait_recv()

    def total(self, rows):
        r = self.r
        return (
            self.parts[r.x * 2 + r.core, rows, :].astype(F32)
            + self.got[3, rows, :].astype(F32)
            + self.got[5, rows, :].astype(F32)
            + self.got[6, rows, :].astype(F32)
        )

    def finish(self):
        for i in range(10):
            self.c[i].wait_send()


def norm_scale(v):
    return lax.rsqrt(jnp.mean(v * v, axis=1, keepdims=True) + EPSILON)


def exchange(number, op, parts, inputs, outs, gather=True, sides=()):
    n_in, n_out = len(inputs), len(outs)
    dma = pltpu.SemaphoreType.DMA

    def kernel(*refs):
        refs = list(refs)

        def take(n):
            taken = refs[:n]
            del refs[:n]
            return taken

        parts_ref, ins = take(1)[0], take(n_in)
        side_ins = [take(len(s.operands)) for s in sides]
        out_refs = take(n_out)
        all_ref = take(1)[0] if gather else None
        side_outs = [take(len(s.shapes)) for s in sides]
        held, got, rs_s, rs_r = take(4)
        if gather:
            own, ag_s, ag_r, loc = take(4)
        ring = Ring()
        peers = [ring.right, ring.left, ring.sibling]
        for s, i, o in zip(sides, side_ins, side_outs):
            s.bind(ring, i, o, take(len(s.scratch)))
            peers += s.peers
        meet(peers)
        scatter = Scatter(ring, parts_ref, held, got, (rs_s, rs_r))
        if gather:
            gath = Gather(ring, own, all_ref, (ag_s, ag_r), loc)
        scatter.begin()
        for s in sides:
            s.start()
        scatter.run()
        for half in range(2):
            scatter.ready(half)

            def body(k, _, half=half):
                rows = pl.ds(half * 64 + k * 16, 16)
                last = op(rows, scatter.total(rows), ins, out_refs)
                if gather:
                    own[rows, :] = last.astype(BF)
                return 0

            lax.fori_loop(0, 4, body, 0)
            if gather:
                gath.start(half)
        if gather:
            gath.forward()
        for s in sides:
            s.middle()
        if gather:
            gath.finish()
        scatter.finish()
        for s in sides:
            s.finish()

    shapes, specs, in_specs, operands, aliases = list(outs), [VM] * n_out, [VM] * (1 + n_in), [parts, *inputs], {}
    scratch = [pltpu.VMEM((4, 128, D), BF), pltpu.VMEM((7, 128, D), BF), dma((10,)), dma((10,))]
    if gather:
        shapes.append(jax.ShapeDtypeStruct((8, 128, D), BF))
        specs.append(HB)
        scratch += [pltpu.VMEM((128, D), BF), dma((14,)), dma((14,)), dma((2,))]
    for s in sides:
        if s.in_place:
            aliases[len(operands)] = len(shapes)
        operands += s.operands
        in_specs += [HB] * len(s.operands)
        shapes += s.shapes
        specs += [HB if s.in_place else VM] * len(s.shapes)
        scratch += s.scratch
    return pl.pallas_call(
        kernel,
        out_shape=shapes,
        in_specs=in_specs,
        out_specs=specs,
        scratch_shapes=scratch,
        input_output_aliases=aliases,
        compiler_params=params(number),
        name="exchange%d" % number,
    )(*operands)


class Side:
    in_place = False

    def middle(self):
        pass


class YSwap(Side):
    in_place = True

    def __init__(self, weights):
        self.operands = [weights]
        self.shapes = [jax.ShapeDtypeStruct(weights.shape, weights.dtype)]
        self.scratch = [pltpu.SemaphoreType.DMA((4,)), pltpu.SemaphoreType.DMA((4,))]

    def bind(self, ring, ins, outs, scratch):
        self.r, self.w, self.sems = ring, outs[0], scratch
        self.peers = list(y_partners())

    def start(self):
        self.c = []
        for dx in range(4):
            x = lax.rem(self.r.x + 4 - dx, 4)
            block = self.w.at[:, :, :, group_lanes(x, lax.axis_index("y_lo"))]
            self.c.append(send(block, block, self.sems, dx, self.peers[dx // 2]))

    def finish(self):
        for c in self.c:
            c.wait()


class Torus:
    def __init__(self):
        self.y_hi, self.y_lo, self.z = lax.axis_index("y_hi"), lax.axis_index("y_lo"), lax.axis_index("z")
        self.y = self.y_hi * 2 + self.y_lo
        self.ys = [(dy, lax.rem(self.y + dy, 4)) for dy in (1, 3, 2)]
        self.zs = [(dz, lax.rem(self.z + dz, 4)) for dz in (1, 3, 2)]
        self.peers = [self.y_device(y) for _, y in self.ys] + [{"z": z} for _, z in self.zs]

    def y_device(self, y):
        return {"y_hi": y // 2, "y_lo": lax.rem(y, 2)}


def lanes_at(start, size):
    return pl.ds(pl.multiple_of(start, 128), size)


def add_up(out, terms, lead, rows):
    steps = rows // 16

    def body(k, _):
        i, r = k // steps, pl.ds(pl.multiple_of(lax.rem(k, steps) * 16, 16), 16)
        total = None
        for at in terms:
            term = at(i, r).astype(F32)
            total = term if total is None else total + term
        out(i, r, total.astype(BF))
        return 0

    lax.fori_loop(0, lead * steps, body, 0)


class SumColumns(Side):
    def __init__(self, grads):
        r = self.rows = grads.shape[2]
        dma = pltpu.SemaphoreType.DMA
        self.operands = [grads]
        self.shapes = [jax.ShapeDtypeStruct((r, 1024), BF)]
        self.scratch = [
            pltpu.VMEM((4, 4, r, 512), BF), pltpu.VMEM((4, 2, 2, r, 512), BF),
            pltpu.VMEM((3, r, 512), BF), pltpu.VMEM((3, r, 512), BF),
            dma((9,)), dma((9,)), dma((6,)), dma((6,)), dma((3,)),
        ]

    def bind(self, ring, ins, outs, scratch):
        (self.g,), (self.out,) = ins, outs
        self.by, self.bz, self.by2, self.bz2, s1, r1, s2, r2, self.loc = scratch
        self.one, self.two = (s1, r1), (s2, r2)
        self.t = Torus()
        self.peers = self.t.peers

    def start(self):
        t, g = self.t, self.g
        self.c = []
        for i, (dy, y) in enumerate(t.ys):
            src = g.at[y // 2, :, :, lanes_at(lax.rem(y, 2) * 1024, 512)]
            self.c.append(send(src, self.by.at[dy], self.one, i, t.y_device(y)))
        for i, (dz, z) in enumerate(t.zs):
            for yl in range(2):
                src = g.at[:, z, :, pl.ds(yl * 1024 + 512, 512)]
                self.c.append(send(src, self.bz.at[dz, yl], self.one, 3 + 2 * i + yl, {"z": z}))
        self.l = [pltpu.make_async_copy(g.at[t.y_hi, :, :, lanes_at(t.y_lo * 1024, 512)], self.by.at[0], self.loc.at[0])]
        for yl in range(2):
            self.l.append(
                pltpu.make_async_copy(g.at[:, t.z, :, pl.ds(yl * 1024 + 512, 512)], self.bz.at[0, yl], self.loc.at[1 + yl])
            )
        for copy in self.l:
            copy.start()

    def middle(self):
        t, by, bz = self.t, self.by, self.bz
        for copy in self.l:
            copy.wait()
        for copy in self.c:
            copy.wait_recv()

        def put_y(i, r, v):
            by[0, i, r, :] = v

        def put_z(i, r, v):
            bz[0, i // 2, lax.rem(i, 2), r, :] = v

        add_up(put_y, [lambda i, r, k=k: by[k, i, r, :] for k in range(4)], 4, self.rows)
        add_up(put_z, [lambda i, r, k=k: bz[k, i // 2, lax.rem(i, 2), r, :] for k in range(4)], 4, self.rows)
        self.c2 = []
        for i, (dz, z) in enumerate(t.zs):
            self.c2.append(send(by.at[0, z], self.by2.at[dz - 1], self.two, i, {"z": z}))
        for i, (dy, y) in enumerate(t.ys):
            self.c2.append(send(bz.at[0, lax.rem(y, 2), y // 2], self.bz2.at[dy - 1], self.two, 3 + i, t.y_device(y)))

    def finish(self):
        t, by, bz, by2, bz2, out = self.t, self.by, self.bz, self.by2, self.bz2, self.out
        for copy in self.c2:
            copy.wait_recv()

        def put_a(i, r, v):
            out[r, 0:512] = v

        def put_b(i, r, v):
            out[r, 512:1024] = v

        add_up(put_a, [lambda i, r: by[0, t.z, r, :]] + [lambda i, r, k=k: by2[k, r, :] for k in range(3)], 1, self.rows)
        add_up(put_b, [lambda i, r: bz[0, t.y_lo, t.y_hi, r, :]] + [lambda i, r, k=k: bz2[k, r, :] for k in range(3)], 1, self.rows)
        for copy in self.c + self.c2:
            copy.wait_send()


class SumRows(Side):
    def __init__(self, grads):
        r = self.rows = grads.shape[1]
        dma = pltpu.SemaphoreType.DMA
        self.operands = [grads]
        self.shapes = [jax.ShapeDtypeStruct((2, r, 128), BF)]
        self.scratch = [
            pltpu.VMEM((4, r, 512), BF), pltpu.VMEM((4, 2, 2, r, 128), BF),
            pltpu.VMEM((3, r, 128), BF), pltpu.VMEM((3, r, 128), BF),
            dma((9,)), dma((9,)), dma((6,)), dma((6,)), dma((3,)),
        ]

    def bind(self, ring, ins, outs, scratch):
        (self.g,), (self.out,) = ins, outs
        self.by, self.bz, self.by2, self.bz2, s1, r1, s2, r2, self.loc = scratch
        self.one, self.two = (s1, r1), (s2, r2)
        self.t = Torus()
        self.peers = self.t.peers

    def start(self):
        t, g = self.t, self.g
        self.c = []
        for i, (dy, y) in enumerate(t.ys):
            src = g.at[lax.rem(y, 2), :, lanes_at((y // 2) * 1024, 512)]
            self.c.append(send(src, self.by.at[dy], self.one, i, t.y_device(y)))
        for i, (dz, z) in enumerate(t.zs):
            for yh in range(2):
                src = g.at[:, :, lanes_at(yh * 1024 + 512 + z * 128, 128)]
                self.c.append(send(src, self.bz.at[dz, yh], self.one, 3 + 2 * i + yh, {"z": z}))
        self.l = [pltpu.make_async_copy(g.at[t.y_lo, :, lanes_at(t.y_hi * 1024, 512)], self.by.at[0], self.loc.at[0])]
        for yh in range(2):
            self.l.append(
                pltpu.make_async_copy(g.at[:, :, lanes_at(yh * 1024 + 512 + t.z * 128, 128)], self.bz.at[0, yh], self.loc.at[1 + yh])
            )
        for copy in self.l:
            copy.start()

    def middle(self):
        t, by, bz = self.t, self.by, self.bz
        for copy in self.l:
            copy.wait()
        for copy in self.c:
            copy.wait_recv()

        def put_y(i, r, v):
            by[0, r, :] = v

        def put_z(i, r, v):
            bz[0, i // 2, lax.rem(i, 2), r, :] = v

        add_up(put_y, [lambda i, r, k=k: by[k, r, :] for k in range(4)], 1, self.rows)
        add_up(put_z, [lambda i, r, k=k: bz[k, i // 2, lax.rem(i, 2), r, :] for k in range(4)], 4, self.rows)
        self.c2 = []
        for i, (dz, z) in enumerate(t.zs):
            self.c2.append(send(by.at[0, :, lanes_at(z * 128, 128)], self.by2.at[dz - 1], self.two, i, {"z": z}))
        for i, (dy, y) in enumerate(t.ys):
            self.c2.append(send(bz.at[0, y // 2, lax.rem(y, 2)], self.bz2.at[dy - 1], self.two, 3 + i, t.y_device(y)))

    def finish(self):
        t, by, bz, by2, bz2, out = self.t, self.by, self.bz, self.by2, self.bz2, self.out
        for copy in self.c2:
            copy.wait_recv()

        def put_a(i, r, v):
            out[0, r, :] = v

        def put_b(i, r, v):
            out[1, r, :] = v

        own = lanes_at(t.z * 128, 128)
        add_up(put_a, [lambda i, r: by[0, r, own]] + [lambda i, r, k=k: by2[k, r, :] for k in range(3)], 1, self.rows)
        add_up(put_b, [lambda i, r: bz[0, t.y_hi, t.y_lo, r, :]] + [lambda i, r, k=k: bz2[k, r, :] for k in range(3)], 1, self.rows)
        for copy in self.c + self.c2:
            copy.wait_send()


def piece_lanes(c, part):
    return lanes_at((c // 4) * 1024 + part * 512 + lax.rem(c, 4) * 128, 128)


class SpreadRows(Side):
    def __init__(self, pieces):
        r = pieces.shape[1]
        dma = pltpu.SemaphoreType.DMA
        self.operands = [pieces]
        self.shapes = [jax.ShapeDtypeStruct((r, D), BF)]
        self.scratch = [dma((14,)), dma((14,)), dma((2,))]

    def bind(self, ring, ins, outs, scratch):
        (self.p,), (self.out,) = ins, outs
        self.sems, self.loc = scratch[:2], scratch[2]
        self.here = lax.axis_index("y_hi") * 4 + lax.axis_index("z")
        self.peers = [ctx_peer(self.here, k) for k in range(1, 8)]

    def start(self):
        self.c = []
        for part in range(2):
            dst = self.out.at[:, piece_lanes(self.here, part)]
            for k in range(1, 8):
                self.c.append(send(self.p.at[part], dst, self.sems, part * 7 + k - 1, self.peers[k - 1]))
            copy = pltpu.make_async_copy(self.p.at[part], dst, self.loc.at[part])
            copy.start()
            self.c.append(copy)

    def finish(self):
        for copy in self.c:
            copy.wait()


def op_mid(rows, total, ins, outs):
    (x_ref,), (y1_ref,) = ins, outs
    y1 = x_ref[rows, :].astype(F32) + total
    y1_ref[rows, :] = y1
    return y1 * norm_scale(y1)


def op_loss(rows, total, ins, outs):
    y1_ref, teacher_ref, valid_ref = ins
    out_ref, dy_ref, loss_ref = outs
    y = y1_ref[rows, :] + total
    out_ref[rows, :] = y.astype(BF)
    miss = y - teacher_ref[rows, :].astype(F32)
    valid = valid_ref[rows, :]
    loss_ref[rows, :] = valid * jnp.mean(miss * miss, axis=1, keepdims=True)
    dy = valid * miss
    dy_ref[rows, :] = dy
    return dy


def back_norm(v, grad, u):
    r = norm_scale(v)
    n = v * r
    return grad + r * (u - n * jnp.mean(u * n, axis=1, keepdims=True))


def op_back(rows, total, ins, outs):
    (y1_ref, dy_ref), (dy1_ref,) = ins, outs
    dy1 = back_norm(y1_ref[rows, :], dy_ref[rows, :], total)
    dy1_ref[rows, :] = dy1
    return dy1


def op_input(rows, total, ins, outs):
    (x_ref, dy1_ref), (grad_ref,) = ins, outs
    grad_ref[rows, :] = back_norm(x_ref[rows, :].astype(F32), dy1_ref[rows, :], total)
    return None


def y_partners():
    y_hi, y_lo = lax.axis_index("y_hi"), lax.axis_index("y_lo")
    return {"y_lo": 1 - y_lo}, {"y_hi": 1 - y_hi, "y_lo": 1 - y_lo}


def group_lanes(x, y_lo):
    return pl.ds(pl.multiple_of(x * 512 + y_lo * 256, 256), 256)


def tp_peers(ring):
    found = []
    for k in range(1, 8):
        dx, dc = k // 2, k % 2
        core = 1 - ring.core if dc else ring.core
        found.append((k, lax.rem(ring.x + dx, 4), core))
    return found


def enter_kernel(
    x_ref, meta_ref, g1_ref, g2_ref, wq_ref, wk_ref, wv_ref, wg_ref, wu_ref, wo_ref,
    n1_ref, metas_ref, wqkv_ref, wos_ref, wt_ref,
    own, w, ag_s, ag_r, loc, meta_s, meta_r, w_s, w_r, y_s, y_r, loc2,
):
    ring = Ring()
    y_lo = lax.axis_index("y_lo")
    near, other = y_partners()
    peers = tp_peers(ring)
    meet([{"x": x, "core": core} for _, x, core in peers] + [near, other])
    here = ring.x * 2 + ring.core
    copies = []
    for k, x, core in peers:
        copies.append(send(meta_ref, metas_ref.at[here], (meta_s, meta_r), k, {"x": x, "core": core}))
    local = [pltpu.make_async_copy(meta_ref, metas_ref.at[here], loc2.at[0])]
    local.append(pltpu.make_async_copy(wo_ref, wos_ref.at[y_lo], loc2.at[1]))
    for c in local:
        c.start()
    for half, device in enumerate((near, other)):
        copies.append(send(wo_ref.at[HALVES[half]], wos_ref.at[y_lo, HALVES[half]], (y_s, y_r), 4 + half, device))

    gath = Gather(ring, own, n1_ref, (ag_s, ag_r), loc)
    for half in range(2):

        def body(k, _, half=half):
            rows = pl.ds(half * 64 + k * 16, 16)
            v = x_ref[rows, :].astype(F32)
            own[rows, :] = (v * norm_scale(v)).astype(BF)
            return 0

        lax.fori_loop(0, 4, body, 0)
        gath.start(half)

    def turned(ref, gain, k):
        tile = ref[:, pl.ds(pl.multiple_of(k * 128, 128), 128)].astype(F32) * gain
        return tile.T.astype(BF)

    g1, g2 = g1_ref[...], g2_ref[...]
    for f in range(16):
        w[(f // 4) * 2 + f % 2, pl.ds((f // 2 % 2) * 128, 128), :] = turned(wq_ref, g1, f)
    for ref, at in ((wk_ref, 256), (wv_ref, 320)):
        for k in range(2):
            tile = turned(ref, g1, k)
            for x in (2 * k, 2 * k + 1):
                part = tile[(x % 2) * 64 : (x % 2) * 64 + 64]
                w[2 * x, pl.ds(at, 64), :] = part
                w[2 * x + 1, pl.ds(at, 64), :] = part
    lanes = pl.ds(pl.multiple_of((ring.x * 4 + y_lo * 2 + ring.core) * 128, 128), 128)
    wcopies = {}
    for k, x, core in peers:
        wcopies[k] = send(w.at[x * 2 + core], wqkv_ref.at[:, lanes], (w_s, w_r), k, {"x": x, "core": core})
    wcopies[0] = pltpu.make_async_copy(w.at[here], wqkv_ref.at[:, lanes], loc2.at[2])
    wcopies[0].start()

    def turn_all(ref, i):
        def body(k, _):
            wt_ref[i, pl.ds(pl.multiple_of(k * 128, 128), 128), :] = turned(ref, g2, k)
            return 0

        lax.fori_loop(0, FF // 128, body, 0)

    turn_all(wg_ref, 0)
    gath.forward()
    turn_all(wu_ref, 1)
    for dx in range(4):
        x = lax.rem(ring.x + 4 - dx, 4)
        if dx == 0:
            wcopies[0].wait()
        else:
            wcopies[2 * dx].wait_recv()
        wcopies[2 * dx + 1].wait_recv()
        block = wqkv_ref.at[:, group_lanes(x, y_lo)]
        copies.append(send(block, block, (y_s, y_r), dx, (near, other)[dx // 2]))
    gath.finish()
    for k in range(1, 8):
        wcopies[k].wait_send()
    for c in copies:
        c.wait()
    for c in local:
        c.wait()


def enter(hidden_in, meta, g1, g2, w_query, w_key, w_value, w_gate, w_up, w_out):
    dma = pltpu.SemaphoreType.DMA
    return pl.pallas_call(
        enter_kernel,
        out_shape=[
            jax.ShapeDtypeStruct((8, 128, D), BF),
            jax.ShapeDtypeStruct((8, 16, 128), jnp.int32),
            jax.ShapeDtypeStruct((384, D), BF),
            jax.ShapeDtypeStruct((2, 128, D), BF),
            jax.ShapeDtypeStruct((2, FF, 128), BF),
        ],
        in_specs=[VM] * 9 + [HB],
        out_specs=[HB, VM, HB, HB, VM],
        scratch_shapes=[
            pltpu.VMEM((128, D), BF), pltpu.VMEM((8, 384, 128), BF),
            dma((14,)), dma((14,)), dma((2,)), dma((8,)), dma((8,)), dma((8,)), dma((8,)), dma((6,)), dma((6,)), dma((3,)),
        ],
        compiler_params=params(5),
        name="enter",
    )(hidden_in, meta, g1, g2, w_query, w_key, w_value, w_gate, w_up, w_out)


def ctx_peer(c, k):
    other = lax.rem(c + k, 8)
    return {"y_hi": other // 4, "z": lax.rem(other, 4)}


def nt(a, b):
    return dot(a, b, 1, 1)


def nn(a, b):
    return dot(a, b, 1, 0)


def key_bias(meta_ref, d, c, bias):
    docs = meta_ref[d].astype(F32)
    query_docs = meta_ref[d, pl.ds(c, 1), :].astype(F32)
    lane = lax.broadcasted_iota(jnp.int32, (128, 128), 1)
    row = lax.broadcasted_iota(jnp.int32, (128, 128), 0)

    def position(owner, i):
        return jnp.where(i < 64, owner * 64 + i, (15 - owner) * 64 + i - 64)

    query_pos = position(c, lane)
    for b in range(8):
        key_docs = jnp.broadcast_to(docs[b : b + 1, :], (128, 128)).T
        good = (query_pos >= position(b, row)) & (key_docs == query_docs)
        bias[pl.ds(b * 128, 128), :] = jnp.where(good, 0.0, NEGATIVE)


def attend_kernel(
    qkv_ref, meta_ref, tab_ref, wt_ref, wdn_ref,
    a_ref, qp_ref, kv_ref, lse_ref, wgu_ref, wd_ref,
    bias, probs, kv_s, kv_r, fw_s, fw_r, w_s, w_r, y_s, y_r, loc,
):
    ring = Ring()
    y_lo = lax.axis_index("y_lo")
    c = lax.axis_index("y_hi") * 4 + lax.axis_index("z")
    near, other = y_partners()
    peers = tp_peers(ring)
    meet([ctx_peer(c, k) for k in range(1, 8)] + [{"x": x, "core": core} for _, x, core in peers] + [near, other])

    lane = lax.broadcasted_iota(jnp.int32, (128, 128), 1)

    def rope(u, i):
        return u * tab_ref[i] + pltpu.roll(u, 96, 1) * tab_ref[i + 1] + pltpu.roll(u, 32, 1) * tab_ref[i + 2]

    for d in range(8):
        kv_ref[d % 2, d // 2, c] = rope(qkv_ref[pl.ds(d * 128, 128), 256:384], 3).astype(BF)
    kv_copies = []
    for k in range(1, 8):
        block = kv_ref.at[ring.core, :, c]
        kv_copies.append(send(block, block, (kv_s, kv_r), k - 1, ctx_peer(c, k)))

    copies, local = [], []
    here = pl.ds(pl.multiple_of((ring.x * 4 + y_lo * 2 + ring.core) * 128, 128), 128)
    for j in range(2):
        rows = pl.ds(pl.multiple_of((ring.x * 4 + 2 * j + ring.core) * 352, 32), 352)
        local.append(pltpu.make_async_copy(wt_ref.at[:, rows], wgu_ref.at[:, j, :, here], loc.at[j]))
    rows = pl.ds(pl.multiple_of(y_lo * 352, 32), 352)
    local.append(pltpu.make_async_copy(wdn_ref, wd_ref.at[rows], loc.at[2]))
    for copy in local:
        copy.start()
    for k, x, core in peers:
        for j in range(2):
            rows = pl.ds(pl.multiple_of((x * 4 + 2 * j + core) * 352, 32), 352)
            copies.append(
                send(wt_ref.at[:, rows], wgu_ref.at[:, j, :, here], (w_s, w_r), k * 2 + j, {"x": x, "core": core})
            )
    for half, device in enumerate((near, other)):
        rows = pl.ds(pl.multiple_of(y_lo * 352 + half * 176, 16), 176)
        copies.append(send(wdn_ref.at[pl.ds(half * 176, 176)], wd_ref.at[rows], (y_s, y_r), half, device))

    def turn_queries(d, _):
        for j in range(2):
            u = rope(qkv_ref[pl.ds(pl.multiple_of(d * 128, 128), 128), pl.ds(j * 128, 128)], 0) * 0.125
            qp_ref[d, pl.ds(j * 256, 128), :] = jnp.where(lane < 64, u, 0.0).astype(BF)
            qp_ref[d, pl.ds(j * 256 + 128, 128), :] = jnp.where(lane < 64, pltpu.roll(u, 64, 1), 0.0).astype(BF)
        return 0

    lax.fori_loop(0, 8, turn_queries, 0)

    forwards = []
    for k in range(1, 8):
        kv_copies[k - 1].wait_recv()
        block = kv_ref.at[ring.core, :, lax.rem(c + 8 - k, 8)]
        forwards.append(send(block, block, (fw_s, fw_r), k - 1, ring.sibling))
    for copy in forwards:
        copy.wait_recv()

    def one(d, _):
        key_bias(meta_ref, d, c, bias)
        kv = kv_ref[lax.rem(d, 2), d // 2].reshape(1024, 128)
        scores = nt(kv, qp_ref[d])
        for h in range(4):
            s = scores[:, h * 128 : (h + 1) * 128] + bias[...]
            top = jnp.max(s, axis=0, keepdims=True)
            e = jnp.exp(s - top)
            total = jnp.sum(e, axis=0, keepdims=True)
            probs[:, h * 128 : (h + 1) * 128] = (e * (1.0 / total)).astype(BF)
            lse_ref[d, :, h * 128 : (h + 1) * 128] = jnp.broadcast_to(top + jnp.log(total), (8, 128))
        mixed = nn(kv.T, probs[...])
        for j in range(2):
            two = jnp.concatenate([mixed[64:, (2 * j) * 128 : (2 * j + 1) * 128], mixed[64:, (2 * j + 1) * 128 : (2 * j + 2) * 128]], axis=0)
            a_ref[pl.ds(pl.multiple_of(d * 128, 128), 128), pl.ds(j * 128, 128)] = two.T.astype(BF)
        return 0

    lax.fori_loop(0, 8, one, 0)
    for copy in kv_copies + forwards:
        copy.wait_send()
    for copy in copies:
        copy.wait()
    for copy in local:
        copy.wait()


def attend(qkv, metas, tabs, wt, w_down):
    dma = pltpu.SemaphoreType.DMA
    return pl.pallas_call(
        attend_kernel,
        out_shape=[
            jax.ShapeDtypeStruct((1024, 256), BF),
            jax.ShapeDtypeStruct((8, 512, 128), BF),
            jax.ShapeDtypeStruct((2, 4, 8, 128, 128), BF),
            jax.ShapeDtypeStruct((8, 8, 512), F32),
            jax.ShapeDtypeStruct((2, 2, 352, D), BF),
            jax.ShapeDtypeStruct((704, D), BF),
        ],
        in_specs=[VM, VM, VM, HB, HB],
        out_specs=[VM, VM, VM, VM, HB, HB],
        scratch_shapes=[
            pltpu.VMEM((1024, 128), F32), pltpu.VMEM((1024, 512), BF),
            dma((7,)), dma((7,)), dma((7,)), dma((7,)), dma((16,)), dma((16,)), dma((2,)), dma((2,)), dma((3,)),
        ],
        compiler_params=params(6),
        name="attend",
    )(qkv, metas, tabs, wt, w_down)


def attend_back_kernel(
    side, qp_ref, kv_ref, lse_ref, meta_ref, tab_ref, da_ref, side_in,
    dqkv_ref, side_out,
    bias, dap, ds, pb, mine, theirs, stage, back, co_s, co_r, kv_s, kv_r, *side_scratch,
):
    ring = Ring()
    c = lax.axis_index("y_hi") * 4 + lax.axis_index("z")
    side.bind(ring, (side_in,), (side_out,), side_scratch)
    meet([ctx_peer(c, k) for k in range(1, 8)] + [ring.sibling] + side.peers)
    side.start()
    lane = lax.broadcasted_iota(jnp.int32, (128, 128), 1)

    def unrope(u, i):
        return u * tab_ref[i] - pltpu.roll(u, 96, 1) * tab_ref[i + 1] - pltpu.roll(u, 32, 1) * tab_ref[i + 2]

    def one(x, core):
        d = x * 2 + core
        rows = pl.ds(pl.multiple_of(d * 128, 128), 128)
        key_bias(meta_ref, d, c, bias)
        for j in range(2):
            tile = da_ref[rows, pl.ds(j * 128, 128)].astype(F32)
            dap[pl.ds(j * 256, 128), :] = jnp.where(lane >= 64, pltpu.roll(tile, 64, 1), 0.0).astype(BF)
            dap[pl.ds(j * 256 + 128, 128), :] = jnp.where(lane >= 64, tile, 0.0).astype(BF)
        kv = kv_ref[core, x].reshape(1024, 128)
        scores = nt(kv, qp_ref[d])
        dprobs = nt(kv, dap[...])
        for h in range(4):
            cols = slice(h * 128, (h + 1) * 128)
            p = jnp.exp(scores[:, cols] + bias[...] - lse_ref[d, 0:1, cols])
            pb[:, cols] = p.astype(BF)
            dp = dprobs[:, cols]
            centre = jnp.sum(p * dp, axis=0, keepdims=True)
            ds[:, cols] = (p * (dp - centre)).astype(BF)
        dkv = nn(ds[...], qp_ref[d]) + nn(pb[...], dap[...])
        dq = nn(kv.T, ds[...]) * 0.125
        for j in range(2):
            two = jnp.concatenate([dq[:64, (2 * j) * 128 : (2 * j + 1) * 128], dq[:64, (2 * j + 1) * 128 : (2 * j + 2) * 128]], axis=0)
            dqkv_ref[rows, pl.ds(j * 128, 128)] = unrope(two.T, 0).astype(BF)
        return dkv

    def to_sibling(x, _):
        mine[x] = one(x, 1 - ring.core).astype(BF).reshape(8, 128, 128)
        send(mine.at[x], theirs.at[x], (co_s, co_r), x, ring.sibling)
        dqkv_ref[pl.ds(pl.multiple_of((x * 2 + 1 - ring.core) * 128, 128), 128), 256:384] = jnp.zeros((128, 128), BF)
        return 0

    lax.fori_loop(0, 4, to_sibling, 0)

    def core_copy(x):
        return pltpu.make_async_remote_copy(
            src_ref=mine.at[x], dst_ref=theirs.at[x], send_sem=co_s.at[x], recv_sem=co_r.at[x],
            device_id=ring.sibling, device_id_type=MESH,
        )

    def kv_copy(x, k):
        return pltpu.make_async_remote_copy(
            src_ref=stage.at[x, lax.rem(c + k, 8)], dst_ref=back.at[x, k - 1], send_sem=kv_s.at[x * 7 + k - 1],
            recv_sem=kv_r.at[x * 7 + k - 1], device_id=ctx_peer(c, k), device_id_type=MESH,
        )

    def to_owners(x, _):
        dkv = one(x, ring.core)
        core_copy(x).wait_recv()
        stage[x] = (dkv + theirs[x].reshape(1024, 128).astype(F32)).astype(BF).reshape(8, 128, 128)
        for k in range(1, 8):
            kv_copy(x, k).start()
        return 0

    side.middle()
    lax.fori_loop(0, 4, to_owners, 0)

    def gather_up(x, _):
        total = stage[x, c].astype(F32)
        for k in range(1, 8):
            kv_copy(x, k).wait_recv()
            total += back[x, k - 1].astype(F32)
        rows = pl.ds(pl.multiple_of((x * 2 + ring.core) * 128, 128), 128)
        dqkv_ref[rows, 256:384] = unrope(total, 3).astype(BF)
        return 0

    lax.fori_loop(0, 4, gather_up, 0)

    def drain(x, _):
        core_copy(x).wait_send()
        for k in range(1, 8):
            kv_copy(x, k).wait_send()
        return 0

    lax.fori_loop(0, 4, drain, 0)
    side.finish()


def attend_back(qp, kv, lse, metas, tabs, da, side):
    dma = pltpu.SemaphoreType.DMA
    return pl.pallas_call(
        functools.partial(attend_back_kernel, side),
        out_shape=[jax.ShapeDtypeStruct((1024, 384), BF)] + side.shapes,
        in_specs=[VM] * 6 + [HB],
        out_specs=[VM, VM],
        scratch_shapes=[
            pltpu.VMEM((1024, 128), F32), pltpu.VMEM((512, 128), BF),
            pltpu.VMEM((1024, 512), BF), pltpu.VMEM((1024, 512), BF),
            pltpu.VMEM((4, 8, 128, 128), BF), pltpu.VMEM((4, 8, 128, 128), BF),
            pltpu.VMEM((4, 8, 128, 128), BF), pltpu.VMEM((4, 7, 128, 128), BF),
            dma((4,)), dma((4,)), dma((28,)), dma((28,)), *side.scratch,
        ],
        compiler_params=params(7),
        name="attend_back",
    )(qp, kv, lse, metas, tabs, da, *side.operands)


def rope_tables(c):
    cos, sin = tables(positions_of(c))
    low = jnp.arange(HD) < HD // 2
    to_low, to_high = jnp.where(low, -sin, 0.0), jnp.where(low, 0.0, sin)
    one, zero = jnp.ones_like(cos), jnp.zeros_like(cos)
    pairs = [(cos, cos), (to_low, to_low), (to_high, to_high), (cos, one), (to_low, zero), (to_high, zero)]
    return jnp.stack([jnp.concatenate(p, axis=1) for p in pairs])


def group_peers():
    x, y_lo, core = lax.axis_index("x"), lax.axis_index("y_lo"), lax.axis_index("core")
    found = []
    for k in range(1, 16):
        dx, dy, dc = k // 4, k // 2 % 2, k % 2
        found.append((k, {"x": lax.rem(x + dx, 4), "y_lo": 1 - y_lo if dy else y_lo, "core": 1 - core if dc else core}))
    return found


def return_kernel(
    stats_ref, gu_ref, qkv_ref, out_ref, dn_ref, g1_ref, g2_ref, wq_ref, wk_ref, wv_ref, wg_ref, wu_ref,
    info_ref, q_ref, k_ref, v_ref, o_ref, gate_ref, up_ref, down_ref, gains_ref,
    st1, st2, mid, got_gu, got_qkv, all_gu, all_qkv, all_out,
    st_s, st_r, st2_s, st2_r, gu_s, gu_r, qkv_s, qkv_r, agu_s, agu_r, aqkv_s, aqkv_r, ao_s, ao_r, loc,
):
    x, y_lo, core = lax.axis_index("x"), lax.axis_index("y_lo"), lax.axis_index("core")
    c = lax.axis_index("y_hi") * 4 + lax.axis_index("z")
    group = group_peers()
    ctx = [(k, ctx_peer(c, k)) for k in range(1, 8)]
    meet([device for _, device in group] + [device for _, device in ctx])
    here16, here8 = x * 4 + y_lo * 2 + core, x * 2 + core

    def same(j):
        return here16 == y_lo * 8 + j

    def owner(j):
        return {"x": y_lo * 2 + j // 4, "y_lo": j // 2 % 2, "core": j % 2}

    moves = ((gu_ref, got_gu, (gu_s, gu_r)), (qkv_ref, got_qkv, (qkv_s, qkv_r)))

    def move(src, dst, sems, j):
        return pltpu.make_async_remote_copy(
            src_ref=src.at[:, pl.ds(j * 128, 128)], dst_ref=dst.at[here8], send_sem=sems[0].at[j], recv_sem=sems[1].at[here8],
            device_id=owner(j), device_id_type=MESH,
        )

    def move_here(src, dst, sems, j):
        return pltpu.make_async_copy(src.at[:, pl.ds(j * 128, 128)], dst.at[here8], sems[1].at[here8])

    for src, dst, sems in moves:
        for j in range(8):

            @pl.when(same(j))
            def _():
                move_here(src, dst, sems, j).start()

            @pl.when(jnp.logical_not(same(j)))
            def _():
                move(src, dst, sems, j).start()

    copies = [send(stats_ref, st1.at[here16], (st_s, st_r), k, device) for k, device in group]
    st1[here16] = stats_ref[...]
    for part in range(2):
        dst = all_out.at[:, piece_lanes(c, part)]
        for k, device in ctx:
            copies.append(send(out_ref.at[part], dst, (ao_s, ao_r), part * 7 + k - 1, device))
        copy = pltpu.make_async_copy(out_ref.at[part], dst, loc.at[part])
        copy.start()
        copies.append(copy)

    for copy in copies[:15]:
        copy.wait_recv()
    total = st1[0]
    for i in range(1, 16):
        total += st1[i]
    mid[...] = total
    st2[c] = total
    copies2 = [send(mid, st2.at[c], (st2_s, st2_r), k - 1, device) for k, device in ctx]

    def from_source(dst, sems, s):
        return pltpu.make_async_copy(dst.at[s], dst.at[s], sems[1].at[s])

    for _, dst, sems in moves:
        for s in range(8):
            from_source(dst, sems, s).wait()

    def gu_rows(s):
        return pl.ds(pl.multiple_of(((s // 2) * 4 + lax.rem(c // 2, 2) * 2 + s % 2) * 352 + lax.rem(c, 2) * 176, 16), 176)

    for s in range(8):
        dst = all_gu.at[c // 4, gu_rows(s)]
        copy = pltpu.make_async_copy(got_gu.at[s], dst, loc.at[2 + s])
        copy.start()
        copies2.append(copy)
        for k, device in ctx:
            copies2.append(send(got_gu.at[s], dst, (agu_s, agu_r), s * 7 + k - 1, device))
    dst = all_qkv.at[:, c]
    copy = pltpu.make_async_copy(got_qkv, dst, loc.at[10])
    copy.start()
    copies2.append(copy)
    for k, device in ctx:
        copies2.append(send(got_qkv, dst, (aqkv_s, aqkv_r), k - 1, device))

    for copy in copies2[:7]:
        copy.wait_recv()
    total = st2[0]
    for i in range(1, 8):
        total += st2[i]
    sums = jnp.sum(total, axis=1, keepdims=True)
    squares, count = sums[0:1], sums[1:2]
    scale = 2.0 / (D * count)
    info_ref[...] = jnp.concatenate([squares / count, scale, jnp.zeros((6, 1), F32)], axis=0) + jnp.zeros((8, 128), F32)

    down_scale = jnp.broadcast_to(scale, (16, 1))

    def scaled(src, dst, rows):
        def body(i, _):
            r = pl.ds(pl.multiple_of(i * 16, 16), 16)
            dst[r, :] = src[r, :].astype(F32) * down_scale
            return 0

        lax.fori_loop(0, rows // 16, body, 0)

    scaled(dn_ref, down_ref, 352)
    for copy in copies[15:]:
        copy.wait()
    scaled(all_out, o_ref, 128)

    for copy in copies2[7:]:
        copy.wait()
    g1, g2 = g1_ref[...], g2_ref[...]
    s1, s2 = g1 * scale, g2 * scale

    sum1 = jnp.zeros((128, 128), F32)
    for s in range(8):
        for j in range(2):
            f = (s // 2) * 4 + j * 2 + s % 2
            part = all_qkv[s].reshape(384, 128)[j * 128 : (j + 1) * 128].astype(F32).T
            sum1 += part * wq_ref[:, f * 128 : (f + 1) * 128].astype(F32)
            q_ref[:, f * 128 : (f + 1) * 128] = part * s1
    for i in range(2):
        both = []
        for xs in (2 * i, 2 * i + 1):
            both.append(
                all_qkv[2 * xs].reshape(384, 128)[256:].astype(F32) + all_qkv[2 * xs + 1].reshape(384, 128)[256:].astype(F32)
            )
        for at, w_ref, g_ref in ((0, wk_ref, k_ref), (64, wv_ref, v_ref)):
            part = jnp.concatenate([both[0][at : at + 64], both[1][at : at + 64]], axis=0).T
            sum1 += part * w_ref[:, i * 128 : (i + 1) * 128].astype(F32)
            g_ref[:, i * 128 : (i + 1) * 128] = part * s1

    def body(k, total):
        at = lanes_at(k * 128, 128)
        rows = pl.ds(pl.multiple_of(k * 128, 128), 128)
        for i, w_ref, g_ref in ((0, wg_ref, gate_ref), (1, wu_ref, up_ref)):
            part = all_gu[i, rows, :].astype(F32).T
            total += part * w_ref[:, at].astype(F32)
            g_ref[:, at] = part * s2
        return total

    sum2 = lax.fori_loop(0, FF // 128, body, jnp.zeros((128, 128), F32))
    gains_ref[0] = jnp.sum(sum1, axis=1, keepdims=True) * scale
    gains_ref[1] = jnp.sum(sum2, axis=1, keepdims=True) * scale
    for copy in copies[:15] + copies2[:7]:
        copy.wait_send()
    for src, dst, sems in moves:
        for j in range(8):

            @pl.when(jnp.logical_not(same(j)))
            def _():
                move(src, dst, sems, j).wait_send()


def return_grads(stats, gu, qkv, out, down, g1, g2, w_query, w_key, w_value, w_gate, w_up):
    dma = pltpu.SemaphoreType.DMA
    f32 = lambda *shape: jax.ShapeDtypeStruct(shape, F32)
    pair = lambda n: [dma((n,)), dma((n,))]
    return pl.pallas_call(
        return_kernel,
        out_shape=[
            f32(8, 128), f32(128, D), f32(128, KVD), f32(128, KVD), f32(128, D), f32(128, FF), f32(128, FF), f32(352, D), f32(2, 128, 1),
        ],
        in_specs=[VM] * 12,
        out_specs=[VM] * 9,
        scratch_shapes=[
            pltpu.VMEM((16, 8, 128), F32), pltpu.VMEM((8, 8, 128), F32), pltpu.VMEM((8, 128), F32),
            pltpu.VMEM((8, 176, 128), BF), pltpu.VMEM((8, 48, 128), BF),
            pltpu.VMEM((2, FF, 128), BF), pltpu.VMEM((8, 8, 48, 128), BF), pltpu.VMEM((128, D), BF),
            *pair(16), *pair(7), *pair(8), *pair(8), *pair(56), *pair(7), *pair(14), dma((11,)),
        ],
        compiler_params=params(8),
        name="return_grads",
    )(stats, gu, qkv, out, down, g1, g2, w_query, w_key, w_value, w_gate, w_up)


def local(hidden_in, teacher, doc_ids, valid_mask, norm1_gain, w_query, w_key, w_value, w_out, norm2_gain, w_gate, w_up, w_down):
    c = lax.axis_index(("y_hi", "z"))
    g1 = norm1_gain.astype(F32)
    g2 = norm2_gain.astype(F32)
    valid = valid_mask.astype(F32)
    tabs = rope_tables(c)
    blocks = doc_ids.reshape(16, 64)
    key_docs = jnp.concatenate([blocks[:8], blocks[:7:-1]], axis=1)
    meta = jnp.concatenate([key_docs, valid_mask[None], jnp.zeros((7, 128), jnp.int32)], axis=0)

    n1_all, metas, wqkv, wo, wt = enter(
        hidden_in, meta, g1[:, None], g2[:, None], w_query, w_key, w_value, w_gate, w_up, w_out
    )
    n1_all = n1_all.reshape(1024, D)
    wo = wo.reshape(256, D)
    qkv = dot(n1_all, wqkv, 1, 1)
    a, qp, kv, lse, wgu, wd = attend(qkv, metas, tabs, wt, w_down)

    def parts(v):
        return v.astype(BF).reshape(8, 128, D)

    wide = jax.ShapeDtypeStruct((128, D), F32)
    y1, n2_all, wgu = exchange(1, op_mid, parts(dot(a, wo, 1, 0)), (hidden_in,), (wide,), sides=[YSwap(wgu)])
    n2_all = n2_all.reshape(1024, D)
    wgu = wgu.reshape(1408, D)
    gate = dot(n2_all, wgu[:704], 1, 1)
    up = dot(n2_all, wgu[704:], 1, 1)
    sg = jax.nn.sigmoid(gate)
    act = gate * sg
    mid = (act * up).astype(BF)
    layer_out, dy, loss_rows, dy_all = exchange(
        2,
        op_loss,
        parts(dot(mid, wd, 1, 0)),
        (y1, teacher, valid[:, None]),
        (jax.ShapeDtypeStruct((128, D), BF), wide, jax.ShapeDtypeStruct((128, 1), F32)),
    )
    dy_all = dy_all.reshape(1024, D)

    grad_down = dot(mid, dy_all, 0, 0).astype(BF)
    dmid = dot(dy_all, wd, 1, 1)
    dgate = (dmid * up * sg * (1.0 + gate * (1.0 - sg))).astype(BF)
    dup = (dmid * act).astype(BF)
    dgu = jnp.concatenate([dgate, dup], axis=1)
    grad_gu = dot(dgu, n2_all, 0, 0).astype(BF)
    dy1, da_all, piece_gu = exchange(
        3, op_back, parts(dot(dgu, wgu, 1, 0)), (y1, dy), (wide,), sides=[SumColumns(grad_gu.reshape(2, 4, 176, D))]
    )
    da_all = da_all.reshape(1024, D)
    da = dot(da_all, wo, 1, 1).astype(BF)
    dqkv, piece_down = attend_back(qp, kv, lse, metas, tabs, da, SumRows(grad_down.reshape(2, 352, D)))
    grad_out = dot(a, da_all, 0, 0).astype(BF)
    grad_qkv = dot(dqkv, n1_all, 0, 0).astype(BF)
    grad_in, piece_qkv, piece_out, all_down = exchange(
        4,
        op_input,
        parts(dot(dqkv, wqkv, 1, 0)),
        (hidden_in, dy1),
        (wide,),
        gather=False,
        sides=[SumColumns(grad_qkv.reshape(2, 4, 48, D)), SumRows(grad_out.reshape(2, 128, D)), SpreadRows(piece_down)],
    )
    stats = jnp.concatenate([loss_rows.reshape(1, 128), valid[None], jnp.zeros((6, 128), F32)], axis=0)
    info, gq, gk, gv, go, gg, gp, gd, gains = return_grads(
        stats, piece_gu, piece_qkv, piece_out, all_down, g1[:, None], g2[:, None], w_query, w_key, w_value, w_gate, w_up
    )
    return (
        layer_out, info[0, 0], grad_in * info[1, 0], gains[0, :, 0], gq, gk, gv, go, gains[1, :, 0], gg, gp, gd,
    )


def solution(mesh):
    fine = Mesh(mesh.devices.reshape(2, 4, 4, 2, 2), AXES)
    rows = ("y_hi", "z", "x", "y_lo", "core")
    fs = ("x", "y_lo", "core")
    token, shard = P(rows, None), P(fs, None)
    return jax.shard_map(
        local,
        mesh=fine,
        in_specs=(token, token, shard, P(rows), P(fs), shard, shard, shard, shard, P(fs), shard, shard, shard),
        out_specs=(token, P(), token, P(fs), shard, shard, shard, shard, P(fs), shard, shard, shard),
        check_vma=False,
    )
```

```python
import functools

import jax
import jax.numpy as jnp
from jax import lax
from jax.experimental import pallas as pl
from jax.experimental.pallas import tpu as pltpu
from jax.sharding import Mesh, PartitionSpec as P

D = 2048
HEADS = 32
KV_HEADS = 4
HD = 64
FF = 5632
KVD = 256
EPSILON = 1e-05
THETA = 10000.0
NEGATIVE = -1e30
AXES = ("y_hi", "z", "x", "y_lo", "core")
BF = jnp.bfloat16
F32 = jnp.float32


def dot(a, b, ca, cb):
    return lax.dot_general(a, b, (((ca,), (cb,)), ((), ())), preferred_element_type=F32)


def tables(positions):
    indices = jnp.arange(HD // 2, dtype=jnp.int32).astype(F32)
    frequency = THETA ** (-(indices * 2.0 / HD))
    angles = positions.astype(F32)[:, None] * frequency[None, :]
    angles = jnp.concatenate([angles, angles], axis=1)
    return jnp.cos(angles), jnp.sin(angles)


def positions_of(c):
    t = jnp.arange(64, dtype=jnp.int32)
    return jnp.concatenate([c * 64 + t, (15 - c) * 64 + t])


MESH = pl.DeviceIdType.MESH
HALVES = (pl.ds(0, 64), pl.ds(64, 64))
VM = pl.BlockSpec(memory_space=pltpu.VMEM)
HB = pl.BlockSpec(memory_space=pl.ANY)


def params(number):
    return pltpu.CompilerParams(collective_id=number, has_side_effects=True, vmem_limit_bytes=56 * 2**20)


def send(src, dst, sems, i, device):
    copy = pltpu.make_async_remote_copy(
        src_ref=src, dst_ref=dst, send_sem=sems[0].at[i], recv_sem=sems[1].at[i], device_id=device, device_id_type=MESH
    )
    copy.start()
    return copy


def meet(devices):
    barrier = pltpu.get_barrier_semaphore()
    for device in devices:
        pl.semaphore_signal(barrier, inc=1, device_id=device, device_id_type=MESH)
    pl.semaphore_wait(barrier, len(devices))


class Ring:
    def __init__(self):
        x, core = lax.axis_index("x"), lax.axis_index("core")
        self.x, self.core = x, core
        self.right_x, self.left_x, self.far_x = lax.rem(x + 1, 4), lax.rem(x + 3, 4), lax.rem(x + 2, 4)
        self.right, self.left, self.sibling = {"x": self.right_x}, {"x": self.left_x}, {"core": 1 - core}


class Gather:
    def __init__(self, ring, own, out, sems, local_sem):
        self.r, self.own, self.out, self.sems, self.local_sem = ring, own, out, sems, local_sem
        self.c = {}

    def slot(self, x, half):
        return self.out.at[x * 2 + self.r.core, HALVES[half]]

    def start(self, half):
        r, src, dst = self.r, self.own.at[HALVES[half]], self.slot(self.r.x, half)
        first, second = (r.right, r.left) if half == 0 else (r.left, r.right)
        i, j = (0, 3) if half == 0 else (2, 1)
        self.c[i] = send(src, dst, self.sems, i, first)
        self.c[j] = send(src, dst, self.sems, j, second)
        self.c[6 + half] = send(src, dst, self.sems, 6 + half, r.sibling)
        copy = pltpu.make_async_copy(src, dst, self.local_sem.at[half])
        copy.start()
        self.c[14 + half] = copy

    def forward(self, between=lambda: None):
        r, c = self.r, self.c
        for step, (got, x, half, onward, core_i) in enumerate((
            (0, r.left_x, 0, (4, r.right), 8),
            (2, r.right_x, 1, (5, r.left), 11),
            (1, r.left_x, 1, None, 9),
            (3, r.right_x, 0, None, 10),
            (4, r.far_x, 0, None, 12),
            (5, r.far_x, 1, None, 13),
        )):
            if step == 2:
                between()
            c[got].wait_recv()
            block = self.slot(x, half)
            if onward is not None:
                c[onward[0]] = send(block, block, self.sems, onward[0], onward[1])
            c[core_i] = send(block, block, self.sems, core_i, r.sibling)

    def finish(self):
        c = self.c
        for i in range(6, 14):
            c[i].wait_recv()
        for i in range(14):
            c[i].wait_send()
        c[14].wait()
        c[15].wait()


def norm_scale(v):
    return lax.rsqrt(jnp.mean(v * v, axis=1, keepdims=True) + EPSILON)


class Side:
    in_place = False

    def middle(self):
        pass


class Torus:
    def __init__(self):
        self.y_hi, self.y_lo, self.z = lax.axis_index("y_hi"), lax.axis_index("y_lo"), lax.axis_index("z")
        self.y = self.y_hi * 2 + self.y_lo
        self.ys = [(dy, lax.rem(self.y + dy, 4)) for dy in (1, 3, 2)]
        self.zs = [(dz, lax.rem(self.z + dz, 4)) for dz in (1, 3, 2)]
        self.peers = [self.y_device(y) for _, y in self.ys] + [{"z": z} for _, z in self.zs]

    def y_device(self, y):
        return {"y_hi": y // 2, "y_lo": lax.rem(y, 2)}


def lanes_at(start, size):
    return pl.ds(pl.multiple_of(start, 128), size)


def add_up(out, terms, lead, rows):
    steps = rows // 16

    def body(k, _):
        i, r = k // steps, pl.ds(pl.multiple_of(lax.rem(k, steps) * 16, 16), 16)
        total = None
        for at in terms:
            term = at(i, r).astype(F32)
            total = term if total is None else total + term
        out(i, r, total.astype(BF))
        return 0

    lax.fori_loop(0, lead * steps, body, 0)


class Ag:
    def __init__(self, ring, buf, sems):
        r = self.r = ring
        self.buf, self.sems = buf, sems
        self.plan = (
            (r.x, 0, r.right), (r.x, 1, r.right), (r.x, 1, r.left), (r.x, 0, r.left),
            (r.left_x, 0, r.right), (r.right_x, 1, r.left),
            (r.x, 0, r.sibling), (r.x, 1, r.sibling),
            (r.left_x, 0, r.sibling), (r.left_x, 1, r.sibling), (r.right_x, 0, r.sibling), (r.right_x, 1, r.sibling),
            (r.far_x, 0, r.sibling), (r.far_x, 1, r.sibling),
        )

    def copy(self, i):
        x, half, device = self.plan[i]
        block = self.buf.at[x * 2 + self.r.core, HALVES[half]]
        return pltpu.make_async_remote_copy(
            src_ref=block, dst_ref=block, send_sem=self.sems[0].at[i], recv_sem=self.sems[1].at[i],
            device_id=device, device_id_type=MESH,
        )

    def begin(self, half):
        for i in ((0, 3, 6), (2, 1, 7))[half]:
            self.copy(i).start()

    def near(self):
        for got, onward in ((0, (4, 8)), (2, (5, 11)), (1, (9,)), (3, (10,))):
            self.copy(got).wait_recv()
            for i in onward:
                self.copy(i).start()

    def far(self):
        for got, onward in ((4, 12), (5, 13)):
            self.copy(got).wait_recv()
            self.copy(onward).start()

    def have(self, *which):
        for i in which:
            self.copy(i).wait_recv()

    def drain(self):
        for i in range(14):
            self.copy(i).wait_send()


class Rs:
    def __init__(self, ring, parts, held, got, sems):
        r = self.r = ring
        self.parts, self.held, self.got, self.sems = parts, held, got, sems
        self.blocks = (r.far_x, r.right_x, r.left_x, r.x)
        a, b = HALVES
        self.plan = {
            4: (held.at[0, a], got.at[4, a], r.right), 5: (held.at[0, b], got.at[4, b], r.left),
            6: (held.at[1, b], got.at[5, b], r.right), 7: (held.at[2, a], got.at[5, a], r.left),
            8: (held.at[1, a], got.at[6, a], r.right), 9: (held.at[2, b], got.at[6, b], r.left),
        }

    def swap(self, i, x):
        return pltpu.make_async_remote_copy(
            src_ref=self.parts.at[x * 2 + 1 - self.r.core], dst_ref=self.got.at[i], send_sem=self.sems[0].at[i],
            recv_sem=self.sems[1].at[i], device_id=self.r.sibling, device_id_type=MESH,
        )

    def copy(self, i):
        if i < 4:
            return self.swap(i, self.blocks[i])
        src, dst, device = self.plan[i]
        return pltpu.make_async_remote_copy(
            src_ref=src, dst_ref=dst, send_sem=self.sems[0].at[i], recv_sem=self.sems[1].at[i],
            device_id=device, device_id_type=MESH,
        )

    def pair(self, i, half):
        x = self.blocks[i]

        def body(k, _):
            rows = pl.ds(half * 64 + k * 16, 16)
            total = self.parts[x * 2 + self.r.core, rows, :].astype(F32) + self.got[i, rows, :].astype(F32)
            self.held[i, rows, :] = total.astype(BF)
            return 0

        lax.fori_loop(0, 4, body, 0)

    def onward(self, i, half):
        def body(k, _):
            rows = pl.ds(half * 64 + k * 16, 16)
            total = self.held[i, rows, :].astype(F32) + self.got[4, rows, :].astype(F32)
            self.held[i, rows, :] = total.astype(BF)
            return 0

        lax.fori_loop(0, 4, body, 0)

    def send_left(self):
        self.copy(2).wait_recv()
        self.pair(2, 0)
        self.copy(7).start()

    def send_right(self):
        self.copy(1).wait_recv()
        self.pair(1, 1)
        self.copy(6).start()

    def send_far(self):
        self.copy(0).wait_recv()
        self.pair(0, 0)
        self.copy(4).start()
        self.pair(0, 1)
        self.copy(5).start()

    def relay(self):
        self.pair(1, 0)
        self.pair(2, 1)
        self.copy(4).wait_recv()
        self.onward(1, 0)
        self.copy(8).start()
        self.copy(5).wait_recv()
        self.onward(2, 1)
        self.copy(9).start()
        self.copy(3).wait_recv()

    def ready(self, half):
        for i in ((7, 8), (6, 9))[half]:
            self.copy(i).wait_recv()

    def total(self, rows):
        r = self.r
        return (
            self.parts[r.x * 2 + r.core, rows, :].astype(F32)
            + self.got[3, rows, :].astype(F32)
            + self.got[5, rows, :].astype(F32)
            + self.got[6, rows, :].astype(F32)
        )

    def drain(self):
        for i in range(10):
            self.copy(i).wait_send()


def middle_kernel(
    side, a_ref, wo_ref, x_ref, teacher_ref, valid_ref, half_w_ref, wd_ref,
    out_ref, loss_ref, dy1_ref, da_ref, dag_out, ggu_ref, piece_ref,
    w, n2, dyg, dag, parts, held, got, y1, dy, gate, up, mid, mid_t, dgate, dup, dg_t, du_t, gd, stage,
    rs1_s, rs1_r, ag1_s, ag1_r, rs2_s, rs2_r, ag2_s, ag2_r, rs3_s, rs3_r, ag3_s, ag3_r, w_s, w_r, loc, *side_scratch,
):
    ring = Ring()
    y_lo = lax.axis_index("y_lo")
    near, other = y_partners()
    side.bind(ring, (gd,), (piece_ref,), side_scratch)
    meet([ring.right, ring.left, ring.sibling, near, other] + side.peers)
    here = ring.x * 2 + ring.core

    wcopies = []
    for dx in range(4):
        lanes = group_lanes(lax.rem(ring.x + 4 - dx, 4), y_lo)
        src, dst = half_w_ref.at[:, :, :, lanes], w.at[:, :, :, lanes]
        wcopies.append(send(src, dst, (w_s, w_r), dx, (near, other)[dx // 2]))
        copy = pltpu.make_async_copy(src, dst, loc.at[dx])
        copy.start()
        wcopies.append(copy)

    def rows_of(x):
        return pl.ds(pl.multiple_of(x * 256, 256), 256)

    def block(buf, x):
        return buf[pl.ds(x * 2, 2)].reshape(256, D)

    def put(x, product):
        def body(k, _):
            lanes = lanes_at(k * 512, 512)
            parts[pl.ds(x * 2, 2), :, lanes] = product(lanes).astype(BF).reshape(2, 128, 512)
            return 0

        lax.fori_loop(0, 4, body, 0)

    def reduced(rs, op, ag, buf):
        for half in range(2):
            rs.ready(half)

            def body(k, _, half=half):
                rows = pl.ds(half * 64 + k * 16, 16)
                buf[here, rows, :] = op(rows, rs.total(rows)).astype(BF)
                return 0

            lax.fori_loop(0, 4, body, 0)
            ag.begin(half)

    def over_blocks(ag, rs, work):
        def step(i, _):
            at = functools.partial(jnp.equal, i)

            @pl.when(at(0))
            def _():
                ag.have(6, 7)

            @pl.when(at(1))
            def _():
                ag.near()
                ag.have(8, 9)

            @pl.when(at(2))
            def _():
                ag.have(10, 11)
                if rs is not None:
                    rs.send_left()

            @pl.when(at(3))
            def _():
                if rs is not None:
                    rs.send_right()
                ag.far()
                ag.have(12, 13)

            x = lax.rem(ring.x + jnp.where(at(1), 3, jnp.where(at(2), 1, jnp.where(at(3), 2, 0))), 4)
            work(x)
            if rs is not None:
                rs.swap(3 - i, x).start()
            return 0

        lax.fori_loop(0, 4, step, 0)

    rs = Rs(ring, parts, held, got, (rs1_s, rs1_r))
    ag = Ag(ring, n2, (ag1_s, ag1_r))
    for i in range(4):
        x = rs.blocks[i]
        put(x, lambda lanes, x=x: nn(a_ref[rows_of(x), :], wo_ref[:, lanes]))
        rs.copy(i).start()
        if i == 1:
            rs.send_far()
        elif i == 2:
            rs.send_right()
        elif i == 3:
            rs.send_left()
    rs.relay()

    def op1(rows, total):
        v = x_ref[rows, :].astype(F32) + total
        y1[rows, :] = v
        return v * norm_scale(v)

    reduced(rs, op1, ag, n2)
    rs.drain()
    for copy in wcopies:
        copy.wait()

    rs = Rs(ring, parts, held, got, (rs2_s, rs2_r))

    def forward(x):
        rows = rows_of(x)
        gate[rows, :] = nt(block(n2, x), w[0].reshape(704, D))
        up[rows, :] = nt(block(n2, x), w[1].reshape(704, D))

        def body(k, _):
            r = pl.ds(pl.multiple_of(x * 256 + k * 32, 32), 32)
            g = gate[r, :]
            mid[pl.ds(pl.multiple_of(k * 32, 32), 32), :] = (g * jax.nn.sigmoid(g) * up[r, :]).astype(BF)
            return 0

        lax.fori_loop(0, 8, body, 0)
        put(x, lambda lanes: nn(mid[...], wd_ref[:, lanes]))
        mid_t[:, rows] = mid[...].T

    over_blocks(ag, rs, forward)
    rs.send_far()
    rs.relay()
    ag.drain()

    def op2(rows, total):
        v = y1[rows, :] + total
        out_ref[rows, :] = v.astype(BF)
        miss = v - teacher_ref[rows, :].astype(F32)
        valid = valid_ref[rows, :]
        loss_ref[rows, :] = valid * jnp.mean(miss * miss, axis=1, keepdims=True)
        dy[rows, :] = valid * miss
        return valid * miss

    ag = Ag(ring, dyg, (ag2_s, ag2_r))
    reduced(rs, op2, ag, dyg)
    rs.drain()

    rs = Rs(ring, parts, held, got, (rs3_s, rs3_r))

    def backward(x):
        rows = rows_of(x)
        dgate_mid = nt(block(dyg, x), wd_ref[...])
        dmid[...] = dgate_mid

        def body(k, _):
            r = pl.ds(pl.multiple_of(x * 256 + k * 32, 32), 32)
            q = pl.ds(pl.multiple_of(k * 32, 32), 32)
            g, dm = gate[r, :], dmid[q, :]
            sg = jax.nn.sigmoid(g)
            dgate[q, :] = (dm * up[r, :] * sg * (1.0 + g * (1.0 - sg))).astype(BF)
            dup[q, :] = (dm * (g * sg)).astype(BF)
            return 0

        lax.fori_loop(0, 8, body, 0)
        put(x, lambda lanes: nn(dgate[...], w[0, :, :, lanes].reshape(704, 512)) + nn(dup[...], w[1, :, :, lanes].reshape(704, 512)))
        dg_t[:, rows] = dgate[...].T
        du_t[:, rows] = dup[...].T

    dmid = stage
    over_blocks(ag, rs, backward)
    rs.send_far()

    def grad_down(k, _):
        lanes = lanes_at(k * 512, 512)
        gd[:, :, lanes] = nn(mid_t[...], dyg[:, :, lanes].reshape(1024, 512)).astype(BF).reshape(2, 352, 512)
        return 0

    lax.fori_loop(0, 4, grad_down, 0)
    side.start()
    rs.relay()
    ag.drain()

    def op3(rows, total):
        v = back_norm(y1[rows, :], dy[rows, :], total)
        dy1_ref[rows, :] = v
        return v

    ag = Ag(ring, dag, (ag3_s, ag3_r))
    reduced(rs, op3, ag, dag)
    rs.drain()

    def grad_gu(first, last):
        def body(k, _):
            lanes = lanes_at(k * 256, 256)
            tokens = n2[:, :, lanes].reshape(1024, 256)
            ggu_ref[0, :, lanes] = nn(dg_t[...], tokens).astype(BF)
            ggu_ref[1, :, lanes] = nn(du_t[...], tokens).astype(BF)
            return 0

        lax.fori_loop(first, last, body, 0)

    def to_attention(x):
        da_ref[rows_of(x), :] = nt(block(dag, x), wo_ref[...]).astype(BF)
        grad_gu(2 * x, 2 * x + 2)

    over_blocks(ag, None, to_attention)
    side.middle()
    copy = pltpu.make_async_copy(dag, dag_out, loc.at[0])
    copy.start()
    ag.drain()
    side.finish()
    copy.wait()


def middle(a, wo, x, teacher, valid, half_w, wd):
    dma = pltpu.SemaphoreType.DMA
    pair = lambda n: [dma((n,)), dma((n,))]
    big = pltpu.VMEM((8, 128, D), BF)
    side = SumRows(jax.ShapeDtypeStruct((2, 352, D), BF))
    return pl.pallas_call(
        functools.partial(middle_kernel, side),
        out_shape=[
            jax.ShapeDtypeStruct((128, D), BF), jax.ShapeDtypeStruct((128, 1), F32), jax.ShapeDtypeStruct((128, D), F32),
            jax.ShapeDtypeStruct((1024, 256), BF), jax.ShapeDtypeStruct((8, 128, D), BF), jax.ShapeDtypeStruct((2, 704, D), BF),
            *side.shapes,
        ],
        in_specs=[VM] * 5 + [HB, VM],
        out_specs=[VM, VM, VM, VM, HB, VM, VM],
        scratch_shapes=[
            pltpu.VMEM((2, 2, 352, D), BF), big, big, big, big, pltpu.VMEM((4, 128, D), BF), pltpu.VMEM((7, 128, D), BF),
            pltpu.VMEM((128, D), F32), pltpu.VMEM((128, D), F32),
            pltpu.VMEM((1024, 704), F32), pltpu.VMEM((1024, 704), F32),
            pltpu.VMEM((256, 704), BF), pltpu.VMEM((704, 1024), BF), pltpu.VMEM((256, 704), BF), pltpu.VMEM((256, 704), BF),
            pltpu.VMEM((704, 1024), BF), pltpu.VMEM((704, 1024), BF), pltpu.VMEM((2, 352, D), BF), pltpu.VMEM((256, 704), F32),
            *pair(10), *pair(14), *pair(10), *pair(14), *pair(10), *pair(14), *pair(4), dma((4,)), *side.scratch,
        ],
        compiler_params=pltpu.CompilerParams(collective_id=1, has_side_effects=True, vmem_limit_bytes=63 * 2**20),
        name="middle",
    )(a, wo, x, teacher, valid, half_w, wd)


class SumColumns(Side):
    def __init__(self, grads):
        r = self.rows = grads.shape[2]
        dma = pltpu.SemaphoreType.DMA
        self.operands = [grads]
        self.shapes = [jax.ShapeDtypeStruct((r, 1024), BF)]
        self.scratch = [
            pltpu.VMEM((4, 4, r, 512), BF), pltpu.VMEM((4, 2, 2, r, 512), BF),
            pltpu.VMEM((3, r, 512), BF), pltpu.VMEM((3, r, 512), BF),
            dma((9,)), dma((9,)), dma((6,)), dma((6,)), dma((3,)),
        ]

    def bind(self, ring, ins, outs, scratch):
        (self.g,), (self.out,) = ins, outs
        self.by, self.bz, self.by2, self.bz2, s1, r1, s2, r2, self.loc = scratch
        self.one, self.two = (s1, r1), (s2, r2)
        self.t = Torus()
        self.peers = self.t.peers

    def start(self):
        t, g = self.t, self.g
        self.c = []
        for i, (dy, y) in enumerate(t.ys):
            src = g.at[y // 2, :, :, lanes_at(lax.rem(y, 2) * 1024, 512)]
            self.c.append(send(src, self.by.at[dy], self.one, i, t.y_device(y)))
        for i, (dz, z) in enumerate(t.zs):
            for yl in range(2):
                src = g.at[:, z, :, pl.ds(yl * 1024 + 512, 512)]
                self.c.append(send(src, self.bz.at[dz, yl], self.one, 3 + 2 * i + yl, {"z": z}))
        self.l = [pltpu.make_async_copy(g.at[t.y_hi, :, :, lanes_at(t.y_lo * 1024, 512)], self.by.at[0], self.loc.at[0])]
        for yl in range(2):
            self.l.append(
                pltpu.make_async_copy(g.at[:, t.z, :, pl.ds(yl * 1024 + 512, 512)], self.bz.at[0, yl], self.loc.at[1 + yl])
            )
        for copy in self.l:
            copy.start()

    def middle(self):
        t, by, bz = self.t, self.by, self.bz
        for copy in self.l:
            copy.wait()
        for copy in self.c:
            copy.wait_recv()

        def put_y(i, r, v):
            by[0, i, r, :] = v

        def put_z(i, r, v):
            bz[0, i // 2, lax.rem(i, 2), r, :] = v

        add_up(put_y, [lambda i, r, k=k: by[k, i, r, :] for k in range(4)], 4, self.rows)
        add_up(put_z, [lambda i, r, k=k: bz[k, i // 2, lax.rem(i, 2), r, :] for k in range(4)], 4, self.rows)
        self.c2 = []
        for i, (dz, z) in enumerate(t.zs):
            self.c2.append(send(by.at[0, z], self.by2.at[dz - 1], self.two, i, {"z": z}))
        for i, (dy, y) in enumerate(t.ys):
            self.c2.append(send(bz.at[0, lax.rem(y, 2), y // 2], self.bz2.at[dy - 1], self.two, 3 + i, t.y_device(y)))

    def finish(self):
        t, by, bz, by2, bz2, out = self.t, self.by, self.bz, self.by2, self.bz2, self.out
        for copy in self.c2:
            copy.wait_recv()

        def put_a(i, r, v):
            out[r, 0:512] = v

        def put_b(i, r, v):
            out[r, 512:1024] = v

        add_up(put_a, [lambda i, r: by[0, t.z, r, :]] + [lambda i, r, k=k: by2[k, r, :] for k in range(3)], 1, self.rows)
        add_up(put_b, [lambda i, r: bz[0, t.y_lo, t.y_hi, r, :]] + [lambda i, r, k=k: bz2[k, r, :] for k in range(3)], 1, self.rows)
        for copy in self.c + self.c2:
            copy.wait_send()


class SumRows(Side):
    def __init__(self, grads):
        r = self.rows = grads.shape[1]
        dma = pltpu.SemaphoreType.DMA
        self.operands = [grads]
        self.shapes = [jax.ShapeDtypeStruct((2, r, 128), BF)]
        self.scratch = [
            pltpu.VMEM((4, r, 512), BF), pltpu.VMEM((4, 2, 2, r, 128), BF),
            pltpu.VMEM((3, r, 128), BF), pltpu.VMEM((3, r, 128), BF),
            dma((9,)), dma((9,)), dma((6,)), dma((6,)), dma((3,)),
        ]

    def bind(self, ring, ins, outs, scratch):
        (self.g,), (self.out,) = ins, outs
        self.by, self.bz, self.by2, self.bz2, s1, r1, s2, r2, self.loc = scratch
        self.one, self.two = (s1, r1), (s2, r2)
        self.t = Torus()
        self.peers = self.t.peers

    def start(self):
        t, g = self.t, self.g
        self.c = []
        for i, (dy, y) in enumerate(t.ys):
            src = g.at[lax.rem(y, 2), :, lanes_at((y // 2) * 1024, 512)]
            self.c.append(send(src, self.by.at[dy], self.one, i, t.y_device(y)))
        for i, (dz, z) in enumerate(t.zs):
            for yh in range(2):
                src = g.at[:, :, lanes_at(yh * 1024 + 512 + z * 128, 128)]
                self.c.append(send(src, self.bz.at[dz, yh], self.one, 3 + 2 * i + yh, {"z": z}))
        self.l = [pltpu.make_async_copy(g.at[t.y_lo, :, lanes_at(t.y_hi * 1024, 512)], self.by.at[0], self.loc.at[0])]
        for yh in range(2):
            self.l.append(
                pltpu.make_async_copy(g.at[:, :, lanes_at(yh * 1024 + 512 + t.z * 128, 128)], self.bz.at[0, yh], self.loc.at[1 + yh])
            )
        for copy in self.l:
            copy.start()

    def middle(self):
        t, by, bz = self.t, self.by, self.bz
        for copy in self.l:
            copy.wait()
        for copy in self.c:
            copy.wait_recv()

        def put_y(i, r, v):
            by[0, r, :] = v

        def put_z(i, r, v):
            bz[0, i // 2, lax.rem(i, 2), r, :] = v

        add_up(put_y, [lambda i, r, k=k: by[k, r, :] for k in range(4)], 1, self.rows)
        add_up(put_z, [lambda i, r, k=k: bz[k, i // 2, lax.rem(i, 2), r, :] for k in range(4)], 4, self.rows)
        self.c2 = []
        for i, (dz, z) in enumerate(t.zs):
            self.c2.append(send(by.at[0, :, lanes_at(z * 128, 128)], self.by2.at[dz - 1], self.two, i, {"z": z}))
        for i, (dy, y) in enumerate(t.ys):
            self.c2.append(send(bz.at[0, y // 2, lax.rem(y, 2)], self.bz2.at[dy - 1], self.two, 3 + i, t.y_device(y)))

    def finish(self):
        t, by, bz, by2, bz2, out = self.t, self.by, self.bz, self.by2, self.bz2, self.out
        for copy in self.c2:
            copy.wait_recv()

        def put_a(i, r, v):
            out[0, r, :] = v

        def put_b(i, r, v):
            out[1, r, :] = v

        own = lanes_at(t.z * 128, 128)
        add_up(put_a, [lambda i, r: by[0, r, own]] + [lambda i, r, k=k: by2[k, r, :] for k in range(3)], 1, self.rows)
        add_up(put_b, [lambda i, r: bz[0, t.y_hi, t.y_lo, r, :]] + [lambda i, r, k=k: bz2[k, r, :] for k in range(3)], 1, self.rows)
        for copy in self.c + self.c2:
            copy.wait_send()


def piece_lanes(c, part):
    return lanes_at((c // 4) * 1024 + part * 512 + lax.rem(c, 4) * 128, 128)


def ctx_at(k):
    y_hi, z = lax.axis_index("y_hi"), lax.axis_index("z")
    y, zz = (1 - y_hi if k // 4 else y_hi), lax.rem(z + k % 4, 4)
    return y * 4 + zz, {"y_hi": y, "z": zz}


class Spread:
    def __init__(self, piece, slot, sems, base, y_first, local):
        self.piece, self.slot, self.sems, self.base, self.y_first, self.local = piece, slot, sems, base, y_first, local

    def copy(self, k, src, c, device):
        return pltpu.make_async_remote_copy(
            src_ref=src, dst_ref=self.slot(c), send_sem=self.sems[0].at[self.base + k - 1],
            recv_sem=self.sems[1].at[self.base + k - 1], device_id=device, device_id_type=MESH,
        )

    def first(self, k):
        here, _ = ctx_at(0)
        return self.copy(k, self.piece, here, ctx_at(k)[1])

    def second(self, dz):
        if self.y_first:
            c, _ = ctx_at(4)
            return self.copy(4 + dz, self.slot(c), c, ctx_at(dz)[1])
        c, _ = ctx_at(4 - dz)
        return self.copy(4 + dz, self.slot(c), c, ctx_at(4)[1])

    def own(self):
        return pltpu.make_async_copy(self.piece, self.slot(ctx_at(0)[0]), self.local)

    def start(self):
        for k in (4, 1, 3, 2) if self.y_first else (1, 3, 2, 4):
            self.first(k).start()
        self.own().start()

    def relay(self):
        if self.y_first:
            self.first(4).wait_recv()
            for dz in (1, 3, 2):
                self.second(dz).start()
        else:
            for dz in (1, 3, 2):
                self.first(dz).wait_recv()
                self.second(dz).start()

    def finish(self):
        if self.y_first:
            for dz in (1, 3, 2):
                self.first(dz).wait_recv()
        else:
            self.first(4).wait_recv()
        for dz in (1, 3, 2):
            self.second(dz).wait_recv()
            self.second(dz).wait_send()
        for k in (1, 2, 3, 4):
            self.first(k).wait_send()
        self.own().wait()


class SpreadRows(Side):
    def __init__(self, pieces):
        r = pieces.shape[1]
        dma = pltpu.SemaphoreType.DMA
        self.operands = [pieces]
        self.shapes = [jax.ShapeDtypeStruct((r, D), BF)]
        self.scratch = [dma((14,)), dma((14,)), dma((2,))]

    def bind(self, ring, ins, outs, scratch):
        (p,), (out,) = ins, outs
        self.peers = [ctx_at(k)[1] for k in range(1, 8)]
        self.s = [
            Spread(
                p.at[part], lambda c, part=part: out.at[:, piece_lanes(c, part)], scratch[:2], part * 7, part == 0,
                scratch[2].at[part],
            )
            for part in range(2)
        ]

    def start(self):
        for s in self.s:
            s.start()

    def middle(self):
        for s in self.s:
            s.relay()

    def finish(self):
        for s in self.s:
            s.finish()


class Move(Side):
    def __init__(self, pieces):
        dma = pltpu.SemaphoreType.DMA
        self.operands = [pieces]
        self.shapes = [jax.ShapeDtypeStruct((8, pieces.shape[0], 128), BF)]
        self.scratch = [dma((8,)), dma((8,))]

    def bind(self, ring, ins, outs, scratch):
        (self.p,), (self.out,), self.sems = ins, outs, scratch
        x, self.y_lo, core = lax.axis_index("x"), lax.axis_index("y_lo"), lax.axis_index("core")
        self.here16, self.here8 = x * 4 + self.y_lo * 2 + core, x * 2 + core
        self.peers = [device for _, device in group_peers()]

    def same(self, j):
        return self.here16 == self.y_lo * 8 + j

    def away(self, j):
        return pltpu.make_async_remote_copy(
            src_ref=self.p.at[:, pl.ds(j * 128, 128)], dst_ref=self.out.at[self.here8], send_sem=self.sems[0].at[j],
            recv_sem=self.sems[1].at[self.here8], device_id={"x": self.y_lo * 2 + j // 4, "y_lo": j // 2 % 2, "core": j % 2},
            device_id_type=MESH,
        )

    def stay(self, j):
        return pltpu.make_async_copy(self.p.at[:, pl.ds(j * 128, 128)], self.out.at[self.here8], self.sems[1].at[self.here8])

    def start(self):
        for j in range(8):

            @pl.when(self.same(j))
            def _():
                self.stay(j).start()

            @pl.when(jnp.logical_not(self.same(j)))
            def _():
                self.away(j).start()

    def arrive(self, s):
        pltpu.make_async_copy(self.out.at[s], self.out.at[s], self.sems[1].at[s]).wait()

    def drain(self):
        for j in range(8):

            @pl.when(jnp.logical_not(self.same(j)))
            def _():
                self.away(j).wait_send()

    def finish(self):
        for s in range(8):
            self.arrive(s)
        self.drain()


def group_peers():
    x, y_lo, core = lax.axis_index("x"), lax.axis_index("y_lo"), lax.axis_index("core")
    found = []
    for k in range(1, 16):
        dx, dy, dc = k // 4, k // 2 % 2, k % 2
        found.append((k, {"x": lax.rem(x + dx, 4), "y_lo": 1 - y_lo if dy else y_lo, "core": 1 - core if dc else core}))
    return found


def last_kernel(
    down, move, cols, rows_side, dqkv_ref, wqkv_ref, n1_ref, a_ref, dag_ref, x_ref, dy1_ref, piece_down_ref, piece_gu_ref,
    grad_ref, down_ref, got_gu_ref, piece_qkv_ref, piece_out_ref,
    parts, held, got, gq, go, dqkv_t, a_t, rs_s, rs_r, *side_scratch,
):
    ring = Ring()
    scratch = list(side_scratch)

    def take(side):
        taken = scratch[: len(side.scratch)]
        del scratch[: len(side.scratch)]
        return taken

    down.bind(ring, (piece_down_ref,), (down_ref,), take(down))
    move.bind(ring, (piece_gu_ref,), (got_gu_ref,), take(move))
    cols.bind(ring, (gq,), (piece_qkv_ref,), take(cols))
    rows_side.bind(ring, (go,), (piece_out_ref,), take(rows_side))
    meet([ring.right, ring.left, ring.sibling] + down.peers + move.peers + cols.peers + rows_side.peers)
    down.start()

    rs = Rs(ring, parts, held, got, (rs_s, rs_r))
    for i in range(4):
        x = rs.blocks[i]

        def body(k, _, x=x):
            lanes = lanes_at(k * 512, 512)
            block = nn(dqkv_ref[pl.ds(pl.multiple_of(x * 256, 256), 256), :], wqkv_ref[:, lanes])
            parts[pl.ds(x * 2, 2), :, lanes] = block.astype(BF).reshape(2, 128, 512)
            return 0

        lax.fori_loop(0, 4, body, 0)
        rs.copy(i).start()
        if i == 1:
            rs.send_far()
        elif i == 2:
            rs.send_right()
        elif i == 3:
            rs.send_left()
    move.start()

    dqkv_t[...] = dqkv_ref[...].T
    a_t[...] = a_ref[...].T

    def grads(k, _):
        lanes = lanes_at(k * 512, 512)
        product = nn(dqkv_t[...], n1_ref[:, :, lanes].reshape(1024, 512))
        gq[:, :, :, lanes] = product.astype(BF).reshape(2, 4, 48, 512)
        product = nn(a_t[...], dag_ref[:, :, lanes].reshape(1024, 512))
        go[:, :, lanes] = product.astype(BF).reshape(2, 128, 512)
        return 0

    lax.fori_loop(0, 4, grads, 0)
    cols.start()
    rows_side.start()
    down.middle()
    rs.relay()
    for half in range(2):
        rs.ready(half)

        def body(k, _, half=half):
            rows = pl.ds(half * 64 + k * 16, 16)
            grad_ref[rows, :] = back_norm(x_ref[rows, :].astype(F32), dy1_ref[rows, :], rs.total(rows))
            return 0

        lax.fori_loop(0, 4, body, 0)
    cols.middle()
    rows_side.middle()
    rs.drain()
    down.finish()
    move.finish()
    cols.finish()
    rows_side.finish()


def last(dqkv, wqkv, n1, a, dag, hidden_in, dy1, piece_down, piece_gu):
    dma = pltpu.SemaphoreType.DMA
    sides = [
        SpreadRows(piece_down), Move(piece_gu),
        SumColumns(jax.ShapeDtypeStruct((2, 4, 48, D), BF)), SumRows(jax.ShapeDtypeStruct((2, 128, D), BF)),
    ]
    return pl.pallas_call(
        functools.partial(last_kernel, *sides),
        out_shape=[jax.ShapeDtypeStruct((128, D), F32)] + [s for side in sides for s in side.shapes],
        in_specs=[VM] * 9,
        out_specs=[VM] * 5,
        scratch_shapes=[
            pltpu.VMEM((8, 128, D), BF), pltpu.VMEM((4, 128, D), BF), pltpu.VMEM((7, 128, D), BF),
            pltpu.VMEM((2, 4, 48, D), BF), pltpu.VMEM((2, 128, D), BF), pltpu.VMEM((384, 1024), BF), pltpu.VMEM((256, 1024), BF),
            dma((10,)), dma((10,)), *[s for side in sides for s in side.scratch],
        ],
        compiler_params=params(4),
        name="last",
    )(dqkv, wqkv, n1, a, dag, hidden_in, dy1, piece_down, piece_gu)


def back_norm(v, grad, u):
    r = norm_scale(v)
    n = v * r
    return grad + r * (u - n * jnp.mean(u * n, axis=1, keepdims=True))


def y_partners():
    y_hi, y_lo = lax.axis_index("y_hi"), lax.axis_index("y_lo")
    return {"y_lo": 1 - y_lo}, {"y_hi": 1 - y_hi, "y_lo": 1 - y_lo}


def group_lanes(x, y_lo):
    return pl.ds(pl.multiple_of(x * 512 + y_lo * 256, 256), 256)


def tp_peers(ring):
    found = []
    for k in range(1, 8):
        dx, dc = k // 2, k % 2
        core = 1 - ring.core if dc else ring.core
        found.append((k, lax.rem(ring.x + dx, 4), core))
    return found


def enter_kernel(
    x_ref, meta_ref, g1_ref, g2_ref, wq_ref, wk_ref, wv_ref, wg_ref, wu_ref, wo_ref,
    n1_ref, metas_ref, wqkv_ref, wos_ref, wt_ref,
    own, w, ag_s, ag_r, loc, meta_s, meta_r, w_s, w_r, y_s, y_r, loc2,
):
    ring = Ring()
    y_lo = lax.axis_index("y_lo")
    near, other = y_partners()
    peers = tp_peers(ring)
    meet([{"x": x, "core": core} for _, x, core in peers] + [near, other])
    here = ring.x * 2 + ring.core
    copies = []
    for k, x, core in peers:
        copies.append(send(meta_ref, metas_ref.at[here], (meta_s, meta_r), k, {"x": x, "core": core}))
    local = [pltpu.make_async_copy(meta_ref, metas_ref.at[here], loc2.at[0])]
    local.append(pltpu.make_async_copy(wo_ref, wos_ref.at[y_lo], loc2.at[1]))
    for c in local:
        c.start()
    for half, device in enumerate((near, other)):
        copies.append(send(wo_ref.at[HALVES[half]], wos_ref.at[y_lo, HALVES[half]], (y_s, y_r), 4 + half, device))

    gath = Gather(ring, own, n1_ref, (ag_s, ag_r), loc)

    def normed(k, _):
        rows = pl.ds(pl.multiple_of(k * 16, 16), 16)
        v = x_ref[rows, :].astype(F32)
        own[rows, :] = (v * norm_scale(v)).astype(BF)
        return 0

    lax.fori_loop(0, 4, normed, 0)
    gath.start(0)

    def turned(ref, gain, k):
        return (ref[:, pl.ds(pl.multiple_of(k * 128, 128), 128)].T.astype(F32) * gain).astype(BF)

    g1, g2 = g1_ref[...], g2_ref[...]
    for f in range(16):
        w[(f // 4) * 2 + f % 2, pl.ds((f // 2 % 2) * 128, 128), :] = turned(wq_ref, g1, f)
    for ref, at in ((wk_ref, 256), (wv_ref, 320)):
        for k in range(2):
            tile = turned(ref, g1, k)
            for x in (2 * k, 2 * k + 1):
                part = tile[(x % 2) * 64 : (x % 2) * 64 + 64]
                w[2 * x, pl.ds(at, 64), :] = part
                w[2 * x + 1, pl.ds(at, 64), :] = part
    lanes = pl.ds(pl.multiple_of((ring.x * 4 + y_lo * 2 + ring.core) * 128, 128), 128)
    wcopies = {}
    for k, x, core in peers:
        wcopies[k] = send(w.at[x * 2 + core], wqkv_ref.at[:, lanes], (w_s, w_r), k, {"x": x, "core": core})
    wcopies[0] = pltpu.make_async_copy(w.at[here], wqkv_ref.at[:, lanes], loc2.at[2])
    wcopies[0].start()

    lax.fori_loop(4, 8, normed, 0)
    gath.start(1)

    def turn_some(ref, i, first, last):
        def body(k, _):
            wt_ref[i, pl.ds(pl.multiple_of(k * 128, 128), 128), :] = turned(ref, g2, k)
            return 0

        lax.fori_loop(first, last, body, 0)

    turn_some(wg_ref, 0, 0, 44)
    for dx in range(4):
        x = lax.rem(ring.x + 4 - dx, 4)
        if dx == 0:
            wcopies[0].wait()
        else:
            wcopies[2 * dx].wait_recv()
        wcopies[2 * dx + 1].wait_recv()
        block = wqkv_ref.at[:, group_lanes(x, y_lo)]
        copies.append(send(block, block, (y_s, y_r), dx, (near, other)[dx // 2]))
    turn_some(wu_ref, 1, 0, 22)
    gath.forward(lambda: turn_some(wu_ref, 1, 22, 44))
    gath.finish()
    for k in range(1, 8):
        wcopies[k].wait_send()
    for c in copies:
        c.wait()
    for c in local:
        c.wait()


def enter(hidden_in, meta, g1, g2, w_query, w_key, w_value, w_gate, w_up, w_out):
    dma = pltpu.SemaphoreType.DMA
    return pl.pallas_call(
        enter_kernel,
        out_shape=[
            jax.ShapeDtypeStruct((8, 128, D), BF),
            jax.ShapeDtypeStruct((8, 16, 128), jnp.int32),
            jax.ShapeDtypeStruct((384, D), BF),
            jax.ShapeDtypeStruct((2, 128, D), BF),
            jax.ShapeDtypeStruct((2, FF, 128), BF),
        ],
        in_specs=[VM] * 10,
        out_specs=[HB, VM, HB, HB, VM],
        scratch_shapes=[
            pltpu.VMEM((128, D), BF), pltpu.VMEM((8, 384, 128), BF),
            dma((14,)), dma((14,)), dma((2,)), dma((8,)), dma((8,)), dma((8,)), dma((8,)), dma((6,)), dma((6,)), dma((3,)),
        ],
        compiler_params=params(5),
        name="enter",
    )(hidden_in, meta, g1, g2, w_query, w_key, w_value, w_gate, w_up, w_out)


def ctx_peer(c, k):
    other = lax.rem(c + k, 8)
    return {"y_hi": other // 4, "z": lax.rem(other, 4)}


def nt(a, b):
    return dot(a, b, 1, 1)


def nn(a, b):
    return dot(a, b, 1, 0)


def key_bias(meta_ref, d, c, bias):
    docs = meta_ref[d].astype(F32)
    query_docs = meta_ref[d, pl.ds(c, 1), :].astype(F32)
    lane = lax.broadcasted_iota(jnp.int32, (128, 128), 1)
    row = lax.broadcasted_iota(jnp.int32, (128, 128), 0)

    def position(owner, i):
        return jnp.where(i < 64, owner * 64 + i, (15 - owner) * 64 + i - 64)

    query_pos = position(c, lane)
    for b in range(8):
        key_docs = jnp.broadcast_to(docs[b : b + 1, :], (128, 128)).T
        good = (query_pos >= position(b, row)) & (key_docs == query_docs)
        bias[pl.ds(b * 128, 128), :] = jnp.where(good, 0.0, NEGATIVE)


def attend_kernel(
    n1_ref, wqkv_ref, meta_ref, tab_ref, wt_ref, wdn_ref,
    a_ref, qp_ref, kv_ref, lse_ref, wgu_ref, wd_ref,
    qkv_ref, bias, probs, kv_s, kv_r, fw_s, fw_r, w_s, w_r, y_s, y_r, loc,
):
    ring = Ring()
    y_lo = lax.axis_index("y_lo")
    c = lax.axis_index("y_hi") * 4 + lax.axis_index("z")
    near, other = y_partners()
    peers = tp_peers(ring)
    meet([ctx_peer(c, k) for k in range(1, 8)] + [{"x": x, "core": core} for _, x, core in peers] + [near, other])

    lane = lax.broadcasted_iota(jnp.int32, (128, 128), 1)

    def rope(u, i):
        return u * tab_ref[i] + pltpu.roll(u, 96, 1) * tab_ref[i + 1] + pltpu.roll(u, 32, 1) * tab_ref[i + 2]

    copies, local = [], []
    here = pl.ds(pl.multiple_of((ring.x * 4 + y_lo * 2 + ring.core) * 128, 128), 128)
    for j in range(2):
        rows = pl.ds(pl.multiple_of((ring.x * 4 + 2 * j + ring.core) * 352, 32), 352)
        local.append(pltpu.make_async_copy(wt_ref.at[:, rows], wgu_ref.at[:, j, :, here], loc.at[j]))
    rows = pl.ds(pl.multiple_of(y_lo * 352, 32), 352)
    local.append(pltpu.make_async_copy(wdn_ref, wd_ref.at[rows], loc.at[2]))
    for copy in local:
        copy.start()
    for k, x, core in peers:
        for j in range(2):
            rows = pl.ds(pl.multiple_of((x * 4 + 2 * j + core) * 352, 32), 352)
            copies.append(
                send(wt_ref.at[:, rows], wgu_ref.at[:, j, :, here], (w_s, w_r), k * 2 + j, {"x": x, "core": core})
            )
    for half, device in enumerate((near, other)):
        rows = pl.ds(pl.multiple_of(y_lo * 352 + half * 176, 16), 176)
        copies.append(send(wdn_ref.at[pl.ds(half * 176, 176)], wd_ref.at[rows], (y_s, y_r), half, device))

    kv_copies = []
    qkv_ref[...] = nt(n1_ref[...], wqkv_ref[...])
    for d in range(8):
        kv_ref[d % 2, d // 2, c] = rope(qkv_ref[pl.ds(d * 128, 128), 256:384], 3).astype(BF)
    for k in range(1, 8):
        block = kv_ref.at[ring.core, :, c]
        kv_copies.append(send(block, block, (kv_s, kv_r), k - 1, ctx_peer(c, k)))

    def turn_queries(d, _):
        for j in range(2):
            u = rope(qkv_ref[pl.ds(pl.multiple_of(d * 128, 128), 128), pl.ds(j * 128, 128)], 0) * 0.125
            qp_ref[d, pl.ds(j * 256, 128), :] = jnp.where(lane < 64, u, 0.0).astype(BF)
            qp_ref[d, pl.ds(j * 256 + 128, 128), :] = jnp.where(lane < 64, pltpu.roll(u, 64, 1), 0.0).astype(BF)
        return 0

    lax.fori_loop(0, 8, turn_queries, 0)

    forwards = []
    for k in range(1, 8):
        kv_copies[k - 1].wait_recv()
        block = kv_ref.at[ring.core, :, lax.rem(c + 8 - k, 8)]
        forwards.append(send(block, block, (fw_s, fw_r), k - 1, ring.sibling))
    for copy in forwards:
        copy.wait_recv()

    def one(d, _):
        key_bias(meta_ref, d, c, bias)
        kv = kv_ref[lax.rem(d, 2), d // 2].reshape(1024, 128)
        scores = nt(kv, qp_ref[d])
        for h in range(4):
            s = scores[:, h * 128 : (h + 1) * 128] + bias[...]
            top = jnp.max(s, axis=0, keepdims=True)
            e = jnp.exp(s - top)
            total = jnp.sum(e, axis=0, keepdims=True)
            probs[:, h * 128 : (h + 1) * 128] = (e * (1.0 / total)).astype(BF)
            lse_ref[d, :, h * 128 : (h + 1) * 128] = jnp.broadcast_to(top + jnp.log(total), (8, 128))
        mixed = nn(kv.T, probs[...])
        for j in range(2):
            two = jnp.concatenate([mixed[64:, (2 * j) * 128 : (2 * j + 1) * 128], mixed[64:, (2 * j + 1) * 128 : (2 * j + 2) * 128]], axis=0)
            a_ref[pl.ds(pl.multiple_of(d * 128, 128), 128), pl.ds(j * 128, 128)] = two.T.astype(BF)
        return 0

    lax.fori_loop(0, 8, one, 0)
    for copy in kv_copies + forwards:
        copy.wait_send()
    for copy in copies:
        copy.wait()
    for copy in local:
        copy.wait()


def attend(n1, wqkv, metas, tabs, wt, w_down):
    dma = pltpu.SemaphoreType.DMA
    return pl.pallas_call(
        attend_kernel,
        out_shape=[
            jax.ShapeDtypeStruct((1024, 256), BF),
            jax.ShapeDtypeStruct((8, 512, 128), BF),
            jax.ShapeDtypeStruct((2, 4, 8, 128, 128), BF),
            jax.ShapeDtypeStruct((8, 8, 512), F32),
            jax.ShapeDtypeStruct((2, 2, 352, D), BF),
            jax.ShapeDtypeStruct((704, D), BF),
        ],
        in_specs=[VM] * 4 + [HB] * 2,
        out_specs=[VM, VM, VM, VM, HB, VM],
        scratch_shapes=[
            pltpu.VMEM((1024, 384), F32),
            pltpu.VMEM((1024, 128), F32), pltpu.VMEM((1024, 512), BF),
            dma((7,)), dma((7,)), dma((7,)), dma((7,)), dma((16,)), dma((16,)), dma((2,)), dma((2,)), dma((3,)),
        ],
        compiler_params=params(6),
        name="attend",
    )(n1, wqkv, metas, tabs, wt, w_down)


def attend_back_kernel(
    side, qp_ref, kv_ref, lse_ref, meta_ref, tab_ref, da_ref, side_in,
    dqkv_ref, side_out,
    bias, dap, ds, pb, mine, theirs, stage, back, co_s, co_r, kv_s, kv_r, *side_scratch,
):
    ring = Ring()
    c = lax.axis_index("y_hi") * 4 + lax.axis_index("z")
    side.bind(ring, (side_in,), (side_out,), side_scratch)
    meet([ctx_peer(c, k) for k in range(1, 8)] + [ring.sibling] + side.peers)
    side.start()
    lane = lax.broadcasted_iota(jnp.int32, (128, 128), 1)

    def unrope(u, i):
        return u * tab_ref[i] - pltpu.roll(u, 96, 1) * tab_ref[i + 1] - pltpu.roll(u, 32, 1) * tab_ref[i + 2]

    def one(x, core):
        d = x * 2 + core
        rows = pl.ds(pl.multiple_of(d * 128, 128), 128)
        key_bias(meta_ref, d, c, bias)
        for j in range(2):
            tile = da_ref[rows, pl.ds(j * 128, 128)].astype(F32)
            dap[pl.ds(j * 256, 128), :] = jnp.where(lane >= 64, pltpu.roll(tile, 64, 1), 0.0).astype(BF)
            dap[pl.ds(j * 256 + 128, 128), :] = jnp.where(lane >= 64, tile, 0.0).astype(BF)
        kv = kv_ref[core, x].reshape(1024, 128)
        scores = nt(kv, qp_ref[d])
        dprobs = nt(kv, dap[...])
        for h in range(4):
            cols = slice(h * 128, (h + 1) * 128)
            p = jnp.exp(scores[:, cols] + bias[...] - lse_ref[d, 0:1, cols])
            pb[:, cols] = p.astype(BF)
            dp = dprobs[:, cols]
            centre = jnp.sum(p * dp, axis=0, keepdims=True)
            ds[:, cols] = (p * (dp - centre)).astype(BF)
        dkv = nn(ds[...], qp_ref[d]) + nn(pb[...], dap[...])
        dq = nn(kv.T, ds[...]) * 0.125
        for j in range(2):
            two = jnp.concatenate([dq[:64, (2 * j) * 128 : (2 * j + 1) * 128], dq[:64, (2 * j + 1) * 128 : (2 * j + 2) * 128]], axis=0)
            dqkv_ref[rows, pl.ds(j * 128, 128)] = unrope(two.T, 0).astype(BF)
        return dkv

    def to_sibling(x, _):
        mine[x] = one(x, 1 - ring.core).astype(BF).reshape(8, 128, 128)
        send(mine.at[x], theirs.at[x], (co_s, co_r), x, ring.sibling)
        dqkv_ref[pl.ds(pl.multiple_of((x * 2 + 1 - ring.core) * 128, 128), 128), 256:384] = jnp.zeros((128, 128), BF)
        return 0

    lax.fori_loop(0, 4, to_sibling, 0)

    def core_copy(x):
        return pltpu.make_async_remote_copy(
            src_ref=mine.at[x], dst_ref=theirs.at[x], send_sem=co_s.at[x], recv_sem=co_r.at[x],
            device_id=ring.sibling, device_id_type=MESH,
        )

    def kv_copy(x, k):
        return pltpu.make_async_remote_copy(
            src_ref=stage.at[x, lax.rem(c + k, 8)], dst_ref=back.at[x, k - 1], send_sem=kv_s.at[x * 7 + k - 1],
            recv_sem=kv_r.at[x * 7 + k - 1], device_id=ctx_peer(c, k), device_id_type=MESH,
        )

    def to_owners(x, _):
        dkv = one(x, ring.core)
        core_copy(x).wait_recv()
        stage[x] = (dkv + theirs[x].reshape(1024, 128).astype(F32)).astype(BF).reshape(8, 128, 128)
        for k in range(1, 8):
            kv_copy(x, k).start()
        return 0

    lax.fori_loop(0, 4, to_owners, 0)
    side.middle()

    def gather_up(x, _):
        total = stage[x, c].astype(F32)
        for k in range(1, 8):
            kv_copy(x, k).wait_recv()
            total += back[x, k - 1].astype(F32)
        rows = pl.ds(pl.multiple_of((x * 2 + ring.core) * 128, 128), 128)
        dqkv_ref[rows, 256:384] = unrope(total, 3).astype(BF)
        return 0

    lax.fori_loop(0, 4, gather_up, 0)

    def drain(x, _):
        core_copy(x).wait_send()
        for k in range(1, 8):
            kv_copy(x, k).wait_send()
        return 0

    lax.fori_loop(0, 4, drain, 0)
    side.finish()


def attend_back(qp, kv, lse, metas, tabs, da, side):
    dma = pltpu.SemaphoreType.DMA
    return pl.pallas_call(
        functools.partial(attend_back_kernel, side),
        out_shape=[jax.ShapeDtypeStruct((1024, 384), BF)] + side.shapes,
        in_specs=[VM] * 6 + [HB],
        out_specs=[VM, VM],
        scratch_shapes=[
            pltpu.VMEM((1024, 128), F32), pltpu.VMEM((512, 128), BF),
            pltpu.VMEM((1024, 512), BF), pltpu.VMEM((1024, 512), BF),
            pltpu.VMEM((4, 8, 128, 128), BF), pltpu.VMEM((4, 8, 128, 128), BF),
            pltpu.VMEM((4, 8, 128, 128), BF), pltpu.VMEM((4, 7, 128, 128), BF),
            dma((4,)), dma((4,)), dma((28,)), dma((28,)), *side.scratch,
        ],
        compiler_params=params(7),
        name="attend_back",
    )(qp, kv, lse, metas, tabs, da, *side.operands)


def rope_tables(c):
    cos, sin = tables(positions_of(c))
    low = jnp.arange(HD) < HD // 2
    to_low, to_high = jnp.where(low, -sin, 0.0), jnp.where(low, 0.0, sin)
    one, zero = jnp.ones_like(cos), jnp.zeros_like(cos)
    pairs = [(cos, cos), (to_low, to_low), (to_high, to_high), (cos, one), (to_low, zero), (to_high, zero)]
    return jnp.stack([jnp.concatenate(p, axis=1) for p in pairs])


def return_kernel(
    move, stats_ref, got_gu, qkv_ref, out_ref,
    info_ref, all_gu, all_qkv, all_out,
    st1, st2, mid, got_qkv,
    st_s, st_r, st2_s, st2_r, agu_s, agu_r, aqkv_s, aqkv_r, ao_s, ao_r, loc, *move_scratch,
):
    x, y_lo, core = lax.axis_index("x"), lax.axis_index("y_lo"), lax.axis_index("core")
    ring = Ring()
    move.bind(ring, (qkv_ref,), (got_qkv,), move_scratch)
    group = group_peers()
    ctx = [(k, ctx_at(k)[1]) for k in range(1, 8)]
    meet([device for _, device in group] + [device for _, device in ctx])
    c, _ = ctx_at(0)
    here16 = x * 4 + y_lo * 2 + core
    move.start()
    copies = [send(stats_ref, st1.at[here16], (st_s, st_r), k, device) for k, device in group]
    st1[here16] = stats_ref[...]

    spreads = []
    for s in range(8):

        def slot(c, s=s):
            rows = ((s // 2) * 4 + lax.rem(c // 2, 2) * 2 + s % 2) * 352 + lax.rem(c, 2) * 176
            return all_gu.at[c // 4, pl.ds(pl.multiple_of(rows, 16), 176)]

        spreads.append(Spread(got_gu.at[s], slot, (agu_s, agu_r), s * 7, s % 3 == 0, loc.at[s]))
    for part in range(2):
        spreads.append(
            Spread(
                out_ref.at[part], lambda c, part=part: all_out.at[:, piece_lanes(c, part)], (ao_s, ao_r), part * 7, part == 0,
                loc.at[8 + part],
            )
        )
    for s in spreads:
        s.start()
    for s in range(8):
        move.arrive(s)
    last_spread = Spread(got_qkv, lambda c: all_qkv.at[:, c], (aqkv_s, aqkv_r), 0, False, loc.at[10])
    last_spread.start()

    for copy in copies:
        copy.wait_recv()
    total = st1[0]
    for i in range(1, 16):
        total += st1[i]
    mid[...] = total
    st2[c] = total
    copies2 = [send(mid, st2.at[c], (st2_s, st2_r), k - 1, device) for k, device in ctx]

    for s in spreads:
        if s.y_first:
            s.relay()
    for s in spreads:
        if not s.y_first:
            s.relay()
    last_spread.relay()

    for copy in copies2:
        copy.wait_recv()
    total = st2[0]
    for i in range(1, 8):
        total += st2[i]
    sums = jnp.sum(total, axis=1, keepdims=True)
    squares, count = sums[0:1], sums[1:2]
    scale = 2.0 / (D * count)
    info_ref[...] = jnp.concatenate([squares / count, scale, jnp.zeros((6, 1), F32)], axis=0) + jnp.zeros((8, 128), F32)

    for s in spreads + [last_spread]:
        s.finish()
    for copy in copies + copies2:
        copy.wait_send()
    move.drain()


def return_grads(stats, got_gu, qkv, out):
    dma = pltpu.SemaphoreType.DMA
    pair = lambda n: [dma((n,)), dma((n,))]
    move = Move(qkv)
    return pl.pallas_call(
        functools.partial(return_kernel, move),
        out_shape=[
            jax.ShapeDtypeStruct((8, 128), F32),
            jax.ShapeDtypeStruct((2, FF, 128), BF),
            jax.ShapeDtypeStruct((8, 8, 48, 128), BF),
            jax.ShapeDtypeStruct((128, D), BF),
        ],
        in_specs=[VM] * 4,
        out_specs=[VM] * 4,
        scratch_shapes=[
            pltpu.VMEM((16, 8, 128), F32), pltpu.VMEM((8, 8, 128), F32), pltpu.VMEM((8, 128), F32), pltpu.VMEM((8, 48, 128), BF),
            *pair(16), *pair(7), *pair(56), *pair(7), *pair(14), dma((11,)), *move.scratch,
        ],
        compiler_params=params(8),
        name="return_grads",
    )(stats, got_gu, qkv, out)


def turn_back_kernel(info_ref, all_ref, gain_ref, wg_ref, wu_ref, down_ref, gate_ref, up_ref, down_out, sum_ref):
    scale = info_ref[1:2, 0:1]
    s = gain_ref[...] * scale

    @pl.when(pl.program_id(0) == 0)
    def _():
        sum_ref[...] = jnp.zeros_like(sum_ref)

    total = jnp.zeros((128, 128), F32)
    for k in range(4):
        at = slice(k * 128, (k + 1) * 128)
        for i, w_ref, g_ref in ((0, wg_ref, gate_ref), (1, wu_ref, up_ref)):
            part = all_ref[i, at, :].T.astype(F32)
            total += part * w_ref[:, at].astype(F32)
            g_ref[:, at] = part * s
    sum_ref[...] += jnp.sum(total, axis=1, keepdims=True) * scale
    down_out[...] = down_ref[...].astype(F32) * scale


def turn_back(info, all_gu, gain, w_gate, w_up, down):
    wide = pl.BlockSpec((128, 512), lambda i: (0, i))
    rows = pl.BlockSpec((32, D), lambda i: (i, 0))
    whole = lambda *shape: pl.BlockSpec(shape, lambda i: (0,) * len(shape))
    f32 = lambda *shape: jax.ShapeDtypeStruct(shape, F32)
    return pl.pallas_call(
        turn_back_kernel,
        grid=(11,),
        out_shape=[f32(128, FF), f32(128, FF), f32(352, D), f32(128, 1)],
        in_specs=[whole(8, 128), pl.BlockSpec((2, 512, 128), lambda i: (0, i, 0)), whole(128, 1), wide, wide, rows],
        out_specs=[wide, wide, rows, whole(128, 1)],
        name="turn_back",
    )(info, all_gu, gain, w_gate, w_up, down)


def turn_back_qkv_kernel(
    info_ref, all_ref, gain_ref, wq_ref, wk_ref, wv_ref, out_ref, gin_ref, q_ref, k_ref, v_ref, sum_ref, o_ref, input_ref
):
    scale = info_ref[1:2, 0:1]
    s1 = gain_ref[...] * scale
    total = jnp.zeros((128, 128), F32)
    for s in range(8):
        for j in range(2):
            f = (s // 2) * 4 + j * 2 + s % 2
            part = all_ref[s, j * 128 : (j + 1) * 128].T.astype(F32)
            total += part * wq_ref[:, f * 128 : (f + 1) * 128].astype(F32)
            q_ref[:, f * 128 : (f + 1) * 128] = part * s1
    for i in range(2):
        both = [all_ref[2 * x, 256:].astype(F32) + all_ref[2 * x + 1, 256:].astype(F32) for x in (2 * i, 2 * i + 1)]
        for at, w_ref, g_ref in ((0, wk_ref, k_ref), (64, wv_ref, v_ref)):
            part = jnp.concatenate([both[0][at : at + 64], both[1][at : at + 64]], axis=0).T
            total += part * w_ref[:, i * 128 : (i + 1) * 128].astype(F32)
            g_ref[:, i * 128 : (i + 1) * 128] = part * s1
    sum_ref[...] = jnp.sum(total, axis=1, keepdims=True) * scale
    o_ref[...] = out_ref[...].astype(F32) * scale
    input_ref[...] = gin_ref[...] * scale


def turn_back_qkv(info, all_qkv, gain, w_query, w_key, w_value, out, grad_in):
    f32 = lambda *shape: jax.ShapeDtypeStruct(shape, F32)
    return pl.pallas_call(
        turn_back_qkv_kernel,
        out_shape=[f32(128, D), f32(128, KVD), f32(128, KVD), f32(128, 1), f32(128, D), f32(128, D)],
        name="turn_back_qkv",
    )(info, all_qkv, gain, w_query, w_key, w_value, out, grad_in)


def local(hidden_in, teacher, doc_ids, valid_mask, norm1_gain, w_query, w_key, w_value, w_out, norm2_gain, w_gate, w_up, w_down):
    c = lax.axis_index(("y_hi", "z"))
    g1 = norm1_gain.astype(F32)
    g2 = norm2_gain.astype(F32)
    valid = valid_mask.astype(F32)
    tabs = rope_tables(c)
    blocks = doc_ids.reshape(16, 64)
    key_docs = jnp.concatenate([blocks[:8], blocks[:7:-1]], axis=1)
    meta = jnp.concatenate([key_docs, valid_mask[None], jnp.zeros((7, 128), jnp.int32)], axis=0)

    n1_all, metas, wqkv, wo, wt = enter(
        hidden_in, meta, g1[None], g2[None], w_query, w_key, w_value, w_gate, w_up, w_out
    )
    n1_all = n1_all.reshape(1024, D)
    wo = wo.reshape(256, D)
    a, qp, kv, lse, wgu, wd = attend(n1_all, wqkv, metas, tabs, wt, w_down)

    layer_out, loss_rows, dy1, da, da_all, grad_gu, piece_down = middle(a, wo, hidden_in, teacher, valid[:, None], wgu, wd)
    dqkv, piece_gu = attend_back(qp, kv, lse, metas, tabs, da, SumColumns(grad_gu.reshape(2, 4, 176, D)))
    grad_in, all_down, got_gu, piece_qkv, piece_out = last(
        dqkv, wqkv, n1_all.reshape(8, 128, D), a, da_all, hidden_in, dy1, piece_down, piece_gu
    )
    stats = jnp.concatenate([loss_rows.reshape(1, 128), valid[None], jnp.zeros((6, 128), F32)], axis=0)
    info, all_gu, all_qkv, all_out = return_grads(stats, got_gu, piece_qkv, piece_out)
    gg, gp, gd, gain2 = turn_back(info, all_gu, g2[:, None], w_gate, w_up, all_down)
    gq, gk, gv, gain1, go, input_grad = turn_back_qkv(
        info, all_qkv.reshape(8, 384, 128), g1[:, None], w_query, w_key, w_value, all_out, grad_in
    )
    return (layer_out, info[0, 0], input_grad, gain1[:, 0], gq, gk, gv, go, gain2[:, 0], gg, gp, gd)


def solution(mesh):
    fine = Mesh(mesh.devices.reshape(2, 4, 4, 2, 2), AXES)
    rows = ("y_hi", "z", "x", "y_lo", "core")
    fs = ("x", "y_lo", "core")
    token, shard = P(rows, None), P(fs, None)
    return jax.shard_map(
        local,
        mesh=fine,
        in_specs=(token, token, shard, P(rows), P(fs), shard, shard, shard, shard, P(fs), shard, shard, shard),
        out_specs=(token, P(), token, P(fs), shard, shard, shard, shard, P(fs), shard, shard, shard),
        check_vma=False,
    )
```

```python
import functools

import jax
import jax.numpy as jnp
from jax import lax
from jax.experimental import pallas as pl
from jax.experimental.pallas import tpu as pltpu
from jax.sharding import Mesh, PartitionSpec as P

D = 2048
HEADS = 32
KV_HEADS = 4
HD = 64
FF = 5632
KVD = 256
EPSILON = 1e-05
THETA = 10000.0
NEGATIVE = -1e30
AXES = ("y_hi", "z", "x", "y_lo", "core")
BF = jnp.bfloat16
F32 = jnp.float32


def dot(a, b, ca, cb):
    return lax.dot_general(a, b, (((ca,), (cb,)), ((), ())), preferred_element_type=F32)


def tables(positions):
    indices = jnp.arange(HD // 2, dtype=jnp.int32).astype(F32)
    frequency = THETA ** (-(indices * 2.0 / HD))
    angles = positions.astype(F32)[:, None] * frequency[None, :]
    angles = jnp.concatenate([angles, angles], axis=1)
    return jnp.cos(angles), jnp.sin(angles)


def positions_of(c):
    t = jnp.arange(64, dtype=jnp.int32)
    return jnp.concatenate([c * 64 + t, (15 - c) * 64 + t])


MESH = pl.DeviceIdType.MESH
HALVES = (pl.ds(0, 64), pl.ds(64, 64))
VM = pl.BlockSpec(memory_space=pltpu.VMEM)
HB = pl.BlockSpec(memory_space=pl.ANY)


def params(number):
    return pltpu.CompilerParams(collective_id=number, has_side_effects=True, vmem_limit_bytes=56 * 2**20)


def send(src, dst, sems, i, device):
    copy = pltpu.make_async_remote_copy(
        src_ref=src, dst_ref=dst, send_sem=sems[0].at[i], recv_sem=sems[1].at[i], device_id=device, device_id_type=MESH
    )
    copy.start()
    return copy


def meet(devices):
    barrier = pltpu.get_barrier_semaphore()
    for device in devices:
        pl.semaphore_signal(barrier, inc=1, device_id=device, device_id_type=MESH)
    pl.semaphore_wait(barrier, len(devices))


class Ring:
    def __init__(self):
        x, core = lax.axis_index("x"), lax.axis_index("core")
        self.x, self.core = x, core
        self.right_x, self.left_x, self.far_x = lax.rem(x + 1, 4), lax.rem(x + 3, 4), lax.rem(x + 2, 4)
        self.right, self.left, self.sibling = {"x": self.right_x}, {"x": self.left_x}, {"core": 1 - core}


def norm_scale(v):
    return lax.rsqrt(jnp.mean(v * v, axis=1, keepdims=True) + EPSILON)


class Side:
    in_place = False

    def middle(self):
        pass


class Torus:
    def __init__(self):
        self.y_hi, self.y_lo, self.z = lax.axis_index("y_hi"), lax.axis_index("y_lo"), lax.axis_index("z")
        self.y = self.y_hi * 2 + self.y_lo
        self.ys = [(dy, lax.rem(self.y + dy, 4)) for dy in (1, 3, 2)]
        self.zs = [(dz, lax.rem(self.z + dz, 4)) for dz in (1, 3, 2)]
        self.peers = [self.y_device(y) for _, y in self.ys] + [{"z": z} for _, z in self.zs]

    def y_device(self, y):
        return {"y_hi": y // 2, "y_lo": lax.rem(y, 2)}


def lanes_at(start, size):
    return pl.ds(pl.multiple_of(start, 128), size)


def add_up(out, terms, lead, rows):
    steps = rows // 16

    def body(k, _):
        i, r = k // steps, pl.ds(pl.multiple_of(lax.rem(k, steps) * 16, 16), 16)
        total = None
        for at in terms:
            term = at(i, r).astype(F32)
            total = term if total is None else total + term
        out(i, r, total.astype(BF))
        return 0

    lax.fori_loop(0, lead * steps, body, 0)


class Ag:
    def __init__(self, ring, buf, sems):
        r = self.r = ring
        self.buf, self.sems = buf, sems
        self.plan = (
            (r.x, 0, r.right), (r.x, 1, r.right), (r.x, 1, r.left), (r.x, 0, r.left),
            (r.left_x, 0, r.right), (r.right_x, 1, r.left),
            (r.x, 0, r.sibling), (r.x, 1, r.sibling),
            (r.left_x, 0, r.sibling), (r.left_x, 1, r.sibling), (r.right_x, 0, r.sibling), (r.right_x, 1, r.sibling),
            (r.far_x, 0, r.sibling), (r.far_x, 1, r.sibling),
        )

    def copy(self, i):
        x, half, device = self.plan[i]
        block = self.buf.at[x * 2 + self.r.core, HALVES[half]]
        return pltpu.make_async_remote_copy(
            src_ref=block, dst_ref=block, send_sem=self.sems[0].at[i], recv_sem=self.sems[1].at[i],
            device_id=device, device_id_type=MESH,
        )

    def begin(self, half):
        for i in ((0, 3, 6), (2, 1, 7))[half]:
            self.copy(i).start()

    def near(self):
        for got, onward in ((0, (4, 8)), (2, (5, 11)), (1, (9,)), (3, (10,))):
            self.copy(got).wait_recv()
            for i in onward:
                self.copy(i).start()

    def far(self):
        for got, onward in ((4, 12), (5, 13)):
            self.copy(got).wait_recv()
            self.copy(onward).start()

    def have(self, *which):
        for i in which:
            self.copy(i).wait_recv()

    def drain(self):
        for i in range(14):
            self.copy(i).wait_send()


class Rs:
    def __init__(self, ring, parts, held, got, sems):
        r = self.r = ring
        self.parts, self.held, self.got, self.sems = parts, held, got, sems
        self.blocks = (r.far_x, r.right_x, r.left_x, r.x)
        a, b = HALVES
        self.plan = {
            4: (held.at[0, a], got.at[4, a], r.right), 5: (held.at[0, b], got.at[4, b], r.left),
            6: (held.at[1, b], got.at[5, b], r.right), 7: (held.at[2, a], got.at[5, a], r.left),
            8: (held.at[1, a], got.at[6, a], r.right), 9: (held.at[2, b], got.at[6, b], r.left),
        }

    def swap(self, i, x):
        return pltpu.make_async_remote_copy(
            src_ref=self.parts.at[x * 2 + 1 - self.r.core], dst_ref=self.got.at[i], send_sem=self.sems[0].at[i],
            recv_sem=self.sems[1].at[i], device_id=self.r.sibling, device_id_type=MESH,
        )

    def copy(self, i):
        if i < 4:
            return self.swap(i, self.blocks[i])
        src, dst, device = self.plan[i]
        return pltpu.make_async_remote_copy(
            src_ref=src, dst_ref=dst, send_sem=self.sems[0].at[i], recv_sem=self.sems[1].at[i],
            device_id=device, device_id_type=MESH,
        )

    def pair(self, i, half):
        x = self.blocks[i]

        def body(k, _):
            rows = pl.ds(half * 64 + k * 16, 16)
            total = self.parts[x * 2 + self.r.core, rows, :].astype(F32) + self.got[i, rows, :].astype(F32)
            self.held[i, rows, :] = total.astype(BF)
            return 0

        lax.fori_loop(0, 4, body, 0)

    def onward(self, i, half):
        def body(k, _):
            rows = pl.ds(half * 64 + k * 16, 16)
            total = self.held[i, rows, :].astype(F32) + self.got[4, rows, :].astype(F32)
            self.held[i, rows, :] = total.astype(BF)
            return 0

        lax.fori_loop(0, 4, body, 0)

    def send_left(self):
        self.copy(2).wait_recv()
        self.pair(2, 0)
        self.copy(7).start()

    def send_right(self):
        self.copy(1).wait_recv()
        self.pair(1, 1)
        self.copy(6).start()

    def send_far(self):
        self.copy(0).wait_recv()
        self.pair(0, 0)
        self.copy(4).start()
        self.pair(0, 1)
        self.copy(5).start()

    def relay(self):
        self.pair(1, 0)
        self.pair(2, 1)
        self.copy(4).wait_recv()
        self.onward(1, 0)
        self.copy(8).start()
        self.copy(5).wait_recv()
        self.onward(2, 1)
        self.copy(9).start()
        self.copy(3).wait_recv()

    def ready(self, half):
        for i in ((7, 8), (6, 9))[half]:
            self.copy(i).wait_recv()

    def total(self, rows):
        r = self.r
        return (
            self.parts[r.x * 2 + r.core, rows, :].astype(F32)
            + self.got[3, rows, :].astype(F32)
            + self.got[5, rows, :].astype(F32)
            + self.got[6, rows, :].astype(F32)
        )

    def drain(self):
        for i in range(10):
            self.copy(i).wait_send()


def middle_kernel(
    down_side, gu_side, a_ref, wo_ref, x_ref, valid_ref, wd_ref, teacher_hbm, half_w_ref,
    out_ref, loss_ref, dy1_ref, da_ref, gout_ref, ggu_ref, piece_ref, gu_piece_ref,
    w, n2, dyg, dag, parts, held, got, y1, gate, up, mid, mid_t, dup, dgu1, dgu2, gd, gu1, dmid,
    rs1_s, rs1_r, ag1_s, ag1_r, rs2_s, rs2_r, ag2_s, ag2_r, rs3_s, rs3_r, ag3_s, ag3_r, w_s, w_r, loc, *side_scratch,
):
    ring = Ring()
    y_lo = lax.axis_index("y_lo")
    near, other = y_partners()
    down_side.bind(ring, (gd,), (piece_ref,), side_scratch[: len(down_side.scratch)])
    gu_side.bind(ring, (gu1,), (gu_piece_ref,), side_scratch[len(down_side.scratch) :])
    meet([ring.right, ring.left, ring.sibling] + Torus().peers)
    here = ring.x * 2 + ring.core
    dy, dgate = dy1_ref, mid
    teacher = dag.at[here]
    teacher_copy = pltpu.make_async_copy(teacher_hbm, teacher, loc.at[4])
    teacher_copy.start()

    wcopies = []
    for dx in range(4):
        lanes = group_lanes(lax.rem(ring.x + 4 - dx, 4), y_lo)
        src, dst = half_w_ref.at[:, :, :, lanes], w.at[:, :, :, lanes]
        wcopies.append(send(src, dst, (w_s, w_r), dx, (near, other)[dx // 2]))
        copy = pltpu.make_async_copy(src, dst, loc.at[dx])
        copy.start()
        wcopies.append(copy)

    def rows_of(x):
        return pl.ds(pl.multiple_of(x * 256, 256), 256)

    def block(buf, x):
        return buf[pl.ds(x * 2, 2)].reshape(256, D)

    def put(x, product):
        def body(k, _):
            lanes = lanes_at(k * 512, 512)
            parts[pl.ds(x * 2, 2), :, lanes] = product(lanes).astype(BF).reshape(2, 128, 512)
            return 0

        lax.fori_loop(0, 4, body, 0)

    def reduced(rs, op, ag, buf):
        for half in range(2):
            rs.ready(half)

            def body(k, _, half=half):
                rows = pl.ds(half * 64 + k * 16, 16)
                buf[here, rows, :] = op(rows, rs.total(rows)).astype(BF)
                return 0

            lax.fori_loop(0, 4, body, 0)
            ag.begin(half)

    def over_blocks(ag, rs, work):
        def step(i, _):
            at = functools.partial(jnp.equal, i)

            @pl.when(at(0))
            def _():
                ag.have(6, 7)

            @pl.when(at(1))
            def _():
                ag.near()
                ag.have(8, 9)

            @pl.when(at(2))
            def _():
                ag.have(10, 11)
                if rs is not None:
                    rs.send_left()

            @pl.when(at(3))
            def _():
                if rs is not None:
                    rs.send_right()
                ag.far()
                ag.have(12, 13)

            x = lax.rem(ring.x + jnp.where(at(1), 3, jnp.where(at(2), 1, jnp.where(at(3), 2, 0))), 4)
            work(x)
            if rs is not None:
                rs.swap(3 - i, x).start()
            return 0

        lax.fori_loop(0, 4, step, 0)

    rs = Rs(ring, parts, held, got, (rs1_s, rs1_r))
    ag = Ag(ring, n2, (ag1_s, ag1_r))
    for i in range(4):
        x = rs.blocks[i]
        put(x, lambda lanes, x=x: nn(a_ref[rows_of(x), :], wo_ref[:, lanes]))
        rs.copy(i).start()
        if i == 1:
            rs.send_far()
        elif i == 2:
            rs.send_right()
        elif i == 3:
            rs.send_left()
    rs.relay()

    def op1(rows, total):
        v = x_ref[rows, :].astype(F32) + total
        y1[rows, :] = v
        return v * norm_scale(v)

    reduced(rs, op1, ag, n2)
    rs.drain()
    for copy in wcopies:
        copy.wait()
    teacher_copy.wait()

    rs = Rs(ring, parts, held, got, (rs2_s, rs2_r))

    def forward(x):
        rows = rows_of(x)
        gate[rows, :] = nt(block(n2, x), w[0].reshape(704, D))
        up[rows, :] = nt(block(n2, x), w[1].reshape(704, D))

        def body(k, _):
            r = pl.ds(pl.multiple_of(x * 256 + k * 32, 32), 32)
            g = gate[r, :]
            mid[pl.ds(pl.multiple_of(k * 32, 32), 32), :] = (g * jax.nn.sigmoid(g) * up[r, :]).astype(BF)
            return 0

        lax.fori_loop(0, 8, body, 0)
        put(x, lambda lanes: nn(mid[...], wd_ref[:, lanes]))
        mid_t[:, rows] = mid[...].T

    over_blocks(ag, rs, forward)
    rs.send_far()
    rs.relay()
    ag.drain()

    def op2(rows, total):
        v = y1[rows, :] + total
        out_ref[rows, :] = v.astype(BF)
        miss = v - dag[here, rows, :].astype(F32)
        valid = valid_ref[rows, :]
        loss_ref[rows, :] = valid * jnp.mean(miss * miss, axis=1, keepdims=True)
        dy[rows, :] = valid * miss
        return valid * miss

    ag = Ag(ring, dyg, (ag2_s, ag2_r))
    reduced(rs, op2, ag, dyg)
    rs.drain()

    rs = Rs(ring, parts, held, got, (rs3_s, rs3_r))

    def backward(x):
        rows = rows_of(x)
        dgate_mid = nt(block(dyg, x), wd_ref[...])
        dmid[...] = dgate_mid

        def body(k, _):
            r = pl.ds(pl.multiple_of(x * 256 + k * 32, 32), 32)
            q = pl.ds(pl.multiple_of(k * 32, 32), 32)
            g, dm = gate[r, :], dmid[q, :]
            sg = jax.nn.sigmoid(g)
            dgate[q, :] = (dm * up[r, :] * sg * (1.0 + g * (1.0 - sg))).astype(BF)
            dup[q, :] = (dm * (g * sg)).astype(BF)
            return 0

        lax.fori_loop(0, 8, body, 0)
        put(x, lambda lanes: nn(dgate[...], w[0, :, :, lanes].reshape(704, 512)) + nn(dup[...], w[1, :, :, lanes].reshape(704, 512)))
        for i, ref in enumerate((dgate, dup)):
            turned = ref[...].T
            for c in range(4):
                dgu1[pl.ds((4 * i + c) * 96, 96), rows] = turned[176 * c : 176 * c + 96]
                dgu2[pl.ds((4 * i + c) * 80, 80), rows] = turned[176 * c + 96 : 176 * c + 176]

    over_blocks(ag, rs, backward)
    rs.send_far()

    def grad_down(k, _):
        lanes = lanes_at(k * 512, 512)
        gd[:, :, lanes] = nn(mid_t[...], dyg[:, :, lanes].reshape(1024, 512)).astype(BF).reshape(2, 352, 512)
        return 0

    lax.fori_loop(0, 4, grad_down, 0)
    down_side.start()
    rs.relay()

    def grad_gu(rows, lhs, out, k):
        lanes = lanes_at(k * 512, 512)
        out[:, :, :, lanes] = nn(lhs[...], n2[:, :, lanes].reshape(1024, 512)).astype(BF).reshape(2, 4, rows, 512)

    def grad_gu1(k, _):
        grad_gu(96, dgu1, gu1, k)
        return 0

    lax.fori_loop(0, 4, grad_gu1, 0)
    gu_side.start()
    ag.drain()

    def op3(rows, total):
        v = back_norm(y1[rows, :], dy[rows, :], total)
        dy1_ref[rows, :] = v
        return v

    ag = Ag(ring, dag, (ag3_s, ag3_r))
    reduced(rs, op3, ag, dag)
    rs.drain()

    def to_attention(x):
        rows = rows_of(x)
        da_ref[rows, :] = nt(block(dag, x), wo_ref[...]).astype(BF)
        mid_t[0:256, rows] = a_ref[rows, :].T
        grad_gu(80, dgu2, ggu_ref, x)

    over_blocks(ag, None, to_attention)
    down_side.middle()
    gu_side.middle()

    def grad_out(k, _):
        lanes = lanes_at(k * 512, 512)
        gout_ref[:, :, lanes] = nn(mid_t[0:256, :], dag[:, :, lanes].reshape(1024, 512)).astype(BF).reshape(2, 128, 512)
        return 0

    lax.fori_loop(0, 4, grad_out, 0)
    ag.drain()
    down_side.finish()
    gu_side.finish()


def middle(a, wo, x, teacher, valid, half_w, wd):
    dma = pltpu.SemaphoreType.DMA
    pair = lambda n: [dma((n,)), dma((n,))]
    big = pltpu.VMEM((8, 128, D), BF)
    sides = [SumRows(jax.ShapeDtypeStruct((2, 352, D), BF), True), SumColumns(jax.ShapeDtypeStruct((2, 4, 96, D), BF), True)]
    return pl.pallas_call(
        functools.partial(middle_kernel, *sides),
        out_shape=[
            jax.ShapeDtypeStruct((128, D), BF), jax.ShapeDtypeStruct((128, 1), F32), jax.ShapeDtypeStruct((128, D), F32),
            jax.ShapeDtypeStruct((1024, 256), BF), jax.ShapeDtypeStruct((2, 128, D), BF), jax.ShapeDtypeStruct((2, 4, 80, D), BF),
            *[s for side in sides for s in side.shapes],
        ],
        in_specs=[VM] * 5 + [HB, HB],
        out_specs=[VM] * 8,
        scratch_shapes=[
            pltpu.VMEM((2, 2, 352, D), BF), big, big, big, big, pltpu.VMEM((3, 128, D), BF), pltpu.VMEM((7, 128, D), BF),
            pltpu.VMEM((128, D), F32),
            pltpu.VMEM((1024, 704), F32), pltpu.VMEM((1024, 704), F32),
            pltpu.VMEM((256, 704), BF), pltpu.VMEM((704, 1024), BF), pltpu.VMEM((256, 704), BF),
            pltpu.VMEM((768, 1024), BF), pltpu.VMEM((640, 1024), BF), pltpu.VMEM((2, 352, D), BF), pltpu.VMEM((2, 4, 96, D), BF),
            pltpu.VMEM((256, 704), F32),
            *pair(10), *pair(14), *pair(10), *pair(14), *pair(10), *pair(14), *pair(4), dma((5,)),
            *[s for side in sides for s in side.scratch],
        ],
        compiler_params=pltpu.CompilerParams(collective_id=1, has_side_effects=True, vmem_limit_bytes=63 * 2**20),
        name="middle",
    )(a, wo, x, valid, wd, teacher, half_w)


class SumColumns(Side):
    def __init__(self, grads, in_vmem=False):
        r = self.rows = grads.shape[2]
        dma = pltpu.SemaphoreType.DMA
        self.first = 0 if in_vmem else 1
        n = 3 + self.first
        self.operands = [grads]
        self.shapes = [jax.ShapeDtypeStruct((r, 1024), BF)]
        self.scratch = [
            pltpu.VMEM((n, 4, r, 512), BF), pltpu.VMEM((n, 2, 2, r, 512), BF),
            pltpu.VMEM((3, r, 512), BF), pltpu.VMEM((3, r, 512), BF),
            dma((9,)), dma((9,)), dma((6,)), dma((6,)), dma((3,)),
        ]

    def bind(self, ring, ins, outs, scratch):
        (self.g,), (self.out,) = ins, outs
        self.by, self.bz, self.by2, self.bz2, s1, r1, s2, r2, self.loc = scratch
        self.one, self.two = (s1, r1), (s2, r2)
        self.t = Torus()
        self.peers = self.t.peers

    def start(self):
        t, g = self.t, self.g
        self.c = []
        for i, (dy, y) in enumerate(t.ys):
            src = g.at[y // 2, :, :, lanes_at(lax.rem(y, 2) * 1024, 512)]
            self.c.append(send(src, self.by.at[dy - 1 + self.first], self.one, i, t.y_device(y)))
        for i, (dz, z) in enumerate(t.zs):
            for yl in range(2):
                src = g.at[:, z, :, pl.ds(yl * 1024 + 512, 512)]
                self.c.append(send(src, self.bz.at[dz - 1 + self.first, yl], self.one, 3 + 2 * i + yl, {"z": z}))
        self.l = []
        if not self.first:
            return
        self.l.append(pltpu.make_async_copy(g.at[t.y_hi, :, :, lanes_at(t.y_lo * 1024, 512)], self.by.at[0], self.loc.at[0]))
        for yl in range(2):
            self.l.append(
                pltpu.make_async_copy(g.at[:, t.z, :, pl.ds(yl * 1024 + 512, 512)], self.bz.at[0, yl], self.loc.at[1 + yl])
            )
        for copy in self.l:
            copy.start()

    def middle(self):
        t, by, bz = self.t, self.by, self.bz
        for copy in self.l:
            copy.wait()
        for copy in self.c:
            copy.wait_recv()

        def put_y(i, r, v):
            by[0, i, r, :] = v

        def put_z(i, r, v):
            bz[0, i // 2, lax.rem(i, 2), r, :] = v

        own_y = [lambda i, r: self.g[t.y_hi, i, r, lanes_at(t.y_lo * 1024, 512)]]
        own_z = [lambda i, r: self.g[lax.rem(i, 2), t.z, r, lanes_at((i // 2) * 1024 + 512, 512)]]
        if self.first:
            own_y, own_z = [], []
        n = 3 + self.first
        add_up(put_y, own_y + [lambda i, r, k=k: by[k, i, r, :] for k in range(n)], 4, self.rows)
        add_up(put_z, own_z + [lambda i, r, k=k: bz[k, i // 2, lax.rem(i, 2), r, :] for k in range(n)], 4, self.rows)
        self.c2 = []
        for i, (dz, z) in enumerate(t.zs):
            self.c2.append(send(by.at[0, z], self.by2.at[dz - 1], self.two, i, {"z": z}))
        for i, (dy, y) in enumerate(t.ys):
            self.c2.append(send(bz.at[0, lax.rem(y, 2), y // 2], self.bz2.at[dy - 1], self.two, 3 + i, t.y_device(y)))

    def finish(self):
        t, by, bz, by2, bz2, out = self.t, self.by, self.bz, self.by2, self.bz2, self.out
        for copy in self.c2:
            copy.wait_recv()

        def put_a(i, r, v):
            out[r, 0:512] = v

        def put_b(i, r, v):
            out[r, 512:1024] = v

        add_up(put_a, [lambda i, r: by[0, t.z, r, :]] + [lambda i, r, k=k: by2[k, r, :] for k in range(3)], 1, self.rows)
        add_up(put_b, [lambda i, r: bz[0, t.y_lo, t.y_hi, r, :]] + [lambda i, r, k=k: bz2[k, r, :] for k in range(3)], 1, self.rows)
        for copy in self.c + self.c2:
            copy.wait_send()


class SumRows(Side):
    def __init__(self, grads, in_vmem=False):
        r = self.rows = grads.shape[1]
        dma = pltpu.SemaphoreType.DMA
        self.first = 0 if in_vmem else 1
        n = 3 + self.first
        self.operands = [grads]
        self.shapes = [jax.ShapeDtypeStruct((2, r, 128), BF)]
        self.scratch = [
            pltpu.VMEM((n, r, 512), BF), pltpu.VMEM((n, 2, 2, r, 128), BF),
            pltpu.VMEM((3, r, 128), BF), pltpu.VMEM((3, r, 128), BF),
            dma((9,)), dma((9,)), dma((6,)), dma((6,)), dma((3,)),
        ]

    def bind(self, ring, ins, outs, scratch):
        (self.g,), (self.out,) = ins, outs
        self.by, self.bz, self.by2, self.bz2, s1, r1, s2, r2, self.loc = scratch
        self.one, self.two = (s1, r1), (s2, r2)
        self.t = Torus()
        self.peers = self.t.peers

    def start(self):
        t, g = self.t, self.g
        self.c = []
        for i, (dy, y) in enumerate(t.ys):
            src = g.at[lax.rem(y, 2), :, lanes_at((y // 2) * 1024, 512)]
            self.c.append(send(src, self.by.at[dy - 1 + self.first], self.one, i, t.y_device(y)))
        for i, (dz, z) in enumerate(t.zs):
            for yh in range(2):
                src = g.at[:, :, lanes_at(yh * 1024 + 512 + z * 128, 128)]
                self.c.append(send(src, self.bz.at[dz - 1 + self.first, yh], self.one, 3 + 2 * i + yh, {"z": z}))
        self.l = []
        if not self.first:
            return
        self.l.append(pltpu.make_async_copy(g.at[t.y_lo, :, lanes_at(t.y_hi * 1024, 512)], self.by.at[0], self.loc.at[0]))
        for yh in range(2):
            self.l.append(
                pltpu.make_async_copy(g.at[:, :, lanes_at(yh * 1024 + 512 + t.z * 128, 128)], self.bz.at[0, yh], self.loc.at[1 + yh])
            )
        for copy in self.l:
            copy.start()

    def middle(self):
        t, by, bz = self.t, self.by, self.bz
        for copy in self.l:
            copy.wait()
        for copy in self.c:
            copy.wait_recv()

        def put_y(i, r, v):
            by[0, r, :] = v

        def put_z(i, r, v):
            bz[0, i // 2, lax.rem(i, 2), r, :] = v

        own_y = [lambda i, r: self.g[t.y_lo, r, lanes_at(t.y_hi * 1024, 512)]]
        own_z = [lambda i, r: self.g[lax.rem(i, 2), r, lanes_at((i // 2) * 1024 + 512 + t.z * 128, 128)]]
        if self.first:
            own_y, own_z = [], []
        n = 3 + self.first
        add_up(put_y, own_y + [lambda i, r, k=k: by[k, r, :] for k in range(n)], 1, self.rows)
        add_up(put_z, own_z + [lambda i, r, k=k: bz[k, i // 2, lax.rem(i, 2), r, :] for k in range(n)], 4, self.rows)
        self.c2 = []
        for i, (dz, z) in enumerate(t.zs):
            self.c2.append(send(by.at[0, :, lanes_at(z * 128, 128)], self.by2.at[dz - 1], self.two, i, {"z": z}))
        for i, (dy, y) in enumerate(t.ys):
            self.c2.append(send(bz.at[0, y // 2, lax.rem(y, 2)], self.bz2.at[dy - 1], self.two, 3 + i, t.y_device(y)))

    def finish(self):
        t, by, bz, by2, bz2, out = self.t, self.by, self.bz, self.by2, self.bz2, self.out
        for copy in self.c2:
            copy.wait_recv()

        def put_a(i, r, v):
            out[0, r, :] = v

        def put_b(i, r, v):
            out[1, r, :] = v

        own = lanes_at(t.z * 128, 128)
        add_up(put_a, [lambda i, r: by[0, r, own]] + [lambda i, r, k=k: by2[k, r, :] for k in range(3)], 1, self.rows)
        add_up(put_b, [lambda i, r: bz[0, t.y_hi, t.y_lo, r, :]] + [lambda i, r, k=k: bz2[k, r, :] for k in range(3)], 1, self.rows)
        for copy in self.c + self.c2:
            copy.wait_send()


def piece_lanes(c, part):
    return lanes_at((c // 4) * 1024 + part * 512 + lax.rem(c, 4) * 128, 128)


def ctx_at(k):
    y_hi, z = lax.axis_index("y_hi"), lax.axis_index("z")
    y, zz = (1 - y_hi if k // 4 else y_hi), lax.rem(z + k % 4, 4)
    return y * 4 + zz, {"y_hi": y, "z": zz}


class Spread:
    def __init__(self, piece, slot, sems, base, y_first, local):
        self.piece, self.slot, self.sems, self.base, self.y_first, self.local = piece, slot, sems, base, y_first, local

    def copy(self, k, src, c, device):
        return pltpu.make_async_remote_copy(
            src_ref=src, dst_ref=self.slot(c), send_sem=self.sems[0].at[self.base + k - 1],
            recv_sem=self.sems[1].at[self.base + k - 1], device_id=device, device_id_type=MESH,
        )

    def first(self, k):
        here, _ = ctx_at(0)
        return self.copy(k, self.piece, here, ctx_at(k)[1])

    def second(self, dz):
        if self.y_first:
            c, _ = ctx_at(4)
            return self.copy(4 + dz, self.slot(c), c, ctx_at(dz)[1])
        c, _ = ctx_at(4 - dz)
        return self.copy(4 + dz, self.slot(c), c, ctx_at(4)[1])

    def own(self):
        return pltpu.make_async_copy(self.piece, self.slot(ctx_at(0)[0]), self.local)

    def start(self):
        for k in (4, 1, 3, 2) if self.y_first else (1, 3, 2, 4):
            self.first(k).start()
        if self.local is not None:
            self.own().start()

    def relay(self):
        if self.y_first:
            self.first(4).wait_recv()
            for dz in (1, 3, 2):
                self.second(dz).start()
        else:
            for dz in (1, 3, 2):
                self.first(dz).wait_recv()
                self.second(dz).start()

    def finish(self):
        if self.y_first:
            for dz in (1, 3, 2):
                self.first(dz).wait_recv()
        else:
            self.first(4).wait_recv()
        for dz in (1, 3, 2):
            self.second(dz).wait_recv()
            self.second(dz).wait_send()
        for k in (1, 2, 3, 4):
            self.first(k).wait_send()
        self.own().wait()


class SpreadRows(Side):
    def __init__(self, pieces):
        r = pieces.shape[1]
        dma = pltpu.SemaphoreType.DMA
        self.operands = [pieces]
        self.shapes = [jax.ShapeDtypeStruct((r, D), BF)]
        self.scratch = [dma((14,)), dma((14,)), dma((2,))]

    def bind(self, ring, ins, outs, scratch):
        (p,), (out,) = ins, outs
        self.peers = [ctx_at(k)[1] for k in range(1, 8)]
        self.s = [
            Spread(
                p.at[part], lambda c, part=part: out.at[:, piece_lanes(c, part)], scratch[:2], part * 7, part == 0,
                scratch[2].at[part],
            )
            for part in range(2)
        ]

    def start(self):
        for s in self.s:
            s.start()

    def middle(self):
        for s in self.s:
            s.relay()

    def finish(self):
        for s in self.s:
            s.finish()


class Move(Side):
    def __init__(self, pieces):
        dma = pltpu.SemaphoreType.DMA
        self.operands = [pieces]
        self.shapes = [jax.ShapeDtypeStruct((8, pieces.shape[0], 128), BF)]
        self.scratch = [dma((8,)), dma((8,))]

    def bind(self, ring, ins, outs, scratch):
        (self.p,), (self.out,), self.sems = ins, outs, scratch
        x, self.y_lo, core = lax.axis_index("x"), lax.axis_index("y_lo"), lax.axis_index("core")
        self.here16, self.here8 = x * 4 + self.y_lo * 2 + core, x * 2 + core
        self.peers = [device for _, device in group_peers()]

    def same(self, j):
        return self.here16 == self.y_lo * 8 + j

    def away(self, j):
        return pltpu.make_async_remote_copy(
            src_ref=self.p.at[:, pl.ds(j * 128, 128)], dst_ref=self.out.at[self.here8], send_sem=self.sems[0].at[j],
            recv_sem=self.sems[1].at[self.here8], device_id={"x": self.y_lo * 2 + j // 4, "y_lo": j // 2 % 2, "core": j % 2},
            device_id_type=MESH,
        )

    def stay(self, j):
        return pltpu.make_async_copy(self.p.at[:, pl.ds(j * 128, 128)], self.out.at[self.here8], self.sems[1].at[self.here8])

    def start(self):
        for j in range(8):

            @pl.when(self.same(j))
            def _():
                self.stay(j).start()

            @pl.when(jnp.logical_not(self.same(j)))
            def _():
                self.away(j).start()

    def arrive(self, s):
        pltpu.make_async_copy(self.out.at[s], self.out.at[s], self.sems[1].at[s]).wait()

    def drain(self):
        for j in range(8):

            @pl.when(jnp.logical_not(self.same(j)))
            def _():
                self.away(j).wait_send()

    def finish(self):
        for s in range(8):
            self.arrive(s)
        self.drain()


def group_peers():
    x, y_lo, core = lax.axis_index("x"), lax.axis_index("y_lo"), lax.axis_index("core")
    found = []
    for k in range(1, 16):
        dx, dy, dc = k // 4, k // 2 % 2, k % 2
        found.append((k, {"x": lax.rem(x + dx, 4), "y_lo": 1 - y_lo if dy else y_lo, "core": 1 - core if dc else core}))
    return found


class SpreadGateUp(Side):
    def __init__(self, pieces, first, into=None):
        self.r, self.first = pieces.shape[1], first
        dma = pltpu.SemaphoreType.DMA
        self.operands = [pieces]
        self.shapes = [jax.ShapeDtypeStruct((2, FF, 128), BF)]
        self.scratch = [dma((56,)), dma((56,)), dma((8,))]

    def bind(self, ring, ins, outs, scratch):
        (got,), (out,) = ins, outs
        self.s = []
        for s in range(8):

            def slot(c, s=s):
                rows = ((s // 2) * 4 + lax.rem(c // 2, 2) * 2 + s % 2) * 352 + lax.rem(c, 2) * 176 + self.first
                return out.at[c // 4, pl.ds(pl.multiple_of(rows, 16), self.r)]

            self.s.append(Spread(got.at[s], slot, scratch[:2], s * 7, s % 3 == 0, scratch[2].at[s]))

    def start(self):
        for s in self.s:
            s.start()

    def middle(self):
        for s in self.s:
            if s.y_first:
                s.relay()
        for s in self.s:
            if not s.y_first:
                s.relay()

    def finish(self):
        for s in self.s:
            s.finish()


def back_norm(v, grad, u):
    r = norm_scale(v)
    n = v * r
    return grad + r * (u - n * jnp.mean(u * n, axis=1, keepdims=True))


def y_partners():
    y_hi, y_lo = lax.axis_index("y_hi"), lax.axis_index("y_lo")
    return {"y_lo": 1 - y_lo}, {"y_hi": 1 - y_hi, "y_lo": 1 - y_lo}


def group_lanes(x, y_lo):
    return pl.ds(pl.multiple_of(x * 512 + y_lo * 256, 256), 256)


def tp_peers(ring):
    found = []
    for k in range(1, 8):
        dx, dc = k // 2, k % 2
        core = 1 - ring.core if dc else ring.core
        found.append((k, lax.rem(ring.x + dx, 4), core))
    return found


def ctx_peer(c, k):
    other = lax.rem(c + k, 8)
    return {"y_hi": other // 4, "z": lax.rem(other, 4)}


def nt(a, b):
    return dot(a, b, 1, 1)


def nn(a, b):
    return dot(a, b, 1, 0)


def key_bias(meta_ref, d, c, bias):
    docs = meta_ref[d].astype(F32)
    query_docs = meta_ref[d, pl.ds(c, 1), :].astype(F32)
    lane = lax.broadcasted_iota(jnp.int32, (128, 128), 1)
    row = lax.broadcasted_iota(jnp.int32, (128, 128), 0)

    def position(owner, i):
        return jnp.where(i < 64, owner * 64 + i, (15 - owner) * 64 + i - 64)

    query_pos = position(c, lane)
    for b in range(8):
        key_docs = jnp.broadcast_to(docs[b : b + 1, :], (128, 128)).T
        good = (query_pos >= position(b, row)) & (key_docs == query_docs)
        bias[pl.ds(b * 128, 128), :] = jnp.where(good, 0.0, NEGATIVE)


def eye():
    return (lax.broadcasted_iota(jnp.int32, (128, 128), 0) == lax.broadcasted_iota(jnp.int32, (128, 128), 1)).astype(BF)


def front_kernel(
    x_ref, meta_ref, g1_ref, g2_ref, wq_ref, wk_ref, wv_ref, wg_ref, wu_ref, wo_ref, wdn_ref, tab_ref,
    a_ref, lse_ref, metas_ref, n1_out, wqkv_out, qp_out, kv_out, wos_ref, wgu_ref, wd_ref,
    n1, wqkv, w, wt, qkv, qp, kv, bias, probs,
    ag_s, ag_r, meta_s, meta_r, w_s, w_r, y_s, y_r, gu_s, gu_r, wd_s, wd_r, kv_s, kv_r, fw_s, fw_r, loc,
):
    ring = Ring()
    y_lo = lax.axis_index("y_lo")
    c, _ = ctx_at(0)
    near, other = y_partners()
    peers = tp_peers(ring)
    meet([{"x": x, "core": core} for _, x, core in peers] + [near, other] + [ctx_at(k)[1] for k in range(1, 8)])
    here = ring.x * 2 + ring.core
    copies, local = [], []

    def copy_here(src, dst):
        copy = pltpu.make_async_copy(src, dst, loc.at[len(local)])
        copy.start()
        local.append(copy)

    ag = Ag(ring, n1, (ag_s, ag_r))

    def normed(k, _):
        rows = pl.ds(pl.multiple_of(k * 16, 16), 16)
        v = x_ref[rows, :].astype(F32)
        n1[here, rows, :] = (v * norm_scale(v)).astype(BF)
        return 0

    lax.fori_loop(0, 4, normed, 0)
    ag.begin(0)
    for k, x, core in peers:
        copies.append(send(meta_ref, metas_ref.at[here], (meta_s, meta_r), k, {"x": x, "core": core}))
    metas_ref[here] = meta_ref[...]

    one_matrix = eye()
    g1, g2 = g1_ref[...], g2_ref[...]

    def turned(ref, gain, k):
        return (nt(one_matrix, ref[:, lanes_at(k * 128, 128)]) * gain).astype(BF)

    for f in range(16):
        w[(f // 4) * 2 + f % 2, pl.ds((f // 2 % 2) * 128, 128), :] = turned(wq_ref, g1, f)
    for ref, at in ((wk_ref, 256), (wv_ref, 320)):
        for k in range(2):
            tile = turned(ref, g1, k)
            for x in (2 * k, 2 * k + 1):
                part = tile[(x % 2) * 64 : (x % 2) * 64 + 64]
                w[2 * x, pl.ds(at, 64), :] = part
                w[2 * x + 1, pl.ds(at, 64), :] = part
    lanes = lanes_at((ring.x * 4 + y_lo * 2 + ring.core) * 128, 128)
    wcopies = {}
    for k, x, core in peers:
        wcopies[k] = send(w.at[x * 2 + core], wqkv.at[:, lanes], (w_s, w_r), k, {"x": x, "core": core})
    wqkv[:, lanes] = w[here]
    lax.fori_loop(4, 8, normed, 0)
    ag.begin(1)

    copy_here(wo_ref, wos_ref.at[y_lo])
    copy_here(wdn_ref, wd_ref.at[pl.ds(pl.multiple_of(y_lo * 352, 32), 352)])
    for half, device in enumerate((near, other)):
        copies.append(send(wo_ref.at[HALVES[half]], wos_ref.at[y_lo, HALVES[half]], (y_s, y_r), 4 + half, device))

    def turn_all(ref, i):
        def body(k, _):
            wt[i, pl.ds(pl.multiple_of(k * 128, 128), 128), :] = turned(ref, g2, k)
            return 0

        lax.fori_loop(0, FF // 128, body, 0)

    turn_all(wg_ref, 0)
    for dx in range(4):
        x = lax.rem(ring.x + 4 - dx, 4)
        if dx > 0:
            wcopies[2 * dx].wait_recv()
        wcopies[2 * dx + 1].wait_recv()
        block = wqkv.at[:, group_lanes(x, y_lo)]
        copies.append(send(block, block, (y_s, y_r), dx, (near, other)[dx // 2]))
    for half, device in enumerate((near, other)):
        rows = pl.ds(pl.multiple_of(y_lo * 352 + half * 176, 16), 176)
        copies.append(send(wdn_ref.at[pl.ds(half * 176, 176)], wd_ref.at[rows], (wd_s, wd_r), half, device))
    ag.near()
    turn_all(wu_ref, 1)
    ag.far()

    for j in range(2):
        rows = pl.ds(pl.multiple_of((ring.x * 4 + 2 * j + ring.core) * 352, 32), 352)
        copy_here(wt.at[:, rows], wgu_ref.at[:, j, :, lanes])
    for k, x, core in peers:
        for j in range(2):
            rows = pl.ds(pl.multiple_of((x * 4 + 2 * j + core) * 352, 32), 352)
            copies.append(
                send(wt.at[:, rows], wgu_ref.at[:, j, :, lanes], (gu_s, gu_r), k * 2 + j, {"x": x, "core": core})
            )

    ag.have(*range(6, 14))
    for copy in copies[9:13]:
        copy.wait_recv()
    qkv[...] = nt(n1[...].reshape(1024, D), wqkv[...])
    copy_here(n1, n1_out)
    copy_here(wqkv, wqkv_out)

    lane = lax.broadcasted_iota(jnp.int32, (128, 128), 1)

    def rope(u, i):
        return u * tab_ref[i] + pltpu.roll(u, 96, 1) * tab_ref[i + 1] + pltpu.roll(u, 32, 1) * tab_ref[i + 2]

    for d in range(8):
        kv[d % 2, d // 2, c] = rope(qkv[pl.ds(d * 128, 128), 256:384], 3).astype(BF)
    spreads = [
        Spread(kv.at[ring.core, x, c], lambda i, x=x: kv.at[ring.core, x, i], (kv_s, kv_r), x * 7, x < 2, None) for x in range(4)
    ]
    for s in spreads:
        s.start()

    def turn_queries(d, _):
        for j in range(2):
            u = rope(qkv[pl.ds(pl.multiple_of(d * 128, 128), 128), pl.ds(j * 128, 128)], 0) * 0.125
            qp[d, pl.ds(j * 256, 128), :] = jnp.where(lane < 64, u, 0.0).astype(BF)
            qp[d, pl.ds(j * 256 + 128, 128), :] = jnp.where(lane < 64, pltpu.roll(u, 64, 1), 0.0).astype(BF)
        return 0

    lax.fori_loop(0, 8, turn_queries, 0)
    copy_here(qp, qp_out)

    forwards = []

    def pass_on(k):
        back = ctx_at(k if k == 4 else k // 4 * 4 + (4 - k % 4))[0]
        block = kv.at[ring.core, :, back]
        forwards.append(send(block, block, (fw_s, fw_r), k - 1, ring.sibling))

    for k in (1, 4, 3, 2):
        for s in spreads:
            s.first(k).wait_recv()
            if k < 4 and not s.y_first:
                s.second(k).start()
            if k == 4 and s.y_first:
                for dz in (1, 3, 2):
                    s.second(dz).start()
        pass_on(k)
    for dz in (1, 3, 2):
        for s in spreads:
            s.second(dz).wait_recv()
        pass_on(4 + dz)
    for copy in forwards:
        copy.wait_recv()
    copy_here(kv, kv_out)
    for copy in copies[:7]:
        copy.wait_recv()

    def one(d, _):
        key_bias(metas_ref, d, c, bias)
        keys = kv[lax.rem(d, 2), d // 2].reshape(1024, 128)
        scores = nt(keys, qp[d])
        for h in range(4):
            s = scores[:, h * 128 : (h + 1) * 128] + bias[...]
            top = jnp.max(s, axis=0, keepdims=True)
            e = jnp.exp(s - top)
            total = jnp.sum(e, axis=0, keepdims=True)
            probs[:, h * 128 : (h + 1) * 128] = (e * (1.0 / total)).astype(BF)
            lse_ref[d, :, h * 128 : (h + 1) * 128] = jnp.broadcast_to(top + jnp.log(total), (8, 128))
        mixed = nn(keys.T, probs[...])
        for j in range(2):
            two = jnp.concatenate([mixed[64:, (2 * j) * 128 : (2 * j + 1) * 128], mixed[64:, (2 * j + 1) * 128 : (2 * j + 2) * 128]], axis=0)
            a_ref[pl.ds(pl.multiple_of(d * 128, 128), 128), pl.ds(j * 128, 128)] = two.T.astype(BF)
        return 0

    lax.fori_loop(0, 8, one, 0)

    ag.drain()
    for k in range(1, 8):
        wcopies[k].wait_send()
    for s in spreads:
        for k in range(1, 5):
            s.first(k).wait_send()
        for dz in (1, 3, 2):
            s.second(dz).wait_send()
    for copy in forwards:
        copy.wait_send()
    for i, copy in enumerate(copies):
        copy.wait_send()
        if i >= 7 and not 9 <= i < 13:
            copy.wait_recv()
    for copy in local:
        copy.wait()


def front(hidden_in, meta, g1, g2, w_query, w_key, w_value, w_gate, w_up, w_out, w_down, tabs):
    dma = pltpu.SemaphoreType.DMA
    pair = lambda n: [dma((n,)), dma((n,))]
    out = lambda *shape: jax.ShapeDtypeStruct(shape, BF)
    return pl.pallas_call(
        front_kernel,
        out_shape=[
            out(1024, 256), jax.ShapeDtypeStruct((8, 8, 512), F32), jax.ShapeDtypeStruct((8, 16, 128), jnp.int32),
            out(8, 128, D), out(384, D), out(8, 512, 128), out(2, 4, 8, 128, 128), out(2, 128, D), out(2, 2, 352, D), out(704, D),
        ],
        in_specs=[VM] * 12,
        out_specs=[VM] * 3 + [HB] * 7,
        scratch_shapes=[
            pltpu.VMEM((8, 128, D), BF), pltpu.VMEM((384, D), BF), pltpu.VMEM((8, 384, 128), BF), pltpu.VMEM((2, FF, 128), BF),
            pltpu.VMEM((1024, 384), F32), pltpu.VMEM((8, 512, 128), BF), pltpu.VMEM((2, 4, 8, 128, 128), BF),
            pltpu.VMEM((1024, 128), F32), pltpu.VMEM((1024, 512), BF),
            *pair(14), *pair(8), *pair(8), *pair(6), *pair(16), *pair(2), *pair(28), *pair(7), dma((8,)),
        ],
        compiler_params=params(5),
        name="front",
    )(hidden_in, meta, g1, g2, w_query, w_key, w_value, w_gate, w_up, w_out, w_down, tabs)


def everyone():
    return [device for _, device in group_peers()] + [ctx_at(k)[1] for k in range(1, 8)] + [y_partners()[1]]


def rope_tables(c):
    cos, sin = tables(positions_of(c))
    low = jnp.arange(HD) < HD // 2
    to_low, to_high = jnp.where(low, -sin, 0.0), jnp.where(low, 0.0, sin)
    one, zero = jnp.ones_like(cos), jnp.zeros_like(cos)
    pairs = [(cos, cos), (to_low, to_low), (to_high, to_high), (cos, one), (to_low, zero), (to_high, zero)]
    return jnp.stack([jnp.concatenate(p, axis=1) for p in pairs])


def tail_kernel(
    sides, qp_ref, kv_ref, lse_ref, meta_ref, tab_ref, da_ref, x_ref, dy1_ref, stats_ref,
    wqkv_hbm, n1_hbm, ggu2_hbm, gout_hbm, piece_down_ref, piece_gu1_ref,
    grad_ref, info_ref, all_down, all_out, all_qkv, all_gu,
    bias, dap, ds, pb, mine, theirs, stage, back, dqkv, dqkv_t, parts, held, got, n1, wqkv, gq,
    piece_gu2, piece_out, piece_qkv, got_gu1, got_gu2, got_qkv, st1, st2, mid,
    co_s, co_r, kv_s, kv_r, rs_s, rs_r, st_s, st_r, st2_s, st2_r, qs_s, qs_r, loc, *side_scratch,
):
    ring = Ring()
    c, _ = ctx_at(0)
    sum_gu2, sum_out, move_gu1, down, out, spread_gu1, move_gu2, sum_qkv, move_qkv, spread_gu2 = sides
    scratch = list(side_scratch)
    places = (
        (ggu2_hbm, piece_gu2), (gout_hbm, piece_out), (piece_gu1_ref, got_gu1), (piece_down_ref, all_down), (piece_out, all_out),
        (got_gu1, all_gu), (piece_gu2, got_gu2), (gq, piece_qkv), (piece_qkv, got_qkv), (got_gu2, all_gu),
    )
    for side, (i, o) in zip(sides, places):
        side.bind(ring, (i,), (o,), scratch[: len(side.scratch)])
        del scratch[: len(side.scratch)]
    loads = [pltpu.make_async_copy(n1_hbm, n1, loc.at[0]), pltpu.make_async_copy(wqkv_hbm, wqkv, loc.at[1])]
    for load in loads:
        load.start()
    meet(everyone())
    sum_gu2.start()
    sum_out.start()
    move_gu1.start()
    group = group_peers()
    here16 = ring.x * 4 + lax.axis_index("y_lo") * 2 + ring.core
    copies = [send(stats_ref, st1.at[here16], (st_s, st_r), k, device) for k, device in group]
    st1[here16] = stats_ref[...]
    lane = lax.broadcasted_iota(jnp.int32, (128, 128), 1)

    def unrope(u, i):
        return u * tab_ref[i] - pltpu.roll(u, 96, 1) * tab_ref[i + 1] - pltpu.roll(u, 32, 1) * tab_ref[i + 2]

    def one(x, core):
        d = x * 2 + core
        rows = pl.ds(pl.multiple_of(d * 128, 128), 128)
        key_bias(meta_ref, d, c, bias)
        for j in range(2):
            tile = da_ref[rows, pl.ds(j * 128, 128)].astype(F32)
            dap[pl.ds(j * 256, 128), :] = jnp.where(lane >= 64, pltpu.roll(tile, 64, 1), 0.0).astype(BF)
            dap[pl.ds(j * 256 + 128, 128), :] = jnp.where(lane >= 64, tile, 0.0).astype(BF)
        kv = kv_ref[core, x].reshape(1024, 128)
        scores = nt(kv, qp_ref[d])
        dprobs = nt(kv, dap[...])
        for h in range(4):
            cols = slice(h * 128, (h + 1) * 128)
            p = jnp.exp(scores[:, cols] + bias[...] - lse_ref[d, 0:1, cols])
            pb[:, cols] = p.astype(BF)
            dp = dprobs[:, cols]
            centre = jnp.sum(p * dp, axis=0, keepdims=True)
            ds[:, cols] = (p * (dp - centre)).astype(BF)
        dkv = nn(ds[...], qp_ref[d]) + nn(pb[...], dap[...])
        dq = nn(kv.T, ds[...]) * 0.125
        for j in range(2):
            two = jnp.concatenate([dq[:64, (2 * j) * 128 : (2 * j + 1) * 128], dq[:64, (2 * j + 1) * 128 : (2 * j + 2) * 128]], axis=0)
            dqkv[rows, pl.ds(j * 128, 128)] = unrope(two.T, 0).astype(BF)
        return dkv

    def core_copy(x):
        return pltpu.make_async_remote_copy(
            src_ref=mine.at[x], dst_ref=theirs.at[x], send_sem=co_s.at[x], recv_sem=co_r.at[x],
            device_id=ring.sibling, device_id_type=MESH,
        )

    def kv_copy(x, k):
        other, device = ctx_at(k)
        return pltpu.make_async_remote_copy(
            src_ref=stage.at[x, other], dst_ref=back.at[x, k - 1], send_sem=kv_s.at[x * 7 + k - 1],
            recv_sem=kv_r.at[x * 7 + k - 1], device_id=device, device_id_type=MESH,
        )

    def to_sibling(x, _):
        mine[x] = one(x, 1 - ring.core).astype(BF).reshape(8, 128, 128)
        core_copy(x).start()
        dqkv[pl.ds(pl.multiple_of((x * 2 + 1 - ring.core) * 128, 128), 128), 256:384] = jnp.zeros((128, 128), BF)
        return 0

    lax.fori_loop(0, 4, to_sibling, 0)
    down.start()
    for copy in copies:
        copy.wait_recv()
    total = st1[0]
    for i in range(1, 16):
        total += st1[i]
    mid[...] = total
    st2[c] = total
    copies2 = [send(mid, st2.at[c], (st2_s, st2_r), k - 1, ctx_at(k)[1]) for k in range(1, 8)]

    def to_owners(x, _):
        dkv = one(x, ring.core)
        core_copy(x).wait_recv()
        stage[x] = (dkv + theirs[x].reshape(1024, 128).astype(F32)).astype(BF).reshape(8, 128, 128)
        for k in range(1, 8):
            kv_copy(x, k).start()
        return 0

    lax.fori_loop(0, 4, to_owners, 0)
    sum_gu2.middle()
    sum_out.middle()
    move_gu1.finish()
    down.middle()

    def gather_up(x, _):
        total = stage[x, c].astype(F32)
        for k in range(1, 8):
            kv_copy(x, k).wait_recv()
            total += back[x, k - 1].astype(F32)
        rows = pl.ds(pl.multiple_of((x * 2 + ring.core) * 128, 128), 128)
        dqkv[rows, 256:384] = unrope(total, 3).astype(BF)
        return 0

    lax.fori_loop(0, 4, gather_up, 0)
    spread_gu1.start()
    for load in loads:
        load.wait()

    rs = Rs(ring, parts, held, got, (rs_s, rs_r))
    for i in range(4):
        x = rs.blocks[i]

        def body(k, _, x=x):
            lanes = lanes_at(k * 512, 512)
            block = nn(dqkv[pl.ds(pl.multiple_of(x * 256, 256), 256), :], wqkv[:, lanes])
            parts[pl.ds(x * 2, 2), :, lanes] = block.astype(BF).reshape(2, 128, 512)
            return 0

        lax.fori_loop(0, 4, body, 0)
        rs.copy(i).start()
        if i == 1:
            rs.send_far()
        elif i == 2:
            rs.send_right()
        elif i == 3:
            rs.send_left()
    dqkv_t[...] = dqkv[...].T

    def grads(k, _):
        lanes = lanes_at(k * 512, 512)
        product = nn(dqkv_t[...], n1[:, :, lanes].reshape(1024, 512))
        gq[:, :, :, lanes] = product.astype(BF).reshape(2, 4, 48, 512)
        return 0

    lax.fori_loop(0, 4, grads, 0)
    sum_qkv.start()
    rs.relay()
    sum_gu2.finish()
    move_gu2.start()
    sum_out.finish()
    out.start()
    spread_gu1.middle()
    for half in range(2):
        rs.ready(half)

        def body(k, _, half=half):
            rows = pl.ds(half * 64 + k * 16, 16)
            grad_ref[rows, :] = back_norm(x_ref[rows, :].astype(F32), dy1_ref[rows, :], rs.total(rows))
            return 0

        lax.fori_loop(0, 4, body, 0)
    move_gu2.finish()
    spread_gu2.start()
    out.middle()
    sum_qkv.middle()
    sum_qkv.finish()
    move_qkv.start()
    spread_gu2.middle()
    move_qkv.finish()
    spread_qkv = Spread(got_qkv, lambda c: all_qkv.at[:, c], (qs_s, qs_r), 0, False, loc.at[2])
    spread_qkv.start()

    for copy in copies2:
        copy.wait_recv()
    total = st2[0]
    for i in range(1, 8):
        total += st2[i]
    sums = jnp.sum(total, axis=1, keepdims=True)
    squares, count = sums[0:1], sums[1:2]
    scale = 2.0 / (D * count)
    info_ref[...] = jnp.concatenate([squares / count, scale, jnp.zeros((6, 1), F32)], axis=0) + jnp.zeros((8, 128), F32)

    spread_qkv.relay()
    rs.drain()
    for copy in copies + copies2:
        copy.wait_send()

    def drain(x, _):
        core_copy(x).wait_send()
        for k in range(1, 8):
            kv_copy(x, k).wait_send()
        return 0

    lax.fori_loop(0, 4, drain, 0)
    down.finish()
    out.finish()
    spread_gu1.finish()
    spread_gu2.finish()
    spread_qkv.finish()


def tail(qp, kv, lse, metas, tabs, da, hidden_in, dy1, stats, wqkv, n1, grad_gu2, grad_out, piece_down, piece_gu1):
    dma = pltpu.SemaphoreType.DMA
    pair = lambda n: [dma((n,)), dma((n,))]
    bf = lambda *shape: jax.ShapeDtypeStruct(shape, BF)
    vm = lambda *shape: pltpu.VMEM(shape, BF)
    sides = [
        SumColumns(grad_gu2), SumRows(grad_out), Move(piece_gu1), SpreadRows(piece_down), SpreadRows(bf(2, 128, 128)),
        SpreadGateUp(bf(8, 96, 128), 0), Move(bf(80, 1024)), SumColumns(bf(2, 4, 48, D), True), Move(bf(48, 1024)),
        SpreadGateUp(bf(8, 80, 128), 96),
    ]
    return pl.pallas_call(
        functools.partial(tail_kernel, sides),
        out_shape=[
            jax.ShapeDtypeStruct((128, D), F32), jax.ShapeDtypeStruct((8, 128), F32),
            bf(352, D), bf(128, D), bf(8, 8, 48, 128), bf(2, FF, 128),
        ],
        in_specs=[VM] * 9 + [HB] * 4 + [VM] * 2,
        out_specs=[VM] * 5 + [HB],
        scratch_shapes=[
            pltpu.VMEM((1024, 128), F32), vm(512, 128), vm(1024, 512), vm(1024, 512),
            vm(4, 8, 128, 128), vm(4, 8, 128, 128), vm(4, 8, 128, 128), vm(4, 7, 128, 128),
            vm(1024, 384), vm(384, 1024), vm(8, 128, D), vm(3, 128, D), vm(7, 128, D), vm(8, 128, D), vm(384, D), vm(2, 4, 48, D),
            vm(80, 1024), vm(2, 128, 128), vm(48, 1024), vm(8, 96, 128), vm(8, 80, 128), vm(8, 48, 128),
            pltpu.VMEM((16, 8, 128), F32), pltpu.VMEM((8, 8, 128), F32), pltpu.VMEM((8, 128), F32),
            *pair(4), *pair(28), *pair(10), *pair(16), *pair(7), *pair(7), dma((3,)),
            *[s for side in sides for s in side.scratch],
        ],
        compiler_params=params(7),
        name="tail",
    )(qp, kv, lse, metas, tabs, da, hidden_in, dy1, stats, wqkv, n1, grad_gu2, grad_out, piece_down, piece_gu1)


def finish_kernel(
    info_ref, gu_ref, g1_ref, g2_ref, wg_ref, wu_ref, down_ref, qkv_ref, wq_ref, wk_ref, wv_ref, out_ref, gin_ref,
    gate_ref, up_ref, down_out, q_ref, k_ref, v_ref, o_ref, input_ref, gain1_ref, gain2_ref,
    total2,
):
    scale = info_ref[1:2, 0:1]
    s1, s2 = g1_ref[...] * scale, g2_ref[...] * scale
    one_matrix = eye()
    step = pl.program_id(0)

    @pl.when(step == 0)
    def _():
        total2[...] = jnp.zeros_like(total2)
        total = jnp.zeros((128, 128), F32)
        for s in range(8):
            for j in range(2):
                f = (s // 2) * 4 + j * 2 + s % 2
                part = nt(one_matrix, qkv_ref[s, j * 128 : (j + 1) * 128])
                total += part * wq_ref[:, f * 128 : (f + 1) * 128].astype(F32)
                q_ref[:, f * 128 : (f + 1) * 128] = part * s1
        for i in range(2):
            both = [qkv_ref[2 * x, 256:].astype(F32) + qkv_ref[2 * x + 1, 256:].astype(F32) for x in (2 * i, 2 * i + 1)]
            for at, w_ref, g_ref in ((0, wk_ref, k_ref), (64, wv_ref, v_ref)):
                part = jnp.concatenate([both[0][at : at + 64], both[1][at : at + 64]], axis=0).T
                total += part * w_ref[:, i * 128 : (i + 1) * 128].astype(F32)
                g_ref[:, i * 128 : (i + 1) * 128] = part * s1
        gain1_ref[...] = jnp.sum(total.T, axis=0, keepdims=True) * scale
        o_ref[...] = out_ref[...].astype(F32) * scale
        input_ref[...] = gin_ref[...] * scale

    total = total2[...]
    for i, w_ref, g_ref in ((0, wg_ref, gate_ref), (1, wu_ref, up_ref)):
        turned = nt(one_matrix, gu_ref[i])
        g_ref[...] = turned * s2
        weighed = turned * w_ref[...].astype(F32)
        for k in range(4):
            total += weighed[:, k * 128 : (k + 1) * 128]
    total2[...] = total
    down_out[...] = down_ref[...].astype(F32) * scale

    @pl.when(step == pl.num_programs(0) - 1)
    def _():
        gain2_ref[...] = jnp.sum(total2[...].T, axis=0, keepdims=True) * scale


def finish(info, all_gu, g1, g2, w_gate, w_up, down, all_qkv, w_query, w_key, w_value, out, grad_in):
    wide = pl.BlockSpec((128, 512), lambda i: (0, i))
    rows = pl.BlockSpec((32, D), lambda i: (i, 0))
    whole = lambda *shape: pl.BlockSpec(shape, lambda i: (0,) * len(shape))
    f32 = lambda *shape: jax.ShapeDtypeStruct(shape, F32)
    return pl.pallas_call(
        finish_kernel,
        grid=(11,),
        out_shape=[
            f32(128, FF), f32(128, FF), f32(352, D), f32(128, D), f32(128, KVD), f32(128, KVD), f32(128, D), f32(128, D),
            f32(1, 128), f32(1, 128),
        ],
        in_specs=[
            whole(8, 128), pl.BlockSpec((2, 512, 128), lambda i: (0, i, 0)), whole(128, 1), whole(128, 1), wide, wide, rows,
            whole(8, 384, 128), whole(128, D), whole(128, KVD), whole(128, KVD), whole(128, D), whole(128, D),
        ],
        out_specs=[
            wide, wide, rows, whole(128, D), whole(128, KVD), whole(128, KVD), whole(128, D), whole(128, D),
            whole(1, 128), whole(1, 128),
        ],
        scratch_shapes=[pltpu.VMEM((128, 128), F32)],
        compiler_params=pltpu.CompilerParams(vmem_limit_bytes=48 * 2**20),
        name="finish",
    )(info, all_gu, g1, g2, w_gate, w_up, down, all_qkv, w_query, w_key, w_value, out, grad_in)


def local(hidden_in, teacher, doc_ids, valid_mask, norm1_gain, w_query, w_key, w_value, w_out, norm2_gain, w_gate, w_up, w_down):
    c = lax.axis_index(("y_hi", "z"))
    g1 = norm1_gain.astype(F32)
    g2 = norm2_gain.astype(F32)
    valid = valid_mask.astype(F32)
    tabs = rope_tables(c)
    blocks = doc_ids.reshape(16, 64)
    key_docs = jnp.concatenate([blocks[:8], blocks[:7:-1]], axis=1)
    meta = jnp.concatenate([key_docs, valid_mask[None], jnp.zeros((7, 128), jnp.int32)], axis=0)

    a, lse, metas, n1, wqkv, qp, kv, wo, wgu, wd = front(
        hidden_in, meta, g1[None], g2[None], w_query, w_key, w_value, w_gate, w_up, w_out, w_down, tabs
    )
    wo = wo.reshape(256, D)
    layer_out, loss_rows, dy1, da, grad_out, grad_gu2, piece_down, piece_gu1 = middle(
        a, wo, hidden_in, teacher, valid[:, None], wgu, wd
    )
    stats = jnp.concatenate([loss_rows.reshape(1, 128), valid[None], jnp.zeros((6, 128), F32)], axis=0)
    grad_in, info, all_down, all_out, all_qkv, all_gu = tail(
        qp, kv, lse, metas, tabs, da, hidden_in, dy1, stats, wqkv, n1, grad_gu2, grad_out, piece_down, piece_gu1
    )
    gg, gp, gd, gq, gk, gv, go, input_grad, gain1, gain2 = finish(
        info, all_gu, g1[:, None], g2[:, None], w_gate, w_up, all_down, all_qkv.reshape(8, 384, 128),
        w_query, w_key, w_value, all_out, grad_in,
    )
    return (layer_out, info[0, 0], input_grad, gain1[0], gq, gk, gv, go, gain2[0], gg, gp, gd)


def solution(mesh):
    fine = Mesh(mesh.devices.reshape(2, 4, 4, 2, 2), AXES)
    rows = ("y_hi", "z", "x", "y_lo", "core")
    fs = ("x", "y_lo", "core")
    token, shard = P(rows, None), P(fs, None)
    return jax.shard_map(
        local,
        mesh=fine,
        in_specs=(token, token, shard, P(rows), P(fs), shard, shard, shard, shard, P(fs), shard, shard, shard),
        out_specs=(token, P(), token, P(fs), shard, shard, shard, shard, P(fs), shard, shard, shard),
        check_vma=False,
    )
```

```python
import functools

import jax
import jax.numpy as jnp
import numpy as np
from jax import lax
from jax.experimental import pallas as pl
from jax.experimental.pallas import tpu as pltpu
from jax.sharding import Mesh, PartitionSpec as P

D = 2048
HEADS = 32
KV_HEADS = 4
HD = 64
FF = 5632
KVD = 256
EPSILON = 1e-05
THETA = 10000.0
NEGATIVE = -1e30
AXES = ("y_hi", "z", "x", "y_lo", "core")
BF = jnp.bfloat16
F32 = jnp.float32


def dot(a, b, ca, cb):
    return lax.dot_general(a, b, (((ca,), (cb,)), ((), ())), preferred_element_type=F32)


def rope_angles():
    frequency = np.float32(THETA) ** (-(np.arange(HD // 2, dtype=np.float32) * np.float32(2.0) / np.float32(HD)))
    c, t = np.arange(8)[:, None], np.arange(64)[None]
    positions = np.concatenate([c * 64 + t, (15 - c) * 64 + t], axis=1).astype(np.float32)
    angles = (positions[:, :, None] * frequency).astype(np.float32).astype(np.float64)
    angles = np.concatenate([angles] * 4, axis=2)
    return np.stack([np.cos(angles), np.sin(angles)], axis=1).astype(np.float32)


def fill_tables(angles, tab):
    cos, sin = angles[0], angles[1]
    lane = lax.broadcasted_iota(jnp.int32, (128, 128), 1)
    low = lax.rem(lane, 64) < 32
    to_low, to_high = jnp.where(low, -sin, 0.0), jnp.where(low, 0.0, sin)
    tab[0], tab[1], tab[2] = cos, to_low, to_high
    tab[3] = jnp.where(lane < 64, cos, 1.0)
    tab[4] = jnp.where(lane < 64, to_low, 0.0)
    tab[5] = jnp.where(lane < 64, to_high, 0.0)


def column(row):
    return jnp.broadcast_to(row, (128, 128)).T


MESH = pl.DeviceIdType.MESH
HALVES = (pl.ds(0, 64), pl.ds(64, 64))
VM = pl.BlockSpec(memory_space=pltpu.VMEM)
HB = pl.BlockSpec(memory_space=pl.ANY)


def params(number):
    return pltpu.CompilerParams(collective_id=number, has_side_effects=True, vmem_limit_bytes=56 * 2**20)


def send(src, dst, sems, i, device):
    copy = pltpu.make_async_remote_copy(
        src_ref=src, dst_ref=dst, send_sem=sems[0].at[i], recv_sem=sems[1].at[i], device_id=device, device_id_type=MESH
    )
    copy.start()
    return copy


def meet(devices):
    barrier = pltpu.get_barrier_semaphore()
    for device in devices:
        pl.semaphore_signal(barrier, inc=1, device_id=device, device_id_type=MESH)
    pl.semaphore_wait(barrier, len(devices))


class Ring:
    def __init__(self):
        x, core = lax.axis_index("x"), lax.axis_index("core")
        self.x, self.core = x, core
        self.right_x, self.left_x, self.far_x = lax.rem(x + 1, 4), lax.rem(x + 3, 4), lax.rem(x + 2, 4)
        self.right, self.left, self.sibling = {"x": self.right_x}, {"x": self.left_x}, {"core": 1 - core}


def norm_scale(v):
    return lax.rsqrt(jnp.mean(v * v, axis=1, keepdims=True) + EPSILON)


class Side:
    in_place = False

    def middle(self):
        pass


def lanes_at(start, size):
    return pl.ds(pl.multiple_of(start, 128), size)


def other_of_pair(i):
    return i + 1 - 2 * lax.rem(i, 2)


class Stream:
    def __init__(self, y_first, mirror, y_index, r, first, own, bufs, sems, base):
        y_hi, y_lo, z = lax.axis_index("y_hi"), lax.axis_index("y_lo"), lax.axis_index("z")
        y = y_hi * 2 + y_lo
        self.r, self.own, self.sems, self.base = r, own, sems, base
        self.b1, self.b2, self.b3, self.b4 = bufs
        axes = []
        for is_y, i in ((True, y), (False, z)) if y_first else ((False, z), (True, y)):
            p, q = (other_of_pair(i), 3 - i) if mirror == 0 else (3 - i, other_of_pair(i))
            beyond = 3 - p if mirror == 0 else other_of_pair(p)
            devices = [{"y_hi": d // 2, "y_lo": lax.rem(d, 2)} if is_y else {"z": d} for d in (p, q)]
            axes.append((i, p, q, beyond, devices))
        (self.i, p, self.q, beyond, self.dev1), (i2, p2, q2, beyond2, self.dev2) = axes
        index = (lambda v: v) if y_first else y_index
        self.at_i, self.at_p, self.at_q, self.at_beyond = index(i2), index(p2), index(q2), index(beyond2)
        self.views = [(view, (slot, *at)) for slot, d in ((1, beyond), (0, p)) for view, at in first(d)]

    def copy(self, k, src, dst, device):
        return pltpu.make_async_remote_copy(
            src_ref=src, dst_ref=dst, send_sem=self.sems[0].at[self.base + k], recv_sem=self.sems[1].at[self.base + k],
            device_id=device, device_id_type=MESH,
        )

    def copies(self, step):
        if step == 1:
            return [self.copy(k, view, self.b1.at[at], self.dev1[0]) for k, (view, at) in enumerate(self.views)]
        if step == 2:
            return [self.copy(8, self.b1.at[1], self.b2, self.dev1[1])]
        if step == 3:
            places = ((1, self.at_beyond), (0, self.at_p))
            return [self.copy(9 + slot, self.b2.at[at], self.b3.at[slot], self.dev2[0]) for slot, at in places]
        return [self.copy(11, self.b3.at[1], self.b4, self.dev2[1])]

    def go(self, step):
        for copy in self.copies(step):
            copy.start()

    def arrived(self, step):
        for copy in self.copies(step):
            copy.wait_recv()

    def add(self, out, terms, lead):
        def body(i, _):
            total = None
            for term in terms:
                v = term(i).astype(F32)
                total = v if total is None else total + v
            out(i, total.astype(BF))
            return 0

        lax.fori_loop(0, lead, body, 0)

    def step2(self):
        self.arrived(1)
        b1 = self.b1
        for slot, d in ((1, self.q), (0, self.i)):

            def put(j, v, slot=slot):
                b1[slot, j, :, :] = v

            self.add(put, [lambda j, d=d: self.own(d, j), lambda j, slot=slot: b1[slot, j, :, :]], 4)
            if slot == 1:
                self.go(2)

    def step3(self):
        self.arrived(2)
        b1, b2 = self.b1, self.b2

        def put(j, v):
            b2[j, :, :] = v

        self.add(put, [lambda j: b1[0, j, :, :], lambda j: b2[j, :, :]], 4)
        self.go(3)

    def step4(self):
        self.arrived(3)
        b2, b3 = self.b2, self.b3
        for slot, place in ((1, self.at_q), (0, self.at_i)):

            def put(j, v, slot=slot):
                b3[slot, :, :] = v

            self.add(
                put,
                [lambda j, p=place: b2[p, :, :], lambda j, slot=slot: b3[slot, :, :]],
                1,
            )
            if slot == 1:
                self.go(4)

    def finish(self, out):
        self.arrived(4)
        b3, b4 = self.b3, self.b4
        self.add(out, [lambda j: b3[0, :, :], lambda j: b4[:, :]], 1)
        for step in (1, 2, 3, 4):
            for copy in self.copies(step):
                copy.wait_send()


class TorusSum(Side):
    def start(self):
        for s in self.s:
            s.go(1)

    def step2(self):
        for s in self.s:
            s.step2()

    def step3(self):
        for s in self.s:
            s.step3()

    def step4(self):
        for s in self.s:
            s.step4()

    def finish(self):
        for s, out in zip(self.s, self.outs):
            s.finish(out)

    def bufs(self, scratch, i):
        return [ref.at[i] for ref in scratch[:4]]


class SumColumns(TorusSum):
    def __init__(self, grads):
        r = self.rows = grads.shape[2]
        dma = pltpu.SemaphoreType.DMA
        self.operands = [grads]
        self.shapes = [jax.ShapeDtypeStruct((r, 1024), BF)]
        self.scratch = [
            pltpu.VMEM((4, 2, 4, r, 256), BF), pltpu.VMEM((4, 4, r, 256), BF), pltpu.VMEM((4, 2, r, 256), BF), pltpu.VMEM((4, r, 256), BF),
            dma((48,)), dma((48,)),
        ]

    def bind(self, ring, ins, outs, scratch):
        (g,), (out,) = ins, outs
        self.s, self.outs = [], []
        for i in range(4):
            y_first, lane = i < 2, i * 256

            def first(d, y_first=y_first, lane=lane):
                if y_first:
                    return [(g.at[d // 2, :, :, lanes_at(lax.rem(d, 2) * 1024 + lane, 256)], ())]
                return [(g.at[:, d, :, pl.ds(yl * 1024 + lane, 256)], (pl.ds(yl * 2, 2),)) for yl in range(2)]

            def own(d, j, y_first=y_first, lane=lane):
                rows = slice(None)
                if y_first:
                    return g[d // 2, j, rows, lanes_at(lax.rem(d, 2) * 1024 + lane, 256)]
                return g[lax.rem(j, 2), d, rows, lanes_at((j // 2) * 1024 + lane, 256)]

            def put(j, v, lane=lane):
                out[:, pl.ds(lane, 256)] = v

            y_index = lambda y: lax.rem(y, 2) * 2 + y // 2
            self.s.append(Stream(y_first, i % 2, y_index, self.rows, first, own, self.bufs(scratch, i), scratch[4:], i * 12))
            self.outs.append(put)


class SumRows(TorusSum):
    def __init__(self, grads):
        r = self.rows = grads.shape[1]
        dma = pltpu.SemaphoreType.DMA
        self.operands = [grads]
        self.shapes = [jax.ShapeDtypeStruct((2, r, 128), BF)]
        h = r // 2
        self.scratch = [
            pltpu.VMEM((4, 2, 4, h, 128), BF), pltpu.VMEM((4, 4, h, 128), BF), pltpu.VMEM((4, 2, h, 128), BF), pltpu.VMEM((4, h, 128), BF),
            dma((48,)), dma((48,)),
        ]

    def bind(self, ring, ins, outs, scratch):
        (g,), (out,) = ins, outs
        self.s, self.outs = [], []
        h = self.rows // 2
        for i in range(4):
            y_first, lane, row = i < 2, (i // 2) * 512, (i % 2) * h

            def first(d, y_first=y_first, lane=lane, row=row):
                half = pl.ds(row, h)
                if y_first:
                    return [
                        (g.at[lax.rem(d, 2), half, lanes_at((d // 2) * 1024 + lane + z * 128, 128)], (z,)) for z in range(4)
                    ]
                return [(g.at[:, half, lanes_at(yh * 1024 + lane + d * 128, 128)], (pl.ds(yh * 2, 2),)) for yh in range(2)]

            def own(d, j, y_first=y_first, lane=lane, row=row):
                rows = pl.ds(row, h)
                if y_first:
                    return g[lax.rem(d, 2), rows, lanes_at((d // 2) * 1024 + lane + j * 128, 128)]
                return g[lax.rem(j, 2), rows, lanes_at((j // 2) * 1024 + lane + d * 128, 128)]

            def put(j, v, i=i, row=row):
                out[i // 2, pl.ds(row, h), :] = v

            self.s.append(Stream(y_first, i % 2, lambda y: y, h, first, own, self.bufs(scratch, i), scratch[4:], i * 12))
            self.outs.append(put)


class Ag:
    def __init__(self, ring, buf, sems):
        r = self.r = ring
        self.buf, self.sems = buf, sems
        self.plan = (
            (r.x, 0, r.right), (r.x, 1, r.right), (r.x, 1, r.left), (r.x, 0, r.left),
            (r.left_x, 0, r.right), (r.right_x, 1, r.left),
            (r.x, 0, r.sibling), (r.x, 1, r.sibling),
            (r.left_x, 0, r.sibling), (r.left_x, 1, r.sibling), (r.right_x, 0, r.sibling), (r.right_x, 1, r.sibling),
            (r.far_x, 0, r.sibling), (r.far_x, 1, r.sibling),
        )

    def copy(self, i):
        x, half, device = self.plan[i]
        block = self.buf.at[x * 2 + self.r.core, HALVES[half]]
        return pltpu.make_async_remote_copy(
            src_ref=block, dst_ref=block, send_sem=self.sems[0].at[i], recv_sem=self.sems[1].at[i],
            device_id=device, device_id_type=MESH,
        )

    def begin(self, half):
        for i in ((0, 3, 6), (2, 1, 7))[half]:
            self.copy(i).start()

    def near(self, steps=slice(None)):
        for got, onward in ((0, (4, 8)), (2, (5, 11)), (1, (9,)), (3, (10,)))[steps]:
            self.copy(got).wait_recv()
            for i in onward:
                self.copy(i).start()

    def far(self):
        for got, onward in ((4, 12), (5, 13)):
            self.copy(got).wait_recv()
            self.copy(onward).start()

    def have(self, *which):
        for i in which:
            self.copy(i).wait_recv()

    def drain(self):
        for i in range(14):
            self.copy(i).wait_send()


class Rs:
    def __init__(self, ring, parts, held, got, sems):
        r = self.r = ring
        self.parts, self.held, self.got, self.sems = parts, held, got, sems
        self.blocks = (r.far_x, r.right_x, r.left_x, r.x)
        a, b = HALVES
        self.plan = {
            4: (held.at[0, a], got.at[4, a], r.right), 5: (held.at[0, b], got.at[4, b], r.left),
            6: (held.at[1, b], got.at[5, b], r.right), 7: (held.at[2, a], got.at[5, a], r.left),
            8: (held.at[1, a], got.at[6, a], r.right), 9: (held.at[2, b], got.at[6, b], r.left),
        }

    def swap(self, i, x):
        return pltpu.make_async_remote_copy(
            src_ref=self.parts.at[x * 2 + 1 - self.r.core], dst_ref=self.got.at[i], send_sem=self.sems[0].at[i],
            recv_sem=self.sems[1].at[i], device_id=self.r.sibling, device_id_type=MESH,
        )

    def copy(self, i):
        if i < 4:
            return self.swap(i, self.blocks[i])
        src, dst, device = self.plan[i]
        return pltpu.make_async_remote_copy(
            src_ref=src, dst_ref=dst, send_sem=self.sems[0].at[i], recv_sem=self.sems[1].at[i],
            device_id=device, device_id_type=MESH,
        )

    def pair(self, i, half):
        x = self.blocks[i]

        def body(k, _):
            rows = pl.ds(half * 64 + k * 16, 16)
            total = self.parts[x * 2 + self.r.core, rows, :].astype(F32) + self.got[i, rows, :].astype(F32)
            self.held[i, rows, :] = total.astype(BF)
            return 0

        lax.fori_loop(0, 4, body, 0)

    def onward(self, i, half):
        def body(k, _):
            rows = pl.ds(half * 64 + k * 16, 16)
            total = self.held[i, rows, :].astype(F32) + self.got[4, rows, :].astype(F32)
            self.held[i, rows, :] = total.astype(BF)
            return 0

        lax.fori_loop(0, 4, body, 0)

    def send_left(self):
        self.copy(2).wait_recv()
        self.pair(2, 0)
        self.copy(7).start()

    def send_right(self):
        self.copy(1).wait_recv()
        self.pair(1, 1)
        self.copy(6).start()

    def send_far(self):
        self.copy(0).wait_recv()
        self.pair(0, 0)
        self.copy(4).start()
        self.pair(0, 1)
        self.copy(5).start()

    def relay(self):
        self.pair(1, 0)
        self.pair(2, 1)
        self.copy(4).wait_recv()
        self.onward(1, 0)
        self.copy(8).start()
        self.copy(5).wait_recv()
        self.onward(2, 1)
        self.copy(9).start()
        self.copy(3).wait_recv()

    def ready(self, half):
        for i in ((7, 8), (6, 9))[half]:
            self.copy(i).wait_recv()

    def total(self, rows):
        r = self.r
        return (
            self.parts[r.x * 2 + r.core, rows, :].astype(F32)
            + self.got[3, rows, :].astype(F32)
            + self.got[5, rows, :].astype(F32)
            + self.got[6, rows, :].astype(F32)
        )

    def drain(self):
        for i in range(10):
            self.copy(i).wait_send()


def middle_kernel(
    down_side, gu_side, a_ref, wo_ref, x_ref, valid_ref, wd_ref, teacher_hbm, half_w_ref,
    out_ref, stats_ref, dy1_ref, da_ref, gout_ref, ggu_ref, piece_ref, gu_piece_ref,
    w, n2, dyg, dag, parts, held, got, y1, gate, up, mid, mid_t, dup, dgu1, dgu2, gd, gu1, dmid, valid_col, loss_col,
    rs1_s, rs1_r, ag1_s, ag1_r, rs2_s, rs2_r, ag2_s, ag2_r, rs3_s, rs3_r, ag3_s, ag3_r, w_s, w_r, loc, *side_scratch,
):
    ring = Ring()
    y_lo = lax.axis_index("y_lo")
    near, other = y_partners()
    down_side.bind(ring, (gd,), (piece_ref,), side_scratch[: len(down_side.scratch)])
    gu_side.bind(ring, (gu1,), (gu_piece_ref,), side_scratch[len(down_side.scratch) :])
    meet([ring.right, ring.left, ring.sibling, near, other] + [{"z": p} for p in (other_of_pair(lax.axis_index("z")), 3 - lax.axis_index("z"))])
    here = ring.x * 2 + ring.core
    dy, dgate = dy1_ref, mid
    teacher = dag.at[here]
    teacher_copy = pltpu.make_async_copy(teacher_hbm, teacher, loc.at[4])
    teacher_copy.start()
    valid_col[...] = column(valid_ref[...].astype(F32))

    wcopies = []
    for dx in range(4):
        lanes = group_lanes(lax.rem(ring.x + 4 - dx, 4), y_lo)
        src, dst = half_w_ref.at[:, :, :, lanes], w.at[:, :, :, lanes]
        wcopies.append(send(src, dst, (w_s, w_r), dx, (near, other)[dx // 2]))
        copy = pltpu.make_async_copy(src, dst, loc.at[dx])
        copy.start()
        wcopies.append(copy)

    def rows_of(x):
        return pl.ds(pl.multiple_of(x * 256, 256), 256)

    def block(buf, x):
        return buf[pl.ds(x * 2, 2)].reshape(256, D)

    def put(x, product):
        def body(k, _):
            lanes = lanes_at(k * 512, 512)
            parts[pl.ds(x * 2, 2), :, lanes] = product(lanes).astype(BF).reshape(2, 128, 512)
            return 0

        lax.fori_loop(0, 4, body, 0)

    def reduced(rs, op, ag, buf):
        for half in range(2):
            rs.ready(half)

            def body(k, _, half=half):
                rows = pl.ds(half * 64 + k * 16, 16)
                buf[here, rows, :] = op(rows, rs.total(rows)).astype(BF)
                return 0

            lax.fori_loop(0, 4, body, 0)
            ag.begin(half)

    def over_blocks(ag, rs, work, first=None, after=()):
        def step(i, _):
            at = functools.partial(jnp.equal, i)

            @pl.when(at(0))
            def _():
                ag.have(6, 7)
                if first is not None:
                    ag.near(slice(2))
                    first()

            @pl.when(at(1))
            def _():
                ag.near(slice(2 if first is not None else 0, 4))
                ag.have(8, 9)

            @pl.when(at(2))
            def _():
                ag.have(10, 11)
                if rs is not None:
                    rs.send_left()

            @pl.when(at(3))
            def _():
                if rs is not None:
                    rs.send_right()
                ag.far()
                ag.have(12, 13)

            x = lax.rem(ring.x + jnp.where(at(1), 3, jnp.where(at(2), 1, jnp.where(at(3), 2, 0))), 4)
            work(x)
            if rs is not None:
                rs.swap(3 - i, x).start()
            for k, then in enumerate(after):
                pl.when(at(k + 1))(then)
            return 0

        lax.fori_loop(0, 4, step, 0)

    rs = Rs(ring, parts, held, got, (rs1_s, rs1_r))
    ag = Ag(ring, n2, (ag1_s, ag1_r))
    for i in range(4):
        x = rs.blocks[i]
        put(x, lambda lanes, x=x: nn(a_ref[rows_of(x), :], wo_ref[:, lanes]))
        rs.copy(i).start()
        if i == 1:
            rs.send_far()
        elif i == 2:
            rs.send_right()
        elif i == 3:
            rs.send_left()
    rs.relay()

    def op1(rows, total):
        v = x_ref[rows, :].astype(F32) + total
        y1[rows, :] = v
        return v * norm_scale(v)

    reduced(rs, op1, ag, n2)
    rs.drain()
    teacher_copy.wait()

    rs = Rs(ring, parts, held, got, (rs2_s, rs2_r))

    def forward(x):
        rows = rows_of(x)
        gate[rows, :] = nt(block(n2, x), w[0].reshape(704, D))
        up[rows, :] = nt(block(n2, x), w[1].reshape(704, D))

        def body(k, _):
            r = pl.ds(pl.multiple_of(x * 256 + k * 32, 32), 32)
            g = gate[r, :]
            mid[pl.ds(pl.multiple_of(k * 32, 32), 32), :] = (g * jax.nn.sigmoid(g) * up[r, :]).astype(BF)
            return 0

        lax.fori_loop(0, 8, body, 0)
        put(x, lambda lanes: nn(mid[...], wd_ref[:, lanes]))
        mid_t[:, rows] = mid[...].T

    def weights_here():
        for copy in wcopies:
            copy.wait()

    over_blocks(ag, rs, forward, weights_here)
    rs.send_far()
    rs.relay()
    ag.drain()

    def op2(rows, total):
        v = y1[rows, :] + total
        out_ref[rows, :] = v.astype(BF)
        miss = v - dag[here, rows, :].astype(F32)
        valid = valid_col[rows, 0:1]
        loss_col[rows, :] = jnp.broadcast_to(valid * jnp.mean(miss * miss, axis=1, keepdims=True), (16, 128))
        dy[rows, :] = valid * miss
        return valid * miss

    ag = Ag(ring, dyg, (ag2_s, ag2_r))
    reduced(rs, op2, ag, dyg)
    rs.drain()
    stats_ref[...] = jnp.concatenate([loss_col[...].T[0:1], valid_ref[...].astype(F32), jnp.zeros((6, 128), F32)], axis=0)

    rs = Rs(ring, parts, held, got, (rs3_s, rs3_r))

    def backward(x):
        rows = rows_of(x)
        dgate_mid = nt(block(dyg, x), wd_ref[...])
        dmid[...] = dgate_mid

        def body(k, _):
            r = pl.ds(pl.multiple_of(x * 256 + k * 32, 32), 32)
            q = pl.ds(pl.multiple_of(k * 32, 32), 32)
            g, dm = gate[r, :], dmid[q, :]
            sg = jax.nn.sigmoid(g)
            dgate[q, :] = (dm * up[r, :] * sg * (1.0 + g * (1.0 - sg))).astype(BF)
            dup[q, :] = (dm * (g * sg)).astype(BF)
            return 0

        lax.fori_loop(0, 8, body, 0)
        put(x, lambda lanes: nn(dgate[...], w[0, :, :, lanes].reshape(704, 512)) + nn(dup[...], w[1, :, :, lanes].reshape(704, 512)))
        for i, ref in enumerate((dgate, dup)):
            turned = ref[...].T
            for c in range(4):
                dgu1[pl.ds((4 * i + c) * 96, 96), rows] = turned[176 * c : 176 * c + 96]
                dgu2[pl.ds((4 * i + c) * 80, 80), rows] = turned[176 * c + 96 : 176 * c + 176]

    over_blocks(ag, rs, backward)
    rs.send_far()

    def grad_down(k, _):
        lanes = lanes_at(k * 512, 512)
        gd[:, :, lanes] = nn(mid_t[...], dyg[:, :, lanes].reshape(1024, 512)).astype(BF).reshape(2, 352, 512)
        return 0

    lax.fori_loop(0, 4, grad_down, 0)
    down_side.start()
    rs.relay()

    def grad_gu(rows, lhs, out, k):
        lanes = lanes_at(k * 512, 512)
        out[:, :, :, lanes] = nn(lhs[...], n2[:, :, lanes].reshape(1024, 512)).astype(BF).reshape(2, 4, rows, 512)

    def grad_gu1(k, _):
        grad_gu(96, dgu1, gu1, k)
        return 0

    lax.fori_loop(0, 4, grad_gu1, 0)
    gu_side.start()
    ag.drain()

    def op3(rows, total):
        v = back_norm(y1[rows, :], dy[rows, :], total)
        dy1_ref[rows, :] = v
        return v

    ag = Ag(ring, dag, (ag3_s, ag3_r))
    reduced(rs, op3, ag, dag)
    rs.drain()

    def to_attention(x):
        rows = rows_of(x)
        da_ref[rows, :] = nt(block(dag, x), wo_ref[...]).astype(BF)
        mid_t[0:256, rows] = a_ref[rows, :].T
        grad_gu(80, dgu2, ggu_ref, x)

    def both(name):
        def then():
            getattr(down_side, name)()
            getattr(gu_side, name)()

        return then

    over_blocks(ag, None, to_attention, after=(both("step2"), both("step3"), both("step4")))

    def grad_out(k, _):
        lanes = lanes_at(k * 512, 512)
        gout_ref[:, :, lanes] = nn(mid_t[0:256, :], dag[:, :, lanes].reshape(1024, 512)).astype(BF).reshape(2, 128, 512)
        return 0

    lax.fori_loop(0, 4, grad_out, 0)
    ag.drain()
    down_side.finish()
    gu_side.finish()


def middle(a, wo, x, teacher, valid, half_w, wd):
    dma = pltpu.SemaphoreType.DMA
    pair = lambda n: [dma((n,)), dma((n,))]
    big = pltpu.VMEM((8, 128, D), BF)
    sides = [SumRows(jax.ShapeDtypeStruct((2, 352, D), BF)), SumColumns(jax.ShapeDtypeStruct((2, 4, 96, D), BF))]
    return pl.pallas_call(
        functools.partial(middle_kernel, *sides),
        out_shape=[
            jax.ShapeDtypeStruct((128, D), BF), jax.ShapeDtypeStruct((8, 128), F32), jax.ShapeDtypeStruct((128, D), F32),
            jax.ShapeDtypeStruct((1024, 256), BF), jax.ShapeDtypeStruct((2, 128, D), BF), jax.ShapeDtypeStruct((2, 4, 80, D), BF),
            *[s for side in sides for s in side.shapes],
        ],
        in_specs=[VM] * 5 + [HB, HB],
        out_specs=[VM] * 8,
        scratch_shapes=[
            pltpu.VMEM((2, 2, 352, D), BF), big, big, big, big, pltpu.VMEM((3, 128, D), BF), pltpu.VMEM((7, 128, D), BF),
            pltpu.VMEM((128, D), F32),
            pltpu.VMEM((1024, 704), F32), pltpu.VMEM((1024, 704), F32),
            pltpu.VMEM((256, 704), BF), pltpu.VMEM((704, 1024), BF), pltpu.VMEM((256, 704), BF),
            pltpu.VMEM((768, 1024), BF), pltpu.VMEM((640, 1024), BF), pltpu.VMEM((2, 352, D), BF), pltpu.VMEM((2, 4, 96, D), BF),
            pltpu.VMEM((256, 704), F32), pltpu.VMEM((128, 128), F32), pltpu.VMEM((128, 128), F32),
            *pair(10), *pair(14), *pair(10), *pair(14), *pair(10), *pair(14), *pair(4), dma((5,)),
            *[s for side in sides for s in side.scratch],
        ],
        compiler_params=pltpu.CompilerParams(collective_id=1, has_side_effects=True, vmem_limit_bytes=63 * 2**20),
        name="middle",
    )(a, wo, x, valid, wd, teacher, half_w)


def piece_lanes(c, part):
    return lanes_at((c // 4) * 1024 + part * 512 + lax.rem(c, 4) * 128, 128)


def ctx_at(k):
    y_hi, z = lax.axis_index("y_hi"), lax.axis_index("z")
    y, zz = (1 - y_hi if k // 4 else y_hi), lax.rem(z + k % 4, 4)
    return y * 4 + zz, {"y_hi": y, "z": zz}


class Spread:
    def __init__(self, piece, slot, sems, base, y_first, local):
        self.piece, self.slot, self.sems, self.base, self.y_first, self.local = piece, slot, sems, base, y_first, local

    def copy(self, k, src, c, device):
        return pltpu.make_async_remote_copy(
            src_ref=src, dst_ref=self.slot(c), send_sem=self.sems[0].at[self.base + k - 1],
            recv_sem=self.sems[1].at[self.base + k - 1], device_id=device, device_id_type=MESH,
        )

    def first(self, k):
        here, _ = ctx_at(0)
        return self.copy(k, self.piece, here, ctx_at(k)[1])

    def second(self, dz):
        if self.y_first:
            c, _ = ctx_at(4)
            return self.copy(4 + dz, self.slot(c), c, ctx_at(dz)[1])
        c, _ = ctx_at(4 - dz)
        return self.copy(4 + dz, self.slot(c), c, ctx_at(4)[1])

    def own(self):
        return pltpu.make_async_copy(self.piece, self.slot(ctx_at(0)[0]), self.local)

    def start(self):
        for k in (4, 1, 3, 2) if self.y_first else (1, 3, 2, 4):
            self.first(k).start()
        if self.local is not None:
            self.own().start()

    def relay(self):
        if self.y_first:
            self.first(4).wait_recv()
            for dz in (1, 3, 2):
                self.second(dz).start()
        else:
            for dz in (1, 3, 2):
                self.first(dz).wait_recv()
                self.second(dz).start()

    def finish(self):
        if self.y_first:
            for dz in (1, 3, 2):
                self.first(dz).wait_recv()
        else:
            self.first(4).wait_recv()
        for dz in (1, 3, 2):
            self.second(dz).wait_recv()
            self.second(dz).wait_send()
        for k in (1, 2, 3, 4):
            self.first(k).wait_send()
        self.own().wait()


class SpreadRows(Side):
    def __init__(self, pieces):
        r = pieces.shape[1]
        dma = pltpu.SemaphoreType.DMA
        self.operands = [pieces]
        self.shapes = [jax.ShapeDtypeStruct((r, D), BF)]
        self.scratch = [dma((14,)), dma((14,)), dma((2,))]

    def bind(self, ring, ins, outs, scratch):
        (p,), (out,) = ins, outs
        self.peers = [ctx_at(k)[1] for k in range(1, 8)]
        self.s = [
            Spread(
                p.at[part], lambda c, part=part: out.at[:, piece_lanes(c, part)], scratch[:2], part * 7, part == 0,
                scratch[2].at[part],
            )
            for part in range(2)
        ]

    def start(self):
        for s in self.s:
            s.start()

    def middle(self):
        for s in self.s:
            s.relay()

    def finish(self):
        for s in self.s:
            s.finish()


class Move(Side):
    def __init__(self, pieces):
        dma = pltpu.SemaphoreType.DMA
        self.operands = [pieces]
        self.shapes = [jax.ShapeDtypeStruct((8, pieces.shape[0], 128), BF)]
        self.scratch = [dma((8,)), dma((8,))]

    def bind(self, ring, ins, outs, scratch):
        (self.p,), (self.out,), self.sems = ins, outs, scratch
        x, self.y_lo, core = lax.axis_index("x"), lax.axis_index("y_lo"), lax.axis_index("core")
        self.here16, self.here8 = x * 4 + self.y_lo * 2 + core, x * 2 + core
        self.peers = [device for _, device in group_peers()]

    def same(self, j):
        return self.here16 == self.y_lo * 8 + j

    def away(self, j):
        return pltpu.make_async_remote_copy(
            src_ref=self.p.at[:, pl.ds(j * 128, 128)], dst_ref=self.out.at[self.here8], send_sem=self.sems[0].at[j],
            recv_sem=self.sems[1].at[self.here8], device_id={"x": self.y_lo * 2 + j // 4, "y_lo": j // 2 % 2, "core": j % 2},
            device_id_type=MESH,
        )

    def stay(self, j):
        return pltpu.make_async_copy(self.p.at[:, pl.ds(j * 128, 128)], self.out.at[self.here8], self.sems[1].at[self.here8])

    def start(self):
        for j in range(8):

            @pl.when(self.same(j))
            def _():
                self.stay(j).start()

            @pl.when(jnp.logical_not(self.same(j)))
            def _():
                self.away(j).start()

    def arrive(self, s):
        pltpu.make_async_copy(self.out.at[s], self.out.at[s], self.sems[1].at[s]).wait()

    def drain(self):
        for j in range(8):

            @pl.when(jnp.logical_not(self.same(j)))
            def _():
                self.away(j).wait_send()

    def finish(self):
        for s in range(8):
            self.arrive(s)
        self.drain()


def group_peers():
    x, y_lo, core = lax.axis_index("x"), lax.axis_index("y_lo"), lax.axis_index("core")
    found = []
    for k in range(1, 16):
        dx, dy, dc = k // 4, k // 2 % 2, k % 2
        found.append((k, {"x": lax.rem(x + dx, 4), "y_lo": 1 - y_lo if dy else y_lo, "core": 1 - core if dc else core}))
    return found


class SpreadGateUp(Side):
    def __init__(self, pieces, first, into=None):
        self.r, self.first = pieces.shape[1], first
        dma = pltpu.SemaphoreType.DMA
        self.operands = [pieces]
        self.shapes = [jax.ShapeDtypeStruct((2, FF, 128), BF)]
        self.scratch = [dma((56,)), dma((56,)), dma((8,))]

    def bind(self, ring, ins, outs, scratch):
        (got,), (out,) = ins, outs
        self.s = []
        for s in range(8):

            def slot(c, s=s):
                rows = ((s // 2) * 4 + lax.rem(c // 2, 2) * 2 + s % 2) * 352 + lax.rem(c, 2) * 176 + self.first
                return out.at[c // 4, pl.ds(pl.multiple_of(rows, 16), self.r)]

            self.s.append(Spread(got.at[s], slot, scratch[:2], s * 7, s % 3 == 0, scratch[2].at[s]))

    def start(self):
        for s in self.s:
            s.start()

    def middle(self):
        for s in self.s:
            if s.y_first:
                s.relay()
        for s in self.s:
            if not s.y_first:
                s.relay()

    def finish(self):
        for s in self.s:
            s.finish()


def back_norm(v, grad, u):
    r = norm_scale(v)
    n = v * r
    return grad + r * (u - n * jnp.mean(u * n, axis=1, keepdims=True))


def y_partners():
    y_hi, y_lo = lax.axis_index("y_hi"), lax.axis_index("y_lo")
    return {"y_lo": 1 - y_lo}, {"y_hi": 1 - y_hi, "y_lo": 1 - y_lo}


def group_lanes(x, y_lo):
    return pl.ds(pl.multiple_of(x * 512 + y_lo * 256, 256), 256)


def tp_peers(ring):
    found = []
    for k in range(1, 8):
        dx, dc = k // 2, k % 2
        core = 1 - ring.core if dc else ring.core
        found.append((k, lax.rem(ring.x + dx, 4), core))
    return found


def ctx_peer(c, k):
    other = lax.rem(c + k, 8)
    return {"y_hi": other // 4, "z": lax.rem(other, 4)}


def nt(a, b):
    return dot(a, b, 1, 1)


def nn(a, b):
    return dot(a, b, 1, 0)


def key_bias(meta_ref, d, c, bias):
    docs = meta_ref[d].astype(F32)
    query_docs = meta_ref[d, pl.ds(c, 1), :].astype(F32)
    lane = lax.broadcasted_iota(jnp.int32, (128, 128), 1)
    row = lax.broadcasted_iota(jnp.int32, (128, 128), 0)

    def position(owner, i):
        return jnp.where(i < 64, owner * 64 + i, (15 - owner) * 64 + i - 64)

    query_pos = position(c, lane)
    for b in range(8):
        key_docs = jnp.broadcast_to(docs[b : b + 1, :], (128, 128)).T
        good = (query_pos >= position(b, row)) & (key_docs == query_docs)
        bias[pl.ds(b * 128, 128), :] = jnp.where(good, 0.0, NEGATIVE)


def eye():
    return (lax.broadcasted_iota(jnp.int32, (128, 128), 0) == lax.broadcasted_iota(jnp.int32, (128, 128), 1)).astype(BF)


def front_kernel(
    x_ref, doc_ref, g1_ref, g2_ref, wq_ref, wk_ref, wv_ref, wg_ref, wu_ref, wo_ref, wdn_ref, angles_hbm,
    a_ref, lse_ref, metas_ref, n1_out, wqkv_out, qp_out, kv_out, wos_ref, wgu_ref, wd_ref,
    n1, wqkv, w, wt, qkv, qp, kv, bias, probs, meta_ref, angles, tab_ref,
    ag_s, ag_r, meta_s, meta_r, w_s, w_r, y_s, y_r, gu_s, gu_r, wd_s, wd_r, kv_s, kv_r, fw_s, fw_r, loc,
):
    ring = Ring()
    y_lo = lax.axis_index("y_lo")
    c, _ = ctx_at(0)
    near, other = y_partners()
    peers = tp_peers(ring)
    meet([{"x": x, "core": core} for _, x, core in peers] + [near, other] + [ctx_at(k)[1] for k in range(1, 8)])
    here = ring.x * 2 + ring.core
    copies, local = [], []

    def copy_here(src, dst):
        copy = pltpu.make_async_copy(src, dst, loc.at[len(local)])
        copy.start()
        local.append(copy)

    ag = Ag(ring, n1, (ag_s, ag_r))

    def normed(k, _):
        rows = pl.ds(pl.multiple_of(k * 16, 16), 16)
        v = x_ref[rows, :].astype(F32)
        n1[here, rows, :] = (v * norm_scale(v)).astype(BF)
        return 0

    lax.fori_loop(0, 4, normed, 0)
    ag.begin(0)
    copy_here(angles_hbm.at[c], angles)
    row = lax.broadcasted_iota(jnp.int32, (1, 128), 1)
    tiles = [doc_ref[:, k * 128 : (k + 1) * 128] for k in range(8)]
    meta_ref[...] = jnp.zeros_like(meta_ref)
    for i in range(8):
        first, second = tiles[i // 2], tiles[(15 - i) // 2]
        if i % 2:
            first, second = pltpu.roll(first, 64, 1), pltpu.roll(second, 64, 1)
        meta_ref[i : i + 1, :] = jnp.where(row < 64, first, second)
    for k, x, core in peers:
        copies.append(send(meta_ref, metas_ref.at[here], (meta_s, meta_r), k, {"x": x, "core": core}))
    metas_ref[here] = meta_ref[...]

    one_matrix = eye()
    g1, g2 = g1_ref[...].astype(F32), g2_ref[...].astype(F32)

    def turned(ref, gain, k):
        return (nt(one_matrix, ref[:, lanes_at(k * 128, 128)]) * gain).astype(BF)

    for f in range(16):
        w[(f // 4) * 2 + f % 2, pl.ds((f // 2 % 2) * 128, 128), :] = turned(wq_ref, g1, f)
    for ref, at in ((wk_ref, 256), (wv_ref, 320)):
        for k in range(2):
            tile = turned(ref, g1, k)
            for x in (2 * k, 2 * k + 1):
                part = tile[(x % 2) * 64 : (x % 2) * 64 + 64]
                w[2 * x, pl.ds(at, 64), :] = part
                w[2 * x + 1, pl.ds(at, 64), :] = part
    lanes = lanes_at((ring.x * 4 + y_lo * 2 + ring.core) * 128, 128)
    wcopies = {}
    for k, x, core in peers:
        wcopies[k] = send(w.at[x * 2 + core], wqkv.at[:, lanes], (w_s, w_r), k, {"x": x, "core": core})
    wqkv[:, lanes] = w[here]
    lax.fori_loop(4, 8, normed, 0)
    ag.begin(1)

    copy_here(wo_ref, wos_ref.at[y_lo])
    copy_here(wdn_ref, wd_ref.at[pl.ds(pl.multiple_of(y_lo * 352, 32), 352)])
    for half, device in enumerate((near, other)):
        copies.append(send(wo_ref.at[HALVES[half]], wos_ref.at[y_lo, HALVES[half]], (y_s, y_r), 4 + half, device))

    def turn_all(ref, i):
        def body(k, _):
            wt[i, pl.ds(pl.multiple_of(k * 128, 128), 128), :] = turned(ref, g2, k)
            return 0

        lax.fori_loop(0, FF // 128, body, 0)

    turn_all(wg_ref, 0)
    for dx in range(4):
        x = lax.rem(ring.x + 4 - dx, 4)
        if dx > 0:
            wcopies[2 * dx].wait_recv()
        wcopies[2 * dx + 1].wait_recv()
        block = wqkv.at[:, group_lanes(x, y_lo)]
        copies.append(send(block, block, (y_s, y_r), dx, (near, other)[dx // 2]))
    for half, device in enumerate((near, other)):
        rows = pl.ds(pl.multiple_of(y_lo * 352 + half * 176, 16), 176)
        copies.append(send(wdn_ref.at[pl.ds(half * 176, 176)], wd_ref.at[rows], (wd_s, wd_r), half, device))
    ag.near()
    turn_all(wu_ref, 1)
    ag.far()

    for j in range(2):
        rows = pl.ds(pl.multiple_of((ring.x * 4 + 2 * j + ring.core) * 352, 32), 352)
        copy_here(wt.at[:, rows], wgu_ref.at[:, j, :, lanes])
    for k, x, core in peers:
        for j in range(2):
            rows = pl.ds(pl.multiple_of((x * 4 + 2 * j + core) * 352, 32), 352)
            copies.append(
                send(wt.at[:, rows], wgu_ref.at[:, j, :, lanes], (gu_s, gu_r), k * 2 + j, {"x": x, "core": core})
            )

    local[0].wait()
    fill_tables(angles, tab_ref)
    ag.have(*range(6, 14))
    for copy in copies[9:13]:
        copy.wait_recv()
    qkv[...] = nt(n1[...].reshape(1024, D), wqkv[...])
    copy_here(n1, n1_out)
    copy_here(wqkv, wqkv_out)

    lane = lax.broadcasted_iota(jnp.int32, (128, 128), 1)

    def rope(u, i):
        return u * tab_ref[i] + pltpu.roll(u, 96, 1) * tab_ref[i + 1] + pltpu.roll(u, 32, 1) * tab_ref[i + 2]

    for d in range(8):
        kv[d % 2, d // 2, c] = rope(qkv[pl.ds(d * 128, 128), 256:384], 3).astype(BF)
    spreads = [
        Spread(kv.at[ring.core, x, c], lambda i, x=x: kv.at[ring.core, x, i], (kv_s, kv_r), x * 7, x < 2, None) for x in range(4)
    ]
    for s in spreads:
        s.start()

    def turn_queries(d, _):
        for j in range(2):
            u = rope(qkv[pl.ds(pl.multiple_of(d * 128, 128), 128), pl.ds(j * 128, 128)], 0) * 0.125
            qp[d, pl.ds(j * 256, 128), :] = jnp.where(lane < 64, u, 0.0).astype(BF)
            qp[d, pl.ds(j * 256 + 128, 128), :] = jnp.where(lane < 64, pltpu.roll(u, 64, 1), 0.0).astype(BF)
        return 0

    lax.fori_loop(0, 8, turn_queries, 0)
    copy_here(qp, qp_out)

    forwards = []

    def pass_on(k):
        back = ctx_at(k if k == 4 else k // 4 * 4 + (4 - k % 4))[0]
        block = kv.at[ring.core, :, back]
        forwards.append(send(block, block, (fw_s, fw_r), k - 1, ring.sibling))

    for k in (1, 4, 3, 2):
        for s in spreads:
            s.first(k).wait_recv()
            if k < 4 and not s.y_first:
                s.second(k).start()
            if k == 4 and s.y_first:
                for dz in (1, 3, 2):
                    s.second(dz).start()
        pass_on(k)
    for dz in (1, 3, 2):
        for s in spreads:
            s.second(dz).wait_recv()
        pass_on(4 + dz)
    for copy in forwards:
        copy.wait_recv()
    copy_here(kv, kv_out)
    for copy in copies[:7]:
        copy.wait_recv()

    def one(d, _):
        key_bias(metas_ref, d, c, bias)
        keys = kv[lax.rem(d, 2), d // 2].reshape(1024, 128)
        scores = nt(keys, qp[d])
        for h in range(4):
            s = scores[:, h * 128 : (h + 1) * 128] + bias[...]
            top = jnp.max(s, axis=0, keepdims=True)
            e = jnp.exp(s - top)
            total = jnp.sum(e, axis=0, keepdims=True)
            probs[:, h * 128 : (h + 1) * 128] = (e * (1.0 / total)).astype(BF)
            lse_ref[d, :, h * 128 : (h + 1) * 128] = jnp.broadcast_to(top + jnp.log(total), (8, 128))
        mixed = nn(keys.T, probs[...])
        for j in range(2):
            two = jnp.concatenate([mixed[64:, (2 * j) * 128 : (2 * j + 1) * 128], mixed[64:, (2 * j + 1) * 128 : (2 * j + 2) * 128]], axis=0)
            a_ref[pl.ds(pl.multiple_of(d * 128, 128), 128), pl.ds(j * 128, 128)] = two.T.astype(BF)
        return 0

    lax.fori_loop(0, 8, one, 0)

    ag.drain()
    for k in range(1, 8):
        wcopies[k].wait_send()
    for s in spreads:
        for k in range(1, 5):
            s.first(k).wait_send()
        for dz in (1, 3, 2):
            s.second(dz).wait_send()
    for copy in forwards:
        copy.wait_send()
    for i, copy in enumerate(copies):
        copy.wait_send()
        if i >= 7 and not 9 <= i < 13:
            copy.wait_recv()
    for copy in local[1:]:
        copy.wait()


def front(hidden_in, docs, g1, g2, w_query, w_key, w_value, w_gate, w_up, w_out, w_down, angles):
    dma = pltpu.SemaphoreType.DMA
    pair = lambda n: [dma((n,)), dma((n,))]
    out = lambda *shape: jax.ShapeDtypeStruct(shape, BF)
    return pl.pallas_call(
        front_kernel,
        out_shape=[
            out(1024, 256), jax.ShapeDtypeStruct((8, 8, 512), F32), jax.ShapeDtypeStruct((8, 16, 128), jnp.int32),
            out(8, 128, D), out(384, D), out(8, 512, 128), out(2, 4, 8, 128, 128), out(2, 128, D), out(2, 2, 352, D), out(704, D),
        ],
        in_specs=[VM] * 11 + [HB],
        out_specs=[VM] * 3 + [HB] * 7,
        scratch_shapes=[
            pltpu.VMEM((8, 128, D), BF), pltpu.VMEM((384, D), BF), pltpu.VMEM((8, 384, 128), BF), pltpu.VMEM((2, FF, 128), BF),
            pltpu.VMEM((1024, 384), F32), pltpu.VMEM((8, 512, 128), BF), pltpu.VMEM((2, 4, 8, 128, 128), BF),
            pltpu.VMEM((1024, 128), F32), pltpu.VMEM((1024, 512), BF),
            pltpu.VMEM((16, 128), jnp.int32), pltpu.VMEM((2, 128, 128), F32), pltpu.VMEM((6, 128, 128), F32),
            *pair(14), *pair(8), *pair(8), *pair(6), *pair(16), *pair(2), *pair(28), *pair(7), dma((9,)),
        ],
        compiler_params=params(5),
        name="front",
    )(hidden_in, docs, g1, g2, w_query, w_key, w_value, w_gate, w_up, w_out, w_down, angles)


def everyone():
    return [device for _, device in group_peers()] + [ctx_at(k)[1] for k in range(1, 8)] + [y_partners()[1]]


def tail_kernel(
    sides, qp_ref, kv_ref, lse_ref, meta_ref, da_ref, x_ref, dy1_ref, stats_ref,
    angles_hbm, wqkv_hbm, n1_hbm, ggu2_ref, gout_ref, piece_down_ref, piece_gu1_ref,
    grad_ref, info_ref, all_down, all_out, all_qkv, all_gu,
    bias, dap, ds, pb, mine, theirs, stage, back, dqkv, dqkv_t, parts, held, got, n1, wqkv, gq,
    piece_gu2, piece_out, piece_qkv, got_gu1, got_gu2, got_qkv, st1, st2, mid, angles, tab_ref,
    co_s, co_r, kv_s, kv_r, rs_s, rs_r, st_s, st_r, st2_s, st2_r, qs_s, qs_r, loc, *side_scratch,
):
    ring = Ring()
    c, _ = ctx_at(0)
    sum_gu2, sum_out, move_gu1, down, out, spread_gu1, move_gu2, sum_qkv, move_qkv, spread_gu2 = sides
    scratch = list(side_scratch)
    places = (
        (ggu2_ref, piece_gu2), (gout_ref, piece_out), (piece_gu1_ref, got_gu1), (piece_down_ref, all_down), (piece_out, all_out),
        (got_gu1, all_gu), (piece_gu2, got_gu2), (gq, piece_qkv), (piece_qkv, got_qkv), (got_gu2, all_gu),
    )
    for side, (i, o) in zip(sides, places):
        side.bind(ring, (i,), (o,), scratch[: len(side.scratch)])
        del scratch[: len(side.scratch)]
    loads = [pltpu.make_async_copy(n1_hbm, n1, loc.at[0]), pltpu.make_async_copy(wqkv_hbm, wqkv, loc.at[1])]
    angles_load = pltpu.make_async_copy(angles_hbm.at[c], angles, loc.at[3])
    for load in loads + [angles_load]:
        load.start()
    meet(everyone())
    sum_gu2.start()
    sum_out.start()
    move_gu1.start()
    group = group_peers()
    here16 = ring.x * 4 + lax.axis_index("y_lo") * 2 + ring.core
    copies = [send(stats_ref, st1.at[here16], (st_s, st_r), k, device) for k, device in group]
    st1[here16] = stats_ref[...]
    lane = lax.broadcasted_iota(jnp.int32, (128, 128), 1)
    angles_load.wait()
    fill_tables(angles, tab_ref)

    def unrope(u, i):
        return u * tab_ref[i] - pltpu.roll(u, 96, 1) * tab_ref[i + 1] - pltpu.roll(u, 32, 1) * tab_ref[i + 2]

    def one(x, core):
        d = x * 2 + core
        rows = pl.ds(pl.multiple_of(d * 128, 128), 128)
        key_bias(meta_ref, d, c, bias)
        for j in range(2):
            tile = da_ref[rows, pl.ds(j * 128, 128)].astype(F32)
            dap[pl.ds(j * 256, 128), :] = jnp.where(lane >= 64, pltpu.roll(tile, 64, 1), 0.0).astype(BF)
            dap[pl.ds(j * 256 + 128, 128), :] = jnp.where(lane >= 64, tile, 0.0).astype(BF)
        kv = kv_ref[core, x].reshape(1024, 128)
        scores = nt(kv, qp_ref[d])
        dprobs = nt(kv, dap[...])
        for h in range(4):
            cols = slice(h * 128, (h + 1) * 128)
            p = jnp.exp(scores[:, cols] + bias[...] - lse_ref[d, 0:1, cols])
            pb[:, cols] = p.astype(BF)
            dp = dprobs[:, cols]
            centre = jnp.sum(p * dp, axis=0, keepdims=True)
            ds[:, cols] = (p * (dp - centre)).astype(BF)
        dkv = nn(ds[...], qp_ref[d]) + nn(pb[...], dap[...])
        dq = nn(kv.T, ds[...]) * 0.125
        for j in range(2):
            two = jnp.concatenate([dq[:64, (2 * j) * 128 : (2 * j + 1) * 128], dq[:64, (2 * j + 1) * 128 : (2 * j + 2) * 128]], axis=0)
            dqkv[rows, pl.ds(j * 128, 128)] = unrope(two.T, 0).astype(BF)
        return dkv

    def core_copy(x):
        return pltpu.make_async_remote_copy(
            src_ref=mine.at[x], dst_ref=theirs.at[x], send_sem=co_s.at[x], recv_sem=co_r.at[x],
            device_id=ring.sibling, device_id_type=MESH,
        )

    def kv_copy(x, k):
        other, device = ctx_at(k)
        return pltpu.make_async_remote_copy(
            src_ref=stage.at[x, other], dst_ref=back.at[x, k - 1], send_sem=kv_s.at[x * 7 + k - 1],
            recv_sem=kv_r.at[x * 7 + k - 1], device_id=device, device_id_type=MESH,
        )

    def both_cores(x, _):
        mine[x] = one(x, 1 - ring.core).astype(BF).reshape(8, 128, 128)
        core_copy(x).start()
        dqkv[pl.ds(pl.multiple_of((x * 2 + 1 - ring.core) * 128, 128), 128), 256:384] = jnp.zeros((128, 128), BF)
        dkv = one(x, ring.core)
        core_copy(x).wait_recv()
        stage[x] = (dkv + theirs[x].reshape(1024, 128).astype(F32)).astype(BF).reshape(8, 128, 128)
        for k in range(1, 8):
            kv_copy(x, k).start()

        @pl.when(x == 1)
        def _():
            sum_gu2.step2()
            sum_out.step2()
            down.start()

        @pl.when(x == 2)
        def _():
            sum_gu2.step3()
            sum_out.step3()

        return 0

    lax.fori_loop(0, 4, both_cores, 0)
    sum_gu2.step4()
    sum_out.step4()
    for copy in copies:
        copy.wait_recv()
    total = st1[0]
    for i in range(1, 16):
        total += st1[i]
    mid[...] = total
    st2[c] = total
    copies2 = [send(mid, st2.at[c], (st2_s, st2_r), k - 1, ctx_at(k)[1]) for k in range(1, 8)]
    sum_gu2.finish()
    move_gu2.start()
    sum_out.finish()
    out.start()
    move_gu1.finish()
    down.middle()

    def gather_up(x, _):
        total = stage[x, c].astype(F32)
        for k in range(1, 8):
            kv_copy(x, k).wait_recv()
            total += back[x, k - 1].astype(F32)
        rows = pl.ds(pl.multiple_of((x * 2 + ring.core) * 128, 128), 128)
        dqkv[rows, 256:384] = unrope(total, 3).astype(BF)
        return 0

    lax.fori_loop(0, 4, gather_up, 0)
    spread_gu1.start()
    for load in loads:
        load.wait()

    rs = Rs(ring, parts, held, got, (rs_s, rs_r))
    for i in range(4):
        x = rs.blocks[i]

        def body(k, _, x=x):
            lanes = lanes_at(k * 512, 512)
            block = nn(dqkv[pl.ds(pl.multiple_of(x * 256, 256), 256), :], wqkv[:, lanes])
            parts[pl.ds(x * 2, 2), :, lanes] = block.astype(BF).reshape(2, 128, 512)
            return 0

        lax.fori_loop(0, 4, body, 0)
        rs.copy(i).start()
        if i == 1:
            rs.send_far()
        elif i == 2:
            rs.send_right()
        elif i == 3:
            rs.send_left()
    dqkv_t[...] = dqkv[...].T

    def grads(k, _):
        lanes = lanes_at(k * 512, 512)
        product = nn(dqkv_t[...], n1[:, :, lanes].reshape(1024, 512))
        gq[:, :, :, lanes] = product.astype(BF).reshape(2, 4, 48, 512)
        return 0

    lax.fori_loop(0, 4, grads, 0)
    sum_qkv.start()
    rs.relay()
    move_gu2.finish()
    spread_gu2.start()
    sum_qkv.step2()
    spread_gu1.middle()
    out.middle()
    sum_qkv.step3()
    for half in range(2):
        rs.ready(half)

        def body(k, _, half=half):
            rows = pl.ds(half * 64 + k * 16, 16)
            grad_ref[rows, :] = back_norm(x_ref[rows, :].astype(F32), dy1_ref[rows, :], rs.total(rows))
            return 0

        lax.fori_loop(0, 4, body, 0)
    sum_qkv.step4()
    sum_qkv.finish()
    move_qkv.start()
    spread_gu2.middle()
    move_qkv.finish()
    spread_qkv = Spread(got_qkv, lambda c: all_qkv.at[:, c], (qs_s, qs_r), 0, False, loc.at[2])
    spread_qkv.start()

    for copy in copies2:
        copy.wait_recv()
    total = st2[0]
    for i in range(1, 8):
        total += st2[i]
    sums = jnp.sum(total, axis=1, keepdims=True)
    squares, count = sums[0:1], sums[1:2]
    scale = 2.0 / (D * count)
    info_ref[...] = jnp.concatenate([squares / count, scale, jnp.zeros((6, 1), F32)], axis=0) + jnp.zeros((8, 128), F32)

    spread_qkv.relay()
    rs.drain()
    for copy in copies + copies2:
        copy.wait_send()

    def drain(x, _):
        core_copy(x).wait_send()
        for k in range(1, 8):
            kv_copy(x, k).wait_send()
        return 0

    lax.fori_loop(0, 4, drain, 0)
    down.finish()
    out.finish()
    spread_gu1.finish()
    spread_gu2.finish()
    spread_qkv.finish()


def tail(qp, kv, lse, metas, da, hidden_in, dy1, stats, angles, wqkv, n1, grad_gu2, grad_out, piece_down, piece_gu1):
    dma = pltpu.SemaphoreType.DMA
    pair = lambda n: [dma((n,)), dma((n,))]
    bf = lambda *shape: jax.ShapeDtypeStruct(shape, BF)
    vm = lambda *shape: pltpu.VMEM(shape, BF)
    sides = [
        SumColumns(grad_gu2), SumRows(grad_out), Move(piece_gu1), SpreadRows(piece_down), SpreadRows(bf(2, 128, 128)),
        SpreadGateUp(bf(8, 96, 128), 0), Move(bf(80, 1024)), SumColumns(bf(2, 4, 48, D)), Move(bf(48, 1024)),
        SpreadGateUp(bf(8, 80, 128), 96),
    ]
    return pl.pallas_call(
        functools.partial(tail_kernel, sides),
        out_shape=[
            jax.ShapeDtypeStruct((128, D), F32), jax.ShapeDtypeStruct((8, 128), F32),
            bf(352, D), bf(128, D), bf(8, 8, 48, 128), bf(2, FF, 128),
        ],
        in_specs=[VM] * 8 + [HB] * 3 + [VM] * 4,
        out_specs=[VM] * 5 + [HB],
        scratch_shapes=[
            pltpu.VMEM((1024, 128), F32), vm(512, 128), vm(1024, 512), vm(1024, 512),
            vm(4, 8, 128, 128), vm(4, 8, 128, 128), vm(4, 8, 128, 128), vm(4, 7, 128, 128),
            vm(1024, 384), vm(384, 1024), vm(8, 128, D), vm(3, 128, D), vm(7, 128, D), vm(8, 128, D), vm(384, D), vm(2, 4, 48, D),
            vm(80, 1024), vm(2, 128, 128), vm(48, 1024), vm(8, 96, 128), vm(8, 80, 128), vm(8, 48, 128),
            pltpu.VMEM((16, 8, 128), F32), pltpu.VMEM((8, 8, 128), F32), pltpu.VMEM((8, 128), F32),
            pltpu.VMEM((2, 128, 128), F32), pltpu.VMEM((6, 128, 128), F32),
            *pair(4), *pair(28), *pair(10), *pair(16), *pair(7), *pair(7), dma((4,)),
            *[s for side in sides for s in side.scratch],
        ],
        compiler_params=params(7),
        name="tail",
    )(qp, kv, lse, metas, da, hidden_in, dy1, stats, angles, wqkv, n1, grad_gu2, grad_out, piece_down, piece_gu1)


def finish_kernel(
    info_ref, gu_ref, g1_ref, g2_ref, wg_ref, wu_ref, down_ref, qkv_ref, wq_ref, wk_ref, wv_ref, out_ref, gin_ref,
    gate_ref, up_ref, down_out, q_ref, k_ref, v_ref, o_ref, input_ref, gain1_ref, gain2_ref, loss_ref,
    total2,
):
    scale = info_ref[1:2, 0:1]
    s1, s2 = column(g1_ref[...].astype(F32) * scale)[:, 0:1], column(g2_ref[...].astype(F32) * scale)[:, 0:1]
    one_matrix = eye()
    step = pl.program_id(0)

    @pl.when(step == 0)
    def _():
        total2[...] = jnp.zeros_like(total2)
        total = jnp.zeros((128, 128), F32)
        for s in range(8):
            for j in range(2):
                f = (s // 2) * 4 + j * 2 + s % 2
                part = nt(one_matrix, qkv_ref[s, j * 128 : (j + 1) * 128])
                total += part * wq_ref[:, f * 128 : (f + 1) * 128].astype(F32)
                q_ref[:, f * 128 : (f + 1) * 128] = part * s1
        for i in range(2):
            both = [qkv_ref[2 * x, 256:].astype(F32) + qkv_ref[2 * x + 1, 256:].astype(F32) for x in (2 * i, 2 * i + 1)]
            for at, w_ref, g_ref in ((0, wk_ref, k_ref), (64, wv_ref, v_ref)):
                part = jnp.concatenate([both[0][at : at + 64], both[1][at : at + 64]], axis=0).T
                total += part * w_ref[:, i * 128 : (i + 1) * 128].astype(F32)
                g_ref[:, i * 128 : (i + 1) * 128] = part * s1
        gain1_ref[...] = jnp.sum(total.T, axis=0, keepdims=True) * scale
        o_ref[...] = out_ref[...].astype(F32) * scale
        input_ref[...] = gin_ref[...] * scale
        loss_ref[...] = info_ref[0:1, 0:1]

    total = total2[...]
    for i, w_ref, g_ref in ((0, wg_ref, gate_ref), (1, wu_ref, up_ref)):
        turned = nt(one_matrix, gu_ref[i])
        g_ref[...] = turned * s2
        weighed = turned * w_ref[...].astype(F32)
        for k in range(11):
            total += weighed[:, k * 128 : (k + 1) * 128]
    total2[...] = total
    down_out[...] = down_ref[...].astype(F32) * scale

    @pl.when(step == pl.num_programs(0) - 1)
    def _():
        gain2_ref[...] = jnp.sum(total2[...].T, axis=0, keepdims=True) * scale


def finish(info, all_gu, g1, g2, w_gate, w_up, down, all_qkv, w_query, w_key, w_value, out, grad_in):
    wide = pl.BlockSpec((128, 1408), lambda i: (0, i))
    rows = pl.BlockSpec((88, D), lambda i: (i, 0))
    whole = lambda *shape: pl.BlockSpec(shape, lambda i: (0,) * len(shape))
    f32 = lambda *shape: jax.ShapeDtypeStruct(shape, F32)
    return pl.pallas_call(
        finish_kernel,
        grid=(4,),
        out_shape=[
            f32(128, FF), f32(128, FF), f32(352, D), f32(128, D), f32(128, KVD), f32(128, KVD), f32(128, D), f32(128, D),
            f32(1, 128), f32(1, 128), f32(1, 1),
        ],
        in_specs=[
            whole(8, 128), pl.BlockSpec((2, 1408, 128), lambda i: (0, i, 0)), whole(1, 128), whole(1, 128), wide, wide, rows,
            whole(8, 384, 128), whole(128, D), whole(128, KVD), whole(128, KVD), whole(128, D), whole(128, D),
        ],
        out_specs=[
            wide, wide, rows, whole(128, D), whole(128, KVD), whole(128, KVD), whole(128, D), whole(128, D),
            whole(1, 128), whole(1, 128), whole(1, 1),
        ],
        scratch_shapes=[pltpu.VMEM((128, 128), F32)],
        compiler_params=pltpu.CompilerParams(vmem_limit_bytes=63 * 2**20),
        name="finish",
    )(info, all_gu, g1, g2, w_gate, w_up, down, all_qkv, w_query, w_key, w_value, out, grad_in)


def local(hidden_in, teacher, doc_ids, valid_mask, norm1_gain, w_query, w_key, w_value, w_out, norm2_gain, w_gate, w_up, w_down):
    g1, g2, valid = norm1_gain[None], norm2_gain[None], valid_mask[None]
    angles = jnp.asarray(rope_angles())
    a, lse, metas, n1, wqkv, qp, kv, wo, wgu, wd = front(
        hidden_in, doc_ids, g1, g2, w_query, w_key, w_value, w_gate, w_up, w_out, w_down, angles
    )
    wo = wo.reshape(256, D)
    layer_out, stats, dy1, da, grad_out, grad_gu2, piece_down, piece_gu1 = middle(a, wo, hidden_in, teacher, valid, wgu, wd)
    grad_in, info, all_down, all_out, all_qkv, all_gu = tail(
        qp, kv, lse, metas, da, hidden_in, dy1, stats, angles, wqkv, n1, grad_gu2, grad_out, piece_down, piece_gu1
    )
    gg, gp, gd, gq, gk, gv, go, input_grad, gain1, gain2, loss = finish(
        info, all_gu, g1, g2, w_gate, w_up, all_down, all_qkv.reshape(8, 384, 128), w_query, w_key, w_value, all_out, grad_in
    )
    return (layer_out, loss[0, 0], input_grad, gain1[0], gq, gk, gv, go, gain2[0], gg, gp, gd)


def solution(mesh):
    fine = Mesh(mesh.devices.reshape(2, 4, 4, 2, 2), AXES)
    rows = ("y_hi", "z", "x", "y_lo", "core")
    fs = ("x", "y_lo", "core")
    token, shard = P(rows, None), P(fs, None)
    return jax.shard_map(
        local,
        mesh=fine,
        in_specs=(token, token, shard, P(rows), P(fs), shard, shard, shard, shard, P(fs), shard, shard, shard),
        out_specs=(token, P(), token, P(fs), shard, shard, shard, shard, P(fs), shard, shard, shard),
        check_vma=False,
    )
```

```python
import functools

import jax
import jax.numpy as jnp
import numpy as np
from jax import lax
from jax.experimental import pallas as pl
from jax.experimental.pallas import tpu as pltpu
from jax.sharding import Mesh, PartitionSpec as P

D = 2048
HEADS = 32
KV_HEADS = 4
HD = 64
FF = 5632
KVD = 256
EPSILON = 1e-05
THETA = 10000.0
NEGATIVE = -1e30
AXES = ("y_hi", "z", "x", "y_lo", "core")
BF = jnp.bfloat16
F32 = jnp.float32


def dot(a, b, ca, cb):
    return lax.dot_general(a, b, (((ca,), (cb,)), ((), ())), preferred_element_type=F32)


def rope_angles():
    frequency = np.float32(THETA) ** (-(np.arange(HD // 2, dtype=np.float32) * np.float32(2.0) / np.float32(HD)))
    c, t = np.arange(8)[:, None], np.arange(64)[None]
    positions = np.concatenate([c * 64 + t, (15 - c) * 64 + t], axis=1).astype(np.float32)
    angles = (positions[:, :, None] * frequency).astype(np.float32).astype(np.float64)
    angles = np.concatenate([angles] * 4, axis=2)
    return np.stack([np.cos(angles), np.sin(angles)], axis=1).astype(np.float32)


def fill_tables(angles, tab):
    cos, sin = angles[0], angles[1]
    lane = lax.broadcasted_iota(jnp.int32, (128, 128), 1)
    low = lax.rem(lane, 64) < 32
    to_low, to_high = jnp.where(low, -sin, 0.0), jnp.where(low, 0.0, sin)
    tab[0], tab[1], tab[2] = cos, to_low, to_high
    tab[3] = jnp.where(lane < 64, cos, 1.0)
    tab[4] = jnp.where(lane < 64, to_low, 0.0)
    tab[5] = jnp.where(lane < 64, to_high, 0.0)


def column(row):
    return jnp.broadcast_to(row, (128, 128)).T


MESH = pl.DeviceIdType.MESH
HALVES = (pl.ds(0, 64), pl.ds(64, 64))
VM = pl.BlockSpec(memory_space=pltpu.VMEM)
HB = pl.BlockSpec(memory_space=pl.ANY)


def params(number):
    return pltpu.CompilerParams(collective_id=number, has_side_effects=True, vmem_limit_bytes=56 * 2**20)


def send(src, dst, sems, i, device):
    copy = pltpu.make_async_remote_copy(
        src_ref=src, dst_ref=dst, send_sem=sems[0].at[i], recv_sem=sems[1].at[i], device_id=device, device_id_type=MESH
    )
    copy.start()
    return copy


def meet(devices):
    barrier = pltpu.get_barrier_semaphore()
    for device in devices:
        pl.semaphore_signal(barrier, inc=1, device_id=device, device_id_type=MESH)
    pl.semaphore_wait(barrier, len(devices))


def loading(kernel, which, n_in, n_out):
    def wrapped(*refs):
        ins, outs, scratch = list(refs[:n_in]), refs[n_in : n_in + n_out], list(refs[n_in + n_out :])
        places, sems, rest = scratch[: len(which)], scratch[len(which)], scratch[len(which) + 1 :]
        copies = []
        for k, i in enumerate(which):
            copies.append(pltpu.make_async_copy(ins[i], places[k], sems.at[k]))
            copies[-1].start()
            ins[i] = places[k]

        def arrive():
            for copy in copies:
                copy.wait()

        kernel(arrive, *ins, *outs, *rest)

    return wrapped


def places_for(inputs, which):
    return [pltpu.VMEM(inputs[i].shape, inputs[i].dtype) for i in which] + [pltpu.SemaphoreType.DMA((len(which),))]


class Ring:
    def __init__(self):
        x, core = lax.axis_index("x"), lax.axis_index("core")
        self.x, self.core = x, core
        self.right_x, self.left_x, self.far_x = lax.rem(x + 1, 4), lax.rem(x + 3, 4), lax.rem(x + 2, 4)
        self.right, self.left, self.sibling = {"x": self.right_x}, {"x": self.left_x}, {"core": 1 - core}


def norm_scale(v):
    return lax.rsqrt(jnp.mean(v * v, axis=1, keepdims=True) + EPSILON)


class Side:
    in_place = False

    def middle(self):
        pass


def lanes_at(start, size):
    return pl.ds(pl.multiple_of(start, 128), size)


def other_of_pair(i):
    return i + 1 - 2 * lax.rem(i, 2)


class Stream:
    def __init__(self, y_first, mirror, y_index, r, first, own, bufs, sems, base):
        y_hi, y_lo, z = lax.axis_index("y_hi"), lax.axis_index("y_lo"), lax.axis_index("z")
        y = y_hi * 2 + y_lo
        self.r, self.own, self.sems, self.base = r, own, sems, base
        self.b1, self.b2, self.b3, self.b4 = bufs
        axes = []
        for is_y, i in ((True, y), (False, z)) if y_first else ((False, z), (True, y)):
            p, q = (other_of_pair(i), 3 - i) if mirror == 0 else (3 - i, other_of_pair(i))
            beyond = 3 - p if mirror == 0 else other_of_pair(p)
            devices = [{"y_hi": d // 2, "y_lo": lax.rem(d, 2)} if is_y else {"z": d} for d in (p, q)]
            axes.append((i, p, q, beyond, devices))
        (self.i, p, self.q, beyond, self.dev1), (i2, p2, q2, beyond2, self.dev2) = axes
        index = (lambda v: v) if y_first else y_index
        self.at_i, self.at_p, self.at_q, self.at_beyond = index(i2), index(p2), index(q2), index(beyond2)
        self.views = [(view, (slot, *at)) for slot, d in ((1, beyond), (0, p)) for view, at in first(d)]

    def copy(self, k, src, dst, device):
        return pltpu.make_async_remote_copy(
            src_ref=src, dst_ref=dst, send_sem=self.sems[0].at[self.base + k], recv_sem=self.sems[1].at[self.base + k],
            device_id=device, device_id_type=MESH,
        )

    def copies(self, step):
        if step == 1:
            return [self.copy(k, view, self.b1.at[at], self.dev1[0]) for k, (view, at) in enumerate(self.views)]
        if step == 2:
            return [self.copy(8, self.b1.at[1], self.b2, self.dev1[1])]
        if step == 3:
            places = ((1, self.at_beyond), (0, self.at_p))
            return [self.copy(9 + slot, self.b2.at[at], self.b3.at[slot], self.dev2[0]) for slot, at in places]
        return [self.copy(11, self.b3.at[1], self.b4, self.dev2[1])]

    def go(self, step):
        for copy in self.copies(step):
            copy.start()

    def arrived(self, step):
        for copy in self.copies(step):
            copy.wait_recv()

    def add(self, out, terms, lead):
        def body(i, _):
            total = None
            for term in terms:
                v = term(i).astype(F32)
                total = v if total is None else total + v
            out(i, total.astype(BF))
            return 0

        lax.fori_loop(0, lead, body, 0)

    def step2(self):
        self.arrived(1)
        b1 = self.b1
        for slot, d in ((1, self.q), (0, self.i)):

            def put(j, v, slot=slot):
                b1[slot, j, :, :] = v

            self.add(put, [lambda j, d=d: self.own(d, j), lambda j, slot=slot: b1[slot, j, :, :]], 4)
            if slot == 1:
                self.go(2)

    def step3(self):
        self.arrived(2)
        b1, b2 = self.b1, self.b2

        def put(j, v):
            b2[j, :, :] = v

        self.add(put, [lambda j: b1[0, j, :, :], lambda j: b2[j, :, :]], 4)
        self.go(3)

    def step4(self):
        self.arrived(3)
        b2, b3 = self.b2, self.b3
        for slot, place in ((1, self.at_q), (0, self.at_i)):

            def put(j, v, slot=slot):
                b3[slot, :, :] = v

            self.add(
                put,
                [lambda j, p=place: b2[p, :, :], lambda j, slot=slot: b3[slot, :, :]],
                1,
            )
            if slot == 1:
                self.go(4)

    def finish(self, out):
        self.arrived(4)
        b3, b4 = self.b3, self.b4
        self.add(out, [lambda j: b3[0, :, :], lambda j: b4[:, :]], 1)
        for step in (1, 2, 3, 4):
            for copy in self.copies(step):
                copy.wait_send()


class TorusSum(Side):
    def start(self):
        for s in self.s:
            s.go(1)

    def step2(self):
        for s in self.s:
            s.step2()

    def step3(self):
        for s in self.s:
            s.step3()

    def step4(self):
        for s in self.s:
            s.step4()

    def finish(self):
        for s, out in zip(self.s, self.outs):
            s.finish(out)

    def bufs(self, scratch, i):
        return [ref.at[i] for ref in scratch[:4]]


class SumColumns(TorusSum):
    def __init__(self, grads):
        r = self.rows = grads.shape[2]
        dma = pltpu.SemaphoreType.DMA
        self.operands = [grads]
        self.shapes = [jax.ShapeDtypeStruct((r, 1024), BF)]
        self.scratch = [
            pltpu.VMEM((4, 2, 4, r, 256), BF), pltpu.VMEM((4, 4, r, 256), BF), pltpu.VMEM((4, 2, r, 256), BF), pltpu.VMEM((4, r, 256), BF),
            dma((48,)), dma((48,)),
        ]

    def bind(self, ring, ins, outs, scratch):
        (g,), (out,) = ins, outs
        self.s, self.outs = [], []
        for i in range(4):
            y_first, lane = i < 2, i * 256

            def first(d, y_first=y_first, lane=lane):
                if y_first:
                    return [(g.at[d // 2, :, :, lanes_at(lax.rem(d, 2) * 1024 + lane, 256)], ())]
                return [(g.at[:, d, :, pl.ds(yl * 1024 + lane, 256)], (pl.ds(yl * 2, 2),)) for yl in range(2)]

            def own(d, j, y_first=y_first, lane=lane):
                rows = slice(None)
                if y_first:
                    return g[d // 2, j, rows, lanes_at(lax.rem(d, 2) * 1024 + lane, 256)]
                return g[lax.rem(j, 2), d, rows, lanes_at((j // 2) * 1024 + lane, 256)]

            def put(j, v, lane=lane):
                out[:, pl.ds(lane, 256)] = v

            y_index = lambda y: lax.rem(y, 2) * 2 + y // 2
            self.s.append(Stream(y_first, i % 2, y_index, self.rows, first, own, self.bufs(scratch, i), scratch[4:], i * 12))
            self.outs.append(put)


class SumRows(TorusSum):
    def __init__(self, grads):
        r = self.rows = grads.shape[1]
        dma = pltpu.SemaphoreType.DMA
        self.operands = [grads]
        self.shapes = [jax.ShapeDtypeStruct((2, r, 128), BF)]
        h = r // 2
        self.scratch = [
            pltpu.VMEM((4, 2, 4, h, 128), BF), pltpu.VMEM((4, 4, h, 128), BF), pltpu.VMEM((4, 2, h, 128), BF), pltpu.VMEM((4, h, 128), BF),
            dma((48,)), dma((48,)),
        ]

    def bind(self, ring, ins, outs, scratch):
        (g,), (out,) = ins, outs
        self.s, self.outs = [], []
        h = self.rows // 2
        for i in range(4):
            y_first, lane, row = i < 2, (i // 2) * 512, (i % 2) * h

            def first(d, y_first=y_first, lane=lane, row=row):
                half = pl.ds(row, h)
                if y_first:
                    return [
                        (g.at[lax.rem(d, 2), half, lanes_at((d // 2) * 1024 + lane + z * 128, 128)], (z,)) for z in range(4)
                    ]
                return [(g.at[:, half, lanes_at(yh * 1024 + lane + d * 128, 128)], (pl.ds(yh * 2, 2),)) for yh in range(2)]

            def own(d, j, y_first=y_first, lane=lane, row=row):
                rows = pl.ds(row, h)
                if y_first:
                    return g[lax.rem(d, 2), rows, lanes_at((d // 2) * 1024 + lane + j * 128, 128)]
                return g[lax.rem(j, 2), rows, lanes_at((j // 2) * 1024 + lane + d * 128, 128)]

            def put(j, v, i=i, row=row):
                out[i // 2, pl.ds(row, h), :] = v

            self.s.append(Stream(y_first, i % 2, lambda y: y, h, first, own, self.bufs(scratch, i), scratch[4:], i * 12))
            self.outs.append(put)


class Ag:
    def __init__(self, ring, buf, sems):
        r = self.r = ring
        self.buf, self.sems = buf, sems
        self.plan = (
            (r.x, 0, r.right), (r.x, 1, r.right), (r.x, 1, r.left), (r.x, 0, r.left),
            (r.left_x, 0, r.right), (r.right_x, 1, r.left),
            (r.x, 0, r.sibling), (r.x, 1, r.sibling),
            (r.left_x, 0, r.sibling), (r.left_x, 1, r.sibling), (r.right_x, 0, r.sibling), (r.right_x, 1, r.sibling),
            (r.far_x, 0, r.sibling), (r.far_x, 1, r.sibling),
        )

    def copy(self, i):
        x, half, device = self.plan[i]
        block = self.buf.at[x * 2 + self.r.core, HALVES[half]]
        return pltpu.make_async_remote_copy(
            src_ref=block, dst_ref=block, send_sem=self.sems[0].at[i], recv_sem=self.sems[1].at[i],
            device_id=device, device_id_type=MESH,
        )

    def begin(self, half):
        for i in ((0, 3, 6), (2, 1, 7))[half]:
            self.copy(i).start()

    def near(self, steps=slice(None)):
        for got, onward in ((0, (4, 8)), (2, (5, 11)), (1, (9,)), (3, (10,)))[steps]:
            self.copy(got).wait_recv()
            for i in onward:
                self.copy(i).start()

    def far(self):
        for got, onward in ((4, 12), (5, 13)):
            self.copy(got).wait_recv()
            self.copy(onward).start()

    def have(self, *which):
        for i in which:
            self.copy(i).wait_recv()

    def drain(self):
        for i in range(14):
            self.copy(i).wait_send()


class Rs:
    def __init__(self, ring, parts, held, got, sems):
        r = self.r = ring
        self.parts, self.held, self.got, self.sems = parts, held, got, sems
        self.blocks = (r.far_x, r.right_x, r.left_x, r.x)
        self.plan = {
            4: (0, 4, 0, r.right), 5: (0, 4, 1, r.left), 6: (1, 5, 1, r.right), 7: (2, 5, 0, r.left),
            8: (1, 6, 0, r.right), 9: (2, 6, 1, r.left),
        }

    def swap(self, i, x):
        return pltpu.make_async_remote_copy(
            src_ref=self.parts.at[x * 2 + 1 - self.r.core], dst_ref=self.got.at[i], send_sem=self.sems[0].at[i],
            recv_sem=self.sems[1].at[i], device_id=self.r.sibling, device_id_type=MESH,
        )

    def copy(self, i, q=0):
        if i < 4:
            return self.swap(i, self.blocks[i])
        block, slot, half, device = self.plan[i]
        rows, sem = pl.ds(half * 64 + q * 32, 32), 4 + (i - 4) * 2 + q
        return pltpu.make_async_remote_copy(
            src_ref=self.held.at[block, rows], dst_ref=self.got.at[slot, rows], send_sem=self.sems[0].at[sem],
            recv_sem=self.sems[1].at[sem], device_id=device, device_id_type=MESH,
        )

    def pair(self, i, half, q):
        x = self.blocks[i]
        for k in range(2):
            rows = pl.ds(half * 64 + q * 32 + k * 16, 16)
            total = self.parts[x * 2 + self.r.core, rows, :].astype(F32) + self.got[i, rows, :].astype(F32)
            self.held[i, rows, :] = total.astype(BF)

    def onward(self, i, half, q):
        for k in range(2):
            rows = pl.ds(half * 64 + q * 32 + k * 16, 16)
            total = self.held[i, rows, :].astype(F32) + self.got[4, rows, :].astype(F32)
            self.held[i, rows, :] = total.astype(BF)

    def send_left(self):
        self.copy(2).wait_recv()
        for q in range(2):
            self.pair(2, 0, q)
            self.copy(7, q).start()

    def send_right(self):
        self.copy(1).wait_recv()
        for q in range(2):
            self.pair(1, 1, q)
            self.copy(6, q).start()

    def send_far(self):
        self.copy(0).wait_recv()
        for q in range(2):
            self.pair(0, 0, q)
            self.copy(4, q).start()
            self.pair(0, 1, q)
            self.copy(5, q).start()

    def relay(self):
        for q in range(2):
            self.pair(1, 0, q)
            self.pair(2, 1, q)
        for q in range(2):
            self.copy(4, q).wait_recv()
            self.onward(1, 0, q)
            self.copy(8, q).start()
            self.copy(5, q).wait_recv()
            self.onward(2, 1, q)
            self.copy(9, q).start()
        self.copy(3).wait_recv()

    def ready(self, half, q):
        for i in ((7, 8), (6, 9))[half]:
            self.copy(i, q).wait_recv()

    def total(self, rows):
        r = self.r
        return (
            self.parts[r.x * 2 + r.core, rows, :].astype(F32)
            + self.got[3, rows, :].astype(F32)
            + self.got[5, rows, :].astype(F32)
            + self.got[6, rows, :].astype(F32)
        )

    def drain(self):
        for i in range(4):
            self.copy(i).wait_send()
        for i in range(4, 10):
            for q in range(2):
                self.copy(i, q).wait_send()


def middle_kernel(
    down_side, gu_side, arrive, a_ref, wo_ref, x_ref, valid_ref, wd_ref, teacher_hbm, half_w_ref,
    out_hbm, stats_ref, dy1_hbm, da_ref, gout_ref, ggu_hbm, piece_ref, gu_piece_ref,
    out_ref, dy1_ref, ggu_ref,
    w, n2, dyg, dag, parts, held, got, y1, gate, up, mid, mid_t, dup, dgu1, dgu2, gd, gu1, dmid, valid_col, loss_col,
    rs1_s, rs1_r, ag1_s, ag1_r, rs2_s, rs2_r, ag2_s, ag2_r, rs3_s, rs3_r, ag3_s, ag3_r, w_s, w_r, loc, *side_scratch,
):
    ring = Ring()
    y_lo = lax.axis_index("y_lo")
    near, other = y_partners()
    down_side.bind(ring, (gd,), (piece_ref,), side_scratch[: len(down_side.scratch)])
    gu_side.bind(ring, (gu1,), (gu_piece_ref,), side_scratch[len(down_side.scratch) :])
    meet([ring.right, ring.left, ring.sibling, near, other] + [{"z": p} for p in (other_of_pair(lax.axis_index("z")), 3 - lax.axis_index("z"))])
    arrive()
    here = ring.x * 2 + ring.core
    dy, dgate = dy1_ref, mid
    teacher = dag.at[here]
    teacher_copy = pltpu.make_async_copy(teacher_hbm, teacher, loc.at[4])
    teacher_copy.start()
    valid_col[...] = column(valid_ref[...].astype(F32))

    wcopies = []
    for dx in range(4):
        lanes = group_lanes(lax.rem(ring.x + 4 - dx, 4), y_lo)
        src, dst = half_w_ref.at[:, :, :, lanes], w.at[:, :, :, lanes]
        wcopies.append(send(src, dst, (w_s, w_r), dx, (near, other)[dx // 2]))
        copy = pltpu.make_async_copy(src, dst, loc.at[dx])
        copy.start()
        wcopies.append(copy)

    def rows_of(x):
        return pl.ds(pl.multiple_of(x * 256, 256), 256)

    def block(buf, x):
        return buf[pl.ds(x * 2, 2)].reshape(256, D)

    def put(x, product):
        def body(k, _):
            lanes = lanes_at(k * 512, 512)
            parts[pl.ds(x * 2, 2), :, lanes] = product(lanes).astype(BF).reshape(2, 128, 512)
            return 0

        lax.fori_loop(0, 4, body, 0)

    def reduced(rs, op, ag, buf):
        for q in range(2):
            for half in range(2):
                rs.ready(half, q)

                def body(k, _, half=half, q=q):
                    rows = pl.ds(pl.multiple_of(half * 64 + q * 32 + k * 16, 16), 16)
                    buf[here, rows, :] = op(rows, rs.total(rows)).astype(BF)
                    return 0

                lax.fori_loop(0, 2, body, 0)
                if q == 1:
                    ag.begin(half)

    def over_blocks(ag, rs, work, first=None, after=()):
        def step(i, _):
            at = functools.partial(jnp.equal, i)

            @pl.when(at(0))
            def _():
                ag.have(6, 7)
                if first is not None:
                    ag.near(slice(2))
                    first()

            @pl.when(at(1))
            def _():
                ag.near(slice(2 if first is not None else 0, 4))
                ag.have(8, 9)

            @pl.when(at(2))
            def _():
                ag.have(10, 11)
                if rs is not None:
                    rs.send_left()

            @pl.when(at(3))
            def _():
                if rs is not None:
                    rs.send_right()
                ag.far()
                ag.have(12, 13)

            x = lax.rem(ring.x + jnp.where(at(1), 3, jnp.where(at(2), 1, jnp.where(at(3), 2, 0))), 4)
            work(x)
            if rs is not None:
                rs.swap(3 - i, x).start()
            for k, then in enumerate(after):
                pl.when(at(k + 1))(then)
            return 0

        lax.fori_loop(0, 4, step, 0)

    rs = Rs(ring, parts, held, got, (rs1_s, rs1_r))
    ag = Ag(ring, n2, (ag1_s, ag1_r))
    for i in range(4):
        x = rs.blocks[i]
        put(x, lambda lanes, x=x: nn(a_ref[rows_of(x), :], wo_ref[:, lanes]))
        rs.copy(i).start()
        if i == 1:
            rs.send_far()
        elif i == 2:
            rs.send_right()
        elif i == 3:
            rs.send_left()
    rs.relay()

    def op1(rows, total):
        v = x_ref[rows, :].astype(F32) + total
        y1[rows, :] = v
        return v * norm_scale(v)

    reduced(rs, op1, ag, n2)
    rs.drain()
    teacher_copy.wait()

    rs = Rs(ring, parts, held, got, (rs2_s, rs2_r))

    def forward(x):
        rows = rows_of(x)
        gate[rows, :] = nt(block(n2, x), w[0].reshape(704, D))
        up[rows, :] = nt(block(n2, x), w[1].reshape(704, D))

        def body(k, _):
            r = pl.ds(pl.multiple_of(x * 256 + k * 32, 32), 32)
            g = gate[r, :]
            mid[pl.ds(pl.multiple_of(k * 32, 32), 32), :] = (g * jax.nn.sigmoid(g) * up[r, :]).astype(BF)
            return 0

        lax.fori_loop(0, 8, body, 0)
        put(x, lambda lanes: nn(mid[...], wd_ref[:, lanes]))
        mid_t[:, rows] = mid[...].T

    def weights_here():
        for copy in wcopies:
            copy.wait()

    over_blocks(ag, rs, forward, weights_here)
    rs.send_far()
    rs.relay()
    ag.drain()

    def op2(rows, total):
        v = y1[rows, :] + total
        out_ref[rows, :] = v.astype(BF)
        miss = v - dag[here, rows, :].astype(F32)
        valid = valid_col[rows, 0:1]
        loss_col[rows, :] = jnp.broadcast_to(valid * jnp.mean(miss * miss, axis=1, keepdims=True), (16, 128))
        dy[rows, :] = valid * miss
        return valid * miss

    ag = Ag(ring, dyg, (ag2_s, ag2_r))
    reduced(rs, op2, ag, dyg)
    rs.drain()
    stats_ref[...] = jnp.concatenate([loss_col[...].T[0:1], valid_ref[...].astype(F32), jnp.zeros((6, 128), F32)], axis=0)

    rs = Rs(ring, parts, held, got, (rs3_s, rs3_r))

    def backward(x):
        rows = rows_of(x)
        dgate_mid = nt(block(dyg, x), wd_ref[...])
        dmid[...] = dgate_mid

        def body(k, _):
            r = pl.ds(pl.multiple_of(x * 256 + k * 32, 32), 32)
            q = pl.ds(pl.multiple_of(k * 32, 32), 32)
            g, dm = gate[r, :], dmid[q, :]
            sg = jax.nn.sigmoid(g)
            dgate[q, :] = (dm * up[r, :] * sg * (1.0 + g * (1.0 - sg))).astype(BF)
            dup[q, :] = (dm * (g * sg)).astype(BF)
            return 0

        lax.fori_loop(0, 8, body, 0)
        put(x, lambda lanes: nn(dgate[...], w[0, :, :, lanes].reshape(704, 512)) + nn(dup[...], w[1, :, :, lanes].reshape(704, 512)))
        for i, ref in enumerate((dgate, dup)):
            turned = ref[...].T
            for c in range(4):
                dgu1[pl.ds((4 * i + c) * 96, 96), rows] = turned[176 * c : 176 * c + 96]
                dgu2[pl.ds((4 * i + c) * 80, 80), rows] = turned[176 * c + 96 : 176 * c + 176]

    over_blocks(ag, rs, backward)
    rs.send_far()

    def grad_down(k, _):
        lanes = lanes_at(k * 512, 512)
        gd[:, :, lanes] = nn(mid_t[...], dyg[:, :, lanes].reshape(1024, 512)).astype(BF).reshape(2, 352, 512)
        return 0

    lax.fori_loop(0, 4, grad_down, 0)
    down_side.start()
    rs.relay()

    def grad_gu(rows, lhs, out, k):
        lanes = lanes_at(k * 512, 512)
        out[:, :, :, lanes] = nn(lhs[...], n2[:, :, lanes].reshape(1024, 512)).astype(BF).reshape(2, 4, rows, 512)

    def grad_gu1(k, _):
        grad_gu(96, dgu1, gu1, k)
        return 0

    lax.fori_loop(0, 4, grad_gu1, 0)
    gu_side.start()
    ag.drain()

    def op3(rows, total):
        v = back_norm(y1[rows, :], dy[rows, :], total)
        dy1_ref[rows, :] = v
        return v

    ag = Ag(ring, dag, (ag3_s, ag3_r))
    reduced(rs, op3, ag, dag)
    rs.drain()

    def to_attention(x):
        rows = rows_of(x)
        da_ref[rows, :] = nt(block(dag, x), wo_ref[...]).astype(BF)
        mid_t[0:256, rows] = a_ref[rows, :].T
        grad_gu(80, dgu2, ggu_ref, x)

    def both(name):
        def then():
            getattr(down_side, name)()
            getattr(gu_side, name)()

        return then

    over_blocks(ag, None, to_attention, after=(both("step2"), both("step3"), both("step4")))
    writes = []
    for k, (src, dst) in enumerate(((out_ref, out_hbm), (dy1_ref, dy1_hbm), (ggu_ref, ggu_hbm))):
        writes.append(pltpu.make_async_copy(src, dst, loc.at[5 + k]))
        writes[-1].start()

    def grad_out(k, _):
        lanes = lanes_at(k * 512, 512)
        gout_ref[:, :, lanes] = nn(mid_t[0:256, :], dag[:, :, lanes].reshape(1024, 512)).astype(BF).reshape(2, 128, 512)
        return 0

    lax.fori_loop(0, 4, grad_out, 0)
    ag.drain()
    down_side.finish()
    gu_side.finish()
    for copy in writes:
        copy.wait()


def middle(a, wo, x, teacher, valid, half_w, wd):
    dma = pltpu.SemaphoreType.DMA
    pair = lambda n: [dma((n,)), dma((n,))]
    big = pltpu.VMEM((8, 128, D), BF)
    sides = [SumRows(jax.ShapeDtypeStruct((2, 352, D), BF)), SumColumns(jax.ShapeDtypeStruct((2, 4, 96, D), BF))]
    inputs = (a, wo, x, valid, wd, teacher, half_w)
    which = (0, 1, 2, 4)
    return pl.pallas_call(
        loading(functools.partial(middle_kernel, *sides), which, 7, 8),
        out_shape=[
            jax.ShapeDtypeStruct((128, D), BF), jax.ShapeDtypeStruct((8, 128), F32), jax.ShapeDtypeStruct((128, D), F32),
            jax.ShapeDtypeStruct((1024, 256), BF), jax.ShapeDtypeStruct((2, 128, D), BF), jax.ShapeDtypeStruct((2, 4, 80, D), BF),
            *[s for side in sides for s in side.shapes],
        ],
        in_specs=[VM if i == 3 else HB for i in range(7)],
        out_specs=[HB, VM, HB, VM, VM, HB, VM, VM],
        scratch_shapes=[
            *places_for(inputs, which),
            pltpu.VMEM((128, D), BF), pltpu.VMEM((128, D), F32), pltpu.VMEM((2, 4, 80, D), BF),
            pltpu.VMEM((2, 2, 352, D), BF), big, big, big, big, pltpu.VMEM((3, 128, D), BF), pltpu.VMEM((7, 128, D), BF),
            pltpu.VMEM((128, D), F32),
            pltpu.VMEM((1024, 704), F32), pltpu.VMEM((1024, 704), F32),
            pltpu.VMEM((256, 704), BF), pltpu.VMEM((704, 1024), BF), pltpu.VMEM((256, 704), BF),
            pltpu.VMEM((768, 1024), BF), pltpu.VMEM((640, 1024), BF), pltpu.VMEM((2, 352, D), BF), pltpu.VMEM((2, 4, 96, D), BF),
            pltpu.VMEM((256, 704), F32), pltpu.VMEM((128, 128), F32), pltpu.VMEM((128, 128), F32),
            *pair(16), *pair(14), *pair(16), *pair(14), *pair(16), *pair(14), *pair(4), dma((8,)),
            *[s for side in sides for s in side.scratch],
        ],
        compiler_params=pltpu.CompilerParams(collective_id=1, has_side_effects=True, vmem_limit_bytes=63 * 2**20),
        name="middle",
    )(*inputs)


def piece_lanes(c, part):
    return lanes_at((c // 4) * 1024 + part * 512 + lax.rem(c, 4) * 128, 128)


def ctx_at(k):
    y_hi, z = lax.axis_index("y_hi"), lax.axis_index("z")
    y, zz = (1 - y_hi if k // 4 else y_hi), lax.rem(z + k % 4, 4)
    return y * 4 + zz, {"y_hi": y, "z": zz}


class Spread:
    def __init__(self, piece, slot, sems, base, y_first, local):
        self.piece, self.slot, self.sems, self.base, self.y_first, self.local = piece, slot, sems, base, y_first, local

    def copy(self, k, src, c, device):
        return pltpu.make_async_remote_copy(
            src_ref=src, dst_ref=self.slot(c), send_sem=self.sems[0].at[self.base + k - 1],
            recv_sem=self.sems[1].at[self.base + k - 1], device_id=device, device_id_type=MESH,
        )

    def first(self, k):
        here, _ = ctx_at(0)
        return self.copy(k, self.piece, here, ctx_at(k)[1])

    def second(self, dz):
        if self.y_first:
            c, _ = ctx_at(4)
            return self.copy(4 + dz, self.slot(c), c, ctx_at(dz)[1])
        c, _ = ctx_at(4 - dz)
        return self.copy(4 + dz, self.slot(c), c, ctx_at(4)[1])

    def own(self):
        return pltpu.make_async_copy(self.piece, self.slot(ctx_at(0)[0]), self.local)

    def start(self):
        for k in (4, 1, 3, 2) if self.y_first else (1, 3, 2, 4):
            self.first(k).start()
        if self.local is not None:
            self.own().start()

    def relay(self):
        if self.y_first:
            self.first(4).wait_recv()
            for dz in (1, 3, 2):
                self.second(dz).start()
        else:
            for dz in (1, 3, 2):
                self.first(dz).wait_recv()
                self.second(dz).start()

    def finish(self):
        if self.y_first:
            for dz in (1, 3, 2):
                self.first(dz).wait_recv()
        else:
            self.first(4).wait_recv()
        for dz in (1, 3, 2):
            self.second(dz).wait_recv()
            self.second(dz).wait_send()
        for k in (1, 2, 3, 4):
            self.first(k).wait_send()
        self.own().wait()


class SpreadRows(Side):
    def __init__(self, pieces):
        r = pieces.shape[1]
        dma = pltpu.SemaphoreType.DMA
        self.operands = [pieces]
        self.shapes = [jax.ShapeDtypeStruct((r, D), BF)]
        self.scratch = [dma((14,)), dma((14,)), dma((2,))]

    def bind(self, ring, ins, outs, scratch):
        (p,), (out,) = ins, outs
        self.peers = [ctx_at(k)[1] for k in range(1, 8)]
        self.s = [
            Spread(
                p.at[part], lambda c, part=part: out.at[:, piece_lanes(c, part)], scratch[:2], part * 7, part == 0,
                scratch[2].at[part],
            )
            for part in range(2)
        ]

    def start(self):
        for s in self.s:
            s.start()

    def middle(self):
        for s in self.s:
            s.relay()

    def finish(self):
        for s in self.s:
            s.finish()


class Move(Side):
    def __init__(self, pieces):
        dma = pltpu.SemaphoreType.DMA
        self.operands = [pieces]
        self.shapes = [jax.ShapeDtypeStruct((8, pieces.shape[0], 128), BF)]
        self.scratch = [dma((8,)), dma((8,))]

    def bind(self, ring, ins, outs, scratch):
        (self.p,), (self.out,), self.sems = ins, outs, scratch
        x, self.y_lo, core = lax.axis_index("x"), lax.axis_index("y_lo"), lax.axis_index("core")
        self.here16, self.here8 = x * 4 + self.y_lo * 2 + core, x * 2 + core
        self.peers = [device for _, device in group_peers()]

    def same(self, j):
        return self.here16 == self.y_lo * 8 + j

    def away(self, j):
        return pltpu.make_async_remote_copy(
            src_ref=self.p.at[:, pl.ds(j * 128, 128)], dst_ref=self.out.at[self.here8], send_sem=self.sems[0].at[j],
            recv_sem=self.sems[1].at[self.here8], device_id={"x": self.y_lo * 2 + j // 4, "y_lo": j // 2 % 2, "core": j % 2},
            device_id_type=MESH,
        )

    def stay(self, j):
        return pltpu.make_async_copy(self.p.at[:, pl.ds(j * 128, 128)], self.out.at[self.here8], self.sems[1].at[self.here8])

    def start(self):
        for j in range(8):

            @pl.when(self.same(j))
            def _():
                self.stay(j).start()

            @pl.when(jnp.logical_not(self.same(j)))
            def _():
                self.away(j).start()

    def arrive(self, s):
        pltpu.make_async_copy(self.out.at[s], self.out.at[s], self.sems[1].at[s]).wait()

    def drain(self):
        for j in range(8):

            @pl.when(jnp.logical_not(self.same(j)))
            def _():
                self.away(j).wait_send()

    def finish(self):
        for s in range(8):
            self.arrive(s)
        self.drain()


def group_peers():
    x, y_lo, core = lax.axis_index("x"), lax.axis_index("y_lo"), lax.axis_index("core")
    found = []
    for k in range(1, 16):
        dx, dy, dc = k // 4, k // 2 % 2, k % 2
        found.append((k, {"x": lax.rem(x + dx, 4), "y_lo": 1 - y_lo if dy else y_lo, "core": 1 - core if dc else core}))
    return found


class SpreadGateUp(Side):
    def __init__(self, pieces, first, into=None):
        self.r, self.first = pieces.shape[1], first
        dma = pltpu.SemaphoreType.DMA
        self.operands = [pieces]
        self.shapes = [jax.ShapeDtypeStruct((2, FF, 128), BF)]
        self.scratch = [dma((56,)), dma((56,)), dma((8,))]

    def bind(self, ring, ins, outs, scratch):
        (got,), (out,) = ins, outs
        self.s = []
        for s in range(8):

            def slot(c, s=s):
                rows = ((s // 2) * 4 + lax.rem(c // 2, 2) * 2 + s % 2) * 352 + lax.rem(c, 2) * 176 + self.first
                return out.at[c // 4, pl.ds(pl.multiple_of(rows, 16), self.r)]

            self.s.append(Spread(got.at[s], slot, scratch[:2], s * 7, s % 3 == 0, scratch[2].at[s]))

    def start(self):
        for s in self.s:
            s.start()

    def middle(self):
        for s in self.s:
            if s.y_first:
                s.relay()
        for s in self.s:
            if not s.y_first:
                s.relay()

    def finish(self):
        for s in self.s:
            s.finish()


def back_norm(v, grad, u):
    r = norm_scale(v)
    n = v * r
    return grad + r * (u - n * jnp.mean(u * n, axis=1, keepdims=True))


def y_partners():
    y_hi, y_lo = lax.axis_index("y_hi"), lax.axis_index("y_lo")
    return {"y_lo": 1 - y_lo}, {"y_hi": 1 - y_hi, "y_lo": 1 - y_lo}


def group_lanes(x, y_lo):
    return pl.ds(pl.multiple_of(x * 512 + y_lo * 256, 256), 256)


def tp_peers(ring):
    found = []
    for k in range(1, 8):
        dx, dc = k // 2, k % 2
        core = 1 - ring.core if dc else ring.core
        found.append((k, lax.rem(ring.x + dx, 4), core))
    return found


def ctx_peer(c, k):
    other = lax.rem(c + k, 8)
    return {"y_hi": other // 4, "z": lax.rem(other, 4)}


def nt(a, b):
    return dot(a, b, 1, 1)


def nn(a, b):
    return dot(a, b, 1, 0)


def key_bias(meta_ref, d, c, bias):
    docs = meta_ref[d].astype(F32)
    query_docs = meta_ref[d, pl.ds(c, 1), :].astype(F32)
    lane = lax.broadcasted_iota(jnp.int32, (128, 128), 1)
    row = lax.broadcasted_iota(jnp.int32, (128, 128), 0)

    def position(owner, i):
        return jnp.where(i < 64, owner * 64 + i, (15 - owner) * 64 + i - 64)

    query_pos = position(c, lane)
    for b in range(8):
        key_docs = jnp.broadcast_to(docs[b : b + 1, :], (128, 128)).T
        good = (query_pos >= position(b, row)) & (key_docs == query_docs)
        bias[pl.ds(b * 128, 128), :] = jnp.where(good, 0.0, NEGATIVE)


def eye():
    return (lax.broadcasted_iota(jnp.int32, (128, 128), 0) == lax.broadcasted_iota(jnp.int32, (128, 128), 1)).astype(BF)


def front_kernel(
    arrive, x_ref, doc_ref, g1_ref, g2_ref, wq_ref, wk_ref, wv_ref, wg_ref, wu_ref, wo_ref, wdn_ref, angles_hbm,
    a_ref, lse_ref, metas_ref, n1_out, wqkv_out, qp_out, kv_out, wos_ref, wgu_ref, wd_ref,
    n1, wqkv, w, wt, qkv, qp, kv, bias, probs, meta_ref, angles, tab_ref,
    ag_s, ag_r, meta_s, meta_r, w_s, w_r, y_s, y_r, gu_s, gu_r, wd_s, wd_r, kv_s, kv_r, fw_s, fw_r, loc,
):
    ring = Ring()
    y_lo = lax.axis_index("y_lo")
    c, _ = ctx_at(0)
    near, other = y_partners()
    peers = tp_peers(ring)
    meet([{"x": x, "core": core} for _, x, core in peers] + [near, other] + [ctx_at(k)[1] for k in range(1, 8)])
    arrive()
    here = ring.x * 2 + ring.core
    copies, local = [], []

    def copy_here(src, dst):
        copy = pltpu.make_async_copy(src, dst, loc.at[len(local)])
        copy.start()
        local.append(copy)

    ag = Ag(ring, n1, (ag_s, ag_r))

    def normed(k, _):
        rows = pl.ds(pl.multiple_of(k * 16, 16), 16)
        v = x_ref[rows, :].astype(F32)
        n1[here, rows, :] = (v * norm_scale(v)).astype(BF)
        return 0

    lax.fori_loop(0, 4, normed, 0)
    ag.begin(0)
    copy_here(angles_hbm.at[c], angles)
    row = lax.broadcasted_iota(jnp.int32, (1, 128), 1)
    tiles = [doc_ref[:, k * 128 : (k + 1) * 128] for k in range(8)]
    meta_ref[...] = jnp.zeros_like(meta_ref)
    for i in range(8):
        first, second = tiles[i // 2], tiles[(15 - i) // 2]
        if i % 2:
            first, second = pltpu.roll(first, 64, 1), pltpu.roll(second, 64, 1)
        meta_ref[i : i + 1, :] = jnp.where(row < 64, first, second)
    for k, x, core in peers:
        copies.append(send(meta_ref, metas_ref.at[here], (meta_s, meta_r), k, {"x": x, "core": core}))
    metas_ref[here] = meta_ref[...]

    one_matrix = eye()
    g1, g2 = g1_ref[...].astype(F32), g2_ref[...].astype(F32)

    def turned(ref, gain, k):
        return (nt(one_matrix, ref[:, lanes_at(k * 128, 128)]) * gain).astype(BF)

    for f in range(16):
        w[(f // 4) * 2 + f % 2, pl.ds((f // 2 % 2) * 128, 128), :] = turned(wq_ref, g1, f)
    for ref, at in ((wk_ref, 256), (wv_ref, 320)):
        for k in range(2):
            tile = turned(ref, g1, k)
            for x in (2 * k, 2 * k + 1):
                part = tile[(x % 2) * 64 : (x % 2) * 64 + 64]
                w[2 * x, pl.ds(at, 64), :] = part
                w[2 * x + 1, pl.ds(at, 64), :] = part
    lanes = lanes_at((ring.x * 4 + y_lo * 2 + ring.core) * 128, 128)
    wcopies = {}
    for k, x, core in peers:
        wcopies[k] = send(w.at[x * 2 + core], wqkv.at[:, lanes], (w_s, w_r), k, {"x": x, "core": core})
    wqkv[:, lanes] = w[here]
    lax.fori_loop(4, 8, normed, 0)
    ag.begin(1)

    copy_here(wo_ref, wos_ref.at[y_lo])
    copy_here(wdn_ref, wd_ref.at[pl.ds(pl.multiple_of(y_lo * 352, 32), 352)])
    for half, device in enumerate((near, other)):
        copies.append(send(wo_ref.at[HALVES[half]], wos_ref.at[y_lo, HALVES[half]], (y_s, y_r), 4 + half, device))

    def turn_all(ref, i):
        def body(k, _):
            wt[i, pl.ds(pl.multiple_of(k * 128, 128), 128), :] = turned(ref, g2, k)
            return 0

        lax.fori_loop(0, FF // 128, body, 0)

    turn_all(wg_ref, 0)
    for dx in range(4):
        x = lax.rem(ring.x + 4 - dx, 4)
        if dx > 0:
            wcopies[2 * dx].wait_recv()
        wcopies[2 * dx + 1].wait_recv()
        block = wqkv.at[:, group_lanes(x, y_lo)]
        copies.append(send(block, block, (y_s, y_r), dx, (near, other)[dx // 2]))
    for half, device in enumerate((near, other)):
        rows = pl.ds(pl.multiple_of(y_lo * 352 + half * 176, 16), 176)
        copies.append(send(wdn_ref.at[pl.ds(half * 176, 176)], wd_ref.at[rows], (wd_s, wd_r), half, device))
    ag.near()
    turn_all(wu_ref, 1)
    ag.far()

    for j in range(2):
        rows = pl.ds(pl.multiple_of((ring.x * 4 + 2 * j + ring.core) * 352, 32), 352)
        copy_here(wt.at[:, rows], wgu_ref.at[:, j, :, lanes])
    for k, x, core in peers:
        for j in range(2):
            rows = pl.ds(pl.multiple_of((x * 4 + 2 * j + core) * 352, 32), 352)
            copies.append(
                send(wt.at[:, rows], wgu_ref.at[:, j, :, lanes], (gu_s, gu_r), k * 2 + j, {"x": x, "core": core})
            )

    local[0].wait()
    fill_tables(angles, tab_ref)
    ag.have(*range(6, 14))
    for copy in copies[9:13]:
        copy.wait_recv()
    qkv[...] = nt(n1[...].reshape(1024, D), wqkv[...])
    copy_here(n1, n1_out)
    copy_here(wqkv, wqkv_out)

    lane = lax.broadcasted_iota(jnp.int32, (128, 128), 1)

    def rope(u, i):
        return u * tab_ref[i] + pltpu.roll(u, 96, 1) * tab_ref[i + 1] + pltpu.roll(u, 32, 1) * tab_ref[i + 2]

    for d in range(8):
        kv[d % 2, d // 2, c] = rope(qkv[pl.ds(d * 128, 128), 256:384], 3).astype(BF)
    spreads = [
        Spread(kv.at[ring.core, x, c], lambda i, x=x: kv.at[ring.core, x, i], (kv_s, kv_r), x * 7, x < 2, None) for x in range(4)
    ]
    for s in spreads:
        s.start()

    def turn_queries(d, _):
        for j in range(2):
            u = rope(qkv[pl.ds(pl.multiple_of(d * 128, 128), 128), pl.ds(j * 128, 128)], 0) * 0.125
            qp[d, pl.ds(j * 256, 128), :] = jnp.where(lane < 64, u, 0.0).astype(BF)
            qp[d, pl.ds(j * 256 + 128, 128), :] = jnp.where(lane < 64, pltpu.roll(u, 64, 1), 0.0).astype(BF)
        return 0

    lax.fori_loop(0, 8, turn_queries, 0)
    copy_here(qp, qp_out)

    forwards = []

    def pass_on(k):
        back = ctx_at(k if k == 4 else k // 4 * 4 + (4 - k % 4))[0]
        block = kv.at[ring.core, :, back]
        forwards.append(send(block, block, (fw_s, fw_r), k - 1, ring.sibling))

    for k in (1, 4, 3, 2):
        for s in spreads:
            s.first(k).wait_recv()
            if k < 4 and not s.y_first:
                s.second(k).start()
            if k == 4 and s.y_first:
                for dz in (1, 3, 2):
                    s.second(dz).start()
        pass_on(k)
    for dz in (1, 3, 2):
        for s in spreads:
            s.second(dz).wait_recv()
        pass_on(4 + dz)
    for copy in forwards:
        copy.wait_recv()
    copy_here(kv, kv_out)
    for copy in copies[:7]:
        copy.wait_recv()

    def one(d, _):
        key_bias(metas_ref, d, c, bias)
        keys = kv[lax.rem(d, 2), d // 2].reshape(1024, 128)
        scores = nt(keys, qp[d])
        for h in range(4):
            s = scores[:, h * 128 : (h + 1) * 128] + bias[...]
            top = jnp.max(s, axis=0, keepdims=True)
            e = jnp.exp(s - top)
            total = jnp.sum(e, axis=0, keepdims=True)
            probs[:, h * 128 : (h + 1) * 128] = (e * (1.0 / total)).astype(BF)
            lse_ref[d, :, h * 128 : (h + 1) * 128] = jnp.broadcast_to(top + jnp.log(total), (8, 128))
        mixed = nn(keys.T, probs[...])
        for j in range(2):
            two = jnp.concatenate([mixed[64:, (2 * j) * 128 : (2 * j + 1) * 128], mixed[64:, (2 * j + 1) * 128 : (2 * j + 2) * 128]], axis=0)
            a_ref[pl.ds(pl.multiple_of(d * 128, 128), 128), pl.ds(j * 128, 128)] = two.T.astype(BF)
        return 0

    lax.fori_loop(0, 8, one, 0)

    ag.drain()
    for k in range(1, 8):
        wcopies[k].wait_send()
    for s in spreads:
        for k in range(1, 5):
            s.first(k).wait_send()
        for dz in (1, 3, 2):
            s.second(dz).wait_send()
    for copy in forwards:
        copy.wait_send()
    for i, copy in enumerate(copies):
        copy.wait_send()
        if i >= 7 and not 9 <= i < 13:
            copy.wait_recv()
    for copy in local[1:]:
        copy.wait()


def front(hidden_in, docs, g1, g2, w_query, w_key, w_value, w_gate, w_up, w_out, w_down, angles):
    dma = pltpu.SemaphoreType.DMA
    pair = lambda n: [dma((n,)), dma((n,))]
    out = lambda *shape: jax.ShapeDtypeStruct(shape, BF)
    inputs = (hidden_in, docs, g1, g2, w_query, w_key, w_value, w_gate, w_up, w_out, w_down, angles)
    which = (0, 4, 5, 6, 7, 8, 9, 10)
    return pl.pallas_call(
        loading(front_kernel, which, 12, 10),
        out_shape=[
            out(1024, 256), jax.ShapeDtypeStruct((8, 8, 512), F32), jax.ShapeDtypeStruct((8, 16, 128), jnp.int32),
            out(8, 128, D), out(384, D), out(8, 512, 128), out(2, 4, 8, 128, 128), out(2, 128, D), out(2, 2, 352, D), out(704, D),
        ],
        in_specs=[HB if i in which or i == 11 else VM for i in range(12)],
        out_specs=[VM] * 3 + [HB] * 7,
        scratch_shapes=[
            *places_for(inputs, which),
            pltpu.VMEM((8, 128, D), BF), pltpu.VMEM((384, D), BF), pltpu.VMEM((8, 384, 128), BF), pltpu.VMEM((2, FF, 128), BF),
            pltpu.VMEM((1024, 384), F32), pltpu.VMEM((8, 512, 128), BF), pltpu.VMEM((2, 4, 8, 128, 128), BF),
            pltpu.VMEM((1024, 128), F32), pltpu.VMEM((1024, 512), BF),
            pltpu.VMEM((16, 128), jnp.int32), pltpu.VMEM((2, 128, 128), F32), pltpu.VMEM((6, 128, 128), F32),
            *pair(14), *pair(8), *pair(8), *pair(6), *pair(16), *pair(2), *pair(28), *pair(7), dma((9,)),
        ],
        compiler_params=params(5),
        name="front",
    )(*inputs)


def everyone():
    return [device for _, device in group_peers()] + [ctx_at(k)[1] for k in range(1, 8)] + [y_partners()[1]]


def tail_kernel(
    sides, arrive, qp_ref, kv_ref, lse_ref, meta_ref, da_ref, x_ref, dy1_ref, stats_ref,
    angles_hbm, wqkv_hbm, n1_hbm, ggu2_ref, gout_ref, piece_down_ref, piece_gu1_ref,
    grad_ref, info_ref, all_down, all_out, all_qkv, all_gu,
    bias, dap, ds, pb, mine, theirs, stage, back, dqkv, dqkv_t, parts, held, got, n1, wqkv, gq,
    piece_gu2, piece_out, piece_qkv, got_gu1, got_gu2, got_qkv, st1, st2, mid, angles, tab_ref,
    co_s, co_r, kv_s, kv_r, rs_s, rs_r, st_s, st_r, st2_s, st2_r, qs_s, qs_r, loc, *side_scratch,
):
    ring = Ring()
    c, _ = ctx_at(0)
    sum_gu2, sum_out, move_gu1, down, out, spread_gu1, move_gu2, sum_qkv, move_qkv, spread_gu2 = sides
    scratch = list(side_scratch)
    places = (
        (ggu2_ref, piece_gu2), (gout_ref, piece_out), (piece_gu1_ref, got_gu1), (piece_down_ref, all_down), (piece_out, all_out),
        (got_gu1, all_gu), (piece_gu2, got_gu2), (gq, piece_qkv), (piece_qkv, got_qkv), (got_gu2, all_gu),
    )
    for side, (i, o) in zip(sides, places):
        side.bind(ring, (i,), (o,), scratch[: len(side.scratch)])
        del scratch[: len(side.scratch)]
    loads = [pltpu.make_async_copy(n1_hbm, n1, loc.at[0]), pltpu.make_async_copy(wqkv_hbm, wqkv, loc.at[1])]
    angles_load = pltpu.make_async_copy(angles_hbm.at[c], angles, loc.at[3])
    for load in loads + [angles_load]:
        load.start()
    meet(everyone())
    arrive()
    sum_gu2.start()
    sum_out.start()
    move_gu1.start()
    group = group_peers()
    here16 = ring.x * 4 + lax.axis_index("y_lo") * 2 + ring.core
    copies = [send(stats_ref, st1.at[here16], (st_s, st_r), k, device) for k, device in group]
    st1[here16] = stats_ref[...]
    lane = lax.broadcasted_iota(jnp.int32, (128, 128), 1)
    angles_load.wait()
    fill_tables(angles, tab_ref)

    def unrope(u, i):
        return u * tab_ref[i] - pltpu.roll(u, 96, 1) * tab_ref[i + 1] - pltpu.roll(u, 32, 1) * tab_ref[i + 2]

    def one(x, core):
        d = x * 2 + core
        rows = pl.ds(pl.multiple_of(d * 128, 128), 128)
        key_bias(meta_ref, d, c, bias)
        for j in range(2):
            tile = da_ref[rows, pl.ds(j * 128, 128)].astype(F32)
            dap[pl.ds(j * 256, 128), :] = jnp.where(lane >= 64, pltpu.roll(tile, 64, 1), 0.0).astype(BF)
            dap[pl.ds(j * 256 + 128, 128), :] = jnp.where(lane >= 64, tile, 0.0).astype(BF)
        kv = kv_ref[core, x].reshape(1024, 128)
        scores = nt(kv, qp_ref[d])
        dprobs = nt(kv, dap[...])
        for h in range(4):
            cols = slice(h * 128, (h + 1) * 128)
            p = jnp.exp(scores[:, cols] + bias[...] - lse_ref[d, 0:1, cols])
            pb[:, cols] = p.astype(BF)
            dp = dprobs[:, cols]
            centre = jnp.sum(p * dp, axis=0, keepdims=True)
            ds[:, cols] = (p * (dp - centre)).astype(BF)
        dkv = nn(ds[...], qp_ref[d]) + nn(pb[...], dap[...])
        dq = nn(kv.T, ds[...]) * 0.125
        for j in range(2):
            two = jnp.concatenate([dq[:64, (2 * j) * 128 : (2 * j + 1) * 128], dq[:64, (2 * j + 1) * 128 : (2 * j + 2) * 128]], axis=0)
            dqkv[rows, pl.ds(j * 128, 128)] = unrope(two.T, 0).astype(BF)
        return dkv

    def core_copy(x):
        return pltpu.make_async_remote_copy(
            src_ref=mine.at[x], dst_ref=theirs.at[x], send_sem=co_s.at[x], recv_sem=co_r.at[x],
            device_id=ring.sibling, device_id_type=MESH,
        )

    def kv_copy(x, k):
        other, device = ctx_at(k)
        return pltpu.make_async_remote_copy(
            src_ref=stage.at[x, other], dst_ref=back.at[x, k - 1], send_sem=kv_s.at[x * 7 + k - 1],
            recv_sem=kv_r.at[x * 7 + k - 1], device_id=device, device_id_type=MESH,
        )

    def both_cores(x, _):
        mine[x] = one(x, 1 - ring.core).astype(BF).reshape(8, 128, 128)
        core_copy(x).start()
        dqkv[pl.ds(pl.multiple_of((x * 2 + 1 - ring.core) * 128, 128), 128), 256:384] = jnp.zeros((128, 128), BF)
        dkv = one(x, ring.core)
        core_copy(x).wait_recv()
        stage[x] = (dkv + theirs[x].reshape(1024, 128).astype(F32)).astype(BF).reshape(8, 128, 128)
        for k in range(1, 8):
            kv_copy(x, k).start()

        @pl.when(x == 1)
        def _():
            sum_gu2.step2()
            sum_out.step2()
            down.start()

        @pl.when(x == 2)
        def _():
            sum_gu2.step3()
            sum_out.step3()

        return 0

    lax.fori_loop(0, 4, both_cores, 0)
    sum_gu2.step4()
    sum_out.step4()
    for copy in copies:
        copy.wait_recv()
    total = st1[0]
    for i in range(1, 16):
        total += st1[i]
    mid[...] = total
    st2[c] = total
    copies2 = [send(mid, st2.at[c], (st2_s, st2_r), k - 1, ctx_at(k)[1]) for k in range(1, 8)]
    sum_gu2.finish()
    move_gu2.start()
    sum_out.finish()
    out.start()
    move_gu1.finish()
    down.middle()

    def gather_up(x, _):
        total = stage[x, c].astype(F32)
        for k in range(1, 8):
            kv_copy(x, k).wait_recv()
            total += back[x, k - 1].astype(F32)
        rows = pl.ds(pl.multiple_of((x * 2 + ring.core) * 128, 128), 128)
        dqkv[rows, 256:384] = unrope(total, 3).astype(BF)
        return 0

    lax.fori_loop(0, 4, gather_up, 0)
    spread_gu1.start()
    for load in loads:
        load.wait()

    rs = Rs(ring, parts, held, got, (rs_s, rs_r))
    for i in range(4):
        x = rs.blocks[i]

        def body(k, _, x=x):
            lanes = lanes_at(k * 512, 512)
            block = nn(dqkv[pl.ds(pl.multiple_of(x * 256, 256), 256), :], wqkv[:, lanes])
            parts[pl.ds(x * 2, 2), :, lanes] = block.astype(BF).reshape(2, 128, 512)
            return 0

        lax.fori_loop(0, 4, body, 0)
        rs.copy(i).start()
        if i == 1:
            rs.send_far()
        elif i == 2:
            rs.send_right()
        elif i == 3:
            rs.send_left()
    dqkv_t[...] = dqkv[...].T

    def grads(k, _):
        lanes = lanes_at(k * 512, 512)
        product = nn(dqkv_t[...], n1[:, :, lanes].reshape(1024, 512))
        gq[:, :, :, lanes] = product.astype(BF).reshape(2, 4, 48, 512)
        return 0

    lax.fori_loop(0, 4, grads, 0)
    sum_qkv.start()
    rs.relay()
    move_gu2.finish()
    spread_gu2.start()
    sum_qkv.step2()
    spread_gu1.middle()
    out.middle()
    sum_qkv.step3()
    for q in range(2):
        for half in range(2):
            rs.ready(half, q)

            def body(k, _, half=half, q=q):
                rows = pl.ds(pl.multiple_of(half * 64 + q * 32 + k * 16, 16), 16)
                grad_ref[rows, :] = back_norm(x_ref[rows, :].astype(F32), dy1_ref[rows, :], rs.total(rows))
                return 0

            lax.fori_loop(0, 2, body, 0)
    sum_qkv.step4()
    sum_qkv.finish()
    move_qkv.start()
    spread_gu2.middle()
    move_qkv.finish()
    spread_qkv = Spread(got_qkv, lambda c: all_qkv.at[:, c], (qs_s, qs_r), 0, False, loc.at[2])
    spread_qkv.start()

    for copy in copies2:
        copy.wait_recv()
    total = st2[0]
    for i in range(1, 8):
        total += st2[i]
    sums = jnp.sum(total, axis=1, keepdims=True)
    squares, count = sums[0:1], sums[1:2]
    scale = 2.0 / (D * count)
    info_ref[...] = jnp.concatenate([squares / count, scale, jnp.zeros((6, 1), F32)], axis=0) + jnp.zeros((8, 128), F32)

    spread_qkv.relay()
    rs.drain()
    for copy in copies + copies2:
        copy.wait_send()

    def drain(x, _):
        core_copy(x).wait_send()
        for k in range(1, 8):
            kv_copy(x, k).wait_send()
        return 0

    lax.fori_loop(0, 4, drain, 0)
    down.finish()
    out.finish()
    spread_gu1.finish()
    spread_gu2.finish()
    spread_qkv.finish()


def tail(qp, kv, lse, metas, da, hidden_in, dy1, stats, angles, wqkv, n1, grad_gu2, grad_out, piece_down, piece_gu1):
    dma = pltpu.SemaphoreType.DMA
    pair = lambda n: [dma((n,)), dma((n,))]
    bf = lambda *shape: jax.ShapeDtypeStruct(shape, BF)
    vm = lambda *shape: pltpu.VMEM(shape, BF)
    sides = [
        SumColumns(grad_gu2), SumRows(grad_out), Move(piece_gu1), SpreadRows(piece_down), SpreadRows(bf(2, 128, 128)),
        SpreadGateUp(bf(8, 96, 128), 0), Move(bf(80, 1024)), SumColumns(bf(2, 4, 48, D)), Move(bf(48, 1024)),
        SpreadGateUp(bf(8, 80, 128), 96),
    ]
    inputs = (qp, kv, lse, metas, da, hidden_in, dy1, stats, angles, wqkv, n1, grad_gu2, grad_out, piece_down, piece_gu1)
    which = (0, 1, 2, 4, 5, 6, 11, 12, 13, 14)
    return pl.pallas_call(
        loading(functools.partial(tail_kernel, sides), which, 15, 6),
        out_shape=[
            jax.ShapeDtypeStruct((128, D), F32), jax.ShapeDtypeStruct((8, 128), F32),
            bf(352, D), bf(128, D), bf(8, 8, 48, 128), bf(2, FF, 128),
        ],
        in_specs=[HB if i in which or 8 <= i < 11 else VM for i in range(15)],
        out_specs=[VM] * 5 + [HB],
        scratch_shapes=[
            *places_for(inputs, which),
            pltpu.VMEM((1024, 128), F32), vm(512, 128), vm(1024, 512), vm(1024, 512),
            vm(4, 8, 128, 128), vm(4, 8, 128, 128), vm(4, 8, 128, 128), vm(4, 7, 128, 128),
            vm(1024, 384), vm(384, 1024), vm(8, 128, D), vm(3, 128, D), vm(7, 128, D), vm(8, 128, D), vm(384, D), vm(2, 4, 48, D),
            vm(80, 1024), vm(2, 128, 128), vm(48, 1024), vm(8, 96, 128), vm(8, 80, 128), vm(8, 48, 128),
            pltpu.VMEM((16, 8, 128), F32), pltpu.VMEM((8, 8, 128), F32), pltpu.VMEM((8, 128), F32),
            pltpu.VMEM((2, 128, 128), F32), pltpu.VMEM((6, 128, 128), F32),
            *pair(4), *pair(28), *pair(16), *pair(16), *pair(7), *pair(7), dma((4,)),
            *[s for side in sides for s in side.scratch],
        ],
        compiler_params=params(7),
        name="tail",
    )(*inputs)


def finish_kernel(
    info_ref, gu_ref, g1_ref, g2_ref, wg_ref, wu_ref, down_ref, qkv_ref, wq_ref, wk_ref, wv_ref, out_ref, gin_ref,
    gate_ref, up_ref, down_out, q_ref, k_ref, v_ref, o_ref, input_ref, gain1_ref, gain2_ref, loss_ref,
    total2,
):
    scale = info_ref[1:2, 0:1]
    s1, s2 = column(g1_ref[...].astype(F32) * scale)[:, 0:1], column(g2_ref[...].astype(F32) * scale)[:, 0:1]
    one_matrix = eye()
    step = pl.program_id(0)

    @pl.when(step == 0)
    def _():
        total2[...] = jnp.zeros_like(total2)
        total = jnp.zeros((128, 128), F32)
        for s in range(8):
            for j in range(2):
                f = (s // 2) * 4 + j * 2 + s % 2
                part = nt(one_matrix, qkv_ref[s, j * 128 : (j + 1) * 128])
                total += part * wq_ref[:, f * 128 : (f + 1) * 128].astype(F32)
                q_ref[:, f * 128 : (f + 1) * 128] = part * s1
        for i in range(2):
            both = [qkv_ref[2 * x, 256:].astype(F32) + qkv_ref[2 * x + 1, 256:].astype(F32) for x in (2 * i, 2 * i + 1)]
            for at, w_ref, g_ref in ((0, wk_ref, k_ref), (64, wv_ref, v_ref)):
                part = jnp.concatenate([both[0][at : at + 64], both[1][at : at + 64]], axis=0).T
                total += part * w_ref[:, i * 128 : (i + 1) * 128].astype(F32)
                g_ref[:, i * 128 : (i + 1) * 128] = part * s1
        gain1_ref[...] = jnp.sum(total.T, axis=0, keepdims=True) * scale
        o_ref[...] = out_ref[...].astype(F32) * scale
        input_ref[...] = gin_ref[...] * scale
        loss_ref[...] = info_ref[0:1, 0:1]

    total = total2[...]
    for i, w_ref, g_ref in ((0, wg_ref, gate_ref), (1, wu_ref, up_ref)):
        turned = nt(one_matrix, gu_ref[i])
        g_ref[...] = turned * s2
        weighed = turned * w_ref[...].astype(F32)
        for k in range(11):
            total += weighed[:, k * 128 : (k + 1) * 128]
    total2[...] = total
    down_out[...] = down_ref[...].astype(F32) * scale

    @pl.when(step == pl.num_programs(0) - 1)
    def _():
        gain2_ref[...] = jnp.sum(total2[...].T, axis=0, keepdims=True) * scale


def finish(info, all_gu, g1, g2, w_gate, w_up, down, all_qkv, w_query, w_key, w_value, out, grad_in):
    wide = pl.BlockSpec((128, 1408), lambda i: (0, i))
    rows = pl.BlockSpec((88, D), lambda i: (i, 0))
    whole = lambda *shape: pl.BlockSpec(shape, lambda i: (0,) * len(shape))
    f32 = lambda *shape: jax.ShapeDtypeStruct(shape, F32)
    return pl.pallas_call(
        finish_kernel,
        grid=(4,),
        out_shape=[
            f32(128, FF), f32(128, FF), f32(352, D), f32(128, D), f32(128, KVD), f32(128, KVD), f32(128, D), f32(128, D),
            f32(1, 128), f32(1, 128), f32(1, 1),
        ],
        in_specs=[
            whole(8, 128), pl.BlockSpec((2, 1408, 128), lambda i: (0, i, 0)), whole(1, 128), whole(1, 128), wide, wide, rows,
            whole(8, 384, 128), whole(128, D), whole(128, KVD), whole(128, KVD), whole(128, D), whole(128, D),
        ],
        out_specs=[
            wide, wide, rows, whole(128, D), whole(128, KVD), whole(128, KVD), whole(128, D), whole(128, D),
            whole(1, 128), whole(1, 128), whole(1, 1),
        ],
        scratch_shapes=[pltpu.VMEM((128, 128), F32)],
        compiler_params=pltpu.CompilerParams(vmem_limit_bytes=63 * 2**20),
        name="finish",
    )(info, all_gu, g1, g2, w_gate, w_up, down, all_qkv, w_query, w_key, w_value, out, grad_in)


def local(hidden_in, teacher, doc_ids, valid_mask, norm1_gain, w_query, w_key, w_value, w_out, norm2_gain, w_gate, w_up, w_down):
    g1, g2, valid = norm1_gain[None], norm2_gain[None], valid_mask[None]
    angles = jnp.asarray(rope_angles())
    a, lse, metas, n1, wqkv, qp, kv, wo, wgu, wd = front(
        hidden_in, doc_ids, g1, g2, w_query, w_key, w_value, w_gate, w_up, w_out, w_down, angles
    )
    wo = wo.reshape(256, D)
    layer_out, stats, dy1, da, grad_out, grad_gu2, piece_down, piece_gu1 = middle(a, wo, hidden_in, teacher, valid, wgu, wd)
    grad_in, info, all_down, all_out, all_qkv, all_gu = tail(
        qp, kv, lse, metas, da, hidden_in, dy1, stats, angles, wqkv, n1, grad_gu2, grad_out, piece_down, piece_gu1
    )
    gg, gp, gd, gq, gk, gv, go, input_grad, gain1, gain2, loss = finish(
        info, all_gu, g1, g2, w_gate, w_up, all_down, all_qkv.reshape(8, 384, 128), w_query, w_key, w_value, all_out, grad_in
    )
    return (layer_out, loss[0, 0], input_grad, gain1[0], gq, gk, gv, go, gain2[0], gg, gp, gd)


def solution(mesh):
    fine = Mesh(mesh.devices.reshape(2, 4, 4, 2, 2), AXES)
    rows = ("y_hi", "z", "x", "y_lo", "core")
    fs = ("x", "y_lo", "core")
    token, shard = P(rows, None), P(fs, None)
    return jax.shard_map(
        local,
        mesh=fine,
        in_specs=(token, token, shard, P(rows), P(fs), shard, shard, shard, shard, P(fs), shard, shard, shard),
        out_specs=(token, P(), token, P(fs), shard, shard, shard, shard, P(fs), shard, shard, shard),
        check_vma=False,
    )
```

```python
import functools

import jax
import jax.numpy as jnp
import numpy as np
from jax import lax
from jax.experimental import pallas as pl
from jax.experimental.pallas import tpu as pltpu
from jax.sharding import Mesh, PartitionSpec as P

D = 2048
HEADS = 32
KV_HEADS = 4
HD = 64
FF = 5632
KVD = 256
EPSILON = 1e-05
THETA = 10000.0
NEGATIVE = -1e30
R1, R2 = 112, 64
AXES = ("y_hi", "z", "x", "y_lo", "core")
BF = jnp.bfloat16
F32 = jnp.float32


def dot(a, b, ca, cb):
    return lax.dot_general(a, b, (((ca,), (cb,)), ((), ())), preferred_element_type=F32)


def rope_angles():
    frequency = np.float32(THETA) ** (-(np.arange(HD // 2, dtype=np.float32) * np.float32(2.0) / np.float32(HD)))
    c, t = np.arange(8)[:, None], np.arange(64)[None]
    positions = np.concatenate([c * 64 + t, (15 - c) * 64 + t], axis=1).astype(np.float32)
    angles = (positions[:, :, None] * frequency).astype(np.float32).astype(np.float64)
    angles = np.concatenate([angles] * 4, axis=2)
    return np.stack([np.cos(angles), np.sin(angles)], axis=1).astype(np.float32)


def fill_tables(angles, tab):
    cos, sin = angles[0], angles[1]
    lane = lax.broadcasted_iota(jnp.int32, (128, 128), 1)
    low = lax.rem(lane, 64) < 32
    to_low, to_high = jnp.where(low, -sin, 0.0), jnp.where(low, 0.0, sin)
    tab[0], tab[1], tab[2] = cos, to_low, to_high
    tab[3] = jnp.where(lane < 64, cos, 1.0)
    tab[4] = jnp.where(lane < 64, to_low, 0.0)
    tab[5] = jnp.where(lane < 64, to_high, 0.0)


def column(row):
    return jnp.broadcast_to(row, (128, 128)).T


MESH = pl.DeviceIdType.MESH
HALVES = (pl.ds(0, 64), pl.ds(64, 64))
VM = pl.BlockSpec(memory_space=pltpu.VMEM)
HB = pl.BlockSpec(memory_space=pl.ANY)


def params(number):
    return pltpu.CompilerParams(collective_id=number, has_side_effects=True, vmem_limit_bytes=56 * 2**20)


def send(src, dst, sems, i, device):
    copy = pltpu.make_async_remote_copy(
        src_ref=src, dst_ref=dst, send_sem=sems[0].at[i], recv_sem=sems[1].at[i], device_id=device, device_id_type=MESH
    )
    copy.start()
    return copy


def meet(devices):
    barrier = pltpu.get_barrier_semaphore()
    for device in devices:
        pl.semaphore_signal(barrier, inc=1, device_id=device, device_id_type=MESH)
    pl.semaphore_wait(barrier, len(devices))


def loading(kernel, which, n_in, n_out):
    def wrapped(*refs):
        ins, outs, scratch = list(refs[:n_in]), refs[n_in : n_in + n_out], list(refs[n_in + n_out :])
        places, sems, rest = scratch[: len(which)], scratch[len(which)], scratch[len(which) + 1 :]
        copies = []
        for k, i in enumerate(which):
            copies.append(pltpu.make_async_copy(ins[i], places[k], sems.at[k]))
            copies[-1].start()
            ins[i] = places[k]

        def arrive():
            for copy in copies:
                copy.wait()

        kernel(arrive, *ins, *outs, *rest)

    return wrapped


def places_for(inputs, which):
    return [pltpu.VMEM(inputs[i].shape, inputs[i].dtype) for i in which] + [pltpu.SemaphoreType.DMA((len(which),))]


class Ring:
    def __init__(self):
        x, core = lax.axis_index("x"), lax.axis_index("core")
        self.x, self.core = x, core
        self.right_x, self.left_x, self.far_x = lax.rem(x + 1, 4), lax.rem(x + 3, 4), lax.rem(x + 2, 4)
        self.right, self.left, self.sibling = {"x": self.right_x}, {"x": self.left_x}, {"core": 1 - core}


def norm_scale(v):
    return lax.rsqrt(jnp.mean(v * v, axis=1, keepdims=True) + EPSILON)


class Side:
    in_place = False

    def middle(self):
        pass


def lanes_at(start, size):
    return pl.ds(pl.multiple_of(start, 128), size)


def other_of_pair(i):
    return i + 1 - 2 * lax.rem(i, 2)


class Stream:
    def __init__(self, y_first, mirror, y_index, r, first, own, bufs, sems, base):
        y_hi, y_lo, z = lax.axis_index("y_hi"), lax.axis_index("y_lo"), lax.axis_index("z")
        y = y_hi * 2 + y_lo
        self.r, self.own, self.sems, self.base = r, own, sems, base
        self.b1, self.b2, self.b3, self.b4 = bufs
        axes = []
        for is_y, i in ((True, y), (False, z)) if y_first else ((False, z), (True, y)):
            p, q = (other_of_pair(i), 3 - i) if mirror == 0 else (3 - i, other_of_pair(i))
            beyond = 3 - p if mirror == 0 else other_of_pair(p)
            devices = [{"y_hi": d // 2, "y_lo": lax.rem(d, 2)} if is_y else {"z": d} for d in (p, q)]
            axes.append((i, p, q, beyond, devices))
        (self.i, p, self.q, beyond, self.dev1), (i2, p2, q2, beyond2, self.dev2) = axes
        index = (lambda v: v) if y_first else y_index
        self.at_i, self.at_p, self.at_q, self.at_beyond = index(i2), index(p2), index(q2), index(beyond2)
        self.views = [(view, (slot, *at)) for slot, d in ((1, beyond), (0, p)) for view, at in first(d)]

    def copy(self, k, src, dst, device):
        return pltpu.make_async_remote_copy(
            src_ref=src, dst_ref=dst, send_sem=self.sems[0].at[self.base + k], recv_sem=self.sems[1].at[self.base + k],
            device_id=device, device_id_type=MESH,
        )

    def copies(self, step):
        if step == 1:
            return [self.copy(k, view, self.b1.at[at], self.dev1[0]) for k, (view, at) in enumerate(self.views)]
        if step == 2:
            return [self.copy(8, self.b1.at[1], self.b2, self.dev1[1])]
        if step == 3:
            places = ((1, self.at_beyond), (0, self.at_p))
            return [self.copy(9 + slot, self.b2.at[at], self.b3.at[slot], self.dev2[0]) for slot, at in places]
        return [self.copy(11, self.b3.at[1], self.b4, self.dev2[1])]

    def go(self, step):
        for copy in self.copies(step):
            copy.start()

    def arrived(self, step):
        for copy in self.copies(step):
            copy.wait_recv()

    def add(self, out, terms, lead):
        def body(i, _):
            total = None
            for term in terms:
                v = term(i).astype(F32)
                total = v if total is None else total + v
            out(i, total.astype(BF))
            return 0

        lax.fori_loop(0, lead, body, 0)

    def step2(self):
        self.arrived(1)
        b1 = self.b1
        for slot, d in ((1, self.q), (0, self.i)):

            def put(j, v, slot=slot):
                b1[slot, j, :, :] = v

            self.add(put, [lambda j, d=d: self.own(d, j), lambda j, slot=slot: b1[slot, j, :, :]], 4)
            if slot == 1:
                self.go(2)

    def step3(self):
        self.arrived(2)
        b1, b2 = self.b1, self.b2

        def put(j, v):
            b2[j, :, :] = v

        self.add(put, [lambda j: b1[0, j, :, :], lambda j: b2[j, :, :]], 4)
        self.go(3)

    def step4(self):
        self.arrived(3)
        b2, b3 = self.b2, self.b3
        for slot, place in ((1, self.at_q), (0, self.at_i)):

            def put(j, v, slot=slot):
                b3[slot, :, :] = v

            self.add(
                put,
                [lambda j, p=place: b2[p, :, :], lambda j, slot=slot: b3[slot, :, :]],
                1,
            )
            if slot == 1:
                self.go(4)

    def finish(self, out):
        self.arrived(4)
        b3, b4 = self.b3, self.b4
        self.add(out, [lambda j: b3[0, :, :], lambda j: b4[:, :]], 1)
        for step in (1, 2, 3, 4):
            for copy in self.copies(step):
                copy.wait_send()


class TorusSum(Side):
    def start(self):
        for s in self.s:
            s.go(1)

    def step2(self):
        for s in self.s:
            s.step2()

    def step3(self):
        for s in self.s:
            s.step3()

    def step4(self):
        for s in self.s:
            s.step4()

    def finish(self):
        for s, out in zip(self.s, self.outs):
            s.finish(out)

    def bufs(self, scratch, i):
        return [ref.at[i] for ref in scratch[:4]]


class SumColumns(TorusSum):
    def __init__(self, grads):
        r = self.rows = grads.shape[2]
        dma = pltpu.SemaphoreType.DMA
        self.operands = [grads]
        self.shapes = [jax.ShapeDtypeStruct((r, 1024), BF)]
        self.scratch = [
            pltpu.VMEM((4, 2, 4, r, 256), BF), pltpu.VMEM((4, 4, r, 256), BF), pltpu.VMEM((4, 2, r, 256), BF), pltpu.VMEM((4, r, 256), BF),
            dma((48,)), dma((48,)),
        ]

    def bind(self, ring, ins, outs, scratch):
        (g,), (out,) = ins, outs
        self.s, self.outs = [], []
        for i in range(4):
            y_first, lane = i < 2, i * 256

            def first(d, y_first=y_first, lane=lane):
                if y_first:
                    return [(g.at[d // 2, :, :, lanes_at(lax.rem(d, 2) * 1024 + lane, 256)], ())]
                return [(g.at[:, d, :, pl.ds(yl * 1024 + lane, 256)], (pl.ds(yl * 2, 2),)) for yl in range(2)]

            def own(d, j, y_first=y_first, lane=lane):
                rows = slice(None)
                if y_first:
                    return g[d // 2, j, rows, lanes_at(lax.rem(d, 2) * 1024 + lane, 256)]
                return g[lax.rem(j, 2), d, rows, lanes_at((j // 2) * 1024 + lane, 256)]

            def put(j, v, lane=lane):
                out[:, pl.ds(lane, 256)] = v

            y_index = lambda y: lax.rem(y, 2) * 2 + y // 2
            self.s.append(Stream(y_first, i % 2, y_index, self.rows, first, own, self.bufs(scratch, i), scratch[4:], i * 12))
            self.outs.append(put)


class SumRows(TorusSum):
    def __init__(self, grads):
        r = self.rows = grads.shape[1]
        dma = pltpu.SemaphoreType.DMA
        self.operands = [grads]
        self.shapes = [jax.ShapeDtypeStruct((2, r, 128), BF)]
        h = r // 2
        self.scratch = [
            pltpu.VMEM((4, 2, 4, h, 128), BF), pltpu.VMEM((4, 4, h, 128), BF), pltpu.VMEM((4, 2, h, 128), BF), pltpu.VMEM((4, h, 128), BF),
            dma((48,)), dma((48,)),
        ]

    def bind(self, ring, ins, outs, scratch):
        (g,), (out,) = ins, outs
        self.s, self.outs = [], []
        h = self.rows // 2
        for i in range(4):
            y_first, lane, row = i < 2, (i // 2) * 512, (i % 2) * h

            def first(d, y_first=y_first, lane=lane, row=row):
                half = pl.ds(row, h)
                if y_first:
                    return [
                        (g.at[lax.rem(d, 2), half, lanes_at((d // 2) * 1024 + lane + z * 128, 128)], (z,)) for z in range(4)
                    ]
                return [(g.at[:, half, lanes_at(yh * 1024 + lane + d * 128, 128)], (pl.ds(yh * 2, 2),)) for yh in range(2)]

            def own(d, j, y_first=y_first, lane=lane, row=row):
                rows = pl.ds(row, h)
                if y_first:
                    return g[lax.rem(d, 2), rows, lanes_at((d // 2) * 1024 + lane + j * 128, 128)]
                return g[lax.rem(j, 2), rows, lanes_at((j // 2) * 1024 + lane + d * 128, 128)]

            def put(j, v, i=i, row=row):
                out[i // 2, pl.ds(row, h), :] = v

            self.s.append(Stream(y_first, i % 2, lambda y: y, h, first, own, self.bufs(scratch, i), scratch[4:], i * 12))
            self.outs.append(put)


class Ag:
    def __init__(self, ring, buf, sems):
        r = self.r = ring
        self.buf, self.sems = buf, sems
        self.plan = (
            (r.x, 0, r.right), (r.x, 1, r.right), (r.x, 1, r.left), (r.x, 0, r.left),
            (r.left_x, 0, r.right), (r.right_x, 1, r.left),
            (r.x, 0, r.sibling), (r.x, 1, r.sibling),
            (r.left_x, 0, r.sibling), (r.left_x, 1, r.sibling), (r.right_x, 0, r.sibling), (r.right_x, 1, r.sibling),
            (r.far_x, 0, r.sibling), (r.far_x, 1, r.sibling),
        )

    def copy(self, i):
        x, half, device = self.plan[i]
        block = self.buf.at[x * 2 + self.r.core, HALVES[half]]
        return pltpu.make_async_remote_copy(
            src_ref=block, dst_ref=block, send_sem=self.sems[0].at[i], recv_sem=self.sems[1].at[i],
            device_id=device, device_id_type=MESH,
        )

    def begin(self, half):
        for i in ((0, 3, 6), (2, 1, 7))[half]:
            self.copy(i).start()

    def near(self, steps=slice(None)):
        for got, onward in ((0, (4, 8)), (2, (5, 11)), (1, (9,)), (3, (10,)))[steps]:
            self.copy(got).wait_recv()
            for i in onward:
                self.copy(i).start()

    def far(self):
        for got, onward in ((4, 12), (5, 13)):
            self.copy(got).wait_recv()
            self.copy(onward).start()

    def have(self, *which):
        for i in which:
            self.copy(i).wait_recv()

    def drain(self):
        for i in range(14):
            self.copy(i).wait_send()


class Rs:
    def __init__(self, ring, parts, held, got, sems):
        r = self.r = ring
        self.parts, self.held, self.got, self.sems = parts, held, got, sems
        self.blocks = (r.far_x, r.right_x, r.left_x, r.x)
        self.plan = {
            4: (0, 4, 0, r.right), 5: (0, 4, 1, r.left), 6: (1, 5, 1, r.right), 7: (2, 5, 0, r.left),
            8: (1, 6, 0, r.right), 9: (2, 6, 1, r.left),
        }

    def swap(self, i, x):
        return pltpu.make_async_remote_copy(
            src_ref=self.parts.at[x * 2 + 1 - self.r.core], dst_ref=self.got.at[i], send_sem=self.sems[0].at[i],
            recv_sem=self.sems[1].at[i], device_id=self.r.sibling, device_id_type=MESH,
        )

    def copy(self, i, q=0):
        if i < 4:
            return self.swap(i, self.blocks[i])
        block, slot, half, device = self.plan[i]
        rows, sem = pl.ds(half * 64 + q * 32, 32), 4 + (i - 4) * 2 + q
        return pltpu.make_async_remote_copy(
            src_ref=self.held.at[block, rows], dst_ref=self.got.at[slot, rows], send_sem=self.sems[0].at[sem],
            recv_sem=self.sems[1].at[sem], device_id=device, device_id_type=MESH,
        )

    def pair(self, i, half, q):
        x = self.blocks[i]
        for k in range(2):
            rows = pl.ds(half * 64 + q * 32 + k * 16, 16)
            total = self.parts[x * 2 + self.r.core, rows, :].astype(F32) + self.got[i, rows, :].astype(F32)
            self.held[i, rows, :] = total.astype(BF)

    def onward(self, i, half, q):
        for k in range(2):
            rows = pl.ds(half * 64 + q * 32 + k * 16, 16)
            total = self.held[i, rows, :].astype(F32) + self.got[4, rows, :].astype(F32)
            self.held[i, rows, :] = total.astype(BF)

    def send_left(self):
        self.copy(2).wait_recv()
        for q in range(2):
            self.pair(2, 0, q)
            self.copy(7, q).start()

    def send_right(self):
        self.copy(1).wait_recv()
        for q in range(2):
            self.pair(1, 1, q)
            self.copy(6, q).start()

    def send_far(self):
        self.copy(0).wait_recv()
        for q in range(2):
            self.pair(0, 0, q)
            self.copy(4, q).start()
            self.pair(0, 1, q)
            self.copy(5, q).start()

    def relay(self):
        for q in range(2):
            self.pair(1, 0, q)
            self.pair(2, 1, q)
        for q in range(2):
            self.copy(4, q).wait_recv()
            self.onward(1, 0, q)
            self.copy(8, q).start()
            self.copy(5, q).wait_recv()
            self.onward(2, 1, q)
            self.copy(9, q).start()
        self.copy(3).wait_recv()

    def ready(self, half, q):
        for i in ((7, 8), (6, 9))[half]:
            self.copy(i, q).wait_recv()

    def total(self, rows):
        r = self.r
        return (
            self.parts[r.x * 2 + r.core, rows, :].astype(F32)
            + self.got[3, rows, :].astype(F32)
            + self.got[5, rows, :].astype(F32)
            + self.got[6, rows, :].astype(F32)
        )

    def drain(self):
        for i in range(4):
            self.copy(i).wait_send()
        for i in range(4, 10):
            for q in range(2):
                self.copy(i, q).wait_send()


def middle_kernel(
    down_side, gu_side, arrive, a_ref, wo_ref, x_ref, valid_ref, wd_ref, teacher_hbm, half_w_ref,
    out_hbm, stats_ref, dy1_hbm, da_ref, gout_ref, ggu_hbm, piece_ref, gu_piece_ref,
    out_ref, dy1_ref, ggu_ref,
    w, n2, dyg, dag, parts, held, got, y1, gate, up, mid, mid_t, dup, dgu1, dgu2, gd, gu1, dmid, valid_col, loss_col,
    rs1_s, rs1_r, ag1_s, ag1_r, rs2_s, rs2_r, ag2_s, ag2_r, rs3_s, rs3_r, ag3_s, ag3_r, w_s, w_r, loc, *side_scratch,
):
    ring = Ring()
    y_lo = lax.axis_index("y_lo")
    near, other = y_partners()
    down_side.bind(ring, (gd,), (piece_ref,), side_scratch[: len(down_side.scratch)])
    gu_side.bind(ring, (gu1,), (gu_piece_ref,), side_scratch[len(down_side.scratch) :])
    meet([ring.right, ring.left, ring.sibling, near, other] + [{"z": p} for p in (other_of_pair(lax.axis_index("z")), 3 - lax.axis_index("z"))])
    arrive()
    here = ring.x * 2 + ring.core
    dy, dgate = dy1_ref, mid
    teacher = dag.at[here]
    teacher_copy = pltpu.make_async_copy(teacher_hbm, teacher, loc.at[4])
    teacher_copy.start()
    valid_col[...] = column(valid_ref[...].astype(F32))

    wcopies = []
    for dx in range(4):
        lanes = group_lanes(lax.rem(ring.x + 4 - dx, 4), y_lo)
        src, dst = half_w_ref.at[:, :, :, lanes], w.at[:, :, :, lanes]
        wcopies.append(send(src, dst, (w_s, w_r), dx, (near, other)[dx // 2]))
        copy = pltpu.make_async_copy(src, dst, loc.at[dx])
        copy.start()
        wcopies.append(copy)

    def rows_of(x):
        return pl.ds(pl.multiple_of(x * 256, 256), 256)

    def block(buf, x):
        return buf[pl.ds(x * 2, 2)].reshape(256, D)

    def put(x, product):
        def body(k, _):
            lanes = lanes_at(k * 512, 512)
            parts[pl.ds(x * 2, 2), :, lanes] = product(lanes).astype(BF).reshape(2, 128, 512)
            return 0

        lax.fori_loop(0, 4, body, 0)

    def reduced(rs, op, ag, buf):
        for q in range(2):
            for half in range(2):
                rs.ready(half, q)

                def body(k, _, half=half, q=q):
                    rows = pl.ds(pl.multiple_of(half * 64 + q * 32 + k * 16, 16), 16)
                    buf[here, rows, :] = op(rows, rs.total(rows)).astype(BF)
                    return 0

                lax.fori_loop(0, 2, body, 0)
                if q == 1:
                    ag.begin(half)

    def over_blocks(ag, rs, work, first=None, after=()):
        def step(i, _):
            at = functools.partial(jnp.equal, i)

            @pl.when(at(0))
            def _():
                ag.have(6, 7)
                if first is not None:
                    ag.near(slice(2))
                    first()

            @pl.when(at(1))
            def _():
                ag.near(slice(2 if first is not None else 0, 4))
                ag.have(8, 9)

            @pl.when(at(2))
            def _():
                ag.have(10, 11)
                if rs is not None:
                    rs.send_left()

            @pl.when(at(3))
            def _():
                if rs is not None:
                    rs.send_right()
                ag.far()
                ag.have(12, 13)

            x = lax.rem(ring.x + jnp.where(at(1), 3, jnp.where(at(2), 1, jnp.where(at(3), 2, 0))), 4)
            work(x, lambda: rs.swap(3 - i, x).start())
            for k, then in enumerate(after):
                pl.when(at(k + 1))(then)
            return 0

        lax.fori_loop(0, 4, step, 0)

    rs = Rs(ring, parts, held, got, (rs1_s, rs1_r))
    ag = Ag(ring, n2, (ag1_s, ag1_r))
    for i in range(4):
        x = rs.blocks[i]
        put(x, lambda lanes, x=x: nn(a_ref[rows_of(x), :], wo_ref[:, lanes]))
        rs.copy(i).start()
        if i == 1:
            rs.send_far()
        elif i == 2:
            rs.send_right()
        elif i == 3:
            rs.send_left()
    rs.relay()

    def op1(rows, total):
        v = x_ref[rows, :].astype(F32) + total
        y1[rows, :] = v
        return v * norm_scale(v)

    reduced(rs, op1, ag, n2)
    rs.drain()
    teacher_copy.wait()

    rs = Rs(ring, parts, held, got, (rs2_s, rs2_r))

    def forward(x, send_parts):
        rows = rows_of(x)
        gate[rows, :] = nt(block(n2, x), w[0].reshape(704, D))
        up[rows, :] = nt(block(n2, x), w[1].reshape(704, D))

        def body(k, _):
            r = pl.ds(pl.multiple_of(x * 256 + k * 32, 32), 32)
            g = gate[r, :]
            mid[pl.ds(pl.multiple_of(k * 32, 32), 32), :] = (g * jax.nn.sigmoid(g) * up[r, :]).astype(BF)
            return 0

        lax.fori_loop(0, 8, body, 0)
        put(x, lambda lanes: nn(mid[...], wd_ref[:, lanes]))
        send_parts()
        mid_t[:, rows] = mid[...].T

    def weights_here():
        for copy in wcopies:
            copy.wait()

    over_blocks(ag, rs, forward, weights_here)
    rs.send_far()
    rs.relay()
    ag.drain()

    def op2(rows, total):
        v = y1[rows, :] + total
        out_ref[rows, :] = v.astype(BF)
        miss = v - dag[here, rows, :].astype(F32)
        valid = valid_col[rows, 0:1]
        loss_col[rows, :] = jnp.broadcast_to(valid * jnp.mean(miss * miss, axis=1, keepdims=True), (16, 128))
        dy[rows, :] = valid * miss
        return valid * miss

    ag = Ag(ring, dyg, (ag2_s, ag2_r))
    reduced(rs, op2, ag, dyg)
    rs.drain()
    stats_ref[...] = jnp.concatenate([loss_col[...].T[0:1], valid_ref[...].astype(F32), jnp.zeros((6, 128), F32)], axis=0)

    rs = Rs(ring, parts, held, got, (rs3_s, rs3_r))

    def backward(x, send_parts):
        rows = rows_of(x)
        dgate_mid = nt(block(dyg, x), wd_ref[...])
        dmid[...] = dgate_mid

        def body(k, _):
            r = pl.ds(pl.multiple_of(x * 256 + k * 32, 32), 32)
            q = pl.ds(pl.multiple_of(k * 32, 32), 32)
            g, dm = gate[r, :], dmid[q, :]
            sg = jax.nn.sigmoid(g)
            dgate[q, :] = (dm * up[r, :] * sg * (1.0 + g * (1.0 - sg))).astype(BF)
            dup[q, :] = (dm * (g * sg)).astype(BF)
            return 0

        lax.fori_loop(0, 8, body, 0)
        put(x, lambda lanes: nn(dgate[...], w[0, :, :, lanes].reshape(704, 512)) + nn(dup[...], w[1, :, :, lanes].reshape(704, 512)))
        send_parts()
        for i, ref in enumerate((dgate, dup)):
            turned = ref[...].T
            for c in range(4):
                dgu1[pl.ds((4 * i + c) * R1, R1), rows] = turned[176 * c : 176 * c + R1]
                dgu2[pl.ds((4 * i + c) * R2, R2), rows] = turned[176 * c + R1 : 176 * c + 176]

    over_blocks(ag, rs, backward)
    rs.send_far()

    def grad_down(k, _):
        lanes = lanes_at(k * 512, 512)
        gd[:, :, lanes] = nn(mid_t[...], dyg[:, :, lanes].reshape(1024, 512)).astype(BF).reshape(2, 352, 512)
        return 0

    lax.fori_loop(0, 4, grad_down, 0)
    down_side.start()
    rs.relay()

    def grad_gu(rows, lhs, out, k):
        lanes = lanes_at(k * 512, 512)
        out[:, :, :, lanes] = nn(lhs[...], n2[:, :, lanes].reshape(1024, 512)).astype(BF).reshape(2, 4, rows, 512)

    def grad_gu1(k, _):
        grad_gu(R1, dgu1, gu1, k)
        return 0

    lax.fori_loop(0, 4, grad_gu1, 0)
    gu_side.start()
    ag.drain()

    def op3(rows, total):
        v = back_norm(y1[rows, :], dy[rows, :], total)
        dy1_ref[rows, :] = v
        return v

    ag = Ag(ring, dag, (ag3_s, ag3_r))
    reduced(rs, op3, ag, dag)
    rs.drain()

    def to_attention(x, _):
        rows = rows_of(x)
        da_ref[rows, :] = nt(block(dag, x), wo_ref[...]).astype(BF)
        mid_t[0:256, rows] = a_ref[rows, :].T
        grad_gu(R2, dgu2, ggu_ref, x)

    def both(name):
        def then():
            getattr(down_side, name)()
            getattr(gu_side, name)()

        return then

    over_blocks(ag, None, to_attention, after=(both("step2"), both("step3"), both("step4")))
    writes = []
    for k, (src, dst) in enumerate(((out_ref, out_hbm), (dy1_ref, dy1_hbm), (ggu_ref, ggu_hbm))):
        writes.append(pltpu.make_async_copy(src, dst, loc.at[5 + k]))
        writes[-1].start()

    def grad_out(k, _):
        lanes = lanes_at(k * 512, 512)
        gout_ref[:, :, lanes] = nn(mid_t[0:256, :], dag[:, :, lanes].reshape(1024, 512)).astype(BF).reshape(2, 128, 512)
        return 0

    lax.fori_loop(0, 4, grad_out, 0)
    ag.drain()
    down_side.finish()
    gu_side.finish()
    for copy in writes:
        copy.wait()


def middle(a, wo, x, teacher, valid, half_w, wd):
    dma = pltpu.SemaphoreType.DMA
    pair = lambda n: [dma((n,)), dma((n,))]
    big = pltpu.VMEM((8, 128, D), BF)
    sides = [SumRows(jax.ShapeDtypeStruct((2, 352, D), BF)), SumColumns(jax.ShapeDtypeStruct((2, 4, R1, D), BF))]
    inputs = (a, wo, x, valid, wd, teacher, half_w)
    which = (0, 1, 2, 4)
    return pl.pallas_call(
        loading(functools.partial(middle_kernel, *sides), which, 7, 8),
        out_shape=[
            jax.ShapeDtypeStruct((128, D), BF), jax.ShapeDtypeStruct((8, 128), F32), jax.ShapeDtypeStruct((128, D), F32),
            jax.ShapeDtypeStruct((1024, 256), BF), jax.ShapeDtypeStruct((2, 128, D), BF), jax.ShapeDtypeStruct((2, 4, R2, D), BF),
            *[s for side in sides for s in side.shapes],
        ],
        in_specs=[VM if i == 3 else HB for i in range(7)],
        out_specs=[HB, VM, HB, VM, VM, HB, VM, VM],
        scratch_shapes=[
            *places_for(inputs, which),
            pltpu.VMEM((128, D), BF), pltpu.VMEM((128, D), F32), pltpu.VMEM((2, 4, R2, D), BF),
            pltpu.VMEM((2, 2, 352, D), BF), big, big, big, big, pltpu.VMEM((3, 128, D), BF), pltpu.VMEM((7, 128, D), BF),
            pltpu.VMEM((128, D), F32),
            pltpu.VMEM((1024, 704), F32), pltpu.VMEM((1024, 704), F32),
            pltpu.VMEM((256, 704), BF), pltpu.VMEM((704, 1024), BF), pltpu.VMEM((256, 704), BF),
            pltpu.VMEM((8 * R1, 1024), BF), pltpu.VMEM((8 * R2, 1024), BF), pltpu.VMEM((2, 352, D), BF), pltpu.VMEM((2, 4, R1, D), BF),
            pltpu.VMEM((256, 704), F32), pltpu.VMEM((128, 128), F32), pltpu.VMEM((128, 128), F32),
            *pair(16), *pair(14), *pair(16), *pair(14), *pair(16), *pair(14), *pair(4), dma((8,)),
            *[s for side in sides for s in side.scratch],
        ],
        compiler_params=pltpu.CompilerParams(collective_id=1, has_side_effects=True, vmem_limit_bytes=63 * 2**20),
        name="middle",
    )(*inputs)


def piece_lanes(c, part):
    return lanes_at((c // 4) * 1024 + part * 512 + lax.rem(c, 4) * 128, 128)


def ctx_at(k):
    y_hi, z = lax.axis_index("y_hi"), lax.axis_index("z")
    y, zz = (1 - y_hi if k // 4 else y_hi), lax.rem(z + k % 4, 4)
    return y * 4 + zz, {"y_hi": y, "z": zz}


class Spread:
    def __init__(self, piece, slot, sems, base, y_first, local):
        self.piece, self.slot, self.sems, self.base, self.y_first, self.local = piece, slot, sems, base, y_first, local

    def copy(self, k, src, c, device):
        return pltpu.make_async_remote_copy(
            src_ref=src, dst_ref=self.slot(c), send_sem=self.sems[0].at[self.base + k - 1],
            recv_sem=self.sems[1].at[self.base + k - 1], device_id=device, device_id_type=MESH,
        )

    def first(self, k):
        here, _ = ctx_at(0)
        return self.copy(k, self.piece, here, ctx_at(k)[1])

    def second(self, dz):
        if self.y_first:
            c, _ = ctx_at(4)
            return self.copy(4 + dz, self.slot(c), c, ctx_at(dz)[1])
        c, _ = ctx_at(4 - dz)
        return self.copy(4 + dz, self.slot(c), c, ctx_at(4)[1])

    def own(self):
        return pltpu.make_async_copy(self.piece, self.slot(ctx_at(0)[0]), self.local)

    def start(self):
        for k in (4, 1, 3, 2) if self.y_first else (1, 3, 2, 4):
            self.first(k).start()
        if self.local is not None:
            self.own().start()

    def relay(self):
        if self.y_first:
            self.first(4).wait_recv()
            for dz in (1, 3, 2):
                self.second(dz).start()
        else:
            for dz in (1, 3, 2):
                self.first(dz).wait_recv()
                self.second(dz).start()

    def finish(self):
        if self.y_first:
            for dz in (1, 3, 2):
                self.first(dz).wait_recv()
        else:
            self.first(4).wait_recv()
        for dz in (1, 3, 2):
            self.second(dz).wait_recv()
            self.second(dz).wait_send()
        for k in (1, 2, 3, 4):
            self.first(k).wait_send()
        self.own().wait()


class SpreadRows(Side):
    def __init__(self, pieces):
        r = pieces.shape[1]
        dma = pltpu.SemaphoreType.DMA
        self.operands = [pieces]
        self.shapes = [jax.ShapeDtypeStruct((r, D), BF)]
        self.scratch = [dma((14,)), dma((14,)), dma((2,))]

    def bind(self, ring, ins, outs, scratch):
        (p,), (out,) = ins, outs
        self.peers = [ctx_at(k)[1] for k in range(1, 8)]
        self.s = [
            Spread(
                p.at[part], lambda c, part=part: out.at[:, piece_lanes(c, part)], scratch[:2], part * 7, part == 0,
                scratch[2].at[part],
            )
            for part in range(2)
        ]

    def start(self):
        for s in self.s:
            s.start()

    def middle(self):
        for s in self.s:
            s.relay()

    def finish(self):
        for s in self.s:
            s.finish()


class Move(Side):
    def __init__(self, pieces):
        dma = pltpu.SemaphoreType.DMA
        self.operands = [pieces]
        self.shapes = [jax.ShapeDtypeStruct((8, pieces.shape[0], 128), BF)]
        self.scratch = [dma((8,)), dma((8,))]

    def bind(self, ring, ins, outs, scratch):
        (self.p,), (self.out,), self.sems = ins, outs, scratch
        x, self.y_lo, core = lax.axis_index("x"), lax.axis_index("y_lo"), lax.axis_index("core")
        self.here16, self.here8 = x * 4 + self.y_lo * 2 + core, x * 2 + core
        self.peers = [device for _, device in group_peers()]

    def same(self, j):
        return self.here16 == self.y_lo * 8 + j

    def away(self, j):
        return pltpu.make_async_remote_copy(
            src_ref=self.p.at[:, pl.ds(j * 128, 128)], dst_ref=self.out.at[self.here8], send_sem=self.sems[0].at[j],
            recv_sem=self.sems[1].at[self.here8], device_id={"x": self.y_lo * 2 + j // 4, "y_lo": j // 2 % 2, "core": j % 2},
            device_id_type=MESH,
        )

    def stay(self, j):
        return pltpu.make_async_copy(self.p.at[:, pl.ds(j * 128, 128)], self.out.at[self.here8], self.sems[1].at[self.here8])

    def start(self):
        for j in range(8):

            @pl.when(self.same(j))
            def _():
                self.stay(j).start()

            @pl.when(jnp.logical_not(self.same(j)))
            def _():
                self.away(j).start()

    def arrive(self, s):
        pltpu.make_async_copy(self.out.at[s], self.out.at[s], self.sems[1].at[s]).wait()

    def drain(self):
        for j in range(8):

            @pl.when(jnp.logical_not(self.same(j)))
            def _():
                self.away(j).wait_send()

    def finish(self):
        for s in range(8):
            self.arrive(s)
        self.drain()


def group_peers():
    x, y_lo, core = lax.axis_index("x"), lax.axis_index("y_lo"), lax.axis_index("core")
    found = []
    for k in range(1, 16):
        dx, dy, dc = k // 4, k // 2 % 2, k % 2
        found.append((k, {"x": lax.rem(x + dx, 4), "y_lo": 1 - y_lo if dy else y_lo, "core": 1 - core if dc else core}))
    return found


class SpreadGateUp(Side):
    def __init__(self, pieces, first, into=None):
        self.r, self.first = pieces.shape[1], first
        dma = pltpu.SemaphoreType.DMA
        self.operands = [pieces]
        self.shapes = [jax.ShapeDtypeStruct((2, FF, 128), BF)]
        self.scratch = [dma((56,)), dma((56,)), dma((8,))]

    def bind(self, ring, ins, outs, scratch):
        (got,), (out,) = ins, outs
        self.s = []
        for s in range(8):

            def slot(c, s=s):
                rows = ((s // 2) * 4 + lax.rem(c // 2, 2) * 2 + s % 2) * 352 + lax.rem(c, 2) * 176 + self.first
                return out.at[c // 4, pl.ds(pl.multiple_of(rows, 16), self.r)]

            self.s.append(Spread(got.at[s], slot, scratch[:2], s * 7, s % 3 == 0, scratch[2].at[s]))

    def start(self):
        for s in self.s:
            s.start()

    def middle(self):
        for s in self.s:
            if s.y_first:
                s.relay()
        for s in self.s:
            if not s.y_first:
                s.relay()

    def finish(self):
        for s in self.s:
            s.finish()


def back_norm(v, grad, u):
    r = norm_scale(v)
    n = v * r
    return grad + r * (u - n * jnp.mean(u * n, axis=1, keepdims=True))


def y_partners():
    y_hi, y_lo = lax.axis_index("y_hi"), lax.axis_index("y_lo")
    return {"y_lo": 1 - y_lo}, {"y_hi": 1 - y_hi, "y_lo": 1 - y_lo}


def group_lanes(x, y_lo):
    return pl.ds(pl.multiple_of(x * 512 + y_lo * 256, 256), 256)


def tp_peers(ring):
    found = []
    for k in range(1, 8):
        dx, dc = k // 2, k % 2
        core = 1 - ring.core if dc else ring.core
        found.append((k, lax.rem(ring.x + dx, 4), core))
    return found


def ctx_peer(c, k):
    other = lax.rem(c + k, 8)
    return {"y_hi": other // 4, "z": lax.rem(other, 4)}


def nt(a, b):
    return dot(a, b, 1, 1)


def nn(a, b):
    return dot(a, b, 1, 0)


def key_bias(meta_ref, d, c, bias):
    docs = meta_ref[d].astype(F32)
    query_docs = meta_ref[d, pl.ds(c, 1), :].astype(F32)
    lane = lax.broadcasted_iota(jnp.int32, (128, 128), 1)
    row = lax.broadcasted_iota(jnp.int32, (128, 128), 0)

    def position(owner, i):
        return jnp.where(i < 64, owner * 64 + i, (15 - owner) * 64 + i - 64)

    query_pos = position(c, lane)
    for b in range(8):
        key_docs = jnp.broadcast_to(docs[b : b + 1, :], (128, 128)).T
        good = (query_pos >= position(b, row)) & (key_docs == query_docs)
        bias[pl.ds(b * 128, 128), :] = jnp.where(good, 0.0, NEGATIVE)


def eye():
    return (lax.broadcasted_iota(jnp.int32, (128, 128), 0) == lax.broadcasted_iota(jnp.int32, (128, 128), 1)).astype(BF)


def front_kernel(
    arrive, x_ref, doc_ref, g1_ref, g2_ref, wq_ref, wk_ref, wv_ref, wg_ref, wu_ref, wo_ref, wdn_ref, angles_hbm,
    a_ref, lse_ref, metas_ref, n1_out, wqkv_out, qp_out, kv_out, wos_ref, wgu_ref, wd_ref,
    n1, wqkv, w, wt, qkv, qp, kv, bias, probs, meta_ref, angles, tab_ref,
    ag_s, ag_r, meta_s, meta_r, w_s, w_r, y_s, y_r, gu_s, gu_r, wd_s, wd_r, kv_s, kv_r, fw_s, fw_r, loc,
):
    ring = Ring()
    y_lo = lax.axis_index("y_lo")
    c, _ = ctx_at(0)
    near, other = y_partners()
    peers = tp_peers(ring)
    meet([{"x": x, "core": core} for _, x, core in peers] + [near, other] + [ctx_at(k)[1] for k in range(1, 8)])
    arrive()
    here = ring.x * 2 + ring.core
    copies, local = [], []

    def copy_here(src, dst):
        copy = pltpu.make_async_copy(src, dst, loc.at[len(local)])
        copy.start()
        local.append(copy)

    ag = Ag(ring, n1, (ag_s, ag_r))

    def normed(k, _):
        rows = pl.ds(pl.multiple_of(k * 16, 16), 16)
        v = x_ref[rows, :].astype(F32)
        n1[here, rows, :] = (v * norm_scale(v)).astype(BF)
        return 0

    lax.fori_loop(0, 4, normed, 0)
    ag.begin(0)
    copy_here(angles_hbm.at[c], angles)
    row = lax.broadcasted_iota(jnp.int32, (1, 128), 1)
    tiles = [doc_ref[:, k * 128 : (k + 1) * 128] for k in range(8)]
    meta_ref[...] = jnp.zeros_like(meta_ref)
    for i in range(8):
        first, second = tiles[i // 2], tiles[(15 - i) // 2]
        if i % 2:
            first, second = pltpu.roll(first, 64, 1), pltpu.roll(second, 64, 1)
        meta_ref[i : i + 1, :] = jnp.where(row < 64, first, second)
    for k, x, core in peers:
        copies.append(send(meta_ref, metas_ref.at[here], (meta_s, meta_r), k, {"x": x, "core": core}))
    metas_ref[here] = meta_ref[...]

    one_matrix = eye()
    g1, g2 = g1_ref[...].astype(F32), g2_ref[...].astype(F32)

    def turned(ref, gain, k):
        return (nt(one_matrix, ref[:, lanes_at(k * 128, 128)]) * gain).astype(BF)

    for f in range(16):
        w[(f // 4) * 2 + f % 2, pl.ds((f // 2 % 2) * 128, 128), :] = turned(wq_ref, g1, f)
    for ref, at in ((wk_ref, 256), (wv_ref, 320)):
        for k in range(2):
            tile = turned(ref, g1, k)
            for x in (2 * k, 2 * k + 1):
                part = tile[(x % 2) * 64 : (x % 2) * 64 + 64]
                w[2 * x, pl.ds(at, 64), :] = part
                w[2 * x + 1, pl.ds(at, 64), :] = part
    lanes = lanes_at((ring.x * 4 + y_lo * 2 + ring.core) * 128, 128)
    wcopies = {}
    for k, x, core in peers:
        wcopies[k] = send(w.at[x * 2 + core], wqkv.at[:, lanes], (w_s, w_r), k, {"x": x, "core": core})
    wqkv[:, lanes] = w[here]
    lax.fori_loop(4, 8, normed, 0)
    ag.begin(1)

    copy_here(wo_ref, wos_ref.at[y_lo])
    copy_here(wdn_ref, wd_ref.at[pl.ds(pl.multiple_of(y_lo * 352, 32), 352)])
    for half, device in enumerate((near, other)):
        copies.append(send(wo_ref.at[HALVES[half]], wos_ref.at[y_lo, HALVES[half]], (y_s, y_r), 4 + half, device))

    def turn_all(ref, i):
        def body(k, _):
            wt[i, pl.ds(pl.multiple_of(k * 128, 128), 128), :] = turned(ref, g2, k)
            return 0

        lax.fori_loop(0, FF // 128, body, 0)

    turn_all(wg_ref, 0)
    for dx in range(4):
        x = lax.rem(ring.x + 4 - dx, 4)
        if dx > 0:
            wcopies[2 * dx].wait_recv()
        wcopies[2 * dx + 1].wait_recv()
        block = wqkv.at[:, group_lanes(x, y_lo)]
        copies.append(send(block, block, (y_s, y_r), dx, (near, other)[dx // 2]))
    for half, device in enumerate((near, other)):
        rows = pl.ds(pl.multiple_of(y_lo * 352 + half * 176, 16), 176)
        copies.append(send(wdn_ref.at[pl.ds(half * 176, 176)], wd_ref.at[rows], (wd_s, wd_r), half, device))
    ag.near()
    turn_all(wu_ref, 1)
    ag.far()

    for j in range(2):
        rows = pl.ds(pl.multiple_of((ring.x * 4 + 2 * j + ring.core) * 352, 32), 352)
        copy_here(wt.at[:, rows], wgu_ref.at[:, j, :, lanes])
    for k, x, core in peers:
        for j in range(2):
            rows = pl.ds(pl.multiple_of((x * 4 + 2 * j + core) * 352, 32), 352)
            copies.append(
                send(wt.at[:, rows], wgu_ref.at[:, j, :, lanes], (gu_s, gu_r), k * 2 + j, {"x": x, "core": core})
            )

    local[0].wait()
    fill_tables(angles, tab_ref)
    ag.have(*range(6, 14))
    for copy in copies[9:13]:
        copy.wait_recv()
    qkv[...] = nt(n1[...].reshape(1024, D), wqkv[...])
    copy_here(n1, n1_out)
    copy_here(wqkv, wqkv_out)

    lane = lax.broadcasted_iota(jnp.int32, (128, 128), 1)

    def rope(u, i):
        return u * tab_ref[i] + pltpu.roll(u, 96, 1) * tab_ref[i + 1] + pltpu.roll(u, 32, 1) * tab_ref[i + 2]

    for d in range(8):
        kv[d % 2, d // 2, c] = rope(qkv[pl.ds(d * 128, 128), 256:384], 3).astype(BF)
    spreads = [
        Spread(kv.at[ring.core, x, c], lambda i, x=x: kv.at[ring.core, x, i], (kv_s, kv_r), x * 7, x < 2, None) for x in range(4)
    ]
    for s in spreads:
        s.start()

    def turn_queries(d, _):
        for j in range(2):
            u = rope(qkv[pl.ds(pl.multiple_of(d * 128, 128), 128), pl.ds(j * 128, 128)], 0) * 0.125
            qp[d, pl.ds(j * 256, 128), :] = jnp.where(lane < 64, u, 0.0).astype(BF)
            qp[d, pl.ds(j * 256 + 128, 128), :] = jnp.where(lane < 64, pltpu.roll(u, 64, 1), 0.0).astype(BF)
        return 0

    lax.fori_loop(0, 8, turn_queries, 0)
    copy_here(qp, qp_out)

    forwards = []

    def pass_on(k):
        back = ctx_at(k if k == 4 else k // 4 * 4 + (4 - k % 4))[0]
        block = kv.at[ring.core, :, back]
        forwards.append(send(block, block, (fw_s, fw_r), k - 1, ring.sibling))

    for k in (1, 4, 3, 2):
        for s in spreads:
            s.first(k).wait_recv()
            if k < 4 and not s.y_first:
                s.second(k).start()
            if k == 4 and s.y_first:
                for dz in (1, 3, 2):
                    s.second(dz).start()
        pass_on(k)
    for dz in (1, 3, 2):
        for s in spreads:
            s.second(dz).wait_recv()
        pass_on(4 + dz)
    for copy in forwards:
        copy.wait_recv()
    copy_here(kv, kv_out)
    for copy in copies[:7]:
        copy.wait_recv()

    def one(d, _):
        key_bias(metas_ref, d, c, bias)
        keys = kv[lax.rem(d, 2), d // 2].reshape(1024, 128)
        scores = nt(keys, qp[d])
        for h in range(4):
            s = scores[:, h * 128 : (h + 1) * 128] + bias[...]
            top = jnp.max(s, axis=0, keepdims=True)
            e = jnp.exp(s - top)
            total = jnp.sum(e, axis=0, keepdims=True)
            probs[:, h * 128 : (h + 1) * 128] = (e * (1.0 / total)).astype(BF)
            lse_ref[d, :, h * 128 : (h + 1) * 128] = jnp.broadcast_to(top + jnp.log(total), (8, 128))
        mixed = nn(keys.T, probs[...])
        for j in range(2):
            two = jnp.concatenate([mixed[64:, (2 * j) * 128 : (2 * j + 1) * 128], mixed[64:, (2 * j + 1) * 128 : (2 * j + 2) * 128]], axis=0)
            a_ref[pl.ds(pl.multiple_of(d * 128, 128), 128), pl.ds(j * 128, 128)] = two.T.astype(BF)
        return 0

    lax.fori_loop(0, 8, one, 0)

    ag.drain()
    for k in range(1, 8):
        wcopies[k].wait_send()
    for s in spreads:
        for k in range(1, 5):
            s.first(k).wait_send()
        for dz in (1, 3, 2):
            s.second(dz).wait_send()
    for copy in forwards:
        copy.wait_send()
    for i, copy in enumerate(copies):
        copy.wait_send()
        if i >= 7 and not 9 <= i < 13:
            copy.wait_recv()
    for copy in local[1:]:
        copy.wait()


def front(hidden_in, docs, g1, g2, w_query, w_key, w_value, w_gate, w_up, w_out, w_down, angles):
    dma = pltpu.SemaphoreType.DMA
    pair = lambda n: [dma((n,)), dma((n,))]
    out = lambda *shape: jax.ShapeDtypeStruct(shape, BF)
    inputs = (hidden_in, docs, g1, g2, w_query, w_key, w_value, w_gate, w_up, w_out, w_down, angles)
    which = (0, 4, 5, 6, 7, 8, 9, 10)
    return pl.pallas_call(
        loading(front_kernel, which, 12, 10),
        out_shape=[
            out(1024, 256), jax.ShapeDtypeStruct((8, 8, 512), F32), jax.ShapeDtypeStruct((8, 16, 128), jnp.int32),
            out(8, 128, D), out(384, D), out(8, 512, 128), out(2, 4, 8, 128, 128), out(2, 128, D), out(2, 2, 352, D), out(704, D),
        ],
        in_specs=[HB if i in which or i == 11 else VM for i in range(12)],
        out_specs=[VM] * 3 + [HB] * 7,
        scratch_shapes=[
            *places_for(inputs, which),
            pltpu.VMEM((8, 128, D), BF), pltpu.VMEM((384, D), BF), pltpu.VMEM((8, 384, 128), BF), pltpu.VMEM((2, FF, 128), BF),
            pltpu.VMEM((1024, 384), F32), pltpu.VMEM((8, 512, 128), BF), pltpu.VMEM((2, 4, 8, 128, 128), BF),
            pltpu.VMEM((1024, 128), F32), pltpu.VMEM((1024, 512), BF),
            pltpu.VMEM((16, 128), jnp.int32), pltpu.VMEM((2, 128, 128), F32), pltpu.VMEM((6, 128, 128), F32),
            *pair(14), *pair(8), *pair(8), *pair(6), *pair(16), *pair(2), *pair(28), *pair(7), dma((9,)),
        ],
        compiler_params=params(5),
        name="front",
    )(*inputs)


def everyone():
    return [device for _, device in group_peers()] + [ctx_at(k)[1] for k in range(1, 8)] + [y_partners()[1]]


def tail_kernel(
    sides, arrive, qp_ref, kv_ref, lse_ref, meta_ref, da_ref, x_ref, dy1_ref, stats_ref,
    angles_hbm, wqkv_hbm, n1_hbm, ggu2_ref, gout_ref, piece_down_ref, piece_gu1_ref,
    grad_ref, info_ref, all_down, all_out, all_qkv, all_gu,
    bias, dap, ds, pb, mine, theirs, stage, back, dqkv, dqkv_t, parts, held, got, n1, wqkv, gq,
    piece_gu2, piece_out, piece_qkv, got_gu1, got_gu2, got_qkv, st1, st2, mid, angles, tab_ref,
    co_s, co_r, kv_s, kv_r, rs_s, rs_r, st_s, st_r, st2_s, st2_r, qs_s, qs_r, loc, *side_scratch,
):
    ring = Ring()
    c, _ = ctx_at(0)
    sum_gu2, sum_out, move_gu1, down, out, spread_gu1, move_gu2, sum_qkv, move_qkv, spread_gu2 = sides
    scratch = list(side_scratch)
    places = (
        (ggu2_ref, piece_gu2), (gout_ref, piece_out), (piece_gu1_ref, got_gu1), (piece_down_ref, all_down), (piece_out, all_out),
        (got_gu1, all_gu), (piece_gu2, got_gu2), (gq, piece_qkv), (piece_qkv, got_qkv), (got_gu2, all_gu),
    )
    for side, (i, o) in zip(sides, places):
        side.bind(ring, (i,), (o,), scratch[: len(side.scratch)])
        del scratch[: len(side.scratch)]
    loads = [pltpu.make_async_copy(n1_hbm, n1, loc.at[0]), pltpu.make_async_copy(wqkv_hbm, wqkv, loc.at[1])]
    angles_load = pltpu.make_async_copy(angles_hbm.at[c], angles, loc.at[3])
    for load in loads + [angles_load]:
        load.start()
    meet(everyone())
    arrive()
    sum_gu2.start()
    sum_out.start()
    move_gu1.start()
    group = group_peers()
    here16 = ring.x * 4 + lax.axis_index("y_lo") * 2 + ring.core
    copies = [send(stats_ref, st1.at[here16], (st_s, st_r), k, device) for k, device in group]
    st1[here16] = stats_ref[...]
    lane = lax.broadcasted_iota(jnp.int32, (128, 128), 1)
    angles_load.wait()
    fill_tables(angles, tab_ref)

    def unrope(u, i):
        return u * tab_ref[i] - pltpu.roll(u, 96, 1) * tab_ref[i + 1] - pltpu.roll(u, 32, 1) * tab_ref[i + 2]

    def one(x, core):
        d = x * 2 + core
        rows = pl.ds(pl.multiple_of(d * 128, 128), 128)
        key_bias(meta_ref, d, c, bias)
        for j in range(2):
            tile = da_ref[rows, pl.ds(j * 128, 128)].astype(F32)
            dap[pl.ds(j * 256, 128), :] = jnp.where(lane >= 64, pltpu.roll(tile, 64, 1), 0.0).astype(BF)
            dap[pl.ds(j * 256 + 128, 128), :] = jnp.where(lane >= 64, tile, 0.0).astype(BF)
        kv = kv_ref[core, x].reshape(1024, 128)
        scores = nt(kv, qp_ref[d])
        dprobs = nt(kv, dap[...])
        for h in range(4):
            cols = slice(h * 128, (h + 1) * 128)
            p = jnp.exp(scores[:, cols] + bias[...] - lse_ref[d, 0:1, cols])
            pb[:, cols] = p.astype(BF)
            dp = dprobs[:, cols]
            centre = jnp.sum(p * dp, axis=0, keepdims=True)
            ds[:, cols] = (p * (dp - centre)).astype(BF)
        dkv = nn(ds[...], qp_ref[d]) + nn(pb[...], dap[...])
        dq = nn(kv.T, ds[...]) * 0.125
        for j in range(2):
            two = jnp.concatenate([dq[:64, (2 * j) * 128 : (2 * j + 1) * 128], dq[:64, (2 * j + 1) * 128 : (2 * j + 2) * 128]], axis=0)
            dqkv[rows, pl.ds(j * 128, 128)] = unrope(two.T, 0).astype(BF)
        return dkv

    def core_copy(x):
        return pltpu.make_async_remote_copy(
            src_ref=mine.at[x], dst_ref=theirs.at[x], send_sem=co_s.at[x], recv_sem=co_r.at[x],
            device_id=ring.sibling, device_id_type=MESH,
        )

    def kv_copy(x, k):
        other, device = ctx_at(k)
        return pltpu.make_async_remote_copy(
            src_ref=stage.at[x, other], dst_ref=back.at[x, k - 1], send_sem=kv_s.at[x * 7 + k - 1],
            recv_sem=kv_r.at[x * 7 + k - 1], device_id=device, device_id_type=MESH,
        )

    def both_cores(x, _):
        mine[x] = one(x, 1 - ring.core).astype(BF).reshape(8, 128, 128)
        core_copy(x).start()
        dqkv[pl.ds(pl.multiple_of((x * 2 + 1 - ring.core) * 128, 128), 128), 256:384] = jnp.zeros((128, 128), BF)
        dkv = one(x, ring.core)
        core_copy(x).wait_recv()
        stage[x] = (dkv + theirs[x].reshape(1024, 128).astype(F32)).astype(BF).reshape(8, 128, 128)
        for k in range(1, 8):
            kv_copy(x, k).start()

        @pl.when(x == 1)
        def _():
            sum_gu2.step2()
            sum_out.step2()
            down.start()

        @pl.when(x == 2)
        def _():
            sum_gu2.step3()
            sum_out.step3()

        return 0

    lax.fori_loop(0, 4, both_cores, 0)
    sum_gu2.step4()
    sum_out.step4()
    for copy in copies:
        copy.wait_recv()
    total = st1[0]
    for i in range(1, 16):
        total += st1[i]
    mid[...] = total
    st2[c] = total
    copies2 = [send(mid, st2.at[c], (st2_s, st2_r), k - 1, ctx_at(k)[1]) for k in range(1, 8)]
    sum_gu2.finish()
    move_gu2.start()
    sum_out.finish()
    out.start()
    move_gu1.finish()
    down.middle()

    def gather_up(x, _):
        total = stage[x, c].astype(F32)
        for k in range(1, 8):
            kv_copy(x, k).wait_recv()
            total += back[x, k - 1].astype(F32)
        rows = pl.ds(pl.multiple_of((x * 2 + ring.core) * 128, 128), 128)
        dqkv[rows, 256:384] = unrope(total, 3).astype(BF)
        return 0

    lax.fori_loop(0, 4, gather_up, 0)
    spread_gu1.start()
    for load in loads:
        load.wait()

    rs = Rs(ring, parts, held, got, (rs_s, rs_r))
    for i in range(4):
        x = rs.blocks[i]

        def body(k, _, x=x):
            lanes = lanes_at(k * 512, 512)
            block = nn(dqkv[pl.ds(pl.multiple_of(x * 256, 256), 256), :], wqkv[:, lanes])
            parts[pl.ds(x * 2, 2), :, lanes] = block.astype(BF).reshape(2, 128, 512)
            return 0

        lax.fori_loop(0, 4, body, 0)
        rs.copy(i).start()
        if i == 1:
            rs.send_far()
        elif i == 2:
            rs.send_right()
        elif i == 3:
            rs.send_left()
    dqkv_t[...] = dqkv[...].T

    def grads(k, _):
        lanes = lanes_at(k * 512, 512)
        product = nn(dqkv_t[...], n1[:, :, lanes].reshape(1024, 512))
        gq[:, :, :, lanes] = product.astype(BF).reshape(2, 4, 48, 512)
        return 0

    lax.fori_loop(0, 4, grads, 0)
    sum_qkv.start()
    rs.relay()
    move_gu2.finish()
    spread_gu2.start()
    sum_qkv.step2()
    spread_gu1.middle()
    out.middle()
    sum_qkv.step3()
    for q in range(2):
        for half in range(2):
            rs.ready(half, q)

            def body(k, _, half=half, q=q):
                rows = pl.ds(pl.multiple_of(half * 64 + q * 32 + k * 16, 16), 16)
                grad_ref[rows, :] = back_norm(x_ref[rows, :].astype(F32), dy1_ref[rows, :], rs.total(rows))
                return 0

            lax.fori_loop(0, 2, body, 0)
    sum_qkv.step4()
    sum_qkv.finish()
    move_qkv.start()
    spread_gu2.middle()
    move_qkv.finish()
    spread_qkv = Spread(got_qkv, lambda c: all_qkv.at[:, c], (qs_s, qs_r), 0, False, loc.at[2])
    spread_qkv.start()

    for copy in copies2:
        copy.wait_recv()
    total = st2[0]
    for i in range(1, 8):
        total += st2[i]
    sums = jnp.sum(total, axis=1, keepdims=True)
    squares, count = sums[0:1], sums[1:2]
    scale = 2.0 / (D * count)
    info_ref[...] = jnp.concatenate([squares / count, scale, jnp.zeros((6, 1), F32)], axis=0) + jnp.zeros((8, 128), F32)

    spread_qkv.relay()
    rs.drain()
    for copy in copies + copies2:
        copy.wait_send()

    def drain(x, _):
        core_copy(x).wait_send()
        for k in range(1, 8):
            kv_copy(x, k).wait_send()
        return 0

    lax.fori_loop(0, 4, drain, 0)
    down.finish()
    out.finish()
    spread_gu1.finish()
    spread_gu2.finish()
    spread_qkv.finish()


def tail(qp, kv, lse, metas, da, hidden_in, dy1, stats, angles, wqkv, n1, grad_gu2, grad_out, piece_down, piece_gu1):
    dma = pltpu.SemaphoreType.DMA
    pair = lambda n: [dma((n,)), dma((n,))]
    bf = lambda *shape: jax.ShapeDtypeStruct(shape, BF)
    vm = lambda *shape: pltpu.VMEM(shape, BF)
    sides = [
        SumColumns(grad_gu2), SumRows(grad_out), Move(piece_gu1), SpreadRows(piece_down), SpreadRows(bf(2, 128, 128)),
        SpreadGateUp(bf(8, R1, 128), 0), Move(bf(R2, 1024)), SumColumns(bf(2, 4, 48, D)), Move(bf(48, 1024)),
        SpreadGateUp(bf(8, R2, 128), R1),
    ]
    inputs = (qp, kv, lse, metas, da, hidden_in, dy1, stats, angles, wqkv, n1, grad_gu2, grad_out, piece_down, piece_gu1)
    which = (0, 1, 2, 4, 5, 6, 11, 12, 13, 14)
    return pl.pallas_call(
        loading(functools.partial(tail_kernel, sides), which, 15, 6),
        out_shape=[
            jax.ShapeDtypeStruct((128, D), F32), jax.ShapeDtypeStruct((8, 128), F32),
            bf(352, D), bf(128, D), bf(8, 8, 48, 128), bf(2, FF, 128),
        ],
        in_specs=[HB if i in which or 8 <= i < 11 else VM for i in range(15)],
        out_specs=[VM] * 5 + [HB],
        scratch_shapes=[
            *places_for(inputs, which),
            pltpu.VMEM((1024, 128), F32), vm(512, 128), vm(1024, 512), vm(1024, 512),
            vm(4, 8, 128, 128), vm(4, 8, 128, 128), vm(4, 8, 128, 128), vm(4, 7, 128, 128),
            vm(1024, 384), vm(384, 1024), vm(8, 128, D), vm(3, 128, D), vm(7, 128, D), vm(8, 128, D), vm(384, D), vm(2, 4, 48, D),
            vm(R2, 1024), vm(2, 128, 128), vm(48, 1024), vm(8, R1, 128), vm(8, R2, 128), vm(8, 48, 128),
            pltpu.VMEM((16, 8, 128), F32), pltpu.VMEM((8, 8, 128), F32), pltpu.VMEM((8, 128), F32),
            pltpu.VMEM((2, 128, 128), F32), pltpu.VMEM((6, 128, 128), F32),
            *pair(4), *pair(28), *pair(16), *pair(16), *pair(7), *pair(7), dma((4,)),
            *[s for side in sides for s in side.scratch],
        ],
        compiler_params=params(7),
        name="tail",
    )(*inputs)


def finish_kernel(
    info_ref, gu_ref, g1_ref, g2_ref, wg_ref, wu_ref, down_ref, qkv_ref, wq_ref, wk_ref, wv_ref, out_ref, gin_ref,
    gate_ref, up_ref, down_out, q_ref, k_ref, v_ref, o_ref, input_ref, gain1_ref, gain2_ref, loss_ref,
    total2,
):
    scale = info_ref[1:2, 0:1]
    s1, s2 = column(g1_ref[...].astype(F32) * scale)[:, 0:1], column(g2_ref[...].astype(F32) * scale)[:, 0:1]
    one_matrix = eye()
    step = pl.program_id(0)

    @pl.when(step == 0)
    def _():
        total2[...] = jnp.zeros_like(total2)
        total = jnp.zeros((128, 128), F32)
        for s in range(8):
            for j in range(2):
                f = (s // 2) * 4 + j * 2 + s % 2
                part = nt(one_matrix, qkv_ref[s, j * 128 : (j + 1) * 128])
                total += part * wq_ref[:, f * 128 : (f + 1) * 128].astype(F32)
                q_ref[:, f * 128 : (f + 1) * 128] = part * s1
        for i in range(2):
            both = [qkv_ref[2 * x, 256:].astype(F32) + qkv_ref[2 * x + 1, 256:].astype(F32) for x in (2 * i, 2 * i + 1)]
            for at, w_ref, g_ref in ((0, wk_ref, k_ref), (64, wv_ref, v_ref)):
                part = jnp.concatenate([both[0][at : at + 64], both[1][at : at + 64]], axis=0).T
                total += part * w_ref[:, i * 128 : (i + 1) * 128].astype(F32)
                g_ref[:, i * 128 : (i + 1) * 128] = part * s1
        gain1_ref[...] = jnp.sum(total.T, axis=0, keepdims=True) * scale
        o_ref[...] = out_ref[...].astype(F32) * scale
        input_ref[...] = gin_ref[...] * scale
        loss_ref[...] = info_ref[0:1, 0:1]

    total = total2[...]
    for i, w_ref, g_ref in ((0, wg_ref, gate_ref), (1, wu_ref, up_ref)):
        turned = nt(one_matrix, gu_ref[i])
        g_ref[...] = turned * s2
        weighed = turned * w_ref[...].astype(F32)
        for k in range(22):
            total += weighed[:, k * 128 : (k + 1) * 128]
    total2[...] = total
    down_out[...] = down_ref[...].astype(F32) * scale

    @pl.when(step == pl.num_programs(0) - 1)
    def _():
        gain2_ref[...] = jnp.sum(total2[...].T, axis=0, keepdims=True) * scale


def finish(info, all_gu, g1, g2, w_gate, w_up, down, all_qkv, w_query, w_key, w_value, out, grad_in):
    wide = pl.BlockSpec((128, 2816), lambda i: (0, i))
    rows = pl.BlockSpec((176, D), lambda i: (i, 0))
    whole = lambda *shape: pl.BlockSpec(shape, lambda i: (0,) * len(shape))
    f32 = lambda *shape: jax.ShapeDtypeStruct(shape, F32)
    return pl.pallas_call(
        finish_kernel,
        grid=(2,),
        out_shape=[
            f32(128, FF), f32(128, FF), f32(352, D), f32(128, D), f32(128, KVD), f32(128, KVD), f32(128, D), f32(128, D),
            f32(1, 128), f32(1, 128), f32(1, 1),
        ],
        in_specs=[
            whole(8, 128), pl.BlockSpec((2, 2816, 128), lambda i: (0, i, 0)), whole(1, 128), whole(1, 128), wide, wide, rows,
            whole(8, 384, 128), whole(128, D), whole(128, KVD), whole(128, KVD), whole(128, D), whole(128, D),
        ],
        out_specs=[
            wide, wide, rows, whole(128, D), whole(128, KVD), whole(128, KVD), whole(128, D), whole(128, D),
            whole(1, 128), whole(1, 128), whole(1, 1),
        ],
        scratch_shapes=[pltpu.VMEM((128, 128), F32)],
        compiler_params=pltpu.CompilerParams(vmem_limit_bytes=63 * 2**20),
        name="finish",
    )(info, all_gu, g1, g2, w_gate, w_up, down, all_qkv, w_query, w_key, w_value, out, grad_in)


def local(hidden_in, teacher, doc_ids, valid_mask, norm1_gain, w_query, w_key, w_value, w_out, norm2_gain, w_gate, w_up, w_down):
    g1, g2, valid = norm1_gain[None], norm2_gain[None], valid_mask[None]
    angles = jnp.asarray(rope_angles())
    a, lse, metas, n1, wqkv, qp, kv, wo, wgu, wd = front(
        hidden_in, doc_ids, g1, g2, w_query, w_key, w_value, w_gate, w_up, w_out, w_down, angles
    )
    wo = wo.reshape(256, D)
    layer_out, stats, dy1, da, grad_out, grad_gu2, piece_down, piece_gu1 = middle(a, wo, hidden_in, teacher, valid, wgu, wd)
    grad_in, info, all_down, all_out, all_qkv, all_gu = tail(
        qp, kv, lse, metas, da, hidden_in, dy1, stats, angles, wqkv, n1, grad_gu2, grad_out, piece_down, piece_gu1
    )
    gg, gp, gd, gq, gk, gv, go, input_grad, gain1, gain2, loss = finish(
        info, all_gu, g1, g2, w_gate, w_up, all_down, all_qkv.reshape(8, 384, 128), w_query, w_key, w_value, all_out, grad_in
    )
    return (layer_out, loss[0, 0], input_grad, gain1[0], gq, gk, gv, go, gain2[0], gg, gp, gd)


def solution(mesh):
    fine = Mesh(mesh.devices.reshape(2, 4, 4, 2, 2), AXES)
    rows = ("y_hi", "z", "x", "y_lo", "core")
    fs = ("x", "y_lo", "core")
    token, shard = P(rows, None), P(fs, None)
    return jax.shard_map(
        local,
        mesh=fine,
        in_specs=(token, token, shard, P(rows), P(fs), shard, shard, shard, shard, P(fs), shard, shard, shard),
        out_specs=(token, P(), token, P(fs), shard, shard, shard, shard, P(fs), shard, shard, shard),
        check_vma=False,
    )
```
